32 devices in a mesh: grid: 8 (over z, y), bundle: 4 (over x, core).
Axes of the slice: x: 2, y: 2, z: 4, core: 2. Of those that a mesh axis runs over, the one named last changes fastest.
Arguments:
- cell_state: float32 [24, 32768], P(None, 'grid'), may hold values from -6 to 6
- pore_volume: float32 [32768], P('grid'), may hold values from 0.5 to 5
- request_cell: int32 [4, 8, 8, 32], P(None, 'grid'), may hold values from 0 to 4095, as said below
- node_slot: int32 [4, 16, 2048], P('bundle', 'grid'), may hold values from 0 to 255, as said below
- line_length: int32 [4, 16], P('bundle', 'grid'), may hold values from 128 to 2048, as said below
- courant: float32 [4, 16, 2048], P('bundle', 'grid'), may hold values from 0.3 to 3
- flux_weight: float32 [4, 16, 2048], P('bundle', 'grid'), may hold values from 0.3 to 3
- inflow: float32 [4, 24], P('bundle'), may hold values from -4 to 4
- interaction: float32 [24, 24], replicated, may hold values from -0.18 to 0.18
Outputs:
- new_state: float32 [24, 32768], P(None, 'grid')
The draws below stay inside these ranges and needn't reach their ends.
Inputs may be any that keep to these rules, and one draw needn't show every extreme that they name: `request_cell`: a cell owner's local cell index; one entry is the last cell. `node_slot`: an index into the 256 slots of the device that holds the streamline, slot o * 32 + c belonging to owner o; the last slot is used. `line_length`: live nodes come first on each streamline; some streamline has 2048 and some has 128.
All inputs are finite; a program needn't handle non-finite values.
Results may differ from the reference program's by a relative error of at most 0.0001.
Values sent between devices are 32-bit elements; how exact they have to be, the bound alone decides.
No kernel may reach another device: no remote copies, remote signals or barrier semaphores. Data moves between devices by JAX's collectives and lax.ppermute only.
A program may use at most 64 MiB of HBM per device.

```python
import math
import jax
import jax.numpy as jnp
from jax import lax

SPECIES = 24
CELLS_DEV = 4096
LINES_DEV = 2
NODES = 2048
CAP = 32
SUB = 2
NEWTON = 3
MIN_NODES = 128
OWNERS = 8
BUNDLES = 4
SLOTS = 256
LINES = 16
CELLS = 32768


def draw_request_cell(key, part):
    values = jax.random.randint(key, (BUNDLES, OWNERS, OWNERS, CAP), 0, CELLS_DEV, dtype=jnp.int32)
    return values.at[0, 0, 0, 0].set(CELLS_DEV - 1)


def draw_node_slot(key, part):
    values = jax.random.randint(key, (BUNDLES, LINES, NODES), 0, SLOTS, dtype=jnp.int32)
    return values.at[0, 0, 0].set(SLOTS - 1)


def draw_line_length(key, part):
    first = jax.random.randint(jax.random.fold_in(key, 11), (BUNDLES, LINES), MIN_NODES, NODES + 1, dtype=jnp.int32)
    second = jax.random.randint(jax.random.fold_in(key, 12), (BUNDLES, LINES), MIN_NODES, NODES + 1, dtype=jnp.int32)
    values = jnp.minimum(first, second)
    values = values.at[:, 0].set(NODES)
    return values.at[:, 1].set(MIN_NODES)


def levels(rng, dims, shards, low, high):
    def one(dim, blocks):
        steps = jax.random.uniform(jax.random.fold_in(jax.random.fold_in(rng, 6), dim), (blocks,), jnp.float32, low / len(shards), high / len(shards))
        return jnp.repeat(jnp.exp(steps), dims[dim] // blocks).reshape((-1,) + (1,) * (len(dims) - dim - 1))

    gain = one(*shards[0])
    for cut in shards[1:]:
        gain = gain * one(*cut)
    return gain


def centred(own_key, shape, scale, reach, cuts=(), held_as=jnp.bfloat16):
    entries = jax.random.normal(own_key, shape, jnp.float32) * scale
    if len(cuts) > 0:
        entries = levels(own_key, shape, cuts, -0.22, 0.18) * entries
    return jnp.clip(entries, min=-reach, max=reach).astype(held_as)


def setup_inputs(seed: int = 0) -> dict:
    splits = jax.random.split(jax.random.key(seed), 10)
    cell_state = centred(splits[0], (SPECIES, CELLS), 1.0, 6.0, ((1, 8),), jnp.float32)
    pore_volume = jnp.clip(jnp.exp(math.log(5.0) - 2.3025851 * jax.random.uniform(splits[1], (CELLS,), jnp.float32) ** levels(splits[1], (CELLS,), ((0, 8),), -0.2, 0.2)), 0.5, 5.0)
    request_cell = draw_request_cell(jax.random.fold_in(splits[9], 71), 0)
    node_slot = draw_node_slot(jax.random.fold_in(splits[9], 71), 0)
    line_length = draw_line_length(jax.random.fold_in(splits[9], 71), 0)
    courant = jnp.clip(jnp.exp(math.log(3.0) - 2.3025851 * jax.random.uniform(splits[5], (BUNDLES, LINES, NODES), jnp.float32) ** levels(splits[5], (BUNDLES, LINES, NODES), ((0, 4), (1, 8)), -0.2, 0.2)), 0.3, 3.0)
    flux_weight = jnp.clip(jnp.exp(math.log(3.0) - 2.3025851 * jax.random.uniform(splits[6], (BUNDLES, LINES, NODES), jnp.float32) ** levels(splits[6], (BUNDLES, LINES, NODES), ((0, 4), (1, 8)), -0.2, 0.2)), 0.3, 3.0)
    inflow = centred(splits[7], (BUNDLES, SPECIES), 1.0, 4.0, ((0, 4),), jnp.float32)
    interaction = centred(splits[8], (SPECIES, SPECIES), 0.06, 0.18, (), jnp.float32)
    return {"cell_state": cell_state, "pore_volume": pore_volume, "request_cell": request_cell, "node_slot": node_slot, "line_length": line_length, "courant": courant, "flux_weight": flux_weight, "inflow": inflow, "interaction": interaction}


def transport(state, rate, entry):
    decay = rate / (1.0 + rate)
    source = state / (1.0 + rate)

    def advance(carry, pieces):
        value = pieces[0] * carry + pieces[1]
        return value, value

    initial = jnp.broadcast_to(entry[:, None], state.shape[:2]).astype(jnp.float32)
    final, values = lax.scan(advance, initial, (decay.T, jnp.transpose(source, (2, 0, 1))))
    return jnp.transpose(values, (1, 2, 0))


def speciate(base, interaction):
    iterate = base
    for step in range(NEWTON):
        iterate = base - jnp.dot(interaction, jnp.tanh(iterate), precision=lax.Precision.HIGHEST)
    return iterate


def reference(cell_state, pore_volume, request_cell, node_slot, line_length, courant, flux_weight, inflow, interaction):
    owners = request_cell.shape[1]
    capacity = request_cell.shape[3]
    species = cell_state.shape[0]
    total_cells = cell_state.shape[1]
    offsets = (jnp.arange(owners * capacity, dtype=jnp.int32) // capacity) * (total_cells // owners)
    slot_cell = jnp.transpose(request_cell, (0, 2, 1, 3)).reshape(BUNDLES, owners * owners * capacity)
    slot_cell = slot_cell + jnp.tile(offsets, owners)[None, :]
    weighted_total = jnp.zeros((species, total_cells), jnp.float32)
    flux_total = jnp.zeros((total_cells,), jnp.float32)
    line_device = jnp.arange(LINES, dtype=jnp.int32) // LINES_DEV
    positions = jnp.arange(NODES, dtype=jnp.int32)
    for bundle in range(BUNDLES):
        flat_index = (line_device[:, None] * (owners * capacity) + node_slot[bundle]).astype(jnp.int32)
        node_cell = slot_cell[bundle][flat_index]
        state = cell_state[:, node_cell]
        for substep in range(SUB):
            state = transport(state, courant[bundle], inflow[bundle])
        result = speciate(state.reshape(species, -1), interaction)
        live_mask = positions[None, :] < line_length[bundle][:, None]
        weight = jnp.where(live_mask, flux_weight[bundle], 0.0).reshape(-1)
        flat_cell = node_cell.reshape(-1)
        weighted_total = weighted_total.at[:, flat_cell].add(result * weight[None, :])
        flux_total = flux_total.at[flat_cell].add(weight)
    return (pore_volume[None, :] * cell_state + weighted_total) / (pore_volume[None, :] + flux_total[None, :])
```

```python
import functools

import jax
import jax.numpy as jnp
from jax import lax
from jax.experimental import pallas as pl
from jax.experimental.pallas import tpu as pltpu
from jax.sharding import PartitionSpec as P

SUB = 2
NEWTON = 3
LANES = 128
ROWS = 8
F32 = jnp.float32
BF16 = jnp.bfloat16
VMEM_BYTES = 32 * 1024 * 1024


def repeat_steps(count, body, carry):
    if count == 1:
        return body(0, carry)
    return lax.fori_loop(0, count, body, carry)


def split(value):
    high = value.astype(BF16)
    low = (value - high.astype(F32)).astype(BF16)
    return high, low


def exchange_groups(tiles, cap):
    tiles = list(tiles)
    lane_group = lax.broadcasted_iota(jnp.int32, tiles[0].shape, 1) // cap
    step = 1
    while step < len(tiles):
        keep = (lane_group & step) == 0
        for i in range(len(tiles)):
            if i & step == 0:
                first, second = tiles[i], tiles[i | step]
                tiles[i] = jnp.where(keep, first, pltpu.roll(second, step * cap, 1))
                tiles[i | step] = jnp.where(keep, pltpu.roll(first, LANES - step * cap, 1), second)
        step *= 2
    return tiles


def spread_rows(block, cap):
    groups = block.shape[0]
    wide = jnp.concatenate([block] * groups, axis=1)
    rows = lax.broadcasted_iota(jnp.int32, wide.shape, 0)
    lanes = lax.broadcasted_iota(jnp.int32, wide.shape, 1) // cap
    return jnp.sum(jnp.where(rows == lanes, wide, 0), axis=0, keepdims=True)


def pick_kernel(cell_ref, request_ref, out_ref):
    species, cells = cell_ref.shape
    owners, cap = request_ref.shape[2:]
    groups = LANES // cap
    chunks = owners // (2 * groups)
    highs = cells // LANES
    bundle = lax.axis_index("bundle")
    cell = cell_ref[...]
    stacked = jnp.concatenate(
        [cell[:, LANES * h : LANES * (h + 1)] for h in range(highs)], axis=0
    )
    left = jnp.concatenate(split(stacked), axis=1)

    def chunk(k, carry):
        first = k * 2 * groups
        block = request_ref[bundle, 0, pl.ds(first, 2 * groups), :]
        index = jnp.concatenate(
            [spread_rows(block[:groups], cap), spread_rows(block[groups:], cap)], axis=1
        )
        low = index % LANES
        high = index // LANES
        hot = (lax.broadcasted_iota(jnp.int32, (LANES, 2 * LANES), 0) == low).astype(F32).astype(BF16)
        right = jnp.concatenate([hot, hot], axis=0)
        product = jnp.dot(left, right, preferred_element_type=F32)
        picked = jnp.zeros((species, 2 * LANES), F32)
        for h in range(highs):
            picked = picked + jnp.where(high == h, product[species * h : species * (h + 1)], 0.0)
        blank = jnp.zeros((groups * ROWS - species, 2 * LANES), F32)
        picked = jnp.concatenate([picked, blank], axis=0)
        for half in range(2):
            tiles = exchange_groups(
                [
                    picked[ROWS * g : ROWS * (g + 1), LANES * half : LANES * (half + 1)]
                    for g in range(groups)
                ],
                cap,
            )
            for j in range(groups):
                out_ref[first + half * groups + j] = tiles[j]
        return carry

    repeat_steps(chunks, chunk, 0)


def lines_kernel(
    copies,
    cap,
    table_ref,
    slot_ref,
    length_ref,
    courant_ref,
    flux_ref,
    inflow_ref,
    interaction_ref,
    out_ref,
):
    owners = table_ref.shape[0]
    species = inflow_ref.shape[1]
    lines, nodes = slot_ref.shape[1:]
    groups = species // ROWS
    all_groups = LANES // cap
    blocks = nodes // LANES
    chunk_owners = 2 * all_groups
    chunks = owners // chunk_owners
    total = lines * blocks

    def row(ref, line, block):
        return jnp.broadcast_to(
            ref[0, line : line + 1, LANES * block : LANES * (block + 1)], (ROWS, LANES)
        )

    slots = [row(slot_ref, line, block) for line in range(lines) for block in range(blocks)]

    def gather(k, state):
        columns = []
        for half in range(2):
            columns.append(
                exchange_groups(
                    [table_ref[k * chunk_owners + half * all_groups + j] for j in range(all_groups)],
                    cap,
                )[:groups]
            )
        pieces = []
        for i in range(total):
            local = slots[i] - k * 2 * LANES
            inside = local % LANES
            lower = local < LANES
            for g in range(groups):
                value = jnp.where(
                    lower,
                    jnp.take_along_axis(columns[0][g], inside, axis=1),
                    jnp.take_along_axis(columns[1][g], inside, axis=1),
                )
                if chunks > 1:
                    value = jnp.where((local >= 0) & (local < 2 * LANES), value, state[i * groups + g])
                pieces.append(value)
        return pieces

    start = repeat_steps(
        chunks, gather, [jnp.zeros((ROWS, LANES), F32)] * (total * groups if chunks > 1 else 0)
    )

    lane = lax.broadcasted_iota(jnp.int32, (ROWS, LANES), 1)
    factors, inverse, ends = [], [], []
    for line in range(lines):
        for block in range(blocks):
            rate = row(courant_ref, line, block)
            scale = 1.0 / (1.0 + rate)
            decay = rate * scale
            steps = []
            step = 1
            while step < LANES:
                masked = jnp.where(lane >= step, decay, 0.0)
                steps.append(masked)
                decay = jnp.where(lane >= step, decay * pltpu.roll(decay, step, 1), decay)
                step *= 2
            steps.append(decay)
            factors.append(steps)
            inverse.append(scale)
            ends.append(jnp.broadcast_to(decay[:, LANES - 1 :], (ROWS, LANES)))

    eye = lax.broadcasted_iota(jnp.int32, (species, LANES), 0) == lax.broadcasted_iota(
        jnp.int32, (species, LANES), 1
    )
    padded = jnp.concatenate(
        [inflow_ref[...], jnp.zeros((1, LANES - species), F32)], axis=1
    )
    column = jnp.sum(jnp.where(eye, padded, 0.0), axis=1, keepdims=True)
    entry = jnp.broadcast_to(column, (species, LANES))

    state = list(start)
    for substep in range(SUB):
        for i in range(total):
            for g in range(groups):
                value = state[i * groups + g] * inverse[i]
                step = 1
                for factor in factors[i][:-1]:
                    value = value + factor * pltpu.roll(value, step, 1)
                    step *= 2
                state[i * groups + g] = value
        for line in range(lines):
            for g in range(groups):
                carry = entry[ROWS * g : ROWS * (g + 1)]
                for block in range(blocks):
                    i = line * blocks + block
                    value = state[i * groups + g]
                    last = jnp.broadcast_to(value[:, LANES - 1 :], (ROWS, LANES))
                    state[i * groups + g] = value + factors[i][-1] * carry
                    carry = last + ends[i] * carry

    base = jnp.concatenate(
        [jnp.concatenate(state[i * groups : (i + 1) * groups], axis=0) for i in range(total)],
        axis=1,
    )

    rows = all_groups * ROWS
    blank = jnp.zeros((rows - species, lines * nodes), F32)
    matrix = interaction_ref[...]
    matrix = jnp.concatenate([matrix, jnp.zeros((species, rows - species), F32)], axis=1)
    matrix = jnp.concatenate([matrix, jnp.zeros((rows - species, rows), F32)], axis=0)
    matrix_high, matrix_low = split(matrix)
    left = jnp.concatenate([matrix_high, matrix_low, matrix_high], axis=1)
    iterate = base
    for step in range(NEWTON):
        high, low = split(jnp.concatenate([jnp.tanh(iterate), blank], axis=0))
        right = jnp.concatenate([high, high, low], axis=0)
        iterate = base - jnp.dot(left, right, preferred_element_type=F32)[:species]

    weights = []
    for line in range(lines):
        for block in range(blocks):
            live = lane + LANES * block < length_ref[0, line]
            weights.append(jnp.where(live, row(flux_ref, line, block), 0.0))
    weight = jnp.concatenate(weights, axis=1)
    first_row = lax.broadcasted_iota(jnp.int32, weight.shape, 0) == 0
    scaled = [iterate[ROWS * g : ROWS * (g + 1)] * weight for g in range(groups)]
    scaled.append(jnp.where(first_row, weight, 0.0))
    high, low = split(jnp.concatenate(scaled, axis=0))
    left = jnp.concatenate([high, low], axis=0)
    slot_row = jnp.concatenate([s[:1] for s in slots], axis=1)

    def scatter(k, carry):
        hot = (
            (
                lax.broadcasted_iota(jnp.int32, (2 * LANES, lines * nodes), 0)
                == slot_row - k * 2 * LANES
            )
            .astype(F32)
            .astype(BF16)
        )
        sums = lax.dot_general(
            left, hot, (((1,), (1,)), ((), ())), preferred_element_type=F32
        )
        sums = sums[:rows] + sums[rows:]
        for half in range(2):
            tiles = exchange_groups(
                [
                    sums[ROWS * g : ROWS * (g + 1), LANES * half : LANES * (half + 1)]
                    for g in range(all_groups)
                ],
                cap,
            )
            for j in range(all_groups):
                for copy in range(copies):
                    out_ref[k * chunk_owners + half * all_groups + j, copy] = tiles[j]
        return carry

    repeat_steps(chunks, scatter, 0)


def blend_kernel(sums_ref, request_ref, cell_ref, pore_ref, out_ref):
    owners, bundles = sums_ref.shape[:2]
    species, cells = cell_ref.shape
    cap = request_ref.shape[3]
    groups = LANES // cap
    rows = groups * ROWS
    width = 2 * LANES
    highs = cells // width
    chunks = owners // ROWS
    tiles_each = bundles // groups

    def chunk(k, total):
        values, indices = [], []
        requests = request_ref[:, 0, pl.ds(k * ROWS, ROWS), :]
        for t in range(tiles_each):
            block = jnp.concatenate([requests[t * groups + j] for j in range(groups)], axis=1)
            for d in range(ROWS):
                tiles = exchange_groups(
                    [sums_ref[k * ROWS + d, t * groups + j] for j in range(groups)], cap
                )
                values.append(jnp.concatenate(tiles, axis=0))
                indices.append(block[d : d + 1])
        value = jnp.concatenate(values, axis=1)
        index = jnp.concatenate(indices, axis=1)
        entries = index.shape[1]
        low = index % width
        high = jnp.broadcast_to(index // width, (2 * ROWS, entries)).astype(F32).astype(BF16)
        hot = (
            (lax.broadcasted_iota(jnp.int32, (width, entries), 0) == low).astype(F32).astype(BF16)
        )
        parts = jnp.concatenate(split(value), axis=0)
        pieces = []
        for h in range(highs):
            mask = high == jnp.array(h, BF16)
            for r in range(2 * rows // (2 * ROWS)):
                piece = parts[2 * ROWS * r : 2 * ROWS * (r + 1)]
                pieces.append(jnp.where(mask, piece, jnp.zeros_like(piece)))
        left = jnp.concatenate(pieces, axis=0)
        product = lax.dot_general(
            left, hot, (((1,), (1,)), ((), ())), preferred_element_type=F32
        )
        return product if chunks == 1 else total + product

    total = repeat_steps(
        chunks, chunk, jnp.zeros((highs * 2 * rows, width), F32) if chunks > 1 else 0
    )
    for h in range(highs):
        part = total[2 * rows * h : 2 * rows * (h + 1)]
        part = part[:rows] + part[rows:]
        pore = pore_ref[:, width * h : width * (h + 1)]
        scale = pore + part[species : species + 1]
        columns = slice(width * h, width * (h + 1))
        out_ref[:, columns] = (pore * cell_ref[:, columns] + part[:species]) / scale


def call(kernel, shape, operands, smem=()):
    vmem = pl.BlockSpec(memory_space=pltpu.VMEM)
    scalar = pl.BlockSpec(memory_space=pltpu.SMEM)
    return pl.pallas_call(
        kernel,
        out_shape=jax.ShapeDtypeStruct(shape, F32),
        in_specs=[scalar if i in smem else vmem for i in range(len(operands))],
        out_specs=vmem,
        compiler_params=pltpu.CompilerParams(vmem_limit_bytes=VMEM_BYTES),
    )(*operands)


def shards(
    bundles,
    cell_state,
    pore_volume,
    request_cell,
    node_slot,
    line_length,
    courant,
    flux_weight,
    inflow,
    interaction,
):
    owners = request_cell.shape[2]
    outgoing = call(pick_kernel, (owners, ROWS, LANES), (cell_state, request_cell))
    table = lax.all_to_all(outgoing, "grid", split_axis=0, concat_axis=0, tiled=True)
    sums = call(
        functools.partial(lines_kernel, bundles, request_cell.shape[3]),
        (owners, bundles, ROWS, LANES),
        (table, node_slot, line_length, courant, flux_weight, inflow, interaction),
        smem=(2,),
    )
    sums = sums.reshape(owners * bundles, ROWS, LANES)
    back = lax.all_to_all(sums, ("grid", "bundle"), split_axis=0, concat_axis=0, tiled=True)
    back = back.reshape(owners, bundles, ROWS, LANES)
    return call(
        blend_kernel,
        cell_state.shape,
        (back, request_cell, cell_state, pore_volume[None, :]),
    )


def solution(mesh):
    placed = (
        P(None, "grid"),
        P("grid"),
        P(None, "grid", None, None),
        P("bundle", "grid", None),
        P("bundle", "grid"),
        P("bundle", "grid", None),
        P("bundle", "grid", None),
        P("bundle", None),
        P(),
    )
    return jax.shard_map(
        functools.partial(shards, mesh.shape["bundle"]),
        mesh=mesh,
        in_specs=placed,
        out_specs=P(None, "grid"),
        check_vma=False,
    )
```

```python
import functools

import jax
import jax.numpy as jnp
from jax import lax
from jax.experimental import pallas as pl
from jax.experimental.pallas import tpu as pltpu
from jax.sharding import PartitionSpec as P

SUB = 2
NEWTON = 3
LANES = 128
ROWS = 8
F32 = jnp.float32
BF16 = jnp.bfloat16
VMEM_BYTES = 32 * 1024 * 1024


def repeat_steps(count, body, carry):
    if count == 1:
        return body(0, carry)
    return lax.fori_loop(0, count, body, carry)


def split(value):
    high = value.astype(BF16)
    low = (value - high.astype(F32)).astype(BF16)
    return high, low


def exchange_groups(tiles, cap):
    tiles = list(tiles)
    lane_group = lax.broadcasted_iota(jnp.int32, tiles[0].shape, 1) // cap
    step = 1
    while step < len(tiles):
        keep = (lane_group & step) == 0
        for i in range(len(tiles)):
            if i & step == 0:
                first, second = tiles[i], tiles[i | step]
                tiles[i] = jnp.where(keep, first, pltpu.roll(second, step * cap, 1))
                tiles[i | step] = jnp.where(keep, pltpu.roll(first, LANES - step * cap, 1), second)
        step *= 2
    return tiles


def spread_rows(block, cap):
    groups = block.shape[0]
    wide = jnp.concatenate([block] * groups, axis=1)
    rows = lax.broadcasted_iota(jnp.int32, wide.shape, 0)
    lanes = lax.broadcasted_iota(jnp.int32, wide.shape, 1) // cap
    return jnp.sum(jnp.where(rows == lanes, wide, 0), axis=0, keepdims=True)


def pick_kernel(cell_ref, request_ref, out_ref):
    species, cells = cell_ref.shape
    owners, cap = request_ref.shape[2:]
    groups = LANES // cap
    chunks = owners // (2 * groups)
    highs = cells // LANES
    bundle = lax.axis_index("bundle")
    cell = cell_ref[...]
    stacked = jnp.concatenate(
        [cell[:, LANES * h : LANES * (h + 1)] for h in range(highs)], axis=0
    )
    left = jnp.concatenate(split(stacked), axis=1)

    def chunk(k, carry):
        first = k * 2 * groups
        block = request_ref[bundle, 0, pl.ds(first, 2 * groups), :]
        index = jnp.concatenate(
            [spread_rows(block[:groups], cap), spread_rows(block[groups:], cap)], axis=1
        )
        low = index % LANES
        high = index // LANES
        hot = (lax.broadcasted_iota(jnp.int32, (LANES, 2 * LANES), 0) == low).astype(F32).astype(BF16)
        right = jnp.concatenate([hot, hot], axis=0)
        product = jnp.dot(left, right, preferred_element_type=F32)
        picked = jnp.zeros((species, 2 * LANES), F32)
        for h in range(highs):
            picked = picked + jnp.where(high == h, product[species * h : species * (h + 1)], 0.0)
        blank = jnp.zeros((groups * ROWS - species, 2 * LANES), F32)
        picked = jnp.concatenate([picked, blank], axis=0)
        for half in range(2):
            tiles = exchange_groups(
                [
                    picked[ROWS * g : ROWS * (g + 1), LANES * half : LANES * (half + 1)]
                    for g in range(groups)
                ],
                cap,
            )
            for j in range(groups):
                out_ref[first + half * groups + j] = tiles[j]
        return carry

    repeat_steps(chunks, chunk, 0)


def to_segments(refs):
    lines, nodes = refs[0].shape[1:]
    blocks = nodes // LANES
    width = lines * blocks
    groups = LANES // width
    stacked = []
    for ref in refs:
        value = ref[0].astype(F32)
        stacked += [value[:, LANES * block : LANES * (block + 1)] for block in range(blocks)]
    stacked.append(jnp.zeros((LANES - width * len(refs), LANES), F32))
    turned = jnp.transpose(jnp.concatenate(stacked, axis=0))
    times = LANES // groups
    return exchange_groups([turned[times * g : times * (g + 1)] for g in range(groups)], width)


def lines_kernel(
    copies,
    cap,
    table_ref,
    slot_ref,
    length_ref,
    courant_ref,
    flux_ref,
    inflow_ref,
    interaction_ref,
    out_ref,
):
    owners = table_ref.shape[0]
    species = inflow_ref.shape[1]
    lines, nodes = slot_ref.shape[1:]
    groups = species // ROWS
    all_groups = LANES // cap
    rows = all_groups * ROWS
    blocks = nodes // LANES
    width = lines * blocks
    segments = LANES // width
    times = LANES // segments
    chunk_owners = 2 * all_groups
    chunks = owners // chunk_owners
    slot, courant, flux = to_segments([slot_ref, courant_ref, flux_ref])[:3]

    def hot(k):
        local = (slot - (k * 2 * LANES)).astype(BF16) if chunks == 1 else (
            slot - lax.convert_element_type(k * 2 * LANES, F32)
        ).astype(BF16)
        index = lax.broadcasted_iota(jnp.int32, (2 * LANES, LANES), 0).astype(F32).astype(BF16)
        one, zero = jnp.ones_like(index), jnp.zeros_like(index)
        return jnp.concatenate(
            [
                jnp.where(jnp.broadcast_to(local[t : t + 1], index.shape) == index, one, zero)
                for t in range(times)
            ],
            axis=1,
        )

    kept = hot(0) if chunks == 1 else None

    def gather(k, state):
        halves = []
        for half in range(2):
            first = k * chunk_owners + half * all_groups
            halves.append(
                jnp.concatenate(
                    exchange_groups([table_ref[first + j] for j in range(all_groups)], cap), axis=0
                )
            )
        left = jnp.concatenate(split(jnp.concatenate(halves, axis=1)), axis=0)
        found = jnp.dot(left, hot(k) if kept is None else kept, preferred_element_type=F32)
        found = found[:species] + found[rows : rows + species]
        return found if chunks == 1 else state + found

    start = repeat_steps(
        chunks, gather, jnp.zeros((species, lines * nodes), F32) if chunks > 1 else 0
    )

    lane = lax.broadcasted_iota(jnp.int32, (ROWS, LANES), 1)
    part = lane // width
    block = (lane % width) // lines
    segment = block * segments + part
    line = lane % lines

    def earlier(value, distance):
        major, minor = distance // segments, distance % segments
        near = pltpu.roll(value, minor * width + major * lines, 1)
        if minor == 0:
            return near
        far = pltpu.roll(value, minor * width + (major + 1) * lines, 1)
        return jnp.where(part >= minor, near, far)

    eye = lax.broadcasted_iota(jnp.int32, (species, LANES), 0) == lax.broadcasted_iota(
        jnp.int32, (species, LANES), 1
    )
    padded = jnp.concatenate([inflow_ref[...], jnp.zeros((1, LANES - species), F32)], axis=1)
    column = jnp.sum(jnp.where(eye, padded, 0.0), axis=1, keepdims=True)
    entry = jnp.broadcast_to(column, (species, LANES))
    entry = [entry[ROWS * g : ROWS * (g + 1)] for g in range(groups)]

    scale = 1.0 / (1.0 + courant)
    decay = courant * scale
    first = [None] * groups
    second = [None] * groups
    local, ones, twos = [], [], []
    for t in range(times):
        scale_t = jnp.broadcast_to(scale[t : t + 1], (ROWS, LANES))
        decay_t = jnp.broadcast_to(decay[t : t + 1], (ROWS, LANES))
        one = decay_t if t == 0 else decay_t * ones[-1]
        two = scale_t * one if t == 0 else scale_t * one + decay_t * twos[-1]
        ones.append(one)
        twos.append(two)
        for g in range(groups):
            value = start[ROWS * g : ROWS * (g + 1), LANES * t : LANES * (t + 1)] * scale_t
            first[g] = value if t == 0 else value + decay_t * first[g]
            value = scale_t * first[g]
            second[g] = value if t == 0 else value + decay_t * second[g]
            local.append(second[g])

    a, b = ones[-1], twos[-1]
    head = segment == 0
    first = [jnp.where(head, f + a * e, f) for f, e in zip(first, entry)]
    second = [jnp.where(head, s + b * e + a * e, s) for s, e in zip(second, entry)]
    distance = 1
    while distance < blocks * segments:
        open_ = segment >= distance
        a_open, b_open = jnp.where(open_, a, 0.0), jnp.where(open_, b, 0.0)
        ahead = [earlier(f, distance) for f in first]
        second = [
            s + b_open * f + a_open * earlier(s, distance) for s, f in zip(second, ahead)
        ]
        first = [f + a_open * e for f, e in zip(first, ahead)]
        if 2 * distance < blocks * segments:
            a_ahead = earlier(a, distance)
            b = b * a_ahead + a * earlier(b, distance)
            a = a * a_ahead
        distance *= 2
    carry_one = [jnp.where(head, e, earlier(f, 1)) for e, f in zip(entry, first)]
    carry_two = [jnp.where(head, e, earlier(s, 1)) for e, s in zip(entry, second)]
    columns = []
    for t in range(times):
        columns.append(
            jnp.concatenate(
                [
                    local[t * groups + g] + twos[t] * carry_one[g] + ones[t] * carry_two[g]
                    for g in range(groups)
                ],
                axis=0,
            )
        )
    base = jnp.concatenate(columns, axis=1)

    blank = jnp.zeros((rows - species, lines * nodes), F32)
    matrix = interaction_ref[...]
    matrix = jnp.concatenate([matrix, jnp.zeros((species, rows - species), F32)], axis=1)
    matrix = jnp.concatenate([matrix, jnp.zeros((rows - species, rows), F32)], axis=0)
    matrix_high, matrix_low = split(matrix)
    left = jnp.concatenate([matrix_high, matrix_low, matrix_high], axis=1)
    iterate = base
    for step in range(NEWTON):
        high, low = split(jnp.concatenate([jnp.tanh(iterate), blank], axis=0))
        right = jnp.concatenate([high, high, low], axis=0)
        iterate = base - jnp.dot(left, right, preferred_element_type=F32)[:species]

    length = jnp.zeros((ROWS, LANES), jnp.int32)
    for one_line in range(lines):
        length = jnp.where(line == one_line, length_ref[0, one_line], length)
    node = block * LANES + part * times
    weights = []
    for t in range(times):
        weights.append(
            jnp.where(node + t < length, jnp.broadcast_to(flux[t : t + 1], (ROWS, LANES)), 0.0)
        )
    weight = jnp.concatenate(weights, axis=1)
    first_row = lax.broadcasted_iota(jnp.int32, weight.shape, 0) == 0
    scaled = [iterate[ROWS * g : ROWS * (g + 1)] * weight for g in range(groups)]
    scaled.append(jnp.where(first_row, weight, 0.0))
    left = jnp.concatenate(split(jnp.concatenate(scaled, axis=0)), axis=0)

    def scatter(k, carry):
        sums = lax.dot_general(
            left,
            hot(k) if kept is None else kept,
            (((1,), (1,)), ((), ())),
            preferred_element_type=F32,
        )
        sums = sums[:rows] + sums[rows:]
        for half in range(2):
            tiles = exchange_groups(
                [
                    sums[ROWS * g : ROWS * (g + 1), LANES * half : LANES * (half + 1)]
                    for g in range(all_groups)
                ],
                cap,
            )
            for j in range(all_groups):
                for copy in range(copies):
                    out_ref[k * chunk_owners + half * all_groups + j, copy] = tiles[j]
        return carry

    repeat_steps(chunks, scatter, 0)


def blend_kernel(sums_ref, request_ref, cell_ref, pore_ref, out_ref):
    owners, bundles = sums_ref.shape[:2]
    species, cells = cell_ref.shape
    cap = request_ref.shape[3]
    groups = LANES // cap
    rows = groups * ROWS
    width = 2 * LANES
    highs = cells // width
    chunks = owners // ROWS
    tiles_each = bundles // groups

    def chunk(k, total):
        values, indices = [], []
        requests = request_ref[:, 0, pl.ds(k * ROWS, ROWS), :]
        for t in range(tiles_each):
            block = jnp.concatenate([requests[t * groups + j] for j in range(groups)], axis=1)
            for d in range(ROWS):
                tiles = exchange_groups(
                    [sums_ref[k * ROWS + d, t * groups + j] for j in range(groups)], cap
                )
                values.append(jnp.concatenate(tiles, axis=0))
                indices.append(block[d : d + 1])
        value = jnp.concatenate(values, axis=1)
        index = jnp.concatenate(indices, axis=1)
        entries = index.shape[1]
        low = index % width
        high = jnp.broadcast_to(index // width, (2 * ROWS, entries)).astype(F32).astype(BF16)
        hot = (
            (lax.broadcasted_iota(jnp.int32, (width, entries), 0) == low).astype(F32).astype(BF16)
        )
        parts = jnp.concatenate(split(value), axis=0)
        pieces = []
        for h in range(highs):
            mask = high == jnp.array(h, BF16)
            for r in range(2 * rows // (2 * ROWS)):
                piece = parts[2 * ROWS * r : 2 * ROWS * (r + 1)]
                pieces.append(jnp.where(mask, piece, jnp.zeros_like(piece)))
        left = jnp.concatenate(pieces, axis=0)
        product = lax.dot_general(
            left, hot, (((1,), (1,)), ((), ())), preferred_element_type=F32
        )
        return product if chunks == 1 else total + product

    total = repeat_steps(
        chunks, chunk, jnp.zeros((highs * 2 * rows, width), F32) if chunks > 1 else 0
    )
    for h in range(highs):
        part = total[2 * rows * h : 2 * rows * (h + 1)]
        part = part[:rows] + part[rows:]
        pore = pore_ref[:, width * h : width * (h + 1)]
        scale = pore + part[species : species + 1]
        columns = slice(width * h, width * (h + 1))
        out_ref[:, columns] = (pore * cell_ref[:, columns] + part[:species]) / scale


def call(kernel, shape, operands, smem=()):
    vmem = pl.BlockSpec(memory_space=pltpu.VMEM)
    scalar = pl.BlockSpec(memory_space=pltpu.SMEM)
    return pl.pallas_call(
        kernel,
        out_shape=jax.ShapeDtypeStruct(shape, F32),
        in_specs=[scalar if i in smem else vmem for i in range(len(operands))],
        out_specs=vmem,
        compiler_params=pltpu.CompilerParams(vmem_limit_bytes=VMEM_BYTES),
    )(*operands)


def shards(
    bundles,
    cell_state,
    pore_volume,
    request_cell,
    node_slot,
    line_length,
    courant,
    flux_weight,
    inflow,
    interaction,
):
    owners = request_cell.shape[2]
    outgoing = call(pick_kernel, (owners, ROWS, LANES), (cell_state, request_cell))
    table = lax.all_to_all(outgoing, "grid", split_axis=0, concat_axis=0, tiled=True)
    sums = call(
        functools.partial(lines_kernel, bundles, request_cell.shape[3]),
        (owners, bundles, ROWS, LANES),
        (table, node_slot, line_length, courant, flux_weight, inflow, interaction),
        smem=(2,),
    )
    sums = sums.reshape(owners * bundles, ROWS, LANES)
    back = lax.all_to_all(sums, ("grid", "bundle"), split_axis=0, concat_axis=0, tiled=True)
    back = back.reshape(owners, bundles, ROWS, LANES)
    return call(
        blend_kernel,
        cell_state.shape,
        (back, request_cell, cell_state, pore_volume[None, :]),
    )


def solution(mesh):
    placed = (
        P(None, "grid"),
        P("grid"),
        P(None, "grid", None, None),
        P("bundle", "grid", None),
        P("bundle", "grid"),
        P("bundle", "grid", None),
        P("bundle", "grid", None),
        P("bundle", None),
        P(),
    )
    return jax.shard_map(
        functools.partial(shards, mesh.shape["bundle"]),
        mesh=mesh,
        in_specs=placed,
        out_specs=P(None, "grid"),
        check_vma=False,
    )
```

```python
import functools

import jax
import jax.numpy as jnp
from jax import lax
from jax.experimental import pallas as pl
from jax.experimental.pallas import tpu as pltpu
from jax.sharding import PartitionSpec as P

SUB = 2
NEWTON = 3
LANES = 128
ROWS = 8
F32 = jnp.float32
BF16 = jnp.bfloat16
VMEM_BYTES = 32 * 1024 * 1024
DIRECT = 16


def repeat_steps(count, body, carry):
    if count == 1:
        return body(0, carry)
    return lax.fori_loop(0, count, body, carry)


def split(value):
    high = value.astype(BF16)
    low = (value - high.astype(F32)).astype(BF16)
    return high, low


def exchange_groups(tiles, cap):
    tiles = list(tiles)
    lane_group = lax.broadcasted_iota(jnp.int32, tiles[0].shape, 1) // cap
    step = 1
    while step < len(tiles):
        keep = (lane_group & step) == 0
        for i in range(len(tiles)):
            if i & step == 0:
                first, second = tiles[i], tiles[i | step]
                tiles[i] = jnp.where(keep, first, pltpu.roll(second, step * cap, 1))
                tiles[i | step] = jnp.where(keep, pltpu.roll(first, LANES - step * cap, 1), second)
        step *= 2
    return tiles


def spread_rows(block, cap):
    groups = block.shape[0]
    wide = jnp.concatenate([block] * groups, axis=1)
    rows = lax.broadcasted_iota(jnp.int32, wide.shape, 0)
    lanes = lax.broadcasted_iota(jnp.int32, wide.shape, 1) // cap
    return jnp.sum(jnp.where(rows == lanes, wide, 0), axis=0, keepdims=True)


def pick_kernel(cell_hbm, request_hbm, *refs):
    *out_refs, cell_ref, request_ref, tile_ref, cell_sem, request_sem = refs
    request_copy = pltpu.make_async_copy(
        request_hbm.at[lax.axis_index("bundle"), 0], request_ref, request_sem
    )
    cell_copy = pltpu.make_async_copy(cell_hbm, cell_ref, cell_sem)
    request_copy.start()
    cell_copy.start()
    species, cells = cell_ref.shape
    owners, cap = request_ref.shape
    groups = LANES // cap
    chunks = owners // (2 * groups)
    highs = cells // LANES
    request_copy.wait()

    def wanted(k):
        block = request_ref[pl.ds(k * 2 * groups, 2 * groups), :]
        index = jnp.concatenate(
            [spread_rows(block[:groups], cap), spread_rows(block[groups:], cap)], axis=1
        )
        low = index % LANES
        high = index // LANES
        hot = (lax.broadcasted_iota(jnp.int32, (LANES, 2 * LANES), 0) == low).astype(F32).astype(BF16)
        return high, jnp.concatenate([hot, hot], axis=0)

    kept = wanted(0) if chunks == 1 else None
    cell_copy.wait()
    cell = cell_ref[...]
    stacked = jnp.concatenate(
        [cell[:, LANES * h : LANES * (h + 1)] for h in range(highs)], axis=0
    )
    left = jnp.concatenate(split(stacked), axis=1)
    direct = len(out_refs) > 1
    into = tile_ref if direct else out_refs[0]

    def chunk(k, carry):
        first = k * 2 * groups
        high, right = wanted(k) if kept is None else kept
        product = jnp.dot(left, right, preferred_element_type=F32)
        picked = jnp.zeros((species, 2 * LANES), F32)
        for h in range(highs):
            picked = picked + jnp.where(high == h, product[species * h : species * (h + 1)], 0.0)
        blank = jnp.zeros((groups * ROWS - species, 2 * LANES), F32)
        picked = jnp.concatenate([picked, blank], axis=0)
        for half in range(2):
            tiles = exchange_groups(
                [
                    picked[ROWS * g : ROWS * (g + 1), LANES * half : LANES * (half + 1)]
                    for g in range(groups)
                ],
                cap,
            )
            for j in range(groups):
                into[first + half * groups + j] = tiles[j]
        return carry

    repeat_steps(chunks, chunk, 0)
    if direct:
        here = lax.axis_index("grid")
        for j in range(owners):
            out_refs[j][...] = tile_ref[lax.rem(here + j, owners)]


def to_segments(refs):
    lines, nodes = refs[0].shape[1:]
    blocks = nodes // LANES
    width = lines * blocks
    groups = LANES // width
    stacked = []
    for ref in refs:
        value = ref[0].astype(F32)
        stacked += [value[:, LANES * block : LANES * (block + 1)] for block in range(blocks)]
    stacked.append(jnp.zeros((LANES - width * len(refs), LANES), F32))
    turned = jnp.transpose(jnp.concatenate(stacked, axis=0))
    times = LANES // groups
    return exchange_groups([turned[times * g : times * (g + 1)] for g in range(groups)], width)


def one_hot(slot, k):
    local = (slot - lax.convert_element_type(k * 2 * LANES, F32)).astype(BF16)
    index = lax.broadcasted_iota(jnp.int32, (2 * LANES, LANES), 0).astype(F32).astype(BF16)
    one, zero = jnp.ones_like(index), jnp.zeros_like(index)
    return jnp.concatenate(
        [
            jnp.where(jnp.broadcast_to(local[t : t + 1], index.shape) == index, one, zero)
            for t in range(slot.shape[0])
        ],
        axis=1,
    )


class Places:
    def __init__(self, lines, nodes):
        self.lines = lines
        self.blocks = nodes // LANES
        self.width = lines * self.blocks
        self.segments = LANES // self.width
        self.times = LANES // self.segments
        lane = lax.broadcasted_iota(jnp.int32, (ROWS, LANES), 1)
        self.part = lane // self.width
        self.block = (lane % self.width) // lines
        self.segment = self.block * self.segments + self.part
        self.line = lane % lines
        self.distances = []
        distance = 1
        while distance < self.blocks * self.segments:
            self.distances.append(distance)
            distance *= 2

    def earlier(self, value, distance):
        major, minor = distance // self.segments, distance % self.segments
        near = pltpu.roll(value, minor * self.width + major * self.lines, 1)
        if minor == 0:
            return near
        far = pltpu.roll(value, minor * self.width + (major + 1) * self.lines, 1)
        return jnp.where(self.part >= minor, near, far)


def prepare_kernel(slot_ref, length_ref, courant_ref, flux_ref, rows_ref, jump_ref, *hot_refs):
    lines, nodes = slot_ref.shape[1:]
    places = Places(lines, nodes)
    times = places.times
    slot, courant, flux = to_segments([slot_ref, courant_ref, flux_ref])[:3]
    scale = 1.0 / (1.0 + courant)
    decay = courant * scale
    rows_ref[0] = scale
    rows_ref[1] = decay
    rows_ref[5] = slot

    one, two = decay[:1], scale[:1] * decay[:1]
    ones, twos = [one], [two]
    for t in range(1, times):
        one = decay[t : t + 1] * one
        two = scale[t : t + 1] * one + decay[t : t + 1] * two
        ones.append(one)
        twos.append(two)
    rows_ref[2] = jnp.concatenate(ones, axis=0)
    rows_ref[3] = jnp.concatenate(twos, axis=0)

    a = jnp.broadcast_to(one, (ROWS, LANES))
    b = jnp.broadcast_to(two, (ROWS, LANES))
    jump_ref[0], jump_ref[1] = a, b
    for i, distance in enumerate(places.distances):
        opened = places.segment >= distance
        jump_ref[2 * i + 2] = jnp.where(opened, a, 0.0)
        jump_ref[2 * i + 3] = jnp.where(opened, b, 0.0)
        ahead = places.earlier(a, distance)
        b = b * ahead + a * places.earlier(b, distance)
        a = a * ahead

    length = jnp.zeros((ROWS, LANES), jnp.int32)
    for line in range(lines):
        length = jnp.where(places.line == line, length_ref[0, line], length)
    start = places.block * LANES + places.part * times - length
    step = lax.broadcasted_iota(jnp.int32, flux.shape, 0)
    rows_ref[4] = jnp.where(step + start[:1] < 0, flux, 0.0)

    for hot_ref in hot_refs:
        hot_ref[...] = one_hot(slot, 0)


def lines_kernel(lines, cap, tables, kept, *refs):
    table_refs, refs = refs[:tables], refs[tables:]
    rows_ref, jump_ref, inflow_ref, interaction_ref = refs[:4]
    refs = refs[4:]
    hot_ref, refs = (refs[0], refs[1:]) if kept else (None, refs)
    *out_refs, tile_ref = refs
    direct = tables > 1
    all_groups = LANES // cap
    owners = tables if direct else table_refs[0].shape[0]
    here = lax.axis_index("grid")
    if direct:
        for j in range(owners):
            tile_ref[lax.rem(here + (owners - j), owners)] = table_refs[j][...]
    table_ref = tile_ref if direct else table_refs[0]
    species = inflow_ref.shape[1]
    times = rows_ref.shape[1]
    nodes = times * LANES // lines
    places = Places(lines, nodes)
    groups = species // ROWS
    rows = all_groups * ROWS
    chunk_owners = 2 * all_groups
    chunks = owners // chunk_owners

    def hot(k):
        return hot_ref[...] if kept else one_hot(rows_ref[5], k)

    def gather(k, state):
        halves = []
        for half in range(2):
            first = k * chunk_owners + half * all_groups
            halves.append(
                jnp.concatenate(
                    exchange_groups([table_ref[first + j] for j in range(all_groups)], cap), axis=0
                )
            )
        left = jnp.concatenate(split(jnp.concatenate(halves, axis=1)), axis=0)
        found = jnp.dot(left, hot(k), preferred_element_type=F32)
        found = found[:species] + found[rows : rows + species]
        return found if chunks == 1 else state + found

    start = repeat_steps(
        chunks, gather, jnp.zeros((species, lines * nodes), F32) if chunks > 1 else 0
    )

    eye = lax.broadcasted_iota(jnp.int32, (species, LANES), 0) == lax.broadcasted_iota(
        jnp.int32, (species, LANES), 1
    )
    padded = jnp.concatenate([inflow_ref[...], jnp.zeros((1, LANES - species), F32)], axis=1)
    column = jnp.sum(jnp.where(eye, padded, 0.0), axis=1, keepdims=True)
    entry = jnp.broadcast_to(column, (species, LANES))
    entry = [entry[ROWS * g : ROWS * (g + 1)] for g in range(groups)]

    def row(kind, t):
        return jnp.broadcast_to(rows_ref[kind, t : t + 1], (ROWS, LANES))

    first = [None] * groups
    second = [None] * groups
    local = []
    for t in range(times):
        scale, decay = row(0, t), row(1, t)
        for g in range(groups):
            value = start[ROWS * g : ROWS * (g + 1), LANES * t : LANES * (t + 1)] * scale
            first[g] = value if t == 0 else value + decay * first[g]
            value = scale * first[g]
            second[g] = value if t == 0 else value + decay * second[g]
            local.append(second[g])

    a, b = jump_ref[0], jump_ref[1]
    head = places.segment == 0
    first = [jnp.where(head, f + a * e, f) for f, e in zip(first, entry)]
    second = [jnp.where(head, s + b * e + a * e, s) for s, e in zip(second, entry)]
    for i, distance in enumerate(places.distances):
        a, b = jump_ref[2 * i + 2], jump_ref[2 * i + 3]
        ahead = [places.earlier(f, distance) for f in first]
        second = [s + b * f + a * places.earlier(s, distance) for s, f in zip(second, ahead)]
        first = [f + a * e for f, e in zip(first, ahead)]
    carry_one = [jnp.where(head, e, places.earlier(f, 1)) for e, f in zip(entry, first)]
    carry_two = [jnp.where(head, e, places.earlier(s, 1)) for e, s in zip(entry, second)]
    columns = []
    for t in range(times):
        one, two = row(2, t), row(3, t)
        columns.append(
            jnp.concatenate(
                [
                    local[t * groups + g] + two * carry_one[g] + one * carry_two[g]
                    for g in range(groups)
                ],
                axis=0,
            )
        )
    base = jnp.concatenate(columns, axis=1)

    blank = jnp.zeros((rows - species, lines * nodes), F32)
    matrix = interaction_ref[...]
    matrix = jnp.concatenate([matrix, jnp.zeros((species, rows - species), F32)], axis=1)
    matrix = jnp.concatenate([matrix, jnp.zeros((rows - species, rows), F32)], axis=0)
    matrix_high, matrix_low = split(matrix)
    left = jnp.concatenate([matrix_high, matrix_low, matrix_high], axis=1)
    iterate = base
    for step in range(NEWTON):
        high, low = split(jnp.concatenate([jnp.tanh(iterate), blank], axis=0))
        right = jnp.concatenate([high, high, low], axis=0)
        iterate = base - jnp.dot(left, right, preferred_element_type=F32)[:species]

    weight = jnp.concatenate([row(4, t) for t in range(times)], axis=1)
    first_row = lax.broadcasted_iota(jnp.int32, weight.shape, 0) == 0
    scaled = [iterate[ROWS * g : ROWS * (g + 1)] * weight for g in range(groups)]
    scaled.append(jnp.where(first_row, weight, 0.0))
    left = jnp.concatenate(split(jnp.concatenate(scaled, axis=0)), axis=0)
    into = tile_ref if direct else out_refs[0]

    def scatter(k, carry):
        sums = lax.dot_general(
            left, hot(k), (((1,), (1,)), ((), ())), preferred_element_type=F32
        )
        sums = sums[:rows] + sums[rows:]
        for half in range(2):
            tiles = exchange_groups(
                [
                    sums[ROWS * g : ROWS * (g + 1), LANES * half : LANES * (half + 1)]
                    for g in range(all_groups)
                ],
                cap,
            )
            for j in range(all_groups):
                into[k * chunk_owners + half * all_groups + j] = tiles[j]
        return carry

    repeat_steps(chunks, scatter, 0)
    if direct:
        for j in range(owners):
            out_refs[j][...] = tile_ref[lax.rem(here + j, owners)]


def blend_kernel(bundles, *refs):
    sums_refs, refs = refs[:bundles], refs[bundles:]
    request_ref, cell_ref, pore_ref, out_ref = refs
    owners = sums_refs[0].shape[0]
    bundle_here = lax.axis_index("bundle")
    species, cells = cell_ref.shape
    cap = request_ref.shape[3]
    groups = LANES // cap
    rows = groups * ROWS
    width = 2 * LANES
    highs = cells // width
    chunks = owners // ROWS
    tiles_each = bundles // groups

    def chunk(k, total):
        values, indices = [], []
        for t in range(tiles_each):
            block = jnp.concatenate(
                [
                    request_ref[
                        lax.rem(bundle_here + (bundles - t * groups - j), bundles),
                        0,
                        pl.ds(k * ROWS, ROWS),
                        :,
                    ]
                    for j in range(groups)
                ],
                axis=1,
            )
            for d in range(ROWS):
                tiles = exchange_groups(
                    [sums_refs[t * groups + j][k * ROWS + d] for j in range(groups)], cap
                )
                values.append(jnp.concatenate(tiles, axis=0))
                indices.append(block[d : d + 1])
        value = jnp.concatenate(values, axis=1)
        index = jnp.concatenate(indices, axis=1)
        entries = index.shape[1]
        low = index % width
        high = jnp.broadcast_to(index // width, (2 * ROWS, entries)).astype(F32).astype(BF16)
        hot = (
            (lax.broadcasted_iota(jnp.int32, (width, entries), 0) == low).astype(F32).astype(BF16)
        )
        parts = jnp.concatenate(split(value), axis=0)
        pieces = []
        for h in range(highs):
            mask = high == jnp.array(h, BF16)
            for r in range(2 * rows // (2 * ROWS)):
                piece = parts[2 * ROWS * r : 2 * ROWS * (r + 1)]
                pieces.append(jnp.where(mask, piece, jnp.zeros_like(piece)))
        left = jnp.concatenate(pieces, axis=0)
        product = lax.dot_general(
            left, hot, (((1,), (1,)), ((), ())), preferred_element_type=F32
        )
        return product if chunks == 1 else total + product

    total = repeat_steps(
        chunks, chunk, jnp.zeros((highs * 2 * rows, width), F32) if chunks > 1 else 0
    )
    for h in range(highs):
        part = total[2 * rows * h : 2 * rows * (h + 1)]
        part = part[:rows] + part[rows:]
        pore = pore_ref[:, width * h : width * (h + 1)]
        scale = pore + part[species : species + 1]
        columns = slice(width * h, width * (h + 1))
        out_ref[:, columns] = (pore * cell_ref[:, columns] + part[:species]) / scale


def call(kernel, shapes, operands, smem=(), hbm=(), scratch=(), flops=0):
    kinds = {i: pltpu.SMEM for i in smem} | {i: pltpu.HBM for i in hbm}
    return pl.pallas_call(
        kernel,
        out_shape=[jax.ShapeDtypeStruct(shape, kind) for shape, kind in shapes],
        in_specs=[
            pl.BlockSpec(memory_space=kinds.get(i, pltpu.VMEM)) for i in range(len(operands))
        ],
        out_specs=[pl.BlockSpec(memory_space=pltpu.VMEM)] * len(shapes),
        scratch_shapes=list(scratch),
        compiler_params=pltpu.CompilerParams(vmem_limit_bytes=VMEM_BYTES),
        cost_estimate=pl.CostEstimate(flops=flops, bytes_accessed=0, transcendentals=0),
    )(*operands)


def send_around(tiles, axis, count):
    return [tiles[0]] + [
        lax.ppermute(tiles[j], axis, [(i, (i + j) % count) for i in range(count)])
        for j in range(1, count)
    ]


def order_kernel(*refs):
    *tile_refs, out_ref = refs
    count = len(tile_refs)
    here = lax.axis_index("grid")
    for j in range(count):
        out_ref[lax.rem(here + (count - j), count)] = tile_refs[j][...]


def by_owner(tiles):
    return call(order_kernel, [((len(tiles), *tiles[0].shape), F32)], tiles)[0]


def shards(
    bundles,
    cell_state,
    pore_volume,
    request_cell,
    node_slot,
    line_length,
    courant,
    flux_weight,
    inflow,
    interaction,
):
    owners, cap = request_cell.shape[2:]
    lines, nodes = node_slot.shape[1:]
    times = lines * nodes // LANES
    direct = owners <= DIRECT
    kept = owners * cap == 2 * LANES
    tile = (ROWS, LANES)
    shapes = [(tile, F32)] * owners if direct else [((owners, *tile), F32)]
    tiles_scratch = pltpu.VMEM((owners, *tile) if direct else (1, *tile), F32)

    def over_grid(tiles):
        if direct:
            return send_around(tiles, "grid", owners)
        return [lax.all_to_all(tiles[0], "grid", split_axis=0, concat_axis=0, tiled=True)]

    outgoing = call(
        pick_kernel,
        shapes,
        (cell_state, request_cell),
        hbm=(0, 1),
        scratch=(
            pltpu.VMEM(cell_state.shape, F32),
            pltpu.VMEM((owners, cap), jnp.int32),
            tiles_scratch,
            pltpu.SemaphoreType.DMA,
            pltpu.SemaphoreType.DMA,
        ),
    )
    jumps = 2
    while 2 ** (jumps // 2 - 1) < nodes // times:
        jumps += 2
    prepared = call(
        prepare_kernel,
        [((6, times, LANES), F32), ((jumps, ROWS, LANES), F32)]
        + ([((2 * LANES, lines * nodes), BF16)] if kept else []),
        (node_slot, line_length, courant, flux_weight),
        smem=(1,),
        flops=10**8,
    )
    tables = over_grid(outgoing)
    sums = call(
        functools.partial(lines_kernel, lines, cap, len(tables), kept),
        shapes,
        (*tables, *prepared[:2], inflow, interaction, *prepared[2:]),
        scratch=(tiles_scratch,),
    )
    sums = over_grid(sums)
    own = sums[0] if not direct else by_owner(sums)
    every = send_around([own] * bundles, "bundle", bundles)
    return call(
        functools.partial(blend_kernel, bundles),
        [(cell_state.shape, F32)],
        (*every, request_cell, cell_state, pore_volume[None, :]),
    )[0]


def solution(mesh):
    placed = (
        P(None, "grid"),
        P("grid"),
        P(None, "grid", None, None),
        P("bundle", "grid", None),
        P("bundle", "grid"),
        P("bundle", "grid", None),
        P("bundle", "grid", None),
        P("bundle", None),
        P(),
    )
    return jax.shard_map(
        functools.partial(shards, mesh.shape["bundle"]),
        mesh=mesh,
        in_specs=placed,
        out_specs=P(None, "grid"),
        check_vma=False,
    )
```

```python
import functools

import jax
import jax.numpy as jnp
from jax import lax
from jax.experimental import pallas as pl
from jax.experimental.pallas import tpu as pltpu
from jax.sharding import PartitionSpec as P

SUB = 2
NEWTON = 3
LANES = 128
ROWS = 8
F32 = jnp.float32
BF16 = jnp.bfloat16
VMEM_BYTES = 32 * 1024 * 1024
WHOLE_BYTES = 63_000_000


def repeat_steps(count, body, carry):
    if count == 1:
        return body(0, carry)
    return lax.fori_loop(0, count, body, carry)


def split(value):
    high = value.astype(BF16)
    low = (value - high.astype(F32)).astype(BF16)
    return high, low


def exchange_groups(tiles, cap):
    tiles = list(tiles)
    lane_group = lax.broadcasted_iota(jnp.int32, tiles[0].shape, 1) // cap
    step = 1
    while step < len(tiles):
        keep = (lane_group & step) == 0
        for i in range(len(tiles)):
            if i & step == 0:
                first, second = tiles[i], tiles[i | step]
                tiles[i] = jnp.where(keep, first, pltpu.roll(second, step * cap, 1))
                tiles[i | step] = jnp.where(keep, pltpu.roll(first, LANES - step * cap, 1), second)
        step *= 2
    return tiles


def spread_rows(block, cap):
    groups = block.shape[0]
    wide = jnp.concatenate([block] * groups, axis=1)
    rows = lax.broadcasted_iota(jnp.int32, wide.shape, 0)
    lanes = lax.broadcasted_iota(jnp.int32, wide.shape, 1) // cap
    return jnp.sum(jnp.where(rows == lanes, wide, 0), axis=0, keepdims=True)


def pick_kernel(cell_hbm, request_hbm, out_ref, cell_ref, request_ref, cell_sem, request_sem):
    request_copy = pltpu.make_async_copy(
        request_hbm.at[lax.axis_index("bundle"), 0], request_ref, request_sem
    )
    cell_copy = pltpu.make_async_copy(cell_hbm, cell_ref, cell_sem)
    request_copy.start()
    cell_copy.start()
    species, cells = cell_ref.shape
    owners, cap = request_ref.shape
    groups = LANES // cap
    chunks = owners // (2 * groups)
    highs = cells // LANES
    request_copy.wait()

    def wanted(k):
        block = request_ref[pl.ds(k * 2 * groups, 2 * groups), :]
        index = jnp.concatenate(
            [spread_rows(block[:groups], cap), spread_rows(block[groups:], cap)], axis=1
        )
        low = index % LANES
        high = index // LANES
        hot = (lax.broadcasted_iota(jnp.int32, (LANES, 2 * LANES), 0) == low).astype(F32).astype(BF16)
        return high, jnp.concatenate([hot, hot], axis=0)

    kept = wanted(0) if chunks == 1 else None
    cell_copy.wait()
    cell = cell_ref[...]
    stacked = jnp.concatenate(
        [cell[:, LANES * h : LANES * (h + 1)] for h in range(highs)], axis=0
    )
    left = jnp.concatenate(split(stacked), axis=1)

    def chunk(k, carry):
        first = k * 2 * groups
        high, right = wanted(k) if kept is None else kept
        product = jnp.dot(left, right, preferred_element_type=F32)
        picked = jnp.zeros((species, 2 * LANES), F32)
        for h in range(highs):
            picked = picked + jnp.where(high == h, product[species * h : species * (h + 1)], 0.0)
        blank = jnp.zeros((groups * ROWS - species, 2 * LANES), F32)
        picked = jnp.concatenate([picked, blank], axis=0)
        for half in range(2):
            tiles = exchange_groups(
                [
                    picked[ROWS * g : ROWS * (g + 1), LANES * half : LANES * (half + 1)]
                    for g in range(groups)
                ],
                cap,
            )
            for j in range(groups):
                out_ref[first + half * groups + j] = tiles[j]
        return carry

    repeat_steps(chunks, chunk, 0)


def to_segments(refs):
    lines, nodes = refs[0].shape[1:]
    blocks = nodes // LANES
    width = lines * blocks
    groups = LANES // width
    stacked = []
    for ref in refs:
        value = ref[0].astype(F32)
        stacked += [value[:, LANES * block : LANES * (block + 1)] for block in range(blocks)]
    stacked.append(jnp.zeros((LANES - width * len(refs), LANES), F32))
    turned = jnp.transpose(jnp.concatenate(stacked, axis=0))
    times = LANES // groups
    return exchange_groups([turned[times * g : times * (g + 1)] for g in range(groups)], width)


def one_hot(slot, k):
    local = (slot - lax.convert_element_type(k * 2 * LANES, F32)).astype(BF16)
    index = lax.broadcasted_iota(jnp.int32, (2 * LANES, LANES), 0).astype(F32).astype(BF16)
    one, zero = jnp.ones_like(index), jnp.zeros_like(index)
    return jnp.concatenate(
        [
            jnp.where(jnp.broadcast_to(local[t : t + 1], index.shape) == index, one, zero)
            for t in range(slot.shape[0])
        ],
        axis=1,
    )


class Places:
    def __init__(self, lines, nodes):
        self.lines = lines
        self.blocks = nodes // LANES
        self.width = lines * self.blocks
        self.segments = LANES // self.width
        self.times = LANES // self.segments
        lane = lax.broadcasted_iota(jnp.int32, (ROWS, LANES), 1)
        self.part = lane // self.width
        self.block = (lane % self.width) // lines
        self.segment = self.block * self.segments + self.part
        self.line = lane % lines
        self.distances = []
        distance = 1
        while distance < self.blocks * self.segments:
            self.distances.append(distance)
            distance *= 2

    def earlier(self, value, distance):
        major, minor = distance // self.segments, distance % self.segments
        near = pltpu.roll(value, minor * self.width + major * self.lines, 1)
        if minor == 0:
            return near
        far = pltpu.roll(value, minor * self.width + (major + 1) * self.lines, 1)
        return jnp.where(self.part >= minor, near, far)


def prepare_kernel(
    slot_ref, length_ref, courant_ref, flux_ref, after_ref, rows_ref, jump_ref, *hot_refs
):
    lines, nodes = slot_ref.shape[1:]
    places = Places(lines, nodes)
    times = places.times
    slot, courant, flux = to_segments([slot_ref, courant_ref, flux_ref])[:3]
    scale = 1.0 / (1.0 + courant)
    decay = courant * scale
    rows_ref[0] = scale
    rows_ref[1] = decay
    rows_ref[5] = slot

    one, two = decay[:1], scale[:1] * decay[:1]
    ones, twos = [one], [two]
    for t in range(1, times):
        one = decay[t : t + 1] * one
        two = scale[t : t + 1] * one + decay[t : t + 1] * two
        ones.append(one)
        twos.append(two)
    rows_ref[2] = jnp.concatenate(ones, axis=0)
    rows_ref[3] = jnp.concatenate(twos, axis=0)

    a = jnp.broadcast_to(one, (ROWS, LANES))
    b = jnp.broadcast_to(two, (ROWS, LANES))
    jump_ref[0], jump_ref[1] = a, b
    for i, distance in enumerate(places.distances):
        opened = places.segment >= distance
        jump_ref[2 * i + 2] = jnp.where(opened, a, 0.0)
        jump_ref[2 * i + 3] = jnp.where(opened, b, 0.0)
        ahead = places.earlier(a, distance)
        b = b * ahead + a * places.earlier(b, distance)
        a = a * ahead

    length = jnp.zeros((ROWS, LANES), jnp.int32)
    for line in range(lines):
        length = jnp.where(places.line == line, length_ref[0, line], length)
    start = places.block * LANES + places.part * times - length
    step = lax.broadcasted_iota(jnp.int32, flux.shape, 0)
    rows_ref[4] = jnp.where(step + start[:1] < 0, flux, 0.0)

    for hot_ref in hot_refs:
        hot_ref[...] = one_hot(slot, 0)


def lines_kernel(lines, cap, table_ref, rows_ref, jump_ref, inflow_ref, interaction_ref, *refs):
    *hot_refs, out_ref = refs
    owners, copies = out_ref.shape[:2]
    all_groups = LANES // cap
    species = inflow_ref.shape[1]
    times = rows_ref.shape[1]
    nodes = times * LANES // lines
    places = Places(lines, nodes)
    groups = species // ROWS
    rows = all_groups * ROWS
    chunk_owners = 2 * all_groups
    chunks = owners // chunk_owners

    def hot(k):
        return hot_refs[0][...] if hot_refs else one_hot(rows_ref[5], k)

    def gather(k, state):
        halves = []
        for half in range(2):
            first = k * chunk_owners + half * all_groups
            halves.append(
                jnp.concatenate(
                    exchange_groups([table_ref[first + j] for j in range(all_groups)], cap), axis=0
                )
            )
        left = jnp.concatenate(split(jnp.concatenate(halves, axis=1)), axis=0)
        found = jnp.dot(left, hot(k), preferred_element_type=F32)
        found = found[:species] + found[rows : rows + species]
        return found if chunks == 1 else state + found

    start = repeat_steps(
        chunks, gather, jnp.zeros((species, lines * nodes), F32) if chunks > 1 else 0
    )

    eye = lax.broadcasted_iota(jnp.int32, (species, LANES), 0) == lax.broadcasted_iota(
        jnp.int32, (species, LANES), 1
    )
    padded = jnp.concatenate([inflow_ref[...], jnp.zeros((1, LANES - species), F32)], axis=1)
    column = jnp.sum(jnp.where(eye, padded, 0.0), axis=1, keepdims=True)
    entry = jnp.broadcast_to(column, (species, LANES))
    entry = [entry[ROWS * g : ROWS * (g + 1)] for g in range(groups)]

    def row(kind, t):
        return jnp.broadcast_to(rows_ref[kind, t : t + 1], (ROWS, LANES))

    first = [None] * groups
    second = [None] * groups
    local = []
    for t in range(times):
        scale, decay = row(0, t), row(1, t)
        for g in range(groups):
            value = start[ROWS * g : ROWS * (g + 1), LANES * t : LANES * (t + 1)] * scale
            first[g] = value if t == 0 else value + decay * first[g]
            value = scale * first[g]
            second[g] = value if t == 0 else value + decay * second[g]
            local.append(second[g])

    a, b = jump_ref[0], jump_ref[1]
    head = places.segment == 0
    first = [jnp.where(head, f + a * e, f) for f, e in zip(first, entry)]
    second = [jnp.where(head, s + b * e + a * e, s) for s, e in zip(second, entry)]
    for i, distance in enumerate(places.distances):
        a, b = jump_ref[2 * i + 2], jump_ref[2 * i + 3]
        ahead = [places.earlier(f, distance) for f in first]
        second = [s + b * f + a * places.earlier(s, distance) for s, f in zip(second, ahead)]
        first = [f + a * e for f, e in zip(first, ahead)]
    carry_one = [jnp.where(head, e, places.earlier(f, 1)) for e, f in zip(entry, first)]
    carry_two = [jnp.where(head, e, places.earlier(s, 1)) for e, s in zip(entry, second)]
    columns = []
    for t in range(times):
        one, two = row(2, t), row(3, t)
        columns.append(
            jnp.concatenate(
                [
                    local[t * groups + g] + two * carry_one[g] + one * carry_two[g]
                    for g in range(groups)
                ],
                axis=0,
            )
        )
    base = jnp.concatenate(columns, axis=1)

    blank = jnp.zeros((rows - species, lines * nodes), F32)
    matrix = interaction_ref[...]
    matrix = jnp.concatenate([matrix, jnp.zeros((species, rows - species), F32)], axis=1)
    matrix = jnp.concatenate([matrix, jnp.zeros((rows - species, rows), F32)], axis=0)
    matrix_high, matrix_low = split(matrix)
    left = jnp.concatenate([matrix_high, matrix_low, matrix_high], axis=1)
    iterate = base
    for step in range(NEWTON):
        high, low = split(jnp.concatenate([jnp.tanh(iterate), blank], axis=0))
        right = jnp.concatenate([high, high, low], axis=0)
        iterate = base - jnp.dot(left, right, preferred_element_type=F32)[:species]

    weight = jnp.concatenate([row(4, t) for t in range(times)], axis=1)
    first_row = lax.broadcasted_iota(jnp.int32, weight.shape, 0) == 0
    scaled = [iterate[ROWS * g : ROWS * (g + 1)] * weight for g in range(groups)]
    scaled.append(jnp.where(first_row, weight, 0.0))
    left = jnp.concatenate(split(jnp.concatenate(scaled, axis=0)), axis=0)

    def scatter(k, carry):
        sums = lax.dot_general(
            left, hot(k), (((1,), (1,)), ((), ())), preferred_element_type=F32
        )
        sums = sums[:rows] + sums[rows:]
        for half in range(2):
            tiles = exchange_groups(
                [
                    sums[ROWS * g : ROWS * (g + 1), LANES * half : LANES * (half + 1)]
                    for g in range(all_groups)
                ],
                cap,
            )
            for j in range(all_groups):
                for copy in range(copies):
                    out_ref[k * chunk_owners + half * all_groups + j, copy] = tiles[j]
        return carry

    repeat_steps(chunks, scatter, 0)


def blend_entries(request_ref, k):
    bundles, cap = request_ref.shape[0], request_ref.shape[3]
    groups = LANES // cap
    pieces = []
    for t in range(bundles // groups):
        block = jnp.concatenate(
            [request_ref[t * groups + j, 0, pl.ds(k * ROWS, ROWS), :] for j in range(groups)],
            axis=1,
        )
        pieces += [block[d : d + 1] for d in range(ROWS)]
    return jnp.concatenate(pieces, axis=1)


def blend_index(request_ref, k):
    width = 2 * LANES
    index = blend_entries(request_ref, k)
    entries = index.shape[1]
    high = jnp.broadcast_to(index // width, (2 * ROWS, entries)).astype(F32).astype(BF16)
    low = jnp.broadcast_to(index % width, (2 * ROWS, entries)).astype(F32).astype(BF16)
    place = lax.broadcasted_iota(jnp.int32, (width, entries), 0).astype(F32).astype(BF16)
    low = jnp.concatenate([low] * (width // (2 * ROWS)), axis=0)
    return high, jnp.where(place == low, jnp.ones_like(place), jnp.zeros_like(place))


def index_kernel(request_ref, after_ref, high_ref, hot_ref):
    high_ref[...], hot_ref[...] = blend_index(request_ref, 0)


def blend_kernel(sums_ref, request_ref, pore_ref, cell_ref, *refs):
    *kept_refs, out_hbm, out_ref, out_sem = refs
    owners, bundles = sums_ref.shape[:2]
    species, cells = cell_ref.shape
    cap = request_ref.shape[3]
    groups = LANES // cap
    rows = groups * ROWS
    width = 2 * LANES
    highs = cells // width
    chunks = owners // ROWS

    def chunk(k, total):
        values = []
        for t in range(bundles // groups):
            for d in range(ROWS):
                tiles = exchange_groups(
                    [sums_ref[k * ROWS + d, t * groups + j] for j in range(groups)], cap
                )
                values.append(jnp.concatenate(tiles, axis=0))
        value = jnp.concatenate(values, axis=1)
        if kept_refs:
            high, hot = kept_refs[0][...], kept_refs[1][...]
        else:
            high, hot = blend_index(request_ref, k)
        parts = jnp.concatenate(split(value), axis=0)
        pieces = []
        for h in range(highs):
            mask = high == jnp.array(h, BF16)
            for r in range(2 * rows // (2 * ROWS)):
                piece = parts[2 * ROWS * r : 2 * ROWS * (r + 1)]
                pieces.append(jnp.where(mask, piece, jnp.zeros_like(piece)))
        left = jnp.concatenate(pieces, axis=0)
        product = lax.dot_general(
            left, hot, (((1,), (1,)), ((), ())), preferred_element_type=F32
        )
        return product if chunks == 1 else total + product

    total = repeat_steps(
        chunks, chunk, jnp.zeros((highs * 2 * rows, width), F32) if chunks > 1 else 0
    )
    copies = []
    for h in range(highs):
        part = total[2 * rows * h : 2 * rows * (h + 1)]
        part = part[:rows] + part[rows:]
        pore = pore_ref[:, width * h : width * (h + 1)]
        scale = pore + part[species : species + 1]
        columns = pl.ds(width * h, width)
        out_ref[:, columns] = (pore * cell_ref[:, columns] + part[:species]) / scale
        if h % 4 == 3:
            columns = pl.ds(width * (h - 3), 4 * width)
            copies.append(
                pltpu.make_async_copy(
                    out_ref.at[:, columns], out_hbm.at[:, columns], out_sem.at[h // 4]
                )
            )
            copies[-1].start()
    for copy in copies:
        copy.wait()


def call(kernel, shapes, operands, kinds={}, scratch=(), flops=0, grant=VMEM_BYTES, out=pltpu.VMEM):
    return pl.pallas_call(
        kernel,
        out_shape=[jax.ShapeDtypeStruct(shape, kind) for shape, kind in shapes],
        in_specs=[
            pl.BlockSpec(memory_space=kinds.get(i, pltpu.VMEM)) for i in range(len(operands))
        ],
        out_specs=[pl.BlockSpec(memory_space=out)] * len(shapes),
        scratch_shapes=list(scratch),
        compiler_params=pltpu.CompilerParams(vmem_limit_bytes=grant),
        cost_estimate=pl.CostEstimate(flops=flops, bytes_accessed=0, transcendentals=0),
    )(*operands)


def shards(
    bundles,
    cell_state,
    pore_volume,
    request_cell,
    node_slot,
    line_length,
    courant,
    flux_weight,
    inflow,
    interaction,
):
    owners, cap = request_cell.shape[2:]
    lines, nodes = node_slot.shape[1:]
    times = lines * nodes // LANES
    cells = cell_state.shape[1]
    tile = (ROWS, LANES)
    outgoing = call(
        pick_kernel,
        [((owners, *tile), F32)],
        (cell_state, request_cell),
        kinds={0: pltpu.HBM, 1: pltpu.HBM},
        scratch=(
            pltpu.VMEM(cell_state.shape, F32),
            pltpu.VMEM((owners, cap), jnp.int32),
            pltpu.SemaphoreType.DMA,
            pltpu.SemaphoreType.DMA,
        ),
        grant=WHOLE_BYTES,
    )[0]
    jumps = 2
    while 2 ** (jumps // 2 - 1) < nodes // times:
        jumps += 2
    prepared = call(
        prepare_kernel,
        [((6, times, LANES), F32), ((jumps, ROWS, LANES), F32)]
        + ([((2 * LANES, lines * nodes), BF16)] if owners * cap == 2 * LANES else []),
        (node_slot, line_length, courant, flux_weight, outgoing),
        kinds={1: pltpu.SMEM, 4: pl.ANY},
        flops=10**9,
    )
    table = lax.all_to_all(outgoing, "grid", split_axis=0, concat_axis=0, tiled=True)
    sums = call(
        functools.partial(lines_kernel, lines, cap),
        [((owners, bundles, *tile), F32)],
        (table, *prepared[:2], inflow, interaction, *prepared[2:]),
    )[0]
    entries = bundles * ROWS * cap
    indexed = []
    if owners == ROWS:
        indexed = call(
            index_kernel,
            [((2 * ROWS, entries), BF16), ((2 * LANES, entries), BF16)],
            (request_cell, sums),
            kinds={1: pl.ANY},
            flops=10**9,
        )
    sums = sums.reshape(owners * bundles, *tile)
    back = lax.all_to_all(sums, ("grid", "bundle"), split_axis=0, concat_axis=0, tiled=True)
    back = back.reshape(owners, bundles, *tile)
    return call(
        blend_kernel,
        [(cell_state.shape, F32)],
        (back, request_cell, pore_volume[None, :], cell_state, *indexed),
        scratch=(pltpu.VMEM(cell_state.shape, F32), pltpu.SemaphoreType.DMA((cells // (8 * LANES),))),
        out=pltpu.HBM,
    )[0]


def solution(mesh):
    placed = (
        P(None, "grid"),
        P("grid"),
        P(None, "grid", None, None),
        P("bundle", "grid", None),
        P("bundle", "grid"),
        P("bundle", "grid", None),
        P("bundle", "grid", None),
        P("bundle", None),
        P(),
    )
    return jax.shard_map(
        functools.partial(shards, mesh.shape["bundle"]),
        mesh=mesh,
        in_specs=placed,
        out_specs=P(None, "grid"),
        check_vma=False,
    )
```

```python
import functools

import jax
import jax.numpy as jnp
from jax import lax
from jax.experimental import pallas as pl
from jax.experimental.pallas import tpu as pltpu
from jax.sharding import PartitionSpec as P

SUB = 2
NEWTON = 3
LANES = 128
ROWS = 8
F32 = jnp.float32
BF16 = jnp.bfloat16
VMEM_BYTES = 32 * 1024 * 1024
PICK_BYTES = 63_000_000


def repeat_steps(count, body, carry):
    if count == 1:
        return body(0, carry)
    return lax.fori_loop(0, count, body, carry)


def rounded(value):
    high = value.astype(BF16).astype(F32)
    return high, value - high


def split(value):
    return jnp.concatenate(rounded(value), axis=0).astype(BF16)


def select_groups(tiles, relative):
    count = len(tiles)
    results = []
    for i in range(count):
        value = tiles[0]
        for j in range(1, count):
            value = jnp.where(relative == (i + j) % count, tiles[j], value)
        results.append(value)
    return results


def lane_groups(cap, turn):
    groups = LANES // cap
    lane = lax.broadcasted_iota(jnp.int32, (ROWS, LANES), 1)
    return (lane // cap + (2 * groups - lax.rem(turn, groups))) % groups


def pack(rows, cap, turn, relative):
    groups = LANES // cap
    turned = [
        pltpu.roll(rows[g], lax.rem(turn + g, groups) * cap, 1) for g in range(groups)
    ]
    return select_groups(turned, relative)


def unpack(tiles, cap, relative, count):
    found = select_groups(tiles, relative)[:count]
    return [
        found[g] if g == 0 else pltpu.roll(found[g], LANES - g * cap, 1) for g in range(count)
    ]


def exchange_groups(tiles, width):
    tiles = list(tiles)
    lane_group = lax.broadcasted_iota(jnp.int32, tiles[0].shape, 1) // width
    step = 1
    while step < len(tiles):
        keep = (lane_group & step) == 0
        for i in range(len(tiles)):
            if i & step == 0:
                first, second = tiles[i], tiles[i | step]
                tiles[i] = jnp.where(keep, first, pltpu.roll(second, step * width, 1))
                tiles[i | step] = jnp.where(
                    keep, pltpu.roll(first, LANES - step * width, 1), second
                )
        step *= 2
    return tiles


def spread_rows(block, cap):
    groups = block.shape[0]
    wide = jnp.concatenate([block] * groups, axis=1)
    rows = lax.broadcasted_iota(jnp.int32, wide.shape, 0)
    lanes = lax.broadcasted_iota(jnp.int32, wide.shape, 1) // cap
    return jnp.sum(jnp.where(rows == lanes, wide, 0), axis=0, keepdims=True)


def pick_kernel(cell_hbm, request_hbm, out_ref, cell_ref, request_ref, cell_sem, request_sem):
    request_copy = pltpu.make_async_copy(
        request_hbm.at[lax.axis_index("bundle"), 0], request_ref, request_sem
    )
    cell_copy = pltpu.make_async_copy(cell_hbm, cell_ref, cell_sem)
    request_copy.start()
    cell_copy.start()
    species, cells = cell_ref.shape
    owners, cap = request_ref.shape
    groups = LANES // cap
    chunks = owners // (2 * groups)
    highs = cells // LANES
    here = lax.axis_index("grid")
    relative = lane_groups(cap, here)
    request_copy.wait()

    def wanted(k):
        block = request_ref[pl.ds(k * 2 * groups, 2 * groups), :]
        index = jnp.concatenate(
            [spread_rows(block[:groups], cap), spread_rows(block[groups:], cap)], axis=1
        )
        low = index % LANES
        high = index // LANES
        hot = (
            (lax.broadcasted_iota(jnp.int32, (LANES, 2 * LANES), 0) == low)
            .astype(F32)
            .astype(BF16)
        )
        return high, jnp.concatenate([hot, hot], axis=0)

    kept = wanted(0) if chunks == 1 else None
    cell_copy.wait()
    cell = cell_ref[...]
    stacked = jnp.concatenate(
        [cell[:, LANES * h : LANES * (h + 1)] for h in range(highs)], axis=0
    )
    left = jnp.concatenate(rounded(stacked), axis=1).astype(BF16)

    def chunk(k, carry):
        first = k * 2 * groups
        high, right = wanted(k) if kept is None else kept
        product = jnp.dot(left, right, preferred_element_type=F32)
        picked = jnp.zeros((species, 2 * LANES), F32)
        for h in range(highs):
            picked = picked + jnp.where(high == h, product[species * h : species * (h + 1)], 0.0)
        blank = jnp.zeros((groups * ROWS - species, 2 * LANES), F32)
        picked = jnp.concatenate([picked, blank], axis=0)
        for half in range(2):
            tiles = pack(
                [
                    picked[ROWS * g : ROWS * (g + 1), LANES * half : LANES * (half + 1)]
                    for g in range(groups)
                ],
                cap,
                here,
                relative,
            )
            for j in range(groups):
                out_ref[first + half * groups + j] = tiles[j]
        return carry

    repeat_steps(chunks, chunk, 0)


def to_segments(values):
    lines, nodes = values[0].shape
    blocks = nodes // LANES
    width = lines * blocks
    groups = LANES // width
    stacked = []
    for value in values:
        value = value.astype(F32)
        stacked += [value[:, LANES * block : LANES * (block + 1)] for block in range(blocks)]
    stacked.append(jnp.zeros((LANES - width * len(values), LANES), F32))
    turned = jnp.transpose(jnp.concatenate(stacked, axis=0))
    times = LANES // groups
    return exchange_groups([turned[times * g : times * (g + 1)] for g in range(groups)], width)


def lines_kernel(
    cap,
    table_ref,
    slot_ref,
    length_ref,
    courant_ref,
    flux_ref,
    inflow_ref,
    interaction_ref,
    out_ref,
):
    owners = table_ref.shape[0]
    copies = out_ref.shape[0] // owners
    species = inflow_ref.shape[1]
    lines, nodes = slot_ref.shape[1:]
    groups = species // ROWS
    all_groups = LANES // cap
    rows = all_groups * ROWS
    sent = out_ref.shape[2] // LANES
    blocks = nodes // LANES
    width = lines * blocks
    segments = LANES // width
    times = LANES // segments
    chunk_owners = 2 * all_groups
    chunks = owners // chunk_owners
    here, bundle = lax.axis_index("grid"), lax.axis_index("bundle")

    slot = slot_ref[0]
    within = (slot + lax.rem(here, all_groups) * cap) % LANES
    slot, courant, flux = to_segments([slot - slot % LANES + within, courant_ref[0], flux_ref[0]])[
        :3
    ]

    def hot(k):
        local = (slot - lax.convert_element_type(k * 2 * LANES, F32)).astype(BF16)
        index = lax.broadcasted_iota(jnp.int32, (2 * LANES, LANES), 0).astype(F32).astype(BF16)
        one, zero = jnp.ones_like(index), jnp.zeros_like(index)
        return jnp.concatenate(
            [
                jnp.where(jnp.broadcast_to(local[t : t + 1], index.shape) == index, one, zero)
                for t in range(times)
            ],
            axis=1,
        )

    kept = hot(0) if chunks == 1 else None

    relative = lane_groups(cap, here)

    def gather(k, state):
        halves = []
        for half in range(2):
            first = k * chunk_owners + half * all_groups
            halves.append(
                jnp.concatenate(
                    unpack(
                        [table_ref[first + j] for j in range(all_groups)], cap, relative, groups
                    ),
                    axis=0,
                )
            )
        left = split(jnp.concatenate(halves, axis=1))
        found = jnp.dot(left, hot(k) if kept is None else kept, preferred_element_type=F32)
        found = found[:species] + found[species:]
        return found if chunks == 1 else state + found

    start = repeat_steps(
        chunks, gather, jnp.zeros((species, lines * nodes), F32) if chunks > 1 else 0
    )

    lane = lax.broadcasted_iota(jnp.int32, (ROWS, LANES), 1)
    part = lane // width
    block = (lane % width) // lines
    segment = block * segments + part
    line = lane % lines

    def earlier(value, distance):
        major, minor = distance // segments, distance % segments
        near = pltpu.roll(value, minor * width + major * lines, 1)
        if minor == 0:
            return near
        far = pltpu.roll(value, minor * width + (major + 1) * lines, 1)
        return jnp.where(part >= minor, near, far)

    eye = lax.broadcasted_iota(jnp.int32, (species, LANES), 0) == lax.broadcasted_iota(
        jnp.int32, (species, LANES), 1
    )
    padded = jnp.concatenate([inflow_ref[...], jnp.zeros((1, LANES - species), F32)], axis=1)
    column = jnp.sum(jnp.where(eye, padded, 0.0), axis=1, keepdims=True)
    entry = jnp.broadcast_to(column, (species, LANES))
    entry = [entry[ROWS * g : ROWS * (g + 1)] for g in range(groups)]

    scale = 1.0 / (1.0 + courant)
    decay = courant * scale
    first = [None] * groups
    second = [None] * groups
    local, ones, twos = [], [], []
    for t in range(times):
        scale_t = jnp.broadcast_to(scale[t : t + 1], (ROWS, LANES))
        decay_t = jnp.broadcast_to(decay[t : t + 1], (ROWS, LANES))
        one = decay_t if t == 0 else decay_t * ones[-1]
        two = scale_t * one if t == 0 else scale_t * one + decay_t * twos[-1]
        ones.append(one)
        twos.append(two)
        for g in range(groups):
            value = start[ROWS * g : ROWS * (g + 1), LANES * t : LANES * (t + 1)] * scale_t
            first[g] = value if t == 0 else value + decay_t * first[g]
            value = scale_t * first[g]
            second[g] = value if t == 0 else value + decay_t * second[g]
            local.append(second[g])

    a, b = ones[-1], twos[-1]
    head = segment == 0
    first = [jnp.where(head, f + a * e, f) for f, e in zip(first, entry)]
    second = [jnp.where(head, s + b * e + a * e, s) for s, e in zip(second, entry)]
    distance = 1
    while distance < blocks * segments:
        opened = segment >= distance
        a_open, b_open = jnp.where(opened, a, 0.0), jnp.where(opened, b, 0.0)
        ahead = [earlier(f, distance) for f in first]
        second = [s + b_open * f + a_open * earlier(s, distance) for s, f in zip(second, ahead)]
        first = [f + a_open * e for f, e in zip(first, ahead)]
        if 2 * distance < blocks * segments:
            a_ahead = earlier(a, distance)
            b = b * a_ahead + a * earlier(b, distance)
            a = a * a_ahead
        distance *= 2
    carry_one = [jnp.where(head, e, earlier(f, 1)) for e, f in zip(entry, first)]
    carry_two = [jnp.where(head, e, earlier(s, 1)) for e, s in zip(entry, second)]
    columns = [
        jnp.concatenate(
            [
                local[t * groups + g] + twos[t] * carry_one[g] + ones[t] * carry_two[g]
                for g in range(groups)
            ],
            axis=0,
        )
        for t in range(times)
    ]

    matrix_high, matrix_low = rounded(interaction_ref[...])
    block_row = jnp.concatenate([matrix_high, matrix_low, matrix_high], axis=1)
    blank = jnp.zeros_like(block_row)
    left = jnp.concatenate(
        [
            jnp.concatenate([block_row, blank], axis=1),
            jnp.concatenate([blank, block_row], axis=1),
        ],
        axis=0,
    ).astype(BF16)
    half = times // 2
    base = jnp.concatenate(
        [
            jnp.concatenate(columns[:half], axis=1),
            jnp.concatenate(columns[half:], axis=1),
        ],
        axis=0,
    )
    iterate = base
    for step in range(NEWTON):
        high, low = rounded(jnp.tanh(iterate))
        right = jnp.concatenate(
            [
                high[:species],
                high[:species],
                low[:species],
                high[species:],
                high[species:],
                low[species:],
            ],
            axis=0,
        ).astype(BF16)
        iterate = base - jnp.dot(left, right, preferred_element_type=F32)
    iterate = jnp.concatenate([iterate[:species], iterate[species:]], axis=1)

    length = jnp.zeros((ROWS, LANES), jnp.int32)
    for one_line in range(lines):
        length = jnp.where(line == one_line, length_ref[0, one_line], length)
    node = block * LANES + part * times
    weight = jnp.concatenate(
        [
            jnp.where(node + t < length, jnp.broadcast_to(flux[t : t + 1], (ROWS, LANES)), 0.0)
            for t in range(times)
        ],
        axis=1,
    )
    first_row = lax.broadcasted_iota(jnp.int32, weight.shape, 0) == 0
    scaled = [iterate[ROWS * g : ROWS * (g + 1)] * weight for g in range(groups)]
    scaled.append(jnp.where(first_row, weight, 0.0))
    left = split(jnp.concatenate(scaled, axis=0))
    relative = lane_groups(cap, here + bundle)

    def scatter(k, carry):
        sums = lax.dot_general(
            left,
            hot(k) if kept is None else kept,
            (((1,), (1,)), ((), ())),
            preferred_element_type=F32,
        )
        sums = sums[:rows] + sums[rows:]
        last = [sums[species : species + 1]]
        last += [
            sums[ROWS * g + r : ROWS * g + r + 1] for g in range(groups) for r in range(sent, ROWS)
        ]
        last.append(jnp.zeros((ROWS - len(last), 2 * LANES), F32))
        sums = jnp.concatenate([sums[:species]] + last, axis=0)
        for half in range(2):
            tiles = pack(
                [
                    sums[ROWS * g : ROWS * (g + 1), LANES * half : LANES * (half + 1)]
                    for g in range(all_groups)
                ],
                cap,
                bundle,
                relative,
            )
            for j in range(all_groups):
                owner = k * chunk_owners + half * all_groups + j
                for copy in range(copies):
                    for r in range(sent):
                        out_ref[owner * copies + copy, :, LANES * r : LANES * (r + 1)] = tiles[j][
                            r : r + 1
                        ]
        return carry

    repeat_steps(chunks, scatter, 0)


def blend_kernel(bundles, sums_ref, request_ref, pore_ref, cell_ref, out_hbm, out_ref, out_sem):
    owners = sums_ref.shape[0] // bundles
    sent = sums_ref.shape[2] // LANES
    species, cells = cell_ref.shape
    cap = request_ref.shape[3]
    all_groups = LANES // cap
    groups = species // ROWS
    width = 2 * LANES
    highs = cells // width
    chunks = owners // ROWS
    here = lax.axis_index("grid")
    sublane = lax.broadcasted_iota(jnp.int32, (ROWS, LANES), 0)

    def tile(device, bundle):
        value = jnp.zeros((ROWS, LANES), F32)
        for r in range(sent):
            row = sums_ref[device * bundles + bundle, :, LANES * r : LANES * (r + 1)]
            value = jnp.where(sublane == r, jnp.broadcast_to(row, (ROWS, LANES)), value)
        return value

    def chunk(k, total):
        values, weights, indices = [], [], []
        for t in range(bundles // all_groups):
            block = jnp.concatenate(
                [
                    request_ref[
                        t * all_groups
                        + lax.rem(x + all_groups - lax.rem(here, all_groups), all_groups),
                        0,
                        pl.ds(k * ROWS, ROWS),
                        :,
                    ]
                    for x in range(all_groups)
                ],
                axis=1,
            )
            straight = block
            for turn in range(1, all_groups):
                block = jnp.where(
                    sublane % all_groups == turn, pltpu.roll(straight, turn * cap, 1), block
                )
            for d in range(ROWS):
                found = unpack(
                    [tile(k * ROWS + d, t * all_groups + j) for j in range(all_groups)],
                    cap,
                    lane_groups(cap, here + d),
                    all_groups,
                )
                weights.append(found[groups][:1])
                spare = 1
                for g in range(groups):
                    for r in range(sent, ROWS):
                        row = jnp.broadcast_to(
                            found[groups][spare : spare + 1], (ROWS, LANES)
                        )
                        found[g] = jnp.where(sublane == r, row, found[g])
                        spare += 1
                values.append(jnp.concatenate(found[:groups], axis=0))
                indices.append(block[d : d + 1])
        parts = split(jnp.concatenate(values, axis=1))
        weight_high, weight_low = rounded(jnp.concatenate(weights, axis=1))
        index = jnp.concatenate(indices, axis=1)
        entries = index.shape[1]
        high = jnp.broadcast_to(index // width, (2 * ROWS, entries)).astype(F32).astype(BF16)
        low = jnp.broadcast_to(index % width, (2 * ROWS, entries)).astype(F32).astype(BF16)
        low = jnp.concatenate([low] * (width // (2 * ROWS)), axis=0)
        place = lax.broadcasted_iota(jnp.int32, (width, entries), 0).astype(F32).astype(BF16)
        hot = jnp.where(place == low, jnp.ones_like(place), jnp.zeros_like(place))
        zero = jnp.zeros((2 * ROWS, entries), BF16)
        pieces = []
        for h in range(highs):
            mask = high == jnp.array(h, BF16)
            for r in range(2 * species // (2 * ROWS)):
                pieces.append(
                    jnp.where(mask, parts[2 * ROWS * r : 2 * ROWS * (r + 1)], zero)
                )
        for first in range(0, highs, 2 * ROWS):
            mask = high == (
                lax.broadcasted_iota(jnp.int32, (2 * ROWS, entries), 0) + first
            ).astype(F32).astype(BF16)
            for part in (weight_high, weight_low):
                row = jnp.broadcast_to(part, (2 * ROWS, entries)).astype(BF16)
                pieces.append(jnp.where(mask, row, zero))
        left = jnp.concatenate(pieces, axis=0)
        product = lax.dot_general(
            left, hot, (((1,), (1,)), ((), ())), preferred_element_type=F32
        )
        return product if chunks == 1 else total + product

    flux_rows = -(-highs // (2 * ROWS)) * 4 * ROWS
    total = repeat_steps(
        chunks,
        chunk,
        jnp.zeros((highs * 2 * species + flux_rows, width), F32) if chunks > 1 else 0,
    )
    flux = total[highs * 2 * species :]
    copies = []
    stride = max(highs // 4, 1)
    for h in range(highs):
        part = total[2 * species * h : 2 * species * (h + 1)]
        part = part[:species] + part[species:]
        row = h // (2 * ROWS) * 4 * ROWS + h % (2 * ROWS)
        pore = pore_ref[:, width * h : width * (h + 1)]
        inverse = 1.0 / (pore + flux[row : row + 1] + flux[row + 2 * ROWS : row + 2 * ROWS + 1])
        columns = pl.ds(width * h, width)
        out_ref[:, columns] = (pore * cell_ref[:, columns] + part) * inverse
        if h % stride == stride - 1:
            columns = pl.ds(width * (h - stride + 1), stride * width)
            copies.append(
                pltpu.make_async_copy(
                    out_ref.at[:, columns], out_hbm.at[:, columns], out_sem.at[h // stride]
                )
            )
            copies[-1].start()
    for copy in copies:
        copy.wait()


def call(kernel, shape, operands, kinds={}, scratch=(), grant=VMEM_BYTES, out=pltpu.VMEM):
    return pl.pallas_call(
        kernel,
        out_shape=jax.ShapeDtypeStruct(shape, F32),
        in_specs=[
            pl.BlockSpec(memory_space=kinds.get(i, pltpu.VMEM)) for i in range(len(operands))
        ],
        out_specs=pl.BlockSpec(memory_space=out),
        scratch_shapes=list(scratch),
        compiler_params=pltpu.CompilerParams(vmem_limit_bytes=grant),
    )(*operands)


def shards(
    bundles,
    cell_state,
    pore_volume,
    request_cell,
    node_slot,
    line_length,
    courant,
    flux_weight,
    inflow,
    interaction,
):
    owners, cap = request_cell.shape[2:]
    sent = -(-(cell_state.shape[0] + 1) // (LANES // cap))
    outgoing = call(
        pick_kernel,
        (owners, ROWS, LANES),
        (cell_state, request_cell),
        kinds={0: pltpu.HBM, 1: pltpu.HBM},
        scratch=(
            pltpu.VMEM(cell_state.shape, F32),
            pltpu.VMEM((owners, cap), jnp.int32),
            pltpu.SemaphoreType.DMA,
            pltpu.SemaphoreType.DMA,
        ),
        grant=PICK_BYTES,
    )
    table = lax.all_to_all(outgoing, "grid", split_axis=0, concat_axis=0, tiled=True)
    sums = call(
        functools.partial(lines_kernel, cap),
        (owners * bundles, 1, sent * LANES),
        (table, node_slot, line_length, courant, flux_weight, inflow, interaction),
        kinds={2: pltpu.SMEM},
    )
    back = lax.all_to_all(sums, ("grid", "bundle"), split_axis=0, concat_axis=0, tiled=True)
    return call(
        functools.partial(blend_kernel, bundles),
        cell_state.shape,
        (back, request_cell, pore_volume[None, :], cell_state),
        scratch=(pltpu.VMEM(cell_state.shape, F32), pltpu.SemaphoreType.DMA((4,))),
        out=pltpu.HBM,
    )


def solution(mesh):
    placed = (
        P(None, "grid"),
        P("grid"),
        P(None, "grid", None, None),
        P("bundle", "grid", None),
        P("bundle", "grid"),
        P("bundle", "grid", None),
        P("bundle", "grid", None),
        P("bundle", None),
        P(),
    )
    return jax.shard_map(
        functools.partial(shards, mesh.shape["bundle"]),
        mesh=mesh,
        in_specs=placed,
        out_specs=P(None, "grid"),
        check_vma=False,
    )
```

```python
import functools

import jax
import jax.numpy as jnp
from jax import lax
from jax.experimental import pallas as pl
from jax.experimental.pallas import tpu as pltpu
from jax.sharding import PartitionSpec as P

SUB = 2
NEWTON = 3
LANES = 128
ROWS = 8
F32 = jnp.float32
BF16 = jnp.bfloat16
VMEM_BYTES = 32 * 1024 * 1024
PICK_BYTES = 63_000_000


def repeat_steps(count, body, carry):
    if count == 1:
        return body(0, carry)
    return lax.fori_loop(0, count, body, carry)


def rounded(value):
    high = value.astype(BF16).astype(F32)
    return high, value - high


def split(value):
    return jnp.concatenate(rounded(value), axis=0).astype(BF16)


def select_groups(tiles, relative):
    count = len(tiles)
    results = []
    for i in range(count):
        value = tiles[0]
        for j in range(1, count):
            value = jnp.where(relative == (i + j) % count, tiles[j], value)
        results.append(value)
    return results


def lane_groups(cap, turn):
    groups = LANES // cap
    lane = lax.broadcasted_iota(jnp.int32, (ROWS, LANES), 1)
    return (lane // cap + (2 * groups - lax.rem(turn, groups))) % groups


def pack(rows, cap, turn, relative):
    groups = LANES // cap
    turned = [
        pltpu.roll(rows[g], lax.rem(turn + g, groups) * cap, 1) for g in range(groups)
    ]
    return select_groups(turned, relative)


def unpack(tiles, cap, relative, count):
    found = select_groups(tiles, relative)[:count]
    return [
        found[g] if g == 0 else pltpu.roll(found[g], LANES - g * cap, 1) for g in range(count)
    ]


def exchange_rows(tiles, count):
    parts = len(tiles)
    depth = ROWS // parts
    place = lax.broadcasted_iota(jnp.int32, tiles[0].shape, 0) // depth
    turned = [tiles[i] if i == 0 else pltpu.roll(tiles[i], depth * i, 0) for i in range(parts)]
    found = select_groups(turned, place)[:count]
    return [
        found[j] if j == 0 else pltpu.roll(found[j], ROWS - depth * j, 0) for j in range(count)
    ]


def exchange_groups(tiles, width):
    tiles = list(tiles)
    lane_group = lax.broadcasted_iota(jnp.int32, tiles[0].shape, 1) // width
    step = 1
    while step < len(tiles):
        keep = (lane_group & step) == 0
        for i in range(len(tiles)):
            if i & step == 0:
                first, second = tiles[i], tiles[i | step]
                tiles[i] = jnp.where(keep, first, pltpu.roll(second, step * width, 1))
                tiles[i | step] = jnp.where(
                    keep, pltpu.roll(first, LANES - step * width, 1), second
                )
        step *= 2
    return tiles


def spread_rows(block, cap):
    groups = block.shape[0]
    wide = jnp.concatenate([block] * groups, axis=1)
    rows = lax.broadcasted_iota(jnp.int32, wide.shape, 0)
    lanes = lax.broadcasted_iota(jnp.int32, wide.shape, 1) // cap
    return jnp.sum(jnp.where(rows == lanes, wide, 0), axis=0, keepdims=True)


def pick_kernel(cell_hbm, request_hbm, out_ref, cell_ref, request_ref, cell_sem, request_sem):
    species = cell_hbm.shape[0]
    share = jnp.minimum(lax.axis_index("bundle"), species // ROWS - 1)
    request_copy = pltpu.make_async_copy(request_hbm, request_ref, request_sem)
    cell_copy = pltpu.make_async_copy(
        cell_hbm.at[pl.ds(pl.multiple_of(share * ROWS, ROWS), ROWS)], cell_ref, cell_sem
    )
    request_copy.start()
    cell_copy.start()
    cells = cell_ref.shape[1]
    bundles, _, owners, cap = request_ref.shape
    groups = LANES // cap
    chunks = owners // (2 * groups)
    highs = cells // LANES
    here = lax.axis_index("grid")
    relative = lane_groups(cap, here)
    request_copy.wait()

    def wanted(k):
        pieces = []
        for bundle in range(bundles):
            block = request_ref[bundle, 0, pl.ds(k * 2 * groups, 2 * groups), :]
            pieces += [spread_rows(block[:groups], cap), spread_rows(block[groups:], cap)]
        index = jnp.concatenate(pieces, axis=1)
        low = index % LANES
        high = jnp.broadcast_to(index // LANES, (ROWS, index.shape[1]))
        hot = (
            (lax.broadcasted_iota(jnp.int32, (LANES, index.shape[1]), 0) == low)
            .astype(F32)
            .astype(BF16)
        )
        return high, jnp.concatenate([hot, hot], axis=0)

    kept = wanted(0) if chunks == 1 else None
    cell_copy.wait()
    cell = cell_ref[...]
    stacked = jnp.concatenate(
        [cell[:, LANES * h : LANES * (h + 1)] for h in range(highs)], axis=0
    )
    left = jnp.concatenate(rounded(stacked), axis=1).astype(BF16)

    def chunk(k, carry):
        first = k * 2 * groups
        high, right = wanted(k) if kept is None else kept
        product = jnp.dot(left, right, preferred_element_type=F32)
        picked = jnp.zeros(high.shape, F32)
        for h in range(highs):
            picked = picked + jnp.where(high == h, product[ROWS * h : ROWS * (h + 1)], 0.0)
        for half in range(2):
            columns = [LANES * (2 * bundle + half) for bundle in range(bundles)]
            tiles = pack(
                exchange_rows([picked[:, c : c + LANES] for c in columns], groups),
                cap,
                here,
                relative,
            )
            for j in range(groups):
                out_ref[first + half * groups + j] = tiles[j]
        return carry

    repeat_steps(chunks, chunk, 0)


def to_segments(values):
    lines, nodes = values[0].shape
    blocks = nodes // LANES
    width = lines * blocks
    groups = LANES // width
    stacked = []
    for value in values:
        value = value.astype(F32)
        stacked += [value[:, LANES * block : LANES * (block + 1)] for block in range(blocks)]
    stacked.append(jnp.zeros((LANES - width * len(values), LANES), F32))
    turned = jnp.transpose(jnp.concatenate(stacked, axis=0))
    times = LANES // groups
    return exchange_groups([turned[times * g : times * (g + 1)] for g in range(groups)], width)


def lines_kernel(
    cap,
    table_ref,
    slot_ref,
    length_ref,
    courant_ref,
    flux_ref,
    inflow_ref,
    interaction_ref,
    out_ref,
):
    owners = table_ref.shape[0]
    copies = out_ref.shape[0] // owners
    species = inflow_ref.shape[1]
    lines, nodes = slot_ref.shape[1:]
    groups = species // ROWS
    all_groups = LANES // cap
    rows = all_groups * ROWS
    sent = out_ref.shape[2] // LANES
    blocks = nodes // LANES
    width = lines * blocks
    segments = LANES // width
    times = LANES // segments
    chunk_owners = 2 * all_groups
    chunks = owners // chunk_owners
    here, bundle = lax.axis_index("grid"), lax.axis_index("bundle")

    slot = slot_ref[0]
    within = (slot + lax.rem(here, all_groups) * cap) % LANES
    slot, courant, flux = to_segments([slot - slot % LANES + within, courant_ref[0], flux_ref[0]])[
        :3
    ]

    def hot(k):
        local = (slot - lax.convert_element_type(k * 2 * LANES, F32)).astype(BF16)
        index = lax.broadcasted_iota(jnp.int32, (2 * LANES, LANES), 0).astype(F32).astype(BF16)
        one, zero = jnp.ones_like(index), jnp.zeros_like(index)
        return jnp.concatenate(
            [
                jnp.where(jnp.broadcast_to(local[t : t + 1], index.shape) == index, one, zero)
                for t in range(times)
            ],
            axis=1,
        )

    kept = hot(0) if chunks == 1 else None

    relative = lane_groups(cap, here)

    def gather(k, state):
        halves = []
        for half in range(2):
            first = k * chunk_owners + half * all_groups
            tiles = unpack(
                [table_ref[first + j] for j in range(all_groups)], cap, relative, all_groups
            )
            halves.append(jnp.concatenate(exchange_rows(tiles, groups), axis=0))
        left = split(jnp.concatenate(halves, axis=1))
        found = jnp.dot(left, hot(k) if kept is None else kept, preferred_element_type=F32)
        found = found[:species] + found[species:]
        return found if chunks == 1 else state + found

    start = repeat_steps(
        chunks, gather, jnp.zeros((species, lines * nodes), F32) if chunks > 1 else 0
    )

    lane = lax.broadcasted_iota(jnp.int32, (ROWS, LANES), 1)
    part = lane // width
    block = (lane % width) // lines
    segment = block * segments + part
    line = lane % lines

    def earlier(value, distance):
        major, minor = distance // segments, distance % segments
        near = pltpu.roll(value, minor * width + major * lines, 1)
        if minor == 0:
            return near
        far = pltpu.roll(value, minor * width + (major + 1) * lines, 1)
        return jnp.where(part >= minor, near, far)

    eye = lax.broadcasted_iota(jnp.int32, (species, LANES), 0) == lax.broadcasted_iota(
        jnp.int32, (species, LANES), 1
    )
    padded = jnp.concatenate([inflow_ref[...], jnp.zeros((1, LANES - species), F32)], axis=1)
    column = jnp.sum(jnp.where(eye, padded, 0.0), axis=1, keepdims=True)
    entry = jnp.broadcast_to(column, (species, LANES))
    entry = [entry[ROWS * g : ROWS * (g + 1)] for g in range(groups)]

    scale = 1.0 / (1.0 + courant)
    decay = courant * scale
    first = [None] * groups
    second = [None] * groups
    local, ones, twos = [], [], []
    for t in range(times):
        scale_t = jnp.broadcast_to(scale[t : t + 1], (ROWS, LANES))
        decay_t = jnp.broadcast_to(decay[t : t + 1], (ROWS, LANES))
        one = decay_t if t == 0 else decay_t * ones[-1]
        two = scale_t * one if t == 0 else scale_t * one + decay_t * twos[-1]
        ones.append(one)
        twos.append(two)
        for g in range(groups):
            value = start[ROWS * g : ROWS * (g + 1), LANES * t : LANES * (t + 1)] * scale_t
            first[g] = value if t == 0 else value + decay_t * first[g]
            value = scale_t * first[g]
            second[g] = value if t == 0 else value + decay_t * second[g]
            local.append(second[g])

    a, b = ones[-1], twos[-1]
    head = segment == 0
    first = [jnp.where(head, f + a * e, f) for f, e in zip(first, entry)]
    second = [jnp.where(head, s + b * e + a * e, s) for s, e in zip(second, entry)]
    distance = 1
    while distance < blocks * segments:
        opened = segment >= distance
        a_open, b_open = jnp.where(opened, a, 0.0), jnp.where(opened, b, 0.0)
        ahead = [earlier(f, distance) for f in first]
        second = [s + b_open * f + a_open * earlier(s, distance) for s, f in zip(second, ahead)]
        first = [f + a_open * e for f, e in zip(first, ahead)]
        if 2 * distance < blocks * segments:
            a_ahead = earlier(a, distance)
            b = b * a_ahead + a * earlier(b, distance)
            a = a * a_ahead
        distance *= 2
    carry_one = [jnp.where(head, e, earlier(f, 1)) for e, f in zip(entry, first)]
    carry_two = [jnp.where(head, e, earlier(s, 1)) for e, s in zip(entry, second)]
    columns = [
        jnp.concatenate(
            [
                local[t * groups + g] + twos[t] * carry_one[g] + ones[t] * carry_two[g]
                for g in range(groups)
            ],
            axis=0,
        )
        for t in range(times)
    ]

    matrix_high, matrix_low = rounded(interaction_ref[...])
    block_row = jnp.concatenate([matrix_high, matrix_low, matrix_high], axis=1)
    blank = jnp.zeros_like(block_row)
    left = jnp.concatenate(
        [
            jnp.concatenate([block_row, blank], axis=1),
            jnp.concatenate([blank, block_row], axis=1),
        ],
        axis=0,
    ).astype(BF16)
    half = times // 2
    base = jnp.concatenate(
        [
            jnp.concatenate(columns[:half], axis=1),
            jnp.concatenate(columns[half:], axis=1),
        ],
        axis=0,
    )
    iterate = base
    for step in range(NEWTON):
        high, low = rounded(jnp.tanh(iterate))
        right = jnp.concatenate(
            [
                high[:species],
                high[:species],
                low[:species],
                high[species:],
                high[species:],
                low[species:],
            ],
            axis=0,
        ).astype(BF16)
        iterate = base - jnp.dot(left, right, preferred_element_type=F32)
    iterate = jnp.concatenate([iterate[:species], iterate[species:]], axis=1)

    length = jnp.zeros((ROWS, LANES), jnp.int32)
    for one_line in range(lines):
        one_length = jnp.broadcast_to(length_ref[:, one_line : one_line + 1], (ROWS, LANES))
        length = jnp.where(line == one_line, one_length, length)
    node = block * LANES + part * times
    weight = jnp.concatenate(
        [
            jnp.where(node + t < length, jnp.broadcast_to(flux[t : t + 1], (ROWS, LANES)), 0.0)
            for t in range(times)
        ],
        axis=1,
    )
    first_row = lax.broadcasted_iota(jnp.int32, weight.shape, 0) == 0
    scaled = [iterate[ROWS * g : ROWS * (g + 1)] * weight for g in range(groups)]
    scaled.append(jnp.where(first_row, weight, 0.0))
    left = split(jnp.concatenate(scaled, axis=0))
    relative = lane_groups(cap, here + bundle)

    def scatter(k, carry):
        sums = lax.dot_general(
            left,
            hot(k) if kept is None else kept,
            (((1,), (1,)), ((), ())),
            preferred_element_type=F32,
        )
        sums = sums[:rows] + sums[rows:]
        last = [sums[species : species + 1]]
        last += [
            sums[ROWS * g + r : ROWS * g + r + 1] for g in range(groups) for r in range(sent, ROWS)
        ]
        last.append(jnp.zeros((ROWS - len(last), 2 * LANES), F32))
        sums = jnp.concatenate([sums[:species]] + last, axis=0)
        for half in range(2):
            tiles = pack(
                [
                    sums[ROWS * g : ROWS * (g + 1), LANES * half : LANES * (half + 1)]
                    for g in range(all_groups)
                ],
                cap,
                bundle,
                relative,
            )
            for j in range(all_groups):
                owner = k * chunk_owners + half * all_groups + j
                for copy in range(copies):
                    for r in range(sent):
                        out_ref[owner * copies + copy, :, LANES * r : LANES * (r + 1)] = tiles[j][
                            r : r + 1
                        ]
        return carry

    repeat_steps(chunks, scatter, 0)


def blend_kernel(bundles, sums_ref, request_ref, pore_ref, cell_ref, out_hbm, out_ref, out_sem):
    owners = sums_ref.shape[0] // bundles
    sent = sums_ref.shape[2] // LANES
    species, cells = cell_ref.shape
    cap = request_ref.shape[3]
    all_groups = LANES // cap
    groups = species // ROWS
    width = 2 * LANES
    highs = cells // width
    chunks = owners // ROWS
    here = lax.axis_index("grid")
    sublane = lax.broadcasted_iota(jnp.int32, (ROWS, LANES), 0)

    def tile(device, bundle):
        value = jnp.zeros((ROWS, LANES), F32)
        for r in range(sent):
            row = sums_ref[device * bundles + bundle, :, LANES * r : LANES * (r + 1)]
            value = jnp.where(sublane == r, jnp.broadcast_to(row, (ROWS, LANES)), value)
        return value

    def chunk(k, total):
        values, weights, indices = [], [], []
        for t in range(bundles // all_groups):
            block = jnp.concatenate(
                [
                    request_ref[
                        t * all_groups
                        + lax.rem(x + all_groups - lax.rem(here, all_groups), all_groups),
                        0,
                        pl.ds(k * ROWS, ROWS),
                        :,
                    ]
                    for x in range(all_groups)
                ],
                axis=1,
            )
            straight = block
            for turn in range(1, all_groups):
                block = jnp.where(
                    sublane % all_groups == turn, pltpu.roll(straight, turn * cap, 1), block
                )
            for d in range(ROWS):
                found = unpack(
                    [tile(k * ROWS + d, t * all_groups + j) for j in range(all_groups)],
                    cap,
                    lane_groups(cap, here + d),
                    all_groups,
                )
                weights.append(found[groups][:1])
                spare = 1
                for g in range(groups):
                    for r in range(sent, ROWS):
                        row = jnp.broadcast_to(
                            found[groups][spare : spare + 1], (ROWS, LANES)
                        )
                        found[g] = jnp.where(sublane == r, row, found[g])
                        spare += 1
                values.append(jnp.concatenate(found[:groups], axis=0))
                indices.append(block[d : d + 1])
        parts = split(jnp.concatenate(values, axis=1))
        weight_high, weight_low = rounded(jnp.concatenate(weights, axis=1))
        index = jnp.concatenate(indices, axis=1)
        entries = index.shape[1]
        high = jnp.broadcast_to(index // width, (2 * ROWS, entries)).astype(F32).astype(BF16)
        low = jnp.broadcast_to(index % width, (2 * ROWS, entries)).astype(F32).astype(BF16)
        low = jnp.concatenate([low] * (width // (2 * ROWS)), axis=0)
        place = lax.broadcasted_iota(jnp.int32, (width, entries), 0).astype(F32).astype(BF16)
        hot = jnp.where(place == low, jnp.ones_like(place), jnp.zeros_like(place))
        zero = jnp.zeros((2 * ROWS, entries), BF16)
        pieces = []
        for h in range(highs):
            mask = high == jnp.array(h, BF16)
            for r in range(2 * species // (2 * ROWS)):
                pieces.append(
                    jnp.where(mask, parts[2 * ROWS * r : 2 * ROWS * (r + 1)], zero)
                )
        for first in range(0, highs, 2 * ROWS):
            mask = high == (
                lax.broadcasted_iota(jnp.int32, (2 * ROWS, entries), 0) + first
            ).astype(F32).astype(BF16)
            for part in (weight_high, weight_low):
                row = jnp.broadcast_to(part, (2 * ROWS, entries)).astype(BF16)
                pieces.append(jnp.where(mask, row, zero))
        left = jnp.concatenate(pieces, axis=0)
        product = lax.dot_general(
            left, hot, (((1,), (1,)), ((), ())), preferred_element_type=F32
        )
        return product if chunks == 1 else total + product

    flux_rows = -(-highs // (2 * ROWS)) * 4 * ROWS
    total = repeat_steps(
        chunks,
        chunk,
        jnp.zeros((highs * 2 * species + flux_rows, width), F32) if chunks > 1 else 0,
    )
    flux = total[highs * 2 * species :]
    copies = []
    stride = max(highs // 4, 1)
    for h in range(highs):
        part = total[2 * species * h : 2 * species * (h + 1)]
        part = part[:species] + part[species:]
        row = h // (2 * ROWS) * 4 * ROWS + h % (2 * ROWS)
        pore = pore_ref[:, width * h : width * (h + 1)]
        inverse = 1.0 / (pore + flux[row : row + 1] + flux[row + 2 * ROWS : row + 2 * ROWS + 1])
        columns = pl.ds(width * h, width)
        out_ref[:, columns] = (pore * cell_ref[:, columns] + part) * inverse
        if h % stride == stride - 1:
            columns = pl.ds(width * (h - stride + 1), stride * width)
            copies.append(
                pltpu.make_async_copy(
                    out_ref.at[:, columns], out_hbm.at[:, columns], out_sem.at[h // stride]
                )
            )
            copies[-1].start()
    for copy in copies:
        copy.wait()


def call(kernel, shape, operands, kinds={}, scratch=(), grant=VMEM_BYTES, out=pltpu.VMEM):
    return pl.pallas_call(
        kernel,
        out_shape=jax.ShapeDtypeStruct(shape, F32),
        in_specs=[
            pl.BlockSpec(memory_space=kinds.get(i, pltpu.VMEM)) for i in range(len(operands))
        ],
        out_specs=pl.BlockSpec(memory_space=out),
        scratch_shapes=list(scratch),
        compiler_params=pltpu.CompilerParams(vmem_limit_bytes=grant),
    )(*operands)


def shards(
    bundles,
    cell_state,
    pore_volume,
    request_cell,
    node_slot,
    line_length,
    courant,
    flux_weight,
    inflow,
    interaction,
):
    owners, cap = request_cell.shape[2:]
    sent = -(-(cell_state.shape[0] + 1) // (LANES // cap))
    outgoing = call(
        pick_kernel,
        (owners, ROWS, LANES),
        (cell_state, request_cell),
        kinds={0: pltpu.HBM, 1: pltpu.HBM},
        scratch=(
            pltpu.VMEM((ROWS, cell_state.shape[1]), F32),
            pltpu.VMEM(request_cell.shape, jnp.int32),
            pltpu.SemaphoreType.DMA,
            pltpu.SemaphoreType.DMA,
        ),
        grant=PICK_BYTES,
    )
    outgoing = outgoing.reshape(owners * bundles, ROWS // bundles, LANES)
    table = lax.all_to_all(outgoing, ("grid", "bundle"), split_axis=0, concat_axis=0, tiled=True)
    table = table.reshape(owners, ROWS, LANES)
    sums = call(
        functools.partial(lines_kernel, cap),
        (owners * bundles, 1, sent * LANES),
        (table, node_slot, line_length, courant, flux_weight, inflow, interaction),
    )
    back = lax.all_to_all(sums, ("grid", "bundle"), split_axis=0, concat_axis=0, tiled=True)
    return call(
        functools.partial(blend_kernel, bundles),
        cell_state.shape,
        (back, request_cell, pore_volume[None, :], cell_state),
        scratch=(pltpu.VMEM(cell_state.shape, F32), pltpu.SemaphoreType.DMA((4,))),
        out=pltpu.HBM,
    )


def solution(mesh):
    placed = (
        P(None, "grid"),
        P("grid"),
        P(None, "grid", None, None),
        P("bundle", "grid", None),
        P("bundle", "grid"),
        P("bundle", "grid", None),
        P("bundle", "grid", None),
        P("bundle", None),
        P(),
    )
    return jax.shard_map(
        functools.partial(shards, mesh.shape["bundle"]),
        mesh=mesh,
        in_specs=placed,
        out_specs=P(None, "grid"),
        check_vma=False,
    )
```

```python
import functools

import jax
import jax.numpy as jnp
from jax import lax
from jax.experimental import pallas as pl
from jax.experimental.pallas import tpu as pltpu
from jax.sharding import PartitionSpec as P

SUB = 2
NEWTON = 3
LANES = 128
ROWS = 8
F32 = jnp.float32
BF16 = jnp.bfloat16
VMEM_BYTES = 32 * 1024 * 1024
PICK_BYTES = 63_000_000
CHUNKS = 4


def repeat_steps(count, body, carry):
    if count == 1:
        return body(0, carry)
    return lax.fori_loop(0, count, body, carry)


def rounded(value):
    high = value.astype(BF16).astype(F32)
    return high, value - high


def split(value):
    return jnp.concatenate(rounded(value), axis=0).astype(BF16)


def select_groups(tiles, relative):
    count = len(tiles)
    results = []
    for i in range(count):
        value = tiles[0]
        for j in range(1, count):
            value = jnp.where(relative == (i + j) % count, tiles[j], value)
        results.append(value)
    return results


def lane_groups(cap, turn):
    groups = LANES // cap
    lane = lax.broadcasted_iota(jnp.int32, (ROWS, LANES), 1)
    return (lane // cap + (2 * groups - lax.rem(turn, groups))) % groups


def pack(rows, cap, turn, relative):
    groups = LANES // cap
    turned = [
        pltpu.roll(rows[g], lax.rem(turn + g, groups) * cap, 1) for g in range(groups)
    ]
    return select_groups(turned, relative)


def unpack(tiles, cap, relative, count):
    found = select_groups(tiles, relative)[:count]
    return [
        found[g] if g == 0 else pltpu.roll(found[g], LANES - g * cap, 1) for g in range(count)
    ]


def exchange_groups(tiles, width):
    tiles = list(tiles)
    lane_group = lax.broadcasted_iota(jnp.int32, tiles[0].shape, 1) // width
    step = 1
    while step < len(tiles):
        keep = (lane_group & step) == 0
        for i in range(len(tiles)):
            if i & step == 0:
                first, second = tiles[i], tiles[i | step]
                tiles[i] = jnp.where(keep, first, pltpu.roll(second, step * width, 1))
                tiles[i | step] = jnp.where(
                    keep, pltpu.roll(first, LANES - step * width, 1), second
                )
        step *= 2
    return tiles


def spread_rows(block, cap):
    groups = block.shape[0]
    wide = jnp.concatenate([block] * groups, axis=1)
    rows = lax.broadcasted_iota(jnp.int32, wide.shape, 0)
    lanes = lax.broadcasted_iota(jnp.int32, wide.shape, 1) // cap
    return jnp.sum(jnp.where(rows == lanes, wide, 0), axis=0, keepdims=True)


def pick_kernel(cell_hbm, request_hbm, out_ref, cell_ref, request_ref, cell_sem, request_sem):
    request_copy = pltpu.make_async_copy(
        request_hbm.at[lax.axis_index("bundle"), 0], request_ref, request_sem
    )
    cell_copy = pltpu.make_async_copy(cell_hbm, cell_ref, cell_sem)
    request_copy.start()
    cell_copy.start()
    species, cells = cell_ref.shape
    owners, cap = request_ref.shape
    groups = LANES // cap
    chunks = owners // (2 * groups)
    highs = cells // LANES
    here = lax.axis_index("grid")
    relative = lane_groups(cap, here)
    request_copy.wait()

    def wanted(k):
        block = request_ref[pl.ds(k * 2 * groups, 2 * groups), :]
        index = jnp.concatenate(
            [spread_rows(block[:groups], cap), spread_rows(block[groups:], cap)], axis=1
        )
        low = index % LANES
        high = index // LANES
        hot = (
            (lax.broadcasted_iota(jnp.int32, (LANES, 2 * LANES), 0) == low)
            .astype(F32)
            .astype(BF16)
        )
        return high, jnp.concatenate([hot, hot], axis=0)

    kept = wanted(0) if chunks == 1 else None
    cell_copy.wait()
    cell = cell_ref[...]
    stacked = jnp.concatenate(
        [cell[:, LANES * h : LANES * (h + 1)] for h in range(highs)], axis=0
    )
    left = jnp.concatenate(rounded(stacked), axis=1).astype(BF16)

    def chunk(k, carry):
        first = k * 2 * groups
        high, right = wanted(k) if kept is None else kept
        product = jnp.dot(left, right, preferred_element_type=F32)
        picked = jnp.zeros((species, 2 * LANES), F32)
        for h in range(highs):
            picked = picked + jnp.where(high == h, product[species * h : species * (h + 1)], 0.0)
        blank = jnp.zeros((groups * ROWS - species, 2 * LANES), F32)
        picked = jnp.concatenate([picked, blank], axis=0)
        for half in range(2):
            tiles = pack(
                [
                    picked[ROWS * g : ROWS * (g + 1), LANES * half : LANES * (half + 1)]
                    for g in range(groups)
                ],
                cap,
                here,
                relative,
            )
            for j in range(groups):
                out_ref[first + half * groups + j] = tiles[j]
        return carry

    repeat_steps(chunks, chunk, 0)


def to_segments(values):
    lines, nodes = values[0].shape
    blocks = nodes // LANES
    width = lines * blocks
    groups = LANES // width
    stacked = []
    for value in values:
        value = value.astype(F32)
        stacked += [value[:, LANES * block : LANES * (block + 1)] for block in range(blocks)]
    stacked.append(jnp.zeros((LANES - width * len(values), LANES), F32))
    turned = jnp.transpose(jnp.concatenate(stacked, axis=0))
    times = LANES // groups
    return exchange_groups([turned[times * g : times * (g + 1)] for g in range(groups)], width)


def lines_kernel(
    cap,
    table_ref,
    slot_ref,
    length_ref,
    courant_ref,
    flux_ref,
    inflow_ref,
    interaction_ref,
    out_ref,
):
    owners = table_ref.shape[0]
    copies = out_ref.shape[0] // owners
    species = inflow_ref.shape[1]
    lines, nodes = slot_ref.shape[1:]
    groups = species // ROWS
    all_groups = LANES // cap
    rows = all_groups * ROWS
    blocks = nodes // LANES
    width = lines * blocks
    segments = LANES // width
    times = LANES // segments
    chunk_owners = 2 * all_groups
    chunks = owners // chunk_owners
    here, bundle = lax.axis_index("grid"), lax.axis_index("bundle")

    slot = slot_ref[0]
    within = (slot + lax.rem(here, all_groups) * cap) % LANES
    slot, courant, flux = to_segments([slot - slot % LANES + within, courant_ref[0], flux_ref[0]])[
        :3
    ]

    def hot(k):
        local = (slot - lax.convert_element_type(k * 2 * LANES, F32)).astype(BF16)
        index = lax.broadcasted_iota(jnp.int32, (2 * LANES, LANES), 0).astype(F32).astype(BF16)
        one, zero = jnp.ones_like(index), jnp.zeros_like(index)
        return jnp.concatenate(
            [
                jnp.where(jnp.broadcast_to(local[t : t + 1], index.shape) == index, one, zero)
                for t in range(times)
            ],
            axis=1,
        )

    kept = hot(0) if chunks == 1 else None

    relative = lane_groups(cap, here)

    def gather(k, state):
        halves = []
        for half in range(2):
            first = k * chunk_owners + half * all_groups
            halves.append(
                jnp.concatenate(
                    unpack(
                        [table_ref[first + j] for j in range(all_groups)], cap, relative, groups
                    ),
                    axis=0,
                )
            )
        left = split(jnp.concatenate(halves, axis=1))
        found = jnp.dot(left, hot(k) if kept is None else kept, preferred_element_type=F32)
        found = found[:species] + found[species:]
        return found if chunks == 1 else state + found

    start = repeat_steps(
        chunks, gather, jnp.zeros((species, lines * nodes), F32) if chunks > 1 else 0
    )

    lane = lax.broadcasted_iota(jnp.int32, (ROWS, LANES), 1)
    part = lane // width
    block = (lane % width) // lines
    segment = block * segments + part
    line = lane % lines

    def earlier(value, distance):
        major, minor = distance // segments, distance % segments
        near = pltpu.roll(value, minor * width + major * lines, 1)
        if minor == 0:
            return near
        far = pltpu.roll(value, minor * width + (major + 1) * lines, 1)
        return jnp.where(part >= minor, near, far)

    eye = lax.broadcasted_iota(jnp.int32, (species, LANES), 0) == lax.broadcasted_iota(
        jnp.int32, (species, LANES), 1
    )
    padded = jnp.concatenate([inflow_ref[...], jnp.zeros((1, LANES - species), F32)], axis=1)
    column = jnp.sum(jnp.where(eye, padded, 0.0), axis=1, keepdims=True)
    entry = jnp.broadcast_to(column, (species, LANES))
    entry = [entry[ROWS * g : ROWS * (g + 1)] for g in range(groups)]

    scale = 1.0 / (1.0 + courant)
    decay = courant * scale
    first = [None] * groups
    second = [None] * groups
    local, ones, twos = [], [], []
    for t in range(times):
        scale_t = jnp.broadcast_to(scale[t : t + 1], (ROWS, LANES))
        decay_t = jnp.broadcast_to(decay[t : t + 1], (ROWS, LANES))
        one = decay_t if t == 0 else decay_t * ones[-1]
        two = scale_t * one if t == 0 else scale_t * one + decay_t * twos[-1]
        ones.append(one)
        twos.append(two)
        for g in range(groups):
            value = start[ROWS * g : ROWS * (g + 1), LANES * t : LANES * (t + 1)] * scale_t
            first[g] = value if t == 0 else value + decay_t * first[g]
            value = scale_t * first[g]
            second[g] = value if t == 0 else value + decay_t * second[g]
            local.append(second[g])

    a, b = ones[-1], twos[-1]
    head = segment == 0
    first = [jnp.where(head, f + a * e, f) for f, e in zip(first, entry)]
    second = [jnp.where(head, s + b * e + a * e, s) for s, e in zip(second, entry)]
    distance = 1
    while distance < blocks * segments:
        run_a, run_b = a, b
        next_first, next_second = first, second
        for k in range(1, 4):
            if k * distance >= blocks * segments:
                break
            opened = segment >= k * distance
            a_open, b_open = jnp.where(opened, run_a, 0.0), jnp.where(opened, run_b, 0.0)
            ahead = [earlier(f, k * distance) for f in first]
            next_first = [n + a_open * f for n, f in zip(next_first, ahead)]
            next_second = [
                n + b_open * f + a_open * earlier(s, k * distance)
                for n, s, f in zip(next_second, second, ahead)
            ]
            a_ahead = earlier(a, k * distance)
            run_b = run_b * a_ahead + run_a * earlier(b, k * distance)
            run_a = run_a * a_ahead
        first, second = next_first, next_second
        a, b = run_a, run_b
        distance *= 4
    carry_one = [jnp.where(head, e, earlier(f, 1)) for e, f in zip(entry, first)]
    carry_two = [jnp.where(head, e, earlier(s, 1)) for e, s in zip(entry, second)]
    columns = [
        jnp.concatenate(
            [
                local[t * groups + g] + twos[t] * carry_one[g] + ones[t] * carry_two[g]
                for g in range(groups)
            ],
            axis=0,
        )
        for t in range(times)
    ]

    matrix_high, matrix_low = rounded(interaction_ref[...])
    block_row = jnp.concatenate([matrix_high, matrix_low, matrix_high], axis=1)
    blank = jnp.zeros_like(block_row)
    left = jnp.concatenate(
        [
            jnp.concatenate([block_row, blank], axis=1),
            jnp.concatenate([blank, block_row], axis=1),
        ],
        axis=0,
    ).astype(BF16)
    half = times // 2
    depth = half // CHUNKS
    bases = [
        jnp.concatenate(
            [
                jnp.concatenate(columns[offset + c * depth : offset + (c + 1) * depth], axis=1)
                for offset in (0, half)
            ],
            axis=0,
        )
        for c in range(CHUNKS)
    ]
    iterates = list(bases)
    for step in range(NEWTON):
        for c in range(CHUNKS):
            high, low = rounded(jnp.tanh(iterates[c]))
            right = jnp.concatenate(
                [
                    high[:species],
                    high[:species],
                    low[:species],
                    high[species:],
                    high[species:],
                    low[species:],
                ],
                axis=0,
            ).astype(BF16)
            iterates[c] = bases[c] - jnp.dot(left, right, preferred_element_type=F32)

    length = jnp.zeros((ROWS, LANES), jnp.int32)
    for one_line in range(lines):
        one_length = jnp.broadcast_to(length_ref[:, one_line : one_line + 1], (ROWS, LANES))
        length = jnp.where(line == one_line, one_length, length)
    node = block * LANES + part * times
    top = lax.broadcasted_iota(jnp.int32, (ROWS, LANES), 0) == 0
    pieces = []
    for t in range(times):
        weight = jnp.broadcast_to(flux[t : t + 1], (ROWS, LANES))
        weight = jnp.where(node + t < length, weight, 0.0)
        chunk, place = t % half // depth, t % half % depth
        found = iterates[chunk][
            t // half * species : (t // half + 1) * species, LANES * place : LANES * (place + 1)
        ]
        scaled = [found[ROWS * g : ROWS * (g + 1)] * weight for g in range(groups)]
        scaled.append(jnp.where(top, weight, 0.0))
        pieces.append(jnp.concatenate(scaled, axis=0))
    left = split(jnp.concatenate(pieces, axis=1))
    relative = lane_groups(cap, here + bundle)

    def scatter(k, carry):
        sums = lax.dot_general(
            left,
            hot(k) if kept is None else kept,
            (((1,), (1,)), ((), ())),
            preferred_element_type=F32,
        )
        sums = sums[:rows] + sums[rows:]
        for half in range(2):
            tiles = pack(
                [
                    sums[ROWS * g : ROWS * (g + 1), LANES * half : LANES * (half + 1)]
                    for g in range(all_groups)
                ],
                cap,
                bundle,
                relative,
            )
            for j in range(all_groups):
                owner = k * chunk_owners + half * all_groups + j
                for copy in range(copies):
                    out_ref[owner * copies + copy] = tiles[j]
        return carry

    repeat_steps(chunks, scatter, 0)


def blend_kernel(bundles, sums_ref, request_ref, pore_ref, cell_ref, out_hbm, out_ref, out_sem):
    owners = sums_ref.shape[0] // bundles
    species, cells = cell_ref.shape
    cap = request_ref.shape[3]
    all_groups = LANES // cap
    groups = species // ROWS
    width = 2 * LANES
    highs = cells // width
    chunks = owners // ROWS
    here = lax.axis_index("grid")
    sublane = lax.broadcasted_iota(jnp.int32, (ROWS, LANES), 0)

    def chunk(k, total):
        values, weights, indices = [], [], []
        for t in range(bundles // all_groups):
            block = jnp.concatenate(
                [
                    request_ref[
                        t * all_groups
                        + lax.rem(x + all_groups - lax.rem(here, all_groups), all_groups),
                        0,
                        pl.ds(k * ROWS, ROWS),
                        :,
                    ]
                    for x in range(all_groups)
                ],
                axis=1,
            )
            straight = block
            for turn in range(1, all_groups):
                block = jnp.where(
                    sublane % all_groups == turn, pltpu.roll(straight, turn * cap, 1), block
                )
            for d in range(ROWS):
                found = unpack(
                    [
                        sums_ref[(k * ROWS + d) * bundles + t * all_groups + j]
                        for j in range(all_groups)
                    ],
                    cap,
                    lane_groups(cap, here + d),
                    all_groups,
                )
                weights.append(found[groups][:1])
                values.append(jnp.concatenate(found[:groups], axis=0))
                indices.append(block[d : d + 1])
        parts = split(jnp.concatenate(values, axis=1))
        weight_high, weight_low = rounded(jnp.concatenate(weights, axis=1))
        index = jnp.concatenate(indices, axis=1)
        entries = index.shape[1]
        high = jnp.broadcast_to(index // width, (2 * ROWS, entries)).astype(F32).astype(BF16)
        low = jnp.broadcast_to(index % width, (2 * ROWS, entries)).astype(F32).astype(BF16)
        low = jnp.concatenate([low] * (width // (2 * ROWS)), axis=0)
        place = lax.broadcasted_iota(jnp.int32, (width, entries), 0).astype(F32).astype(BF16)
        hot = jnp.where(place == low, jnp.ones_like(place), jnp.zeros_like(place))
        zero = jnp.zeros((2 * ROWS, entries), BF16)
        pieces = []
        for h in range(highs):
            mask = high == jnp.array(h, BF16)
            for r in range(2 * species // (2 * ROWS)):
                pieces.append(
                    jnp.where(mask, parts[2 * ROWS * r : 2 * ROWS * (r + 1)], zero)
                )
        for first in range(0, highs, 2 * ROWS):
            mask = high == (
                lax.broadcasted_iota(jnp.int32, (2 * ROWS, entries), 0) + first
            ).astype(F32).astype(BF16)
            for part in (weight_high, weight_low):
                row = jnp.broadcast_to(part, (2 * ROWS, entries)).astype(BF16)
                pieces.append(jnp.where(mask, row, zero))
        left = jnp.concatenate(pieces, axis=0)
        product = lax.dot_general(
            left, hot, (((1,), (1,)), ((), ())), preferred_element_type=F32
        )
        return product if chunks == 1 else total + product

    flux_rows = -(-highs // (2 * ROWS)) * 4 * ROWS
    total = repeat_steps(
        chunks,
        chunk,
        jnp.zeros((highs * 2 * species + flux_rows, width), F32) if chunks > 1 else 0,
    )
    flux = total[highs * 2 * species :]
    copies = []
    stride = max(highs // 4, 1)
    for h in range(highs):
        part = total[2 * species * h : 2 * species * (h + 1)]
        part = part[:species] + part[species:]
        row = h // (2 * ROWS) * 4 * ROWS + h % (2 * ROWS)
        pore = pore_ref[:, width * h : width * (h + 1)]
        inverse = 1.0 / (pore + flux[row : row + 1] + flux[row + 2 * ROWS : row + 2 * ROWS + 1])
        columns = pl.ds(width * h, width)
        out_ref[:, columns] = (pore * cell_ref[:, columns] + part) * inverse
        if h % stride == stride - 1:
            columns = pl.ds(width * (h - stride + 1), stride * width)
            copies.append(
                pltpu.make_async_copy(
                    out_ref.at[:, columns], out_hbm.at[:, columns], out_sem.at[h // stride]
                )
            )
            copies[-1].start()
    for copy in copies:
        copy.wait()


def call(kernel, shape, operands, kinds={}, scratch=(), grant=VMEM_BYTES, out=pltpu.VMEM):
    return pl.pallas_call(
        kernel,
        out_shape=jax.ShapeDtypeStruct(shape, F32),
        in_specs=[
            pl.BlockSpec(memory_space=kinds.get(i, pltpu.VMEM)) for i in range(len(operands))
        ],
        out_specs=pl.BlockSpec(memory_space=out),
        scratch_shapes=list(scratch),
        compiler_params=pltpu.CompilerParams(vmem_limit_bytes=grant),
    )(*operands)


def shards(
    bundles,
    cell_state,
    pore_volume,
    request_cell,
    node_slot,
    line_length,
    courant,
    flux_weight,
    inflow,
    interaction,
):
    owners, cap = request_cell.shape[2:]
    outgoing = call(
        pick_kernel,
        (owners, ROWS, LANES),
        (cell_state, request_cell),
        kinds={0: pltpu.HBM, 1: pltpu.HBM},
        scratch=(
            pltpu.VMEM(cell_state.shape, F32),
            pltpu.VMEM((owners, cap), jnp.int32),
            pltpu.SemaphoreType.DMA,
            pltpu.SemaphoreType.DMA,
        ),
        grant=PICK_BYTES,
    )
    table = lax.all_to_all(outgoing, "grid", split_axis=0, concat_axis=0, tiled=True)
    sums = call(
        functools.partial(lines_kernel, cap),
        (owners * bundles, ROWS, LANES),
        (table, node_slot, line_length, courant, flux_weight, inflow, interaction),
    )
    back = lax.all_to_all(sums, ("grid", "bundle"), split_axis=0, concat_axis=0, tiled=True)
    return call(
        functools.partial(blend_kernel, bundles),
        cell_state.shape,
        (back, request_cell, pore_volume[None, :], cell_state),
        scratch=(pltpu.VMEM(cell_state.shape, F32), pltpu.SemaphoreType.DMA((4,))),
        out=pltpu.HBM,
    )


def solution(mesh):
    placed = (
        P(None, "grid"),
        P("grid"),
        P(None, "grid", None, None),
        P("bundle", "grid", None),
        P("bundle", "grid"),
        P("bundle", "grid", None),
        P("bundle", "grid", None),
        P("bundle", None),
        P(),
    )
    return jax.shard_map(
        functools.partial(shards, mesh.shape["bundle"]),
        mesh=mesh,
        in_specs=placed,
        out_specs=P(None, "grid"),
        check_vma=False,
    )
```

```python
import functools

import jax
import jax.numpy as jnp
from jax import lax
from jax.experimental import pallas as pl
from jax.experimental.pallas import tpu as pltpu
from jax.sharding import PartitionSpec as P

SUB = 2
NEWTON = 3
LANES = 128
ROWS = 8
F32 = jnp.float32
BF16 = jnp.bfloat16
VMEM_BYTES = 32 * 1024 * 1024
CHUNKS = 4


def repeat_steps(count, body, carry):
    if count == 1:
        return body(0, carry)
    return lax.fori_loop(0, count, body, carry)


def rounded(value):
    high = value.astype(BF16).astype(F32)
    return high, value - high


def split(value):
    return jnp.concatenate(rounded(value), axis=0).astype(BF16)


def select_groups(tiles, relative):
    count = len(tiles)
    results = []
    for i in range(count):
        value = tiles[0]
        for j in range(1, count):
            value = jnp.where(relative == (i + j) % count, tiles[j], value)
        results.append(value)
    return results


def lane_groups(cap, turn):
    groups = LANES // cap
    lane = lax.broadcasted_iota(jnp.int32, (ROWS, LANES), 1)
    return (lane // cap + (2 * groups - lax.rem(turn, groups))) % groups


def pack(rows, cap, turn, relative):
    groups = LANES // cap
    turned = [
        pltpu.roll(rows[g], lax.rem(turn + g, groups) * cap, 1) for g in range(groups)
    ]
    return select_groups(turned, relative)


def unpack(tiles, cap, relative, count):
    found = select_groups(tiles, relative)[:count]
    return [
        found[g] if g == 0 else pltpu.roll(found[g], LANES - g * cap, 1) for g in range(count)
    ]


def exchange_groups(tiles, width):
    tiles = list(tiles)
    lane_group = lax.broadcasted_iota(jnp.int32, tiles[0].shape, 1) // width
    step = 1
    while step < len(tiles):
        keep = (lane_group & step) == 0
        for i in range(len(tiles)):
            if i & step == 0:
                first, second = tiles[i], tiles[i | step]
                tiles[i] = jnp.where(keep, first, pltpu.roll(second, step * width, 1))
                tiles[i | step] = jnp.where(
                    keep, pltpu.roll(first, LANES - step * width, 1), second
                )
        step *= 2
    return tiles


def spread_rows(block, cap):
    groups = block.shape[0]
    wide = jnp.concatenate([block] * groups, axis=1)
    rows = lax.broadcasted_iota(jnp.int32, wide.shape, 0)
    lanes = lax.broadcasted_iota(jnp.int32, wide.shape, 1) // cap
    return jnp.sum(jnp.where(rows == lanes, wide, 0), axis=0, keepdims=True)


def first_kernel(out_ref):
    out_ref[...] = jnp.zeros_like(out_ref)


def pick_kernel(cell_ref, request_ref, first_ref, out_ref):
    species, cells = cell_ref.shape
    owners, cap = request_ref.shape[2:]
    bundle = lax.axis_index("bundle")
    groups = LANES // cap
    chunks = owners // (2 * groups)
    highs = cells // LANES
    here = lax.axis_index("grid")
    relative = lane_groups(cap, here)

    def wanted(k):
        block = request_ref[bundle, 0, pl.ds(k * 2 * groups, 2 * groups), :]
        index = jnp.concatenate(
            [spread_rows(block[:groups], cap), spread_rows(block[groups:], cap)], axis=1
        )
        low = index % LANES
        high = index // LANES
        hot = (
            (lax.broadcasted_iota(jnp.int32, (LANES, 2 * LANES), 0) == low)
            .astype(F32)
            .astype(BF16)
        )
        return high, jnp.concatenate([hot, hot], axis=0)

    kept = wanted(0) if chunks == 1 else None
    cell = cell_ref[...]
    stacked = jnp.concatenate(
        [cell[:, LANES * h : LANES * (h + 1)] for h in range(highs)], axis=0
    )
    left = jnp.concatenate(rounded(stacked), axis=1).astype(BF16)

    def chunk(k, carry):
        first = k * 2 * groups
        high, right = wanted(k) if kept is None else kept
        product = jnp.dot(left, right, preferred_element_type=F32)
        picked = jnp.zeros((species, 2 * LANES), F32)
        for h in range(highs):
            picked = picked + jnp.where(high == h, product[species * h : species * (h + 1)], 0.0)
        blank = jnp.zeros((groups * ROWS - species, 2 * LANES), F32)
        picked = jnp.concatenate([picked, blank], axis=0)
        for half in range(2):
            tiles = pack(
                [
                    picked[ROWS * g : ROWS * (g + 1), LANES * half : LANES * (half + 1)]
                    for g in range(groups)
                ],
                cap,
                here,
                relative,
            )
            for j in range(groups):
                out_ref[first + half * groups + j] = tiles[j]
        return carry

    repeat_steps(chunks, chunk, 0)


def to_segments(values):
    lines, nodes = values[0].shape
    blocks = nodes // LANES
    width = lines * blocks
    groups = LANES // width
    stacked = []
    for value in values:
        value = value.astype(F32)
        stacked += [value[:, LANES * block : LANES * (block + 1)] for block in range(blocks)]
    stacked.append(jnp.zeros((LANES - width * len(values), LANES), F32))
    turned = jnp.transpose(jnp.concatenate(stacked, axis=0))
    times = LANES // groups
    return exchange_groups([turned[times * g : times * (g + 1)] for g in range(groups)], width)


def lines_kernel(
    cap,
    table_ref,
    slot_ref,
    length_ref,
    courant_ref,
    flux_ref,
    inflow_ref,
    interaction_ref,
    out_ref,
):
    owners = table_ref.shape[0]
    copies = out_ref.shape[0] // owners
    species = inflow_ref.shape[1]
    lines, nodes = slot_ref.shape[1:]
    groups = species // ROWS
    all_groups = LANES // cap
    rows = all_groups * ROWS
    blocks = nodes // LANES
    width = lines * blocks
    segments = LANES // width
    times = LANES // segments
    chunk_owners = 2 * all_groups
    chunks = owners // chunk_owners
    here, bundle = lax.axis_index("grid"), lax.axis_index("bundle")

    slot = slot_ref[0]
    within = (slot + lax.rem(here, all_groups) * cap) % LANES
    slot, courant, flux = to_segments([slot - slot % LANES + within, courant_ref[0], flux_ref[0]])[
        :3
    ]

    def hot(k):
        local = (slot - lax.convert_element_type(k * 2 * LANES, F32)).astype(BF16)
        index = lax.broadcasted_iota(jnp.int32, (2 * LANES, LANES), 0).astype(F32).astype(BF16)
        one, zero = jnp.ones_like(index), jnp.zeros_like(index)
        return jnp.concatenate(
            [
                jnp.where(jnp.broadcast_to(local[t : t + 1], index.shape) == index, one, zero)
                for t in range(times)
            ],
            axis=1,
        )

    kept = hot(0) if chunks == 1 else None

    relative = lane_groups(cap, here)

    def gather(k, state):
        halves = []
        for half in range(2):
            first = k * chunk_owners + half * all_groups
            halves.append(
                jnp.concatenate(
                    unpack(
                        [table_ref[first + j] for j in range(all_groups)], cap, relative, groups
                    ),
                    axis=0,
                )
            )
        left = split(jnp.concatenate(halves, axis=1))
        found = jnp.dot(left, hot(k) if kept is None else kept, preferred_element_type=F32)
        found = found[:species] + found[species:]
        return found if chunks == 1 else state + found

    start = repeat_steps(
        chunks, gather, jnp.zeros((species, lines * nodes), F32) if chunks > 1 else 0
    )

    lane = lax.broadcasted_iota(jnp.int32, (ROWS, LANES), 1)
    part = lane // width
    block = (lane % width) // lines
    segment = block * segments + part
    line = lane % lines

    def earlier(value, distance):
        major, minor = distance // segments, distance % segments
        near = pltpu.roll(value, minor * width + major * lines, 1)
        if minor == 0:
            return near
        far = pltpu.roll(value, minor * width + (major + 1) * lines, 1)
        return jnp.where(part >= minor, near, far)

    eye = lax.broadcasted_iota(jnp.int32, (species, LANES), 0) == lax.broadcasted_iota(
        jnp.int32, (species, LANES), 1
    )
    padded = jnp.concatenate([inflow_ref[...], jnp.zeros((1, LANES - species), F32)], axis=1)
    column = jnp.sum(jnp.where(eye, padded, 0.0), axis=1, keepdims=True)
    entry = jnp.broadcast_to(column, (species, LANES))
    entry = [entry[ROWS * g : ROWS * (g + 1)] for g in range(groups)]

    scale = 1.0 / (1.0 + courant)
    decay = courant * scale
    first = [None] * groups
    second = [None] * groups
    local, ones, twos = [], [], []
    for t in range(times):
        scale_t = jnp.broadcast_to(scale[t : t + 1], (ROWS, LANES))
        decay_t = jnp.broadcast_to(decay[t : t + 1], (ROWS, LANES))
        one = decay_t if t == 0 else decay_t * ones[-1]
        two = scale_t * one if t == 0 else scale_t * one + decay_t * twos[-1]
        ones.append(one)
        twos.append(two)
        for g in range(groups):
            value = start[ROWS * g : ROWS * (g + 1), LANES * t : LANES * (t + 1)] * scale_t
            first[g] = value if t == 0 else value + decay_t * first[g]
            value = scale_t * first[g]
            second[g] = value if t == 0 else value + decay_t * second[g]
            local.append(second[g])

    a, b = ones[-1], twos[-1]
    head = segment == 0
    first = [jnp.where(head, f + a * e, f) for f, e in zip(first, entry)]
    second = [jnp.where(head, s + b * e + a * e, s) for s, e in zip(second, entry)]
    distance = 1
    while distance < blocks * segments:
        run_a, run_b = a, b
        next_first, next_second = first, second
        for k in range(1, 4):
            if k * distance >= blocks * segments:
                break
            opened = segment >= k * distance
            a_open, b_open = jnp.where(opened, run_a, 0.0), jnp.where(opened, run_b, 0.0)
            ahead = [earlier(f, k * distance) for f in first]
            next_first = [n + a_open * f for n, f in zip(next_first, ahead)]
            next_second = [
                n + b_open * f + a_open * earlier(s, k * distance)
                for n, s, f in zip(next_second, second, ahead)
            ]
            a_ahead = earlier(a, k * distance)
            run_b = run_b * a_ahead + run_a * earlier(b, k * distance)
            run_a = run_a * a_ahead
        first, second = next_first, next_second
        a, b = run_a, run_b
        distance *= 4
    carry_one = [jnp.where(head, e, earlier(f, 1)) for e, f in zip(entry, first)]
    carry_two = [jnp.where(head, e, earlier(s, 1)) for e, s in zip(entry, second)]
    columns = [
        jnp.concatenate(
            [
                local[t * groups + g] + twos[t] * carry_one[g] + ones[t] * carry_two[g]
                for g in range(groups)
            ],
            axis=0,
        )
        for t in range(times)
    ]

    matrix_high, matrix_low = rounded(interaction_ref[...])
    block_row = jnp.concatenate([matrix_high, matrix_low, matrix_high], axis=1)
    blank = jnp.zeros_like(block_row)
    left = jnp.concatenate(
        [
            jnp.concatenate([block_row, blank], axis=1),
            jnp.concatenate([blank, block_row], axis=1),
        ],
        axis=0,
    ).astype(BF16)
    half = times // 2
    depth = half // CHUNKS
    bases = [
        jnp.concatenate(
            [
                jnp.concatenate(columns[offset + c * depth : offset + (c + 1) * depth], axis=1)
                for offset in (0, half)
            ],
            axis=0,
        )
        for c in range(CHUNKS)
    ]
    iterates = list(bases)
    for step in range(NEWTON):
        for c in range(CHUNKS):
            high, low = rounded(jnp.tanh(iterates[c]))
            right = jnp.concatenate(
                [
                    high[:species],
                    high[:species],
                    low[:species],
                    high[species:],
                    high[species:],
                    low[species:],
                ],
                axis=0,
            ).astype(BF16)
            iterates[c] = bases[c] - jnp.dot(left, right, preferred_element_type=F32)

    length = jnp.zeros((ROWS, LANES), jnp.int32)
    for one_line in range(lines):
        one_length = jnp.broadcast_to(length_ref[:, one_line : one_line + 1], (ROWS, LANES))
        length = jnp.where(line == one_line, one_length, length)
    node = block * LANES + part * times
    top = lax.broadcasted_iota(jnp.int32, (ROWS, LANES), 0) == 0
    pieces = []
    for t in range(times):
        weight = jnp.broadcast_to(flux[t : t + 1], (ROWS, LANES))
        weight = jnp.where(node + t < length, weight, 0.0)
        chunk, place = t % half // depth, t % half % depth
        found = iterates[chunk][
            t // half * species : (t // half + 1) * species, LANES * place : LANES * (place + 1)
        ]
        scaled = [found[ROWS * g : ROWS * (g + 1)] * weight for g in range(groups)]
        scaled.append(jnp.where(top, weight, 0.0))
        pieces.append(jnp.concatenate(scaled, axis=0))
    left = split(jnp.concatenate(pieces, axis=1))
    relative = lane_groups(cap, here + bundle)

    def scatter(k, carry):
        sums = lax.dot_general(
            left,
            hot(k) if kept is None else kept,
            (((1,), (1,)), ((), ())),
            preferred_element_type=F32,
        )
        sums = sums[:rows] + sums[rows:]
        for half in range(2):
            tiles = pack(
                [
                    sums[ROWS * g : ROWS * (g + 1), LANES * half : LANES * (half + 1)]
                    for g in range(all_groups)
                ],
                cap,
                bundle,
                relative,
            )
            for j in range(all_groups):
                owner = k * chunk_owners + half * all_groups + j
                for copy in range(copies):
                    out_ref[owner * copies + copy] = tiles[j]
        return carry

    repeat_steps(chunks, scatter, 0)


def blend_kernel(bundles, sums_ref, request_ref, pore_ref, cell_ref, out_hbm, out_ref, out_sem):
    owners = sums_ref.shape[0] // bundles
    species, cells = cell_ref.shape
    cap = request_ref.shape[3]
    all_groups = LANES // cap
    groups = species // ROWS
    width = 2 * LANES
    highs = cells // width
    chunks = owners // ROWS
    here = lax.axis_index("grid")
    sublane = lax.broadcasted_iota(jnp.int32, (ROWS, LANES), 0)

    def chunk(k, total):
        values, weights, indices = [], [], []
        for t in range(bundles // all_groups):
            block = jnp.concatenate(
                [
                    request_ref[
                        t * all_groups
                        + lax.rem(x + all_groups - lax.rem(here, all_groups), all_groups),
                        0,
                        pl.ds(k * ROWS, ROWS),
                        :,
                    ]
                    for x in range(all_groups)
                ],
                axis=1,
            )
            straight = block
            for turn in range(1, all_groups):
                block = jnp.where(
                    sublane % all_groups == turn, pltpu.roll(straight, turn * cap, 1), block
                )
            for d in range(ROWS):
                found = unpack(
                    [
                        sums_ref[(k * ROWS + d) * bundles + t * all_groups + j]
                        for j in range(all_groups)
                    ],
                    cap,
                    lane_groups(cap, here + d),
                    all_groups,
                )
                weights.append(found[groups][:1])
                values.append(jnp.concatenate(found[:groups], axis=0))
                indices.append(block[d : d + 1])
        parts = split(jnp.concatenate(values, axis=1))
        weight_high, weight_low = rounded(jnp.concatenate(weights, axis=1))
        index = jnp.concatenate(indices, axis=1)
        entries = index.shape[1]
        high = jnp.broadcast_to(index // width, (2 * ROWS, entries)).astype(F32).astype(BF16)
        low = jnp.broadcast_to(index % width, (2 * ROWS, entries)).astype(F32).astype(BF16)
        low = jnp.concatenate([low] * (width // (2 * ROWS)), axis=0)
        place = lax.broadcasted_iota(jnp.int32, (width, entries), 0).astype(F32).astype(BF16)
        hot = jnp.where(place == low, jnp.ones_like(place), jnp.zeros_like(place))
        zero = jnp.zeros((2 * ROWS, entries), BF16)
        pieces = []
        for h in range(highs):
            mask = high == jnp.array(h, BF16)
            for r in range(2 * species // (2 * ROWS)):
                pieces.append(
                    jnp.where(mask, parts[2 * ROWS * r : 2 * ROWS * (r + 1)], zero)
                )
        for first in range(0, highs, 2 * ROWS):
            mask = high == (
                lax.broadcasted_iota(jnp.int32, (2 * ROWS, entries), 0) + first
            ).astype(F32).astype(BF16)
            for part in (weight_high, weight_low):
                row = jnp.broadcast_to(part, (2 * ROWS, entries)).astype(BF16)
                pieces.append(jnp.where(mask, row, zero))
        left = jnp.concatenate(pieces, axis=0)
        product = lax.dot_general(
            left, hot, (((1,), (1,)), ((), ())), preferred_element_type=F32
        )
        return product if chunks == 1 else total + product

    flux_rows = -(-highs // (2 * ROWS)) * 4 * ROWS
    total = repeat_steps(
        chunks,
        chunk,
        jnp.zeros((highs * 2 * species + flux_rows, width), F32) if chunks > 1 else 0,
    )
    flux = total[highs * 2 * species :]
    copies = []
    stride = max(highs // 4, 1)
    for h in range(highs):
        part = total[2 * species * h : 2 * species * (h + 1)]
        part = part[:species] + part[species:]
        row = h // (2 * ROWS) * 4 * ROWS + h % (2 * ROWS)
        pore = pore_ref[:, width * h : width * (h + 1)]
        inverse = 1.0 / (pore + flux[row : row + 1] + flux[row + 2 * ROWS : row + 2 * ROWS + 1])
        columns = pl.ds(width * h, width)
        out_ref[:, columns] = (pore * cell_ref[:, columns] + part) * inverse
        if h % stride == stride - 1:
            columns = pl.ds(width * (h - stride + 1), stride * width)
            copies.append(
                pltpu.make_async_copy(
                    out_ref.at[:, columns], out_hbm.at[:, columns], out_sem.at[h // stride]
                )
            )
            copies[-1].start()
    for copy in copies:
        copy.wait()


def call(kernel, shape, operands, kinds={}, scratch=(), out=pltpu.VMEM, flops=0):
    return pl.pallas_call(
        kernel,
        out_shape=jax.ShapeDtypeStruct(shape, F32),
        in_specs=[
            pl.BlockSpec(memory_space=kinds.get(i, pltpu.VMEM)) for i in range(len(operands))
        ],
        out_specs=pl.BlockSpec(memory_space=out),
        scratch_shapes=list(scratch),
        compiler_params=pltpu.CompilerParams(vmem_limit_bytes=VMEM_BYTES),
        cost_estimate=pl.CostEstimate(flops=flops, bytes_accessed=0, transcendentals=0),
    )(*operands)


def shards(
    bundles,
    cell_state,
    pore_volume,
    request_cell,
    node_slot,
    line_length,
    courant,
    flux_weight,
    inflow,
    interaction,
):
    owners, cap = request_cell.shape[2:]
    first = call(first_kernel, (ROWS, LANES), (), flops=10**9)
    outgoing = call(
        pick_kernel,
        (owners, ROWS, LANES),
        (cell_state, request_cell, first),
    )
    table = lax.all_to_all(outgoing, "grid", split_axis=0, concat_axis=0, tiled=True)
    sums = call(
        functools.partial(lines_kernel, cap),
        (owners * bundles, ROWS, LANES),
        (table, node_slot, line_length, courant, flux_weight, inflow, interaction),
    )
    back = lax.all_to_all(sums, ("grid", "bundle"), split_axis=0, concat_axis=0, tiled=True)
    return call(
        functools.partial(blend_kernel, bundles),
        cell_state.shape,
        (back, request_cell, pore_volume[None, :], cell_state),
        scratch=(pltpu.VMEM(cell_state.shape, F32), pltpu.SemaphoreType.DMA((4,))),
        out=pltpu.HBM,
    )


def solution(mesh):
    placed = (
        P(None, "grid"),
        P("grid"),
        P(None, "grid", None, None),
        P("bundle", "grid", None),
        P("bundle", "grid"),
        P("bundle", "grid", None),
        P("bundle", "grid", None),
        P("bundle", None),
        P(),
    )
    return jax.shard_map(
        functools.partial(shards, mesh.shape["bundle"]),
        mesh=mesh,
        in_specs=placed,
        out_specs=P(None, "grid"),
        check_vma=False,
    )
```

```python
import functools

import jax
import jax.numpy as jnp
from jax import lax
from jax.experimental import pallas as pl
from jax.experimental.pallas import tpu as pltpu
from jax.sharding import PartitionSpec as P

SUB = 2
NEWTON = 3
LANES = 128
ROWS = 8
F32 = jnp.float32
BF16 = jnp.bfloat16
VMEM_BYTES = 32 * 1024 * 1024
CHUNKS = 4
GATHERED = 16


def repeat_steps(count, body, carry):
    if count == 1:
        return body(0, carry)
    return lax.fori_loop(0, count, body, carry)


def rounded(value):
    high = value.astype(BF16).astype(F32)
    return high, value - high


def split(value):
    return jnp.concatenate(rounded(value), axis=0).astype(BF16)


def select_groups(tiles, relative):
    count = len(tiles)
    results = []
    for i in range(count):
        value = tiles[0]
        for j in range(1, count):
            value = jnp.where(relative == (i + j) % count, tiles[j], value)
        results.append(value)
    return results


def lane_groups(cap, turn):
    groups = LANES // cap
    lane = lax.broadcasted_iota(jnp.int32, (ROWS, LANES), 1)
    return (lane // cap + (2 * groups - lax.rem(turn, groups))) % groups


def pack(rows, cap, turn, relative):
    groups = LANES // cap
    turned = [
        pltpu.roll(rows[g], lax.rem(turn + g, groups) * cap, 1) for g in range(groups)
    ]
    return select_groups(turned, relative)


def unpack(tiles, cap, relative, count):
    found = select_groups(tiles, relative)[:count]
    return [
        found[g] if g == 0 else pltpu.roll(found[g], LANES - g * cap, 1) for g in range(count)
    ]


def exchange_groups(tiles, width):
    tiles = list(tiles)
    lane_group = lax.broadcasted_iota(jnp.int32, tiles[0].shape, 1) // width
    step = 1
    while step < len(tiles):
        keep = (lane_group & step) == 0
        for i in range(len(tiles)):
            if i & step == 0:
                first, second = tiles[i], tiles[i | step]
                tiles[i] = jnp.where(keep, first, pltpu.roll(second, step * width, 1))
                tiles[i | step] = jnp.where(
                    keep, pltpu.roll(first, LANES - step * width, 1), second
                )
        step *= 2
    return tiles


def spread_rows(block, cap):
    groups = block.shape[0]
    wide = jnp.concatenate([block] * groups, axis=1)
    rows = lax.broadcasted_iota(jnp.int32, wide.shape, 0)
    lanes = lax.broadcasted_iota(jnp.int32, wide.shape, 1) // cap
    return jnp.sum(jnp.where(rows == lanes, wide, 0), axis=0, keepdims=True)


def first_kernel(out_ref):
    out_ref[...] = jnp.zeros_like(out_ref)


def pick_kernel(cell_ref, request_ref, first_ref, out_ref):
    species, cells = cell_ref.shape
    owners, cap = request_ref.shape[2:]
    bundle = lax.axis_index("bundle")
    groups = LANES // cap
    chunks = owners // (2 * groups)
    highs = cells // LANES
    here = lax.axis_index("grid")
    relative = lane_groups(cap, here)

    def wanted(k):
        block = request_ref[bundle, 0, pl.ds(k * 2 * groups, 2 * groups), :]
        index = jnp.concatenate(
            [spread_rows(block[:groups], cap), spread_rows(block[groups:], cap)], axis=1
        )
        low = index % LANES
        high = index // LANES
        hot = (
            (lax.broadcasted_iota(jnp.int32, (LANES, 2 * LANES), 0) == low)
            .astype(F32)
            .astype(BF16)
        )
        return high, jnp.concatenate([hot, hot], axis=0)

    kept = wanted(0) if chunks == 1 else None
    cell = cell_ref[...]
    stacked = jnp.concatenate(
        [cell[:, LANES * h : LANES * (h + 1)] for h in range(highs)], axis=0
    )
    left = jnp.concatenate(rounded(stacked), axis=1).astype(BF16)

    def chunk(k, carry):
        first = k * 2 * groups
        high, right = wanted(k) if kept is None else kept
        product = jnp.dot(left, right, preferred_element_type=F32)
        picked = jnp.zeros((species, 2 * LANES), F32)
        for h in range(highs):
            picked = picked + jnp.where(high == h, product[species * h : species * (h + 1)], 0.0)
        blank = jnp.zeros((groups * ROWS - species, 2 * LANES), F32)
        picked = jnp.concatenate([picked, blank], axis=0)
        for half in range(2):
            tiles = pack(
                [
                    picked[ROWS * g : ROWS * (g + 1), LANES * half : LANES * (half + 1)]
                    for g in range(groups)
                ],
                cap,
                here,
                relative,
            )
            for j in range(groups):
                out_ref[first + half * groups + j] = tiles[j]
        return carry

    repeat_steps(chunks, chunk, 0)


def to_segments(values):
    lines, nodes = values[0].shape
    blocks = nodes // LANES
    width = lines * blocks
    groups = LANES // width
    stacked = []
    for value in values:
        value = value.astype(F32)
        stacked += [value[:, LANES * block : LANES * (block + 1)] for block in range(blocks)]
    stacked.append(jnp.zeros((LANES - width * len(values), LANES), F32))
    turned = jnp.transpose(jnp.concatenate(stacked, axis=0))
    times = LANES // groups
    return exchange_groups([turned[times * g : times * (g + 1)] for g in range(groups)], width)


def lines_kernel(
    copies,
    cap,
    table_ref,
    slot_ref,
    length_ref,
    courant_ref,
    flux_ref,
    inflow_ref,
    interaction_ref,
    out_ref,
):
    owners = out_ref.shape[0] // copies
    species = inflow_ref.shape[1]
    lines, nodes = slot_ref.shape[1:]
    groups = species // ROWS
    all_groups = LANES // cap
    rows = all_groups * ROWS
    blocks = nodes // LANES
    width = lines * blocks
    segments = LANES // width
    times = LANES // segments
    chunk_owners = 2 * all_groups
    chunks = owners // chunk_owners
    here, bundle = lax.axis_index("grid"), lax.axis_index("bundle")

    slot = slot_ref[0]
    within = (slot + lax.rem(here, all_groups) * cap) % LANES
    slot, courant, flux = to_segments([slot - slot % LANES + within, courant_ref[0], flux_ref[0]])[
        :3
    ]

    def hot(k):
        local = (slot - lax.convert_element_type(k * 2 * LANES, F32)).astype(BF16)
        index = lax.broadcasted_iota(jnp.int32, (2 * LANES, LANES), 0).astype(F32).astype(BF16)
        one, zero = jnp.ones_like(index), jnp.zeros_like(index)
        return jnp.concatenate(
            [
                jnp.where(jnp.broadcast_to(local[t : t + 1], index.shape) == index, one, zero)
                for t in range(times)
            ],
            axis=1,
        )

    kept = hot(0) if chunks == 1 else None

    relative = lane_groups(cap, here)

    def incoming(owner):
        return table_ref[owner * owners + here if table_ref.shape[0] > owners else owner]

    def gather(k, state):
        halves = []
        for half in range(2):
            first = k * chunk_owners + half * all_groups
            halves.append(
                jnp.concatenate(
                    unpack(
                        [incoming(first + j) for j in range(all_groups)], cap, relative, groups
                    ),
                    axis=0,
                )
            )
        left = split(jnp.concatenate(halves, axis=1))
        found = jnp.dot(left, hot(k) if kept is None else kept, preferred_element_type=F32)
        found = found[:species] + found[species:]
        return found if chunks == 1 else state + found

    start = repeat_steps(
        chunks, gather, jnp.zeros((species, lines * nodes), F32) if chunks > 1 else 0
    )

    lane = lax.broadcasted_iota(jnp.int32, (ROWS, LANES), 1)
    part = lane // width
    block = (lane % width) // lines
    segment = block * segments + part
    line = lane % lines

    def earlier(value, distance):
        major, minor = distance // segments, distance % segments
        near = pltpu.roll(value, minor * width + major * lines, 1)
        if minor == 0:
            return near
        far = pltpu.roll(value, minor * width + (major + 1) * lines, 1)
        return jnp.where(part >= minor, near, far)

    eye = lax.broadcasted_iota(jnp.int32, (species, LANES), 0) == lax.broadcasted_iota(
        jnp.int32, (species, LANES), 1
    )
    padded = jnp.concatenate([inflow_ref[...], jnp.zeros((1, LANES - species), F32)], axis=1)
    column = jnp.sum(jnp.where(eye, padded, 0.0), axis=1, keepdims=True)
    entry = jnp.broadcast_to(column, (species, LANES))
    entry = [entry[ROWS * g : ROWS * (g + 1)] for g in range(groups)]

    scale = 1.0 / (1.0 + courant)
    decay = courant * scale
    first = [None] * groups
    second = [None] * groups
    local, ones, twos = [], [], []
    for t in range(times):
        scale_t = jnp.broadcast_to(scale[t : t + 1], (ROWS, LANES))
        decay_t = jnp.broadcast_to(decay[t : t + 1], (ROWS, LANES))
        one = decay_t if t == 0 else decay_t * ones[-1]
        two = scale_t * one if t == 0 else scale_t * one + decay_t * twos[-1]
        ones.append(one)
        twos.append(two)
        for g in range(groups):
            value = start[ROWS * g : ROWS * (g + 1), LANES * t : LANES * (t + 1)] * scale_t
            first[g] = value if t == 0 else value + decay_t * first[g]
            value = scale_t * first[g]
            second[g] = value if t == 0 else value + decay_t * second[g]
            local.append(second[g])

    a, b = ones[-1], twos[-1]
    head = segment == 0
    first = [jnp.where(head, f + a * e, f) for f, e in zip(first, entry)]
    second = [jnp.where(head, s + b * e + a * e, s) for s, e in zip(second, entry)]
    distance = 1
    while distance < blocks * segments:
        run_a, run_b = a, b
        next_first, next_second = first, second
        for k in range(1, 4):
            if k * distance >= blocks * segments:
                break
            opened = segment >= k * distance
            a_open, b_open = jnp.where(opened, run_a, 0.0), jnp.where(opened, run_b, 0.0)
            ahead = [earlier(f, k * distance) for f in first]
            next_first = [n + a_open * f for n, f in zip(next_first, ahead)]
            next_second = [
                n + b_open * f + a_open * earlier(s, k * distance)
                for n, s, f in zip(next_second, second, ahead)
            ]
            a_ahead = earlier(a, k * distance)
            run_b = run_b * a_ahead + run_a * earlier(b, k * distance)
            run_a = run_a * a_ahead
        first, second = next_first, next_second
        a, b = run_a, run_b
        distance *= 4
    carry_one = [jnp.where(head, e, earlier(f, 1)) for e, f in zip(entry, first)]
    carry_two = [jnp.where(head, e, earlier(s, 1)) for e, s in zip(entry, second)]
    columns = [
        jnp.concatenate(
            [
                local[t * groups + g] + twos[t] * carry_one[g] + ones[t] * carry_two[g]
                for g in range(groups)
            ],
            axis=0,
        )
        for t in range(times)
    ]

    matrix_high, matrix_low = rounded(interaction_ref[...])
    block_row = jnp.concatenate([matrix_high, matrix_low, matrix_high], axis=1)
    blank = jnp.zeros_like(block_row)
    left = jnp.concatenate(
        [
            jnp.concatenate([block_row, blank], axis=1),
            jnp.concatenate([blank, block_row], axis=1),
        ],
        axis=0,
    ).astype(BF16)
    half = times // 2
    depth = half // CHUNKS
    bases = [
        jnp.concatenate(
            [
                jnp.concatenate(columns[offset + c * depth : offset + (c + 1) * depth], axis=1)
                for offset in (0, half)
            ],
            axis=0,
        )
        for c in range(CHUNKS)
    ]
    iterates = list(bases)
    for step in range(NEWTON):
        for c in range(CHUNKS):
            high, low = rounded(jnp.tanh(iterates[c]))
            right = jnp.concatenate(
                [
                    high[:species],
                    high[:species],
                    low[:species],
                    high[species:],
                    high[species:],
                    low[species:],
                ],
                axis=0,
            ).astype(BF16)
            iterates[c] = bases[c] - jnp.dot(left, right, preferred_element_type=F32)

    length = jnp.zeros((ROWS, LANES), jnp.int32)
    for one_line in range(lines):
        one_length = jnp.broadcast_to(length_ref[:, one_line : one_line + 1], (ROWS, LANES))
        length = jnp.where(line == one_line, one_length, length)
    node = block * LANES + part * times
    top = lax.broadcasted_iota(jnp.int32, (ROWS, LANES), 0) == 0
    pieces = []
    for t in range(times):
        weight = jnp.broadcast_to(flux[t : t + 1], (ROWS, LANES))
        weight = jnp.where(node + t < length, weight, 0.0)
        chunk, place = t % half // depth, t % half % depth
        found = iterates[chunk][
            t // half * species : (t // half + 1) * species, LANES * place : LANES * (place + 1)
        ]
        scaled = [found[ROWS * g : ROWS * (g + 1)] * weight for g in range(groups)]
        scaled.append(jnp.where(top, weight, 0.0))
        pieces.append(jnp.concatenate(scaled, axis=0))
    left = split(jnp.concatenate(pieces, axis=1))
    relative = lane_groups(cap, here + bundle)

    def scatter(k, carry):
        sums = lax.dot_general(
            left,
            hot(k) if kept is None else kept,
            (((1,), (1,)), ((), ())),
            preferred_element_type=F32,
        )
        sums = sums[:rows] + sums[rows:]
        for half in range(2):
            tiles = pack(
                [
                    sums[ROWS * g : ROWS * (g + 1), LANES * half : LANES * (half + 1)]
                    for g in range(all_groups)
                ],
                cap,
                bundle,
                relative,
            )
            for j in range(all_groups):
                owner = k * chunk_owners + half * all_groups + j
                for copy in range(copies):
                    out_ref[owner * copies + copy] = tiles[j]
        return carry

    repeat_steps(chunks, scatter, 0)


def blend_kernel(bundles, sums_ref, request_ref, pore_ref, cell_ref, out_hbm, out_ref, out_sem):
    owners = sums_ref.shape[0] // bundles
    species, cells = cell_ref.shape
    cap = request_ref.shape[3]
    all_groups = LANES // cap
    groups = species // ROWS
    width = 2 * LANES
    highs = cells // width
    chunks = owners // ROWS
    here = lax.axis_index("grid")
    sublane = lax.broadcasted_iota(jnp.int32, (ROWS, LANES), 0)

    def chunk(k, total):
        values, weights, indices = [], [], []
        for t in range(bundles // all_groups):
            block = jnp.concatenate(
                [
                    request_ref[
                        t * all_groups
                        + lax.rem(x + all_groups - lax.rem(here, all_groups), all_groups),
                        0,
                        pl.ds(k * ROWS, ROWS),
                        :,
                    ]
                    for x in range(all_groups)
                ],
                axis=1,
            )
            straight = block
            for turn in range(1, all_groups):
                block = jnp.where(
                    sublane % all_groups == turn, pltpu.roll(straight, turn * cap, 1), block
                )
            for d in range(ROWS):
                found = unpack(
                    [
                        sums_ref[(k * ROWS + d) * bundles + t * all_groups + j]
                        for j in range(all_groups)
                    ],
                    cap,
                    lane_groups(cap, here + d),
                    all_groups,
                )
                weights.append(found[groups][:1])
                values.append(jnp.concatenate(found[:groups], axis=0))
                indices.append(block[d : d + 1])
        parts = split(jnp.concatenate(values, axis=1))
        weight_high, weight_low = rounded(jnp.concatenate(weights, axis=1))
        index = jnp.concatenate(indices, axis=1)
        entries = index.shape[1]
        high = jnp.broadcast_to(index // width, (2 * ROWS, entries)).astype(F32).astype(BF16)
        low = jnp.broadcast_to(index % width, (2 * ROWS, entries)).astype(F32).astype(BF16)
        low = jnp.concatenate([low] * (width // (2 * ROWS)), axis=0)
        place = lax.broadcasted_iota(jnp.int32, (width, entries), 0).astype(F32).astype(BF16)
        hot = jnp.where(place == low, jnp.ones_like(place), jnp.zeros_like(place))
        zero = jnp.zeros((2 * ROWS, entries), BF16)
        pieces = []
        for h in range(highs):
            mask = high == jnp.array(h, BF16)
            for r in range(2 * species // (2 * ROWS)):
                pieces.append(
                    jnp.where(mask, parts[2 * ROWS * r : 2 * ROWS * (r + 1)], zero)
                )
        for first in range(0, highs, 2 * ROWS):
            mask = high == (
                lax.broadcasted_iota(jnp.int32, (2 * ROWS, entries), 0) + first
            ).astype(F32).astype(BF16)
            for part in (weight_high, weight_low):
                row = jnp.broadcast_to(part, (2 * ROWS, entries)).astype(BF16)
                pieces.append(jnp.where(mask, row, zero))
        left = jnp.concatenate(pieces, axis=0)
        product = lax.dot_general(
            left, hot, (((1,), (1,)), ((), ())), preferred_element_type=F32
        )
        return product if chunks == 1 else total + product

    flux_rows = -(-highs // (2 * ROWS)) * 4 * ROWS
    total = repeat_steps(
        chunks,
        chunk,
        jnp.zeros((highs * 2 * species + flux_rows, width), F32) if chunks > 1 else 0,
    )
    flux = total[highs * 2 * species :]
    copies = []
    stride = max(highs // 4, 1)
    for h in range(highs):
        part = total[2 * species * h : 2 * species * (h + 1)]
        part = part[:species] + part[species:]
        row = h // (2 * ROWS) * 4 * ROWS + h % (2 * ROWS)
        pore = pore_ref[:, width * h : width * (h + 1)]
        inverse = 1.0 / (pore + flux[row : row + 1] + flux[row + 2 * ROWS : row + 2 * ROWS + 1])
        columns = pl.ds(width * h, width)
        out_ref[:, columns] = (pore * cell_ref[:, columns] + part) * inverse
        if h % stride == stride - 1:
            columns = pl.ds(width * (h - stride + 1), stride * width)
            copies.append(
                pltpu.make_async_copy(
                    out_ref.at[:, columns], out_hbm.at[:, columns], out_sem.at[h // stride]
                )
            )
            copies[-1].start()
    for copy in copies:
        copy.wait()


def call(kernel, shape, operands, kinds={}, scratch=(), out=pltpu.VMEM, flops=0):
    return pl.pallas_call(
        kernel,
        out_shape=jax.ShapeDtypeStruct(shape, F32),
        in_specs=[
            pl.BlockSpec(memory_space=kinds.get(i, pltpu.VMEM)) for i in range(len(operands))
        ],
        out_specs=pl.BlockSpec(memory_space=out),
        scratch_shapes=list(scratch),
        compiler_params=pltpu.CompilerParams(vmem_limit_bytes=VMEM_BYTES),
        cost_estimate=pl.CostEstimate(flops=flops, bytes_accessed=0, transcendentals=0),
    )(*operands)


def shards(
    bundles,
    cell_state,
    pore_volume,
    request_cell,
    node_slot,
    line_length,
    courant,
    flux_weight,
    inflow,
    interaction,
):
    owners, cap = request_cell.shape[2:]
    first = call(first_kernel, (ROWS, LANES), (), flops=10**9)
    outgoing = call(
        pick_kernel,
        (owners, ROWS, LANES),
        (cell_state, request_cell, first),
    )
    if owners <= GATHERED:
        table = lax.all_gather(outgoing, "grid", axis=0, tiled=True)
    else:
        table = lax.all_to_all(outgoing, "grid", split_axis=0, concat_axis=0, tiled=True)
    sums = call(
        functools.partial(lines_kernel, bundles, cap),
        (owners * bundles, ROWS, LANES),
        (table, node_slot, line_length, courant, flux_weight, inflow, interaction),
    )
    back = lax.all_to_all(sums, ("grid", "bundle"), split_axis=0, concat_axis=0, tiled=True)
    return call(
        functools.partial(blend_kernel, bundles),
        cell_state.shape,
        (back, request_cell, pore_volume[None, :], cell_state),
        scratch=(pltpu.VMEM(cell_state.shape, F32), pltpu.SemaphoreType.DMA((4,))),
        out=pltpu.HBM,
    )


def solution(mesh):
    placed = (
        P(None, "grid"),
        P("grid"),
        P(None, "grid", None, None),
        P("bundle", "grid", None),
        P("bundle", "grid"),
        P("bundle", "grid", None),
        P("bundle", "grid", None),
        P("bundle", None),
        P(),
    )
    return jax.shard_map(
        functools.partial(shards, mesh.shape["bundle"]),
        mesh=mesh,
        in_specs=placed,
        out_specs=P(None, "grid"),
        check_vma=False,
    )
```

```python
import functools

import jax
import jax.numpy as jnp
from jax import lax
from jax.experimental import pallas as pl
from jax.experimental.pallas import tpu as pltpu
from jax.sharding import PartitionSpec as P

SUB = 2
NEWTON = 3
LANES = 128
ROWS = 8
F32 = jnp.float32
BF16 = jnp.bfloat16
VMEM_BYTES = 32 * 1024 * 1024
CHUNKS = 4


def repeat_steps(count, body, carry):
    if count == 1:
        return body(0, carry)
    return lax.fori_loop(0, count, body, carry)


def rounded(value):
    high = value.astype(BF16).astype(F32)
    return high, value - high


def split(value):
    return jnp.concatenate(rounded(value), axis=0).astype(BF16)


def select_groups(tiles, relative):
    count = len(tiles)
    results = []
    for i in range(count):
        value = tiles[0]
        for j in range(1, count):
            value = jnp.where(relative == (i + j) % count, tiles[j], value)
        results.append(value)
    return results


def lane_groups(cap, turn):
    groups = LANES // cap
    lane = lax.broadcasted_iota(jnp.int32, (ROWS, LANES), 1)
    return (lane // cap + (2 * groups - lax.rem(turn, groups))) % groups


def pack(rows, cap, turn, relative):
    groups = LANES // cap
    turned = [
        pltpu.roll(rows[g], lax.rem(turn + g, groups) * cap, 1) for g in range(groups)
    ]
    return select_groups(turned, relative)


def unpack(tiles, cap, relative, count):
    found = select_groups(tiles, relative)[:count]
    return [
        found[g] if g == 0 else pltpu.roll(found[g], LANES - g * cap, 1) for g in range(count)
    ]


def exchange_groups(tiles, width):
    tiles = list(tiles)
    lane_group = lax.broadcasted_iota(jnp.int32, tiles[0].shape, 1) // width
    step = 1
    while step < len(tiles):
        keep = (lane_group & step) == 0
        for i in range(len(tiles)):
            if i & step == 0:
                first, second = tiles[i], tiles[i | step]
                tiles[i] = jnp.where(keep, first, pltpu.roll(second, step * width, 1))
                tiles[i | step] = jnp.where(
                    keep, pltpu.roll(first, LANES - step * width, 1), second
                )
        step *= 2
    return tiles


def spread_rows(block, cap):
    groups = block.shape[0]
    wide = jnp.concatenate([block] * groups, axis=1)
    rows = lax.broadcasted_iota(jnp.int32, wide.shape, 0)
    lanes = lax.broadcasted_iota(jnp.int32, wide.shape, 1) // cap
    return jnp.sum(jnp.where(rows == lanes, wide, 0), axis=0, keepdims=True)


def first_kernel(out_ref):
    out_ref[...] = jnp.zeros_like(out_ref)


def pick_kernel(cell_ref, request_ref, first_ref, out_ref):
    species, cells = cell_ref.shape
    owners, cap = request_ref.shape[2:]
    bundle = lax.axis_index("bundle")
    groups = LANES // cap
    chunks = owners // (2 * groups)
    highs = cells // LANES
    here = lax.axis_index("grid")
    relative = lane_groups(cap, here)

    def wanted(k):
        block = request_ref[bundle, 0, pl.ds(k * 2 * groups, 2 * groups), :]
        index = jnp.concatenate(
            [spread_rows(block[:groups], cap), spread_rows(block[groups:], cap)], axis=1
        )
        low = index % LANES
        high = index // LANES
        hot = (
            (lax.broadcasted_iota(jnp.int32, (LANES, 2 * LANES), 0) == low)
            .astype(F32)
            .astype(BF16)
        )
        return high, jnp.concatenate([hot, hot], axis=0)

    kept = wanted(0) if chunks == 1 else None
    cell = cell_ref[...]
    stacked = jnp.concatenate(
        [cell[:, LANES * h : LANES * (h + 1)] for h in range(highs)], axis=0
    )
    left = jnp.concatenate(rounded(stacked), axis=1).astype(BF16)

    def chunk(k, carry):
        first = k * 2 * groups
        high, right = wanted(k) if kept is None else kept
        product = jnp.dot(left, right, preferred_element_type=F32)
        picked = jnp.zeros((species, 2 * LANES), F32)
        for h in range(highs):
            picked = picked + jnp.where(high == h, product[species * h : species * (h + 1)], 0.0)
        blank = jnp.zeros((groups * ROWS - species, 2 * LANES), F32)
        picked = jnp.concatenate([picked, blank], axis=0)
        for half in range(2):
            tiles = pack(
                [
                    picked[ROWS * g : ROWS * (g + 1), LANES * half : LANES * (half + 1)]
                    for g in range(groups)
                ],
                cap,
                here,
                relative,
            )
            for j in range(groups):
                out_ref[first + half * groups + j] = tiles[j]
        return carry

    repeat_steps(chunks, chunk, 0)


def to_segments(values, width):
    groups = LANES // width
    stacked = [value.astype(F32) for value in values]
    stacked.append(jnp.zeros((LANES - width * len(values), LANES), F32))
    turned = jnp.transpose(jnp.concatenate(stacked, axis=0))
    times = LANES // groups
    return exchange_groups([turned[times * g : times * (g + 1)] for g in range(groups)], width)


def lines_kernel(
    lines,
    cap,
    table_ref,
    slot_ref,
    length_ref,
    courant_ref,
    flux_ref,
    inflow_ref,
    interaction_ref,
    out_ref,
    rows_ref,
):
    owners = table_ref.shape[0]
    copies = out_ref.shape[0] // owners
    species = inflow_ref.shape[1]
    width = slot_ref.shape[0]
    nodes = width * LANES // lines
    groups = species // ROWS
    all_groups = LANES // cap
    rows = all_groups * ROWS
    blocks = nodes // LANES
    segments = LANES // width
    times = LANES // segments
    chunk_owners = 2 * all_groups
    chunks = owners // chunk_owners
    here, bundle = lax.axis_index("grid"), lax.axis_index("bundle")

    slot = slot_ref[...]
    within = (slot + lax.rem(here, all_groups) * cap) % LANES
    slot, courant, flux = to_segments(
        [slot - slot % LANES + within, courant_ref[...], flux_ref[...]], width
    )[:3]
    scale = 1.0 / (1.0 + courant)
    rows_ref[0] = scale
    rows_ref[1] = courant * scale
    rows_ref[2] = flux
    rows_ref[3] = slot

    def row(kind, t, depth=ROWS):
        return jnp.broadcast_to(rows_ref[kind, t : t + 1], (depth, LANES))

    def hot(k):
        index = lax.broadcasted_iota(jnp.int32, (2 * LANES, LANES), 0).astype(F32).astype(BF16)
        one, zero = jnp.ones_like(index), jnp.zeros_like(index)
        base = lax.convert_element_type(k * 2 * LANES, F32)
        columns = []
        for t in range(times):
            local = (row(3, t, 2 * ROWS) - base).astype(BF16)
            local = jnp.concatenate([local] * (LANES // ROWS), axis=0)
            columns.append(jnp.where(local == index, one, zero))
        return jnp.concatenate(columns, axis=1)

    kept = hot(0) if chunks == 1 else None

    relative = lane_groups(cap, here)

    def gather(k, state):
        halves = []
        for half in range(2):
            first = k * chunk_owners + half * all_groups
            halves.append(
                jnp.concatenate(
                    unpack(
                        [table_ref[first + j] for j in range(all_groups)], cap, relative, groups
                    ),
                    axis=0,
                )
            )
        left = split(jnp.concatenate(halves, axis=1))
        found = jnp.dot(left, hot(k) if kept is None else kept, preferred_element_type=F32)
        found = found[:species] + found[species:]
        return found if chunks == 1 else state + found

    start = repeat_steps(
        chunks, gather, jnp.zeros((species, lines * nodes), F32) if chunks > 1 else 0
    )

    lane = lax.broadcasted_iota(jnp.int32, (ROWS, LANES), 1)
    part = lane // width
    block = (lane % width) // lines
    segment = block * segments + part
    line = lane % lines

    def earlier(value, distance):
        major, minor = distance // segments, distance % segments
        near = pltpu.roll(value, minor * width + major * lines, 1)
        if minor == 0:
            return near
        far = pltpu.roll(value, minor * width + (major + 1) * lines, 1)
        return jnp.where(part >= minor, near, far)

    eye = lax.broadcasted_iota(jnp.int32, (species, LANES), 0) == lax.broadcasted_iota(
        jnp.int32, (species, LANES), 1
    )
    padded = jnp.concatenate([inflow_ref[...], jnp.zeros((1, LANES - species), F32)], axis=1)
    column = jnp.sum(jnp.where(eye, padded, 0.0), axis=1, keepdims=True)
    entry = jnp.broadcast_to(column, (species, LANES))
    entry = [entry[ROWS * g : ROWS * (g + 1)] for g in range(groups)]

    first = [None] * groups
    second = [None] * groups
    local, ones, twos = [], [], []
    for t in range(times):
        scale_t, decay_t = row(0, t), row(1, t)
        one = decay_t if t == 0 else decay_t * ones[-1]
        two = scale_t * one if t == 0 else scale_t * one + decay_t * twos[-1]
        ones.append(one)
        twos.append(two)
        for g in range(groups):
            value = start[ROWS * g : ROWS * (g + 1), LANES * t : LANES * (t + 1)] * scale_t
            first[g] = value if t == 0 else value + decay_t * first[g]
            value = scale_t * first[g]
            second[g] = value if t == 0 else value + decay_t * second[g]
            local.append(second[g])

    a, b = ones[-1], twos[-1]
    head = segment == 0
    first = [jnp.where(head, f + a * e, f) for f, e in zip(first, entry)]
    second = [jnp.where(head, s + b * e + a * e, s) for s, e in zip(second, entry)]
    distance = 1
    while distance < blocks * segments:
        run_a, run_b = a, b
        next_first, next_second = first, second
        for k in range(1, 4):
            if k * distance >= blocks * segments:
                break
            opened = segment >= k * distance
            a_open, b_open = jnp.where(opened, run_a, 0.0), jnp.where(opened, run_b, 0.0)
            ahead = [earlier(f, k * distance) for f in first]
            next_first = [n + a_open * f for n, f in zip(next_first, ahead)]
            next_second = [
                n + b_open * f + a_open * earlier(s, k * distance)
                for n, s, f in zip(next_second, second, ahead)
            ]
            a_ahead = earlier(a, k * distance)
            run_b = run_b * a_ahead + run_a * earlier(b, k * distance)
            run_a = run_a * a_ahead
        first, second = next_first, next_second
        a, b = run_a, run_b
        distance *= 4
    carry_one = [jnp.where(head, e, earlier(f, 1)) for e, f in zip(entry, first)]
    carry_two = [jnp.where(head, e, earlier(s, 1)) for e, s in zip(entry, second)]
    columns = [
        jnp.concatenate(
            [
                local[t * groups + g] + twos[t] * carry_one[g] + ones[t] * carry_two[g]
                for g in range(groups)
            ],
            axis=0,
        )
        for t in range(times)
    ]

    matrix_high, matrix_low = rounded(interaction_ref[...])
    block_row = jnp.concatenate([matrix_high, matrix_low, matrix_high], axis=1)
    blank = jnp.zeros_like(block_row)
    left = jnp.concatenate(
        [
            jnp.concatenate([block_row, blank], axis=1),
            jnp.concatenate([blank, block_row], axis=1),
        ],
        axis=0,
    ).astype(BF16)
    half = times // 2
    depth = half // CHUNKS
    bases = [
        jnp.concatenate(
            [
                jnp.concatenate(columns[offset + c * depth : offset + (c + 1) * depth], axis=1)
                for offset in (0, half)
            ],
            axis=0,
        )
        for c in range(CHUNKS)
    ]
    iterates = list(bases)
    for step in range(NEWTON):
        for c in range(CHUNKS):
            high, low = rounded(jnp.tanh(iterates[c]))
            right = jnp.concatenate(
                [
                    high[:species],
                    high[:species],
                    low[:species],
                    high[species:],
                    high[species:],
                    low[species:],
                ],
                axis=0,
            ).astype(BF16)
            iterates[c] = bases[c] - jnp.dot(left, right, preferred_element_type=F32)

    length = jnp.zeros((ROWS, LANES), jnp.int32)
    for one_line in range(lines):
        one_length = jnp.broadcast_to(length_ref[:, one_line : one_line + 1], (ROWS, LANES))
        length = jnp.where(line == one_line, one_length, length)
    node = block * LANES + part * times
    top = lax.broadcasted_iota(jnp.int32, (ROWS, LANES), 0) == 0
    pieces = []
    for t in range(times):
        weight = jnp.where(node + t < length, row(2, t), 0.0)
        chunk, place = t % half // depth, t % half % depth
        found = iterates[chunk][
            t // half * species : (t // half + 1) * species, LANES * place : LANES * (place + 1)
        ]
        scaled = [found[ROWS * g : ROWS * (g + 1)] * weight for g in range(groups)]
        scaled.append(jnp.where(top, weight, 0.0))
        pieces.append(jnp.concatenate(scaled, axis=0))
    left = split(jnp.concatenate(pieces, axis=1))
    relative = lane_groups(cap, here + bundle)

    def scatter(k, carry):
        sums = lax.dot_general(
            left,
            hot(k) if kept is None else kept,
            (((1,), (1,)), ((), ())),
            preferred_element_type=F32,
        )
        sums = sums[:rows] + sums[rows:]
        for half in range(2):
            tiles = pack(
                [
                    sums[ROWS * g : ROWS * (g + 1), LANES * half : LANES * (half + 1)]
                    for g in range(all_groups)
                ],
                cap,
                bundle,
                relative,
            )
            for j in range(all_groups):
                owner = k * chunk_owners + half * all_groups + j
                for copy in range(copies):
                    out_ref[owner * copies + copy] = tiles[j]
        return carry

    repeat_steps(chunks, scatter, 0)


def blend_kernel(bundles, sums_ref, request_ref, pore_ref, cell_ref, out_hbm, out_ref, out_sem):
    owners = sums_ref.shape[0] // bundles
    species, cells = cell_ref.shape
    cap = request_ref.shape[3]
    all_groups = LANES // cap
    groups = species // ROWS
    width = 2 * LANES
    highs = cells // width
    chunks = owners // ROWS
    here = lax.axis_index("grid")
    sublane = lax.broadcasted_iota(jnp.int32, (ROWS, LANES), 0)

    def chunk(k, total):
        values, weights, indices = [], [], []
        for t in range(bundles // all_groups):
            block = jnp.concatenate(
                [
                    request_ref[
                        t * all_groups
                        + lax.rem(x + all_groups - lax.rem(here, all_groups), all_groups),
                        0,
                        pl.ds(k * ROWS, ROWS),
                        :,
                    ]
                    for x in range(all_groups)
                ],
                axis=1,
            )
            straight = block
            for turn in range(1, all_groups):
                block = jnp.where(
                    sublane % all_groups == turn, pltpu.roll(straight, turn * cap, 1), block
                )
            for d in range(ROWS):
                found = unpack(
                    [
                        sums_ref[(k * ROWS + d) * bundles + t * all_groups + j]
                        for j in range(all_groups)
                    ],
                    cap,
                    lane_groups(cap, here + d),
                    all_groups,
                )
                weights.append(found[groups][:1])
                values.append(jnp.concatenate(found[:groups], axis=0))
                indices.append(block[d : d + 1])
        parts = split(jnp.concatenate(values, axis=1))
        weight_high, weight_low = rounded(jnp.concatenate(weights, axis=1))
        index = jnp.concatenate(indices, axis=1)
        entries = index.shape[1]
        high = jnp.broadcast_to(index // width, (2 * ROWS, entries)).astype(F32).astype(BF16)
        low = jnp.broadcast_to(index % width, (2 * ROWS, entries)).astype(F32).astype(BF16)
        low = jnp.concatenate([low] * (width // (2 * ROWS)), axis=0)
        place = lax.broadcasted_iota(jnp.int32, (width, entries), 0).astype(F32).astype(BF16)
        hot = jnp.where(place == low, jnp.ones_like(place), jnp.zeros_like(place))
        zero = jnp.zeros((2 * ROWS, entries), BF16)
        pieces = []
        for h in range(highs):
            mask = high == jnp.array(h, BF16)
            for r in range(2 * species // (2 * ROWS)):
                pieces.append(
                    jnp.where(mask, parts[2 * ROWS * r : 2 * ROWS * (r + 1)], zero)
                )
        for first in range(0, highs, 2 * ROWS):
            mask = high == (
                lax.broadcasted_iota(jnp.int32, (2 * ROWS, entries), 0) + first
            ).astype(F32).astype(BF16)
            for part in (weight_high, weight_low):
                row = jnp.broadcast_to(part, (2 * ROWS, entries)).astype(BF16)
                pieces.append(jnp.where(mask, row, zero))
        left = jnp.concatenate(pieces, axis=0)
        product = lax.dot_general(
            left, hot, (((1,), (1,)), ((), ())), preferred_element_type=F32
        )
        return product if chunks == 1 else total + product

    flux_rows = -(-highs // (2 * ROWS)) * 4 * ROWS
    total = repeat_steps(
        chunks,
        chunk,
        jnp.zeros((highs * 2 * species + flux_rows, width), F32) if chunks > 1 else 0,
    )
    flux = total[highs * 2 * species :]
    copies = []
    stride = max(highs // 4, 1)
    for h in range(highs):
        part = total[2 * species * h : 2 * species * (h + 1)]
        part = part[:species] + part[species:]
        row = h // (2 * ROWS) * 4 * ROWS + h % (2 * ROWS)
        pore = pore_ref[:, width * h : width * (h + 1)]
        inverse = 1.0 / (pore + flux[row : row + 1] + flux[row + 2 * ROWS : row + 2 * ROWS + 1])
        columns = pl.ds(width * h, width)
        out_ref[:, columns] = (pore * cell_ref[:, columns] + part) * inverse
        if h % stride == stride - 1:
            columns = pl.ds(width * (h - stride + 1), stride * width)
            copies.append(
                pltpu.make_async_copy(
                    out_ref.at[:, columns], out_hbm.at[:, columns], out_sem.at[h // stride]
                )
            )
            copies[-1].start()
    for copy in copies:
        copy.wait()


def call(kernel, shape, operands, kinds={}, scratch=(), out=pltpu.VMEM, flops=0):
    return pl.pallas_call(
        kernel,
        out_shape=jax.ShapeDtypeStruct(shape, F32),
        in_specs=[
            pl.BlockSpec(memory_space=kinds.get(i, pltpu.VMEM)) for i in range(len(operands))
        ],
        out_specs=pl.BlockSpec(memory_space=out),
        scratch_shapes=list(scratch),
        compiler_params=pltpu.CompilerParams(vmem_limit_bytes=VMEM_BYTES),
        cost_estimate=pl.CostEstimate(flops=flops, bytes_accessed=0, transcendentals=0),
    )(*operands)


def shards(
    bundles,
    cell_state,
    pore_volume,
    request_cell,
    node_slot,
    line_length,
    courant,
    flux_weight,
    inflow,
    interaction,
):
    owners, cap = request_cell.shape[2:]
    first = call(first_kernel, (ROWS, LANES), (), flops=10**9)
    outgoing = call(
        pick_kernel,
        (owners, ROWS, LANES),
        (cell_state, request_cell, first),
    )
    table = lax.all_to_all(outgoing, "grid", split_axis=0, concat_axis=0, tiled=True)
    lines, nodes = node_slot.shape[1:]
    blocks = nodes // LANES

    def by_block(value):
        return value.reshape(lines, blocks, LANES).swapaxes(0, 1).reshape(blocks * lines, LANES)

    sums = call(
        functools.partial(lines_kernel, lines, cap),
        (owners * bundles, ROWS, LANES),
        (
            table,
            by_block(node_slot),
            line_length,
            by_block(courant),
            by_block(flux_weight),
            inflow,
            interaction,
        ),
        scratch=(pltpu.VMEM((4, lines * blocks, LANES), F32),),
    )
    back = lax.all_to_all(sums, ("grid", "bundle"), split_axis=0, concat_axis=0, tiled=True)
    return call(
        functools.partial(blend_kernel, bundles),
        cell_state.shape,
        (back, request_cell, pore_volume[None, :], cell_state),
        scratch=(pltpu.VMEM(cell_state.shape, F32), pltpu.SemaphoreType.DMA((4,))),
        out=pltpu.HBM,
    )


def solution(mesh):
    placed = (
        P(None, "grid"),
        P("grid"),
        P(None, "grid", None, None),
        P("bundle", "grid", None),
        P("bundle", "grid"),
        P("bundle", "grid", None),
        P("bundle", "grid", None),
        P("bundle", None),
        P(),
    )
    return jax.shard_map(
        functools.partial(shards, mesh.shape["bundle"]),
        mesh=mesh,
        in_specs=placed,
        out_specs=P(None, "grid"),
        check_vma=False,
    )
```

```python
import functools

import jax
import jax.numpy as jnp
from jax import lax
from jax.experimental import pallas as pl
from jax.experimental.pallas import tpu as pltpu
from jax.sharding import PartitionSpec as P

SUB = 2
NEWTON = 3
LANES = 128
ROWS = 8
F32 = jnp.float32
BF16 = jnp.bfloat16
VMEM_BYTES = 32 * 1024 * 1024
CHUNKS = 4
PAIRED = 16


def repeat_steps(count, body, carry):
    if count == 1:
        return body(0, carry)
    return lax.fori_loop(0, count, body, carry)


def rounded(value):
    high = value.astype(BF16).astype(F32)
    return high, value - high


def split(value):
    return jnp.concatenate(rounded(value), axis=0).astype(BF16)


def select_groups(tiles, relative):
    count = len(tiles)
    results = []
    for i in range(count):
        value = tiles[0]
        for j in range(1, count):
            value = jnp.where(relative == (i + j) % count, tiles[j], value)
        results.append(value)
    return results


def lane_groups(cap, turn):
    groups = LANES // cap
    lane = lax.broadcasted_iota(jnp.int32, (ROWS, LANES), 1)
    return (lane // cap + (2 * groups - lax.rem(turn, groups))) % groups


def pack(rows, cap, turn, relative):
    groups = LANES // cap
    turned = [
        pltpu.roll(rows[g], lax.rem(turn + g, groups) * cap, 1) for g in range(groups)
    ]
    return select_groups(turned, relative)


def unpack(tiles, cap, relative, count):
    found = select_groups(tiles, relative)[:count]
    return [
        found[g] if g == 0 else pltpu.roll(found[g], LANES - g * cap, 1) for g in range(count)
    ]


def exchange_groups(tiles, width):
    tiles = list(tiles)
    lane_group = lax.broadcasted_iota(jnp.int32, tiles[0].shape, 1) // width
    step = 1
    while step < len(tiles):
        keep = (lane_group & step) == 0
        for i in range(len(tiles)):
            if i & step == 0:
                first, second = tiles[i], tiles[i | step]
                tiles[i] = jnp.where(keep, first, pltpu.roll(second, step * width, 1))
                tiles[i | step] = jnp.where(
                    keep, pltpu.roll(first, LANES - step * width, 1), second
                )
        step *= 2
    return tiles


def spread_rows(block, cap):
    groups = block.shape[0]
    wide = jnp.concatenate([block] * groups, axis=1)
    rows = lax.broadcasted_iota(jnp.int32, wide.shape, 0)
    lanes = lax.broadcasted_iota(jnp.int32, wide.shape, 1) // cap
    return jnp.sum(jnp.where(rows == lanes, wide, 0), axis=0, keepdims=True)


def first_kernel(out_ref):
    out_ref[...] = jnp.zeros_like(out_ref)


def pick_kernel(cell_ref, request_ref, first_ref, length_ref, inflow_ref, *refs):
    *out_refs, tile_ref = refs
    species, cells = cell_ref.shape
    owners, cap = request_ref.shape[2:]
    bundle = lax.axis_index("bundle")
    groups = LANES // cap
    chunks = owners // (2 * groups)
    highs = cells // LANES
    here = lax.axis_index("grid")
    relative = lane_groups(cap, here)

    def wanted(k):
        block = request_ref[bundle, 0, pl.ds(k * 2 * groups, 2 * groups), :]
        index = jnp.concatenate(
            [spread_rows(block[:groups], cap), spread_rows(block[groups:], cap)], axis=1
        )
        low = index % LANES
        high = index // LANES
        hot = (
            (lax.broadcasted_iota(jnp.int32, (LANES, 2 * LANES), 0) == low)
            .astype(F32)
            .astype(BF16)
        )
        return high, jnp.concatenate([hot, hot], axis=0)

    kept = wanted(0) if chunks == 1 else None
    cell = cell_ref[...]
    stacked = jnp.concatenate(
        [cell[:, LANES * h : LANES * (h + 1)] for h in range(highs)], axis=0
    )
    left = jnp.concatenate(rounded(stacked), axis=1).astype(BF16)

    def chunk(k, carry):
        first = k * 2 * groups
        high, right = wanted(k) if kept is None else kept
        product = jnp.dot(left, right, preferred_element_type=F32)
        picked = jnp.zeros((species, 2 * LANES), F32)
        for h in range(highs):
            picked = picked + jnp.where(high == h, product[species * h : species * (h + 1)], 0.0)
        blank = jnp.zeros((groups * ROWS - species, 2 * LANES), F32)
        picked = jnp.concatenate([picked, blank], axis=0)
        for half in range(2):
            tiles = pack(
                [
                    picked[ROWS * g : ROWS * (g + 1), LANES * half : LANES * (half + 1)]
                    for g in range(groups)
                ],
                cap,
                here,
                relative,
            )
            for j in range(groups):
                tile_ref[first + half * groups + j] = tiles[j]
        return carry

    repeat_steps(chunks, chunk, 0)
    if len(out_refs) == 1:
        out_refs[0][...] = tile_ref[...]
    else:
        keep_ref, send_ref = out_refs
        for r in range(owners // 2):
            keep_ref[0, r] = tile_ref[here ^ r]
            send_ref[0, r] = tile_ref[here ^ (r + owners // 2)]


def repack_kernel(old_ref, new_ref, keep_ref, send_ref):
    sources, count = old_ref.shape[0], old_ref.shape[1] // 2
    for i, ref in enumerate((old_ref, new_ref)):
        for s in range(sources):
            keep_ref[i * sources + s] = ref[s, :count]
            send_ref[i * sources + s] = ref[s, count:]


def exchange_pairs(keep, send, count):
    bit = count // 2
    while True:
        received = lax.ppermute(send, "grid", [(i, i ^ bit) for i in range(count)])
        if bit == 1:
            return keep, received
        sources, tiles = keep.shape[:2]
        shape = (2 * sources, tiles // 2, ROWS, LANES)
        keep, send = call(repack_kernel, [shape] * 2, (keep, received))
        bit //= 2


def source_order(count):
    order = [0]
    bit = count // 2
    while bit:
        order += [s ^ bit for s in order]
        bit //= 2
    return order


def to_segments(values, width):
    groups = LANES // width
    stacked = [value.astype(F32) for value in values]
    stacked.append(jnp.zeros((LANES - width * len(values), LANES), F32))
    turned = jnp.transpose(jnp.concatenate(stacked, axis=0))
    times = LANES // groups
    return exchange_groups([turned[times * g : times * (g + 1)] for g in range(groups)], width)


def lines_kernel(
    lines,
    cap,
    owners,
    slot_ref,
    length_ref,
    courant_ref,
    flux_ref,
    inflow_ref,
    interaction_ref,
    *refs,
):
    *table_refs, out_ref, rows_ref, table_ref = refs
    if len(table_refs) == 1:
        table_ref = table_refs[0]
    else:
        order = source_order(owners)
        for i in range(owners):
            ref = table_refs[i // (owners // 2)]
            table_ref[lax.axis_index("grid") ^ order[i]] = ref[i % (owners // 2), 0]
    copies = out_ref.shape[0] // owners
    species = inflow_ref.shape[1]
    width = slot_ref.shape[0]
    nodes = width * LANES // lines
    groups = species // ROWS
    all_groups = LANES // cap
    rows = all_groups * ROWS
    blocks = nodes // LANES
    segments = LANES // width
    times = LANES // segments
    chunk_owners = 2 * all_groups
    chunks = owners // chunk_owners
    here, bundle = lax.axis_index("grid"), lax.axis_index("bundle")

    slot = slot_ref[...]
    within = (slot + lax.rem(here, all_groups) * cap) % LANES
    slot, courant, flux = to_segments(
        [slot - slot % LANES + within, courant_ref[...], flux_ref[...]], width
    )[:3]
    scale = 1.0 / (1.0 + courant)
    rows_ref[0] = scale
    rows_ref[1] = courant * scale
    rows_ref[2] = flux
    rows_ref[3] = slot

    def row(kind, t, depth=ROWS):
        return jnp.broadcast_to(rows_ref[kind, t : t + 1], (depth, LANES))

    def hot(k):
        index = lax.broadcasted_iota(jnp.int32, (2 * LANES, LANES), 0).astype(F32).astype(BF16)
        one, zero = jnp.ones_like(index), jnp.zeros_like(index)
        base = lax.convert_element_type(k * 2 * LANES, F32)
        columns = []
        for t in range(times):
            local = (row(3, t, 2 * ROWS) - base).astype(BF16)
            local = jnp.concatenate([local] * (LANES // ROWS), axis=0)
            columns.append(jnp.where(local == index, one, zero))
        return jnp.concatenate(columns, axis=1)

    kept = hot(0) if chunks == 1 else None

    relative = lane_groups(cap, here)

    def gather(k, state):
        halves = []
        for half in range(2):
            first = k * chunk_owners + half * all_groups
            halves.append(
                jnp.concatenate(
                    unpack(
                        [table_ref[first + j] for j in range(all_groups)], cap, relative, groups
                    ),
                    axis=0,
                )
            )
        left = split(jnp.concatenate(halves, axis=1))
        found = jnp.dot(left, hot(k) if kept is None else kept, preferred_element_type=F32)
        found = found[:species] + found[species:]
        return found if chunks == 1 else state + found

    start = repeat_steps(
        chunks, gather, jnp.zeros((species, lines * nodes), F32) if chunks > 1 else 0
    )

    lane = lax.broadcasted_iota(jnp.int32, (ROWS, LANES), 1)
    part = lane // width
    block = (lane % width) // lines
    segment = block * segments + part
    line = lane % lines

    def earlier(value, distance):
        major, minor = distance // segments, distance % segments
        near = pltpu.roll(value, minor * width + major * lines, 1)
        if minor == 0:
            return near
        far = pltpu.roll(value, minor * width + (major + 1) * lines, 1)
        return jnp.where(part >= minor, near, far)

    eye = lax.broadcasted_iota(jnp.int32, (species, LANES), 0) == lax.broadcasted_iota(
        jnp.int32, (species, LANES), 1
    )
    padded = jnp.concatenate([inflow_ref[...], jnp.zeros((1, LANES - species), F32)], axis=1)
    column = jnp.sum(jnp.where(eye, padded, 0.0), axis=1, keepdims=True)
    entry = jnp.broadcast_to(column, (species, LANES))
    entry = [entry[ROWS * g : ROWS * (g + 1)] for g in range(groups)]

    first = [None] * groups
    second = [None] * groups
    local, ones, twos = [], [], []
    for t in range(times):
        scale_t, decay_t = row(0, t), row(1, t)
        one = decay_t if t == 0 else decay_t * ones[-1]
        two = scale_t * one if t == 0 else scale_t * one + decay_t * twos[-1]
        ones.append(one)
        twos.append(two)
        for g in range(groups):
            value = start[ROWS * g : ROWS * (g + 1), LANES * t : LANES * (t + 1)] * scale_t
            first[g] = value if t == 0 else value + decay_t * first[g]
            value = scale_t * first[g]
            second[g] = value if t == 0 else value + decay_t * second[g]
            local.append(second[g])

    a, b = ones[-1], twos[-1]
    head = segment == 0
    first = [jnp.where(head, f + a * e, f) for f, e in zip(first, entry)]
    second = [jnp.where(head, s + b * e + a * e, s) for s, e in zip(second, entry)]
    distance = 1
    while distance < blocks * segments:
        run_a, run_b = a, b
        next_first, next_second = first, second
        for k in range(1, 4):
            if k * distance >= blocks * segments:
                break
            opened = segment >= k * distance
            a_open, b_open = jnp.where(opened, run_a, 0.0), jnp.where(opened, run_b, 0.0)
            ahead = [earlier(f, k * distance) for f in first]
            next_first = [n + a_open * f for n, f in zip(next_first, ahead)]
            next_second = [
                n + b_open * f + a_open * earlier(s, k * distance)
                for n, s, f in zip(next_second, second, ahead)
            ]
            a_ahead = earlier(a, k * distance)
            run_b = run_b * a_ahead + run_a * earlier(b, k * distance)
            run_a = run_a * a_ahead
        first, second = next_first, next_second
        a, b = run_a, run_b
        distance *= 4
    carry_one = [jnp.where(head, e, earlier(f, 1)) for e, f in zip(entry, first)]
    carry_two = [jnp.where(head, e, earlier(s, 1)) for e, s in zip(entry, second)]
    columns = [
        jnp.concatenate(
            [
                local[t * groups + g] + twos[t] * carry_one[g] + ones[t] * carry_two[g]
                for g in range(groups)
            ],
            axis=0,
        )
        for t in range(times)
    ]

    matrix_high, matrix_low = rounded(interaction_ref[...])
    block_row = jnp.concatenate([matrix_high, matrix_low, matrix_high], axis=1)
    blank = jnp.zeros_like(block_row)
    left = jnp.concatenate(
        [
            jnp.concatenate([block_row, blank], axis=1),
            jnp.concatenate([blank, block_row], axis=1),
        ],
        axis=0,
    ).astype(BF16)
    half = times // 2
    depth = half // CHUNKS
    bases = [
        jnp.concatenate(
            [
                jnp.concatenate(columns[offset + c * depth : offset + (c + 1) * depth], axis=1)
                for offset in (0, half)
            ],
            axis=0,
        )
        for c in range(CHUNKS)
    ]
    iterates = list(bases)
    for step in range(NEWTON):
        for c in range(CHUNKS):
            high, low = rounded(jnp.tanh(iterates[c]))
            right = jnp.concatenate(
                [
                    high[:species],
                    high[:species],
                    low[:species],
                    high[species:],
                    high[species:],
                    low[species:],
                ],
                axis=0,
            ).astype(BF16)
            iterates[c] = bases[c] - jnp.dot(left, right, preferred_element_type=F32)

    length = jnp.zeros((ROWS, LANES), jnp.int32)
    for one_line in range(lines):
        one_length = jnp.broadcast_to(length_ref[:, one_line : one_line + 1], (ROWS, LANES))
        length = jnp.where(line == one_line, one_length, length)
    node = block * LANES + part * times
    top = lax.broadcasted_iota(jnp.int32, (ROWS, LANES), 0) == 0
    pieces = []
    for t in range(times):
        weight = jnp.where(node + t < length, row(2, t), 0.0)
        chunk, place = t % half // depth, t % half % depth
        found = iterates[chunk][
            t // half * species : (t // half + 1) * species, LANES * place : LANES * (place + 1)
        ]
        scaled = [found[ROWS * g : ROWS * (g + 1)] * weight for g in range(groups)]
        scaled.append(jnp.where(top, weight, 0.0))
        pieces.append(jnp.concatenate(scaled, axis=0))
    left = split(jnp.concatenate(pieces, axis=1))
    relative = lane_groups(cap, here + bundle)

    def scatter(k, carry):
        sums = lax.dot_general(
            left,
            hot(k) if kept is None else kept,
            (((1,), (1,)), ((), ())),
            preferred_element_type=F32,
        )
        sums = sums[:rows] + sums[rows:]
        for half in range(2):
            tiles = pack(
                [
                    sums[ROWS * g : ROWS * (g + 1), LANES * half : LANES * (half + 1)]
                    for g in range(all_groups)
                ],
                cap,
                bundle,
                relative,
            )
            for j in range(all_groups):
                owner = k * chunk_owners + half * all_groups + j
                for copy in range(copies):
                    out_ref[owner * copies + copy] = tiles[j]
        return carry

    repeat_steps(chunks, scatter, 0)


def blend_kernel(bundles, sums_ref, request_ref, pore_ref, cell_ref, out_hbm, out_ref, out_sem):
    owners = sums_ref.shape[0] // bundles
    species, cells = cell_ref.shape
    cap = request_ref.shape[3]
    all_groups = LANES // cap
    groups = species // ROWS
    width = 2 * LANES
    highs = cells // width
    chunks = owners // ROWS
    here = lax.axis_index("grid")
    sublane = lax.broadcasted_iota(jnp.int32, (ROWS, LANES), 0)

    def chunk(k, total):
        values, weights, indices = [], [], []
        for t in range(bundles // all_groups):
            block = jnp.concatenate(
                [
                    request_ref[
                        t * all_groups
                        + lax.rem(x + all_groups - lax.rem(here, all_groups), all_groups),
                        0,
                        pl.ds(k * ROWS, ROWS),
                        :,
                    ]
                    for x in range(all_groups)
                ],
                axis=1,
            )
            straight = block
            for turn in range(1, all_groups):
                block = jnp.where(
                    sublane % all_groups == turn, pltpu.roll(straight, turn * cap, 1), block
                )
            for d in range(ROWS):
                found = unpack(
                    [
                        sums_ref[(k * ROWS + d) * bundles + t * all_groups + j]
                        for j in range(all_groups)
                    ],
                    cap,
                    lane_groups(cap, here + d),
                    all_groups,
                )
                weights.append(found[groups][:1])
                values.append(jnp.concatenate(found[:groups], axis=0))
                indices.append(block[d : d + 1])
        parts = split(jnp.concatenate(values, axis=1))
        weight_high, weight_low = rounded(jnp.concatenate(weights, axis=1))
        index = jnp.concatenate(indices, axis=1)
        entries = index.shape[1]
        high = jnp.broadcast_to(index // width, (2 * ROWS, entries)).astype(F32).astype(BF16)
        low = jnp.broadcast_to(index % width, (2 * ROWS, entries)).astype(F32).astype(BF16)
        low = jnp.concatenate([low] * (width // (2 * ROWS)), axis=0)
        place = lax.broadcasted_iota(jnp.int32, (width, entries), 0).astype(F32).astype(BF16)
        hot = jnp.where(place == low, jnp.ones_like(place), jnp.zeros_like(place))
        zero = jnp.zeros((2 * ROWS, entries), BF16)
        pieces = []
        for h in range(highs):
            mask = high == jnp.array(h, BF16)
            for r in range(2 * species // (2 * ROWS)):
                pieces.append(
                    jnp.where(mask, parts[2 * ROWS * r : 2 * ROWS * (r + 1)], zero)
                )
        for first in range(0, highs, 2 * ROWS):
            mask = high == (
                lax.broadcasted_iota(jnp.int32, (2 * ROWS, entries), 0) + first
            ).astype(F32).astype(BF16)
            for part in (weight_high, weight_low):
                row = jnp.broadcast_to(part, (2 * ROWS, entries)).astype(BF16)
                pieces.append(jnp.where(mask, row, zero))
        left = jnp.concatenate(pieces, axis=0)
        product = lax.dot_general(
            left, hot, (((1,), (1,)), ((), ())), preferred_element_type=F32
        )
        return product if chunks == 1 else total + product

    flux_rows = -(-highs // (2 * ROWS)) * 4 * ROWS
    total = repeat_steps(
        chunks,
        chunk,
        jnp.zeros((highs * 2 * species + flux_rows, width), F32) if chunks > 1 else 0,
    )
    flux = total[highs * 2 * species :]
    copies = []
    stride = max(highs // 4, 1)
    for h in range(highs):
        part = total[2 * species * h : 2 * species * (h + 1)]
        part = part[:species] + part[species:]
        row = h // (2 * ROWS) * 4 * ROWS + h % (2 * ROWS)
        pore = pore_ref[:, width * h : width * (h + 1)]
        inverse = 1.0 / (pore + flux[row : row + 1] + flux[row + 2 * ROWS : row + 2 * ROWS + 1])
        columns = pl.ds(width * h, width)
        out_ref[:, columns] = (pore * cell_ref[:, columns] + part) * inverse
        if h % stride == stride - 1:
            columns = pl.ds(width * (h - stride + 1), stride * width)
            copies.append(
                pltpu.make_async_copy(
                    out_ref.at[:, columns], out_hbm.at[:, columns], out_sem.at[h // stride]
                )
            )
            copies[-1].start()
    for copy in copies:
        copy.wait()


def call(kernel, shapes, operands, kinds={}, scratch=(), out=pltpu.VMEM, flops=0):
    return pl.pallas_call(
        kernel,
        out_shape=[jax.ShapeDtypeStruct(shape, F32) for shape in shapes],
        in_specs=[
            pl.BlockSpec(memory_space=kinds.get(i, pltpu.VMEM)) for i in range(len(operands))
        ],
        out_specs=[pl.BlockSpec(memory_space=out)] * len(shapes),
        scratch_shapes=list(scratch),
        compiler_params=pltpu.CompilerParams(vmem_limit_bytes=VMEM_BYTES),
        cost_estimate=pl.CostEstimate(flops=flops, bytes_accessed=0, transcendentals=0),
    )(*operands)


def shards(
    bundles,
    cell_state,
    pore_volume,
    request_cell,
    node_slot,
    line_length,
    courant,
    flux_weight,
    inflow,
    interaction,
):
    owners, cap = request_cell.shape[2:]
    tile = (ROWS, LANES)
    paired = owners <= PAIRED and owners & (owners - 1) == 0
    halves = [(1, owners // 2, *tile)] * 2
    first = call(first_kernel, [tile], (), flops=10**9)[0]
    outgoing = call(
        pick_kernel,
        halves if paired else [(owners, *tile)],
        (cell_state, request_cell, first, line_length, inflow),
        scratch=(pltpu.VMEM((owners, *tile), F32),),
    )
    if paired:
        tables = exchange_pairs(*outgoing, owners)
    else:
        tables = [lax.all_to_all(outgoing[0], "grid", split_axis=0, concat_axis=0, tiled=True)]
    lines, nodes = node_slot.shape[1:]
    blocks = nodes // LANES

    def by_block(value):
        return value.reshape(lines, blocks, LANES).swapaxes(0, 1).reshape(blocks * lines, LANES)

    sums = call(
        functools.partial(lines_kernel, lines, cap, owners),
        [(owners * bundles, *tile)],
        (
            by_block(node_slot),
            line_length,
            by_block(courant),
            by_block(flux_weight),
            inflow,
            interaction,
            *tables,
        ),
        scratch=(
            pltpu.VMEM((4, lines * blocks, LANES), F32),
            pltpu.VMEM((owners, *tile) if paired else (1, *tile), F32),
        ),
    )[0]
    back = lax.all_to_all(sums, ("grid", "bundle"), split_axis=0, concat_axis=0, tiled=True)
    return call(
        functools.partial(blend_kernel, bundles),
        [cell_state.shape],
        (back, request_cell, pore_volume[None, :], cell_state),
        scratch=(pltpu.VMEM(cell_state.shape, F32), pltpu.SemaphoreType.DMA((4,))),
        out=pltpu.HBM,
    )[0]


def solution(mesh):
    placed = (
        P(None, "grid"),
        P("grid"),
        P(None, "grid", None, None),
        P("bundle", "grid", None),
        P("bundle", "grid"),
        P("bundle", "grid", None),
        P("bundle", "grid", None),
        P("bundle", None),
        P(),
    )
    return jax.shard_map(
        functools.partial(shards, mesh.shape["bundle"]),
        mesh=mesh,
        in_specs=placed,
        out_specs=P(None, "grid"),
        check_vma=False,
    )
```

```python
import functools

import jax
import jax.numpy as jnp
from jax import lax
from jax.experimental import pallas as pl
from jax.experimental.pallas import tpu as pltpu
from jax.sharding import PartitionSpec as P

SUB = 2
NEWTON = 3
LANES = 128
ROWS = 8
F32 = jnp.float32
BF16 = jnp.bfloat16
VMEM_BYTES = 32 * 1024 * 1024
CHUNKS = 4


def repeat_steps(count, body, carry):
    if count == 1:
        return body(0, carry)
    return lax.fori_loop(0, count, body, carry)


def rounded(value):
    high = value.astype(BF16).astype(F32)
    return high, value - high


def split(value):
    return jnp.concatenate(rounded(value), axis=0).astype(BF16)


def select_groups(tiles, relative):
    count = len(tiles)
    results = []
    for i in range(count):
        value = tiles[0]
        for j in range(1, count):
            value = jnp.where(relative == (i + j) % count, tiles[j], value)
        results.append(value)
    return results


def lane_groups(cap, turn):
    groups = LANES // cap
    lane = lax.broadcasted_iota(jnp.int32, (ROWS, LANES), 1)
    return (lane // cap + (2 * groups - lax.rem(turn, groups))) % groups


def pack(rows, cap, turn, relative):
    groups = LANES // cap
    turned = [
        pltpu.roll(rows[g], lax.rem(turn + g, groups) * cap, 1) for g in range(groups)
    ]
    return select_groups(turned, relative)


def unpack(tiles, cap, relative, count):
    found = select_groups(tiles, relative)[:count]
    return [
        found[g] if g == 0 else pltpu.roll(found[g], LANES - g * cap, 1) for g in range(count)
    ]


def exchange_groups(tiles, width):
    tiles = list(tiles)
    lane_group = lax.broadcasted_iota(jnp.int32, tiles[0].shape, 1) // width
    step = 1
    while step < len(tiles):
        keep = (lane_group & step) == 0
        for i in range(len(tiles)):
            if i & step == 0:
                first, second = tiles[i], tiles[i | step]
                tiles[i] = jnp.where(keep, first, pltpu.roll(second, step * width, 1))
                tiles[i | step] = jnp.where(
                    keep, pltpu.roll(first, LANES - step * width, 1), second
                )
        step *= 2
    return tiles


def spread_rows(block, cap):
    groups = block.shape[0]
    wide = jnp.concatenate([block] * groups, axis=1)
    rows = lax.broadcasted_iota(jnp.int32, wide.shape, 0)
    lanes = lax.broadcasted_iota(jnp.int32, wide.shape, 1) // cap
    return jnp.sum(jnp.where(rows == lanes, wide, 0), axis=0, keepdims=True)


def first_kernel(out_ref):
    out_ref[...] = jnp.zeros_like(out_ref)


def pick_kernel(cell_ref, request_ref, first_ref, length_ref, inflow_ref, out_ref):
    species, cells = cell_ref.shape
    owners, cap = request_ref.shape[2:]
    bundle = lax.axis_index("bundle")
    groups = LANES // cap
    chunks = owners // (2 * groups)
    highs = cells // LANES
    here = lax.axis_index("grid")
    relative = lane_groups(cap, here)

    def wanted(k):
        block = request_ref[bundle, 0, pl.ds(k * 2 * groups, 2 * groups), :]
        index = jnp.concatenate(
            [spread_rows(block[:groups], cap), spread_rows(block[groups:], cap)], axis=1
        )
        low = index % LANES
        high = index // LANES
        hot = (
            (lax.broadcasted_iota(jnp.int32, (LANES, 2 * LANES), 0) == low)
            .astype(F32)
            .astype(BF16)
        )
        return high, jnp.concatenate([hot, hot], axis=0)

    kept = wanted(0) if chunks == 1 else None
    cell = cell_ref[...]
    stacked = jnp.concatenate(
        [cell[:, LANES * h : LANES * (h + 1)] for h in range(highs)], axis=0
    )
    left = jnp.concatenate(rounded(stacked), axis=1).astype(BF16)

    def chunk(k, carry):
        first = k * 2 * groups
        high, right = wanted(k) if kept is None else kept
        product = jnp.dot(left, right, preferred_element_type=F32)
        picked = jnp.zeros((species, 2 * LANES), F32)
        for h in range(highs):
            picked = picked + jnp.where(high == h, product[species * h : species * (h + 1)], 0.0)
        blank = jnp.zeros((groups * ROWS - species, 2 * LANES), F32)
        picked = jnp.concatenate([picked, blank], axis=0)
        for half in range(2):
            tiles = pack(
                [
                    picked[ROWS * g : ROWS * (g + 1), LANES * half : LANES * (half + 1)]
                    for g in range(groups)
                ],
                cap,
                here,
                relative,
            )
            for j in range(groups):
                out_ref[first + half * groups + j] = tiles[j]
        return carry

    repeat_steps(chunks, chunk, 0)


def to_segments(values, width):
    groups = LANES // width
    stacked = [value.astype(F32) for value in values]
    stacked.append(jnp.zeros((LANES - width * len(values), LANES), F32))
    turned = jnp.transpose(jnp.concatenate(stacked, axis=0))
    times = LANES // groups
    return exchange_groups([turned[times * g : times * (g + 1)] for g in range(groups)], width)


def lines_kernel(
    lines,
    cap,
    table_ref,
    slot_ref,
    length_ref,
    courant_ref,
    flux_ref,
    inflow_ref,
    interaction_ref,
    out_ref,
    rows_ref,
):
    owners = table_ref.shape[0]
    copies = out_ref.shape[0] // owners
    species = inflow_ref.shape[1]
    width = slot_ref.shape[0]
    nodes = width * LANES // lines
    groups = species // ROWS
    all_groups = LANES // cap
    rows = all_groups * ROWS
    blocks = nodes // LANES
    segments = LANES // width
    times = LANES // segments
    chunk_owners = 2 * all_groups
    chunks = owners // chunk_owners
    here, bundle = lax.axis_index("grid"), lax.axis_index("bundle")

    slot = slot_ref[...]
    within = (slot + lax.rem(here, all_groups) * cap) % LANES
    slot, courant, flux = to_segments(
        [slot - slot % LANES + within, courant_ref[...], flux_ref[...]], width
    )[:3]
    scale = 1.0 / (1.0 + courant)
    rows_ref[0] = scale
    rows_ref[1] = courant * scale
    rows_ref[2] = flux
    rows_ref[3] = slot

    def row(kind, t, depth=ROWS):
        return jnp.broadcast_to(rows_ref[kind, t : t + 1], (depth, LANES))

    def hot(k):
        index = lax.broadcasted_iota(jnp.int32, (2 * LANES, LANES), 0).astype(F32).astype(BF16)
        one, zero = jnp.ones_like(index), jnp.zeros_like(index)
        base = lax.convert_element_type(k * 2 * LANES, F32)
        columns = []
        for t in range(times):
            local = (row(3, t, 2 * ROWS) - base).astype(BF16)
            local = jnp.concatenate([local] * (LANES // ROWS), axis=0)
            columns.append(jnp.where(local == index, one, zero))
        return jnp.concatenate(columns, axis=1)

    kept = hot(0) if chunks == 1 else None

    relative = lane_groups(cap, here)

    def gather(k, state):
        halves = []
        for half in range(2):
            first = k * chunk_owners + half * all_groups
            halves.append(
                jnp.concatenate(
                    unpack(
                        [table_ref[first + j] for j in range(all_groups)], cap, relative, groups
                    ),
                    axis=0,
                )
            )
        left = split(jnp.concatenate(halves, axis=1))
        found = jnp.dot(left, hot(k) if kept is None else kept, preferred_element_type=F32)
        found = found[:species] + found[species:]
        return found if chunks == 1 else state + found

    start = repeat_steps(
        chunks, gather, jnp.zeros((species, lines * nodes), F32) if chunks > 1 else 0
    )

    lane = lax.broadcasted_iota(jnp.int32, (ROWS, LANES), 1)
    part = lane // width
    block = (lane % width) // lines
    segment = block * segments + part
    line = lane % lines

    def earlier(value, distance):
        major, minor = distance // segments, distance % segments
        near = pltpu.roll(value, minor * width + major * lines, 1)
        if minor == 0:
            return near
        far = pltpu.roll(value, minor * width + (major + 1) * lines, 1)
        return jnp.where(part >= minor, near, far)

    eye = lax.broadcasted_iota(jnp.int32, (species, LANES), 0) == lax.broadcasted_iota(
        jnp.int32, (species, LANES), 1
    )
    padded = jnp.concatenate([inflow_ref[...], jnp.zeros((1, LANES - species), F32)], axis=1)
    column = jnp.sum(jnp.where(eye, padded, 0.0), axis=1, keepdims=True)
    entry = jnp.broadcast_to(column, (species, LANES))
    entry = [entry[ROWS * g : ROWS * (g + 1)] for g in range(groups)]

    first = [None] * groups
    second = [None] * groups
    local, ones, twos = [], [], []
    for t in range(times):
        scale_t, decay_t = row(0, t), row(1, t)
        one = decay_t if t == 0 else decay_t * ones[-1]
        two = scale_t * one if t == 0 else scale_t * one + decay_t * twos[-1]
        ones.append(one)
        twos.append(two)
        for g in range(groups):
            value = start[ROWS * g : ROWS * (g + 1), LANES * t : LANES * (t + 1)] * scale_t
            first[g] = value if t == 0 else value + decay_t * first[g]
            value = scale_t * first[g]
            second[g] = value if t == 0 else value + decay_t * second[g]
            local.append(second[g])

    a, b = ones[-1], twos[-1]
    head = segment == 0
    first = [jnp.where(head, f + a * e, f) for f, e in zip(first, entry)]
    second = [jnp.where(head, s + b * e + a * e, s) for s, e in zip(second, entry)]
    distance = 1
    while distance < blocks * segments:
        run_a, run_b = a, b
        next_first, next_second = first, second
        for k in range(1, 4):
            if k * distance >= blocks * segments:
                break
            opened = segment >= k * distance
            a_open, b_open = jnp.where(opened, run_a, 0.0), jnp.where(opened, run_b, 0.0)
            ahead = [earlier(f, k * distance) for f in first]
            next_first = [n + a_open * f for n, f in zip(next_first, ahead)]
            next_second = [
                n + b_open * f + a_open * earlier(s, k * distance)
                for n, s, f in zip(next_second, second, ahead)
            ]
            a_ahead = earlier(a, k * distance)
            run_b = run_b * a_ahead + run_a * earlier(b, k * distance)
            run_a = run_a * a_ahead
        first, second = next_first, next_second
        a, b = run_a, run_b
        distance *= 4
    carry_one = [jnp.where(head, e, earlier(f, 1)) for e, f in zip(entry, first)]
    carry_two = [jnp.where(head, e, earlier(s, 1)) for e, s in zip(entry, second)]
    columns = [
        jnp.concatenate(
            [
                local[t * groups + g] + twos[t] * carry_one[g] + ones[t] * carry_two[g]
                for g in range(groups)
            ],
            axis=0,
        )
        for t in range(times)
    ]

    matrix_high, matrix_low = rounded(interaction_ref[...])
    block_row = jnp.concatenate([matrix_high, matrix_low, matrix_high], axis=1)
    blank = jnp.zeros_like(block_row)
    left = jnp.concatenate(
        [
            jnp.concatenate([block_row, blank], axis=1),
            jnp.concatenate([blank, block_row], axis=1),
        ],
        axis=0,
    ).astype(BF16)
    half = times // 2
    depth = half // CHUNKS
    bases = [
        jnp.concatenate(
            [
                jnp.concatenate(columns[offset + c * depth : offset + (c + 1) * depth], axis=1)
                for offset in (0, half)
            ],
            axis=0,
        )
        for c in range(CHUNKS)
    ]
    iterates = list(bases)
    for step in range(NEWTON):
        for c in range(CHUNKS):
            high, low = rounded(1.0 - 2.0 / (jnp.exp(2.0 * iterates[c]) + 1.0))
            right = jnp.concatenate(
                [
                    high[:species],
                    high[:species],
                    low[:species],
                    high[species:],
                    high[species:],
                    low[species:],
                ],
                axis=0,
            ).astype(BF16)
            iterates[c] = bases[c] - jnp.dot(left, right, preferred_element_type=F32)

    length = jnp.zeros((ROWS, LANES), jnp.int32)
    for one_line in range(lines):
        one_length = jnp.broadcast_to(length_ref[:, one_line : one_line + 1], (ROWS, LANES))
        length = jnp.where(line == one_line, one_length, length)
    node = block * LANES + part * times
    top = lax.broadcasted_iota(jnp.int32, (ROWS, LANES), 0) == 0
    pieces = []
    for t in range(times):
        weight = jnp.where(node + t < length, row(2, t), 0.0)
        chunk, place = t % half // depth, t % half % depth
        found = iterates[chunk][
            t // half * species : (t // half + 1) * species, LANES * place : LANES * (place + 1)
        ]
        scaled = [found[ROWS * g : ROWS * (g + 1)] * weight for g in range(groups)]
        scaled.append(jnp.where(top, weight, 0.0))
        pieces.append(jnp.concatenate(scaled, axis=0))
    left = split(jnp.concatenate(pieces, axis=1))
    relative = lane_groups(cap, here + bundle)

    def scatter(k, carry):
        sums = lax.dot_general(
            left,
            hot(k) if kept is None else kept,
            (((1,), (1,)), ((), ())),
            preferred_element_type=F32,
        )
        sums = sums[:rows] + sums[rows:]
        for half in range(2):
            tiles = pack(
                [
                    sums[ROWS * g : ROWS * (g + 1), LANES * half : LANES * (half + 1)]
                    for g in range(all_groups)
                ],
                cap,
                bundle,
                relative,
            )
            for j in range(all_groups):
                owner = k * chunk_owners + half * all_groups + j
                for copy in range(copies):
                    out_ref[owner * copies + copy] = tiles[j]
        return carry

    repeat_steps(chunks, scatter, 0)


def blend_kernel(bundles, sums_ref, request_ref, pore_ref, cell_ref, out_hbm, out_ref, out_sem):
    owners = sums_ref.shape[0] // bundles
    species, cells = cell_ref.shape
    cap = request_ref.shape[3]
    all_groups = LANES // cap
    groups = species // ROWS
    width = 2 * LANES
    highs = cells // width
    chunks = owners // ROWS
    here = lax.axis_index("grid")
    sublane = lax.broadcasted_iota(jnp.int32, (ROWS, LANES), 0)

    def chunk(k, total):
        values, weights, indices = [], [], []
        for t in range(bundles // all_groups):
            block = jnp.concatenate(
                [
                    request_ref[
                        t * all_groups
                        + lax.rem(x + all_groups - lax.rem(here, all_groups), all_groups),
                        0,
                        pl.ds(k * ROWS, ROWS),
                        :,
                    ]
                    for x in range(all_groups)
                ],
                axis=1,
            )
            straight = block
            for turn in range(1, all_groups):
                block = jnp.where(
                    sublane % all_groups == turn, pltpu.roll(straight, turn * cap, 1), block
                )
            for d in range(ROWS):
                found = unpack(
                    [
                        sums_ref[(k * ROWS + d) * bundles + t * all_groups + j]
                        for j in range(all_groups)
                    ],
                    cap,
                    lane_groups(cap, here + d),
                    all_groups,
                )
                weights.append(found[groups][:1])
                values.append(jnp.concatenate(found[:groups], axis=0))
                indices.append(block[d : d + 1])
        parts = split(jnp.concatenate(values, axis=1))
        weight_high, weight_low = rounded(jnp.concatenate(weights, axis=1))
        index = jnp.concatenate(indices, axis=1)
        entries = index.shape[1]
        high = jnp.broadcast_to(index // width, (2 * ROWS, entries)).astype(F32).astype(BF16)
        low = jnp.broadcast_to(index % width, (2 * ROWS, entries)).astype(F32).astype(BF16)
        low = jnp.concatenate([low] * (width // (2 * ROWS)), axis=0)
        place = lax.broadcasted_iota(jnp.int32, (width, entries), 0).astype(F32).astype(BF16)
        hot = jnp.where(place == low, jnp.ones_like(place), jnp.zeros_like(place))
        zero = jnp.zeros((2 * ROWS, entries), BF16)
        pieces = []
        for h in range(highs):
            mask = high == jnp.array(h, BF16)
            for r in range(2 * species // (2 * ROWS)):
                pieces.append(
                    jnp.where(mask, parts[2 * ROWS * r : 2 * ROWS * (r + 1)], zero)
                )
        for first in range(0, highs, 2 * ROWS):
            mask = high == (
                lax.broadcasted_iota(jnp.int32, (2 * ROWS, entries), 0) + first
            ).astype(F32).astype(BF16)
            for part in (weight_high, weight_low):
                row = jnp.broadcast_to(part, (2 * ROWS, entries)).astype(BF16)
                pieces.append(jnp.where(mask, row, zero))
        left = jnp.concatenate(pieces, axis=0)
        product = lax.dot_general(
            left, hot, (((1,), (1,)), ((), ())), preferred_element_type=F32
        )
        return product if chunks == 1 else total + product

    flux_rows = -(-highs // (2 * ROWS)) * 4 * ROWS
    total = repeat_steps(
        chunks,
        chunk,
        jnp.zeros((highs * 2 * species + flux_rows, width), F32) if chunks > 1 else 0,
    )
    flux = total[highs * 2 * species :]
    copies = []
    stride = max(highs // 4, 1)
    for h in range(highs):
        part = total[2 * species * h : 2 * species * (h + 1)]
        part = part[:species] + part[species:]
        row = h // (2 * ROWS) * 4 * ROWS + h % (2 * ROWS)
        pore = pore_ref[:, width * h : width * (h + 1)]
        inverse = 1.0 / (pore + flux[row : row + 1] + flux[row + 2 * ROWS : row + 2 * ROWS + 1])
        columns = pl.ds(width * h, width)
        out_ref[:, columns] = (pore * cell_ref[:, columns] + part) * inverse
        if h % stride == stride - 1:
            columns = pl.ds(width * (h - stride + 1), stride * width)
            copies.append(
                pltpu.make_async_copy(
                    out_ref.at[:, columns], out_hbm.at[:, columns], out_sem.at[h // stride]
                )
            )
            copies[-1].start()
    for copy in copies:
        copy.wait()


def call(kernel, shape, operands, kinds={}, scratch=(), out=pltpu.VMEM, flops=0):
    return pl.pallas_call(
        kernel,
        out_shape=jax.ShapeDtypeStruct(shape, F32),
        in_specs=[
            pl.BlockSpec(memory_space=kinds.get(i, pltpu.VMEM)) for i in range(len(operands))
        ],
        out_specs=pl.BlockSpec(memory_space=out),
        scratch_shapes=list(scratch),
        compiler_params=pltpu.CompilerParams(vmem_limit_bytes=VMEM_BYTES),
        cost_estimate=pl.CostEstimate(flops=flops, bytes_accessed=0, transcendentals=0),
    )(*operands)


def shards(
    bundles,
    cell_state,
    pore_volume,
    request_cell,
    node_slot,
    line_length,
    courant,
    flux_weight,
    inflow,
    interaction,
):
    owners, cap = request_cell.shape[2:]
    first = call(first_kernel, (ROWS, LANES), (), flops=10**9)
    outgoing = call(
        pick_kernel,
        (owners, ROWS, LANES),
        (cell_state, request_cell, first, line_length, inflow),
    )
    table = lax.all_to_all(outgoing, "grid", split_axis=0, concat_axis=0, tiled=True)
    lines, nodes = node_slot.shape[1:]
    blocks = nodes // LANES

    def by_block(value):
        return value.reshape(lines, blocks, LANES).swapaxes(0, 1).reshape(blocks * lines, LANES)

    sums = call(
        functools.partial(lines_kernel, lines, cap),
        (owners * bundles, ROWS, LANES),
        (
            table,
            by_block(node_slot),
            line_length,
            by_block(courant),
            by_block(flux_weight),
            inflow,
            interaction,
        ),
        scratch=(pltpu.VMEM((4, lines * blocks, LANES), F32),),
    )
    back = lax.all_to_all(sums, ("grid", "bundle"), split_axis=0, concat_axis=0, tiled=True)
    return call(
        functools.partial(blend_kernel, bundles),
        cell_state.shape,
        (back, request_cell, pore_volume[None, :], cell_state),
        scratch=(pltpu.VMEM(cell_state.shape, F32), pltpu.SemaphoreType.DMA((4,))),
        out=pltpu.HBM,
    )


def solution(mesh):
    placed = (
        P(None, "grid"),
        P("grid"),
        P(None, "grid", None, None),
        P("bundle", "grid", None),
        P("bundle", "grid"),
        P("bundle", "grid", None),
        P("bundle", "grid", None),
        P("bundle", None),
        P(),
    )
    return jax.shard_map(
        functools.partial(shards, mesh.shape["bundle"]),
        mesh=mesh,
        in_specs=placed,
        out_specs=P(None, "grid"),
        check_vma=False,
    )
```

```python
import functools

import jax
import jax.numpy as jnp
from jax import lax
from jax.experimental import pallas as pl
from jax.experimental.pallas import tpu as pltpu
from jax.sharding import PartitionSpec as P

SUB = 2
NEWTON = 3
LANES = 128
ROWS = 8
F32 = jnp.float32
BF16 = jnp.bfloat16
VMEM_BYTES = 32 * 1024 * 1024
CHUNKS = 4


def repeat_steps(count, body, carry):
    if count == 1:
        return body(0, carry)
    return lax.fori_loop(0, count, body, carry)


def rounded(value):
    high = value.astype(BF16).astype(F32)
    return high, value - high


def parts(value):
    high = value.astype(BF16)
    return high, (value - high.astype(F32)).astype(BF16)


def split(value):
    return jnp.concatenate(rounded(value), axis=0).astype(BF16)


def select_groups(tiles, relative):
    count = len(tiles)
    results = []
    for i in range(count):
        value = tiles[0]
        for j in range(1, count):
            value = jnp.where(relative == (i + j) % count, tiles[j], value)
        results.append(value)
    return results


def lane_groups(cap, turn):
    groups = LANES // cap
    lane = lax.broadcasted_iota(jnp.int32, (ROWS, LANES), 1)
    return (lane // cap + (2 * groups - lax.rem(turn, groups))) % groups


def pack(rows, cap, turn, relative):
    groups = LANES // cap
    turned = [
        pltpu.roll(rows[g], lax.rem(turn + g, groups) * cap, 1) for g in range(groups)
    ]
    return select_groups(turned, relative)


def unpack(tiles, cap, relative, count):
    found = select_groups(tiles, relative)[:count]
    return [
        found[g] if g == 0 else pltpu.roll(found[g], LANES - g * cap, 1) for g in range(count)
    ]


def exchange_groups(tiles, width):
    tiles = list(tiles)
    lane_group = lax.broadcasted_iota(jnp.int32, tiles[0].shape, 1) // width
    step = 1
    while step < len(tiles):
        keep = (lane_group & step) == 0
        for i in range(len(tiles)):
            if i & step == 0:
                first, second = tiles[i], tiles[i | step]
                tiles[i] = jnp.where(keep, first, pltpu.roll(second, step * width, 1))
                tiles[i | step] = jnp.where(
                    keep, pltpu.roll(first, LANES - step * width, 1), second
                )
        step *= 2
    return tiles


def spread_rows(block, cap):
    groups = block.shape[0]
    wide = jnp.concatenate([block] * groups, axis=1)
    rows = lax.broadcasted_iota(jnp.int32, wide.shape, 0)
    lanes = lax.broadcasted_iota(jnp.int32, wide.shape, 1) // cap
    return jnp.sum(jnp.where(rows == lanes, wide, 0), axis=0, keepdims=True)


def first_kernel(out_ref):
    out_ref[...] = jnp.zeros_like(out_ref)


def pick_kernel(cell_ref, request_ref, first_ref, length_ref, inflow_ref, out_ref):
    species, cells = cell_ref.shape
    owners, cap = request_ref.shape[2:]
    bundle = lax.axis_index("bundle")
    groups = LANES // cap
    chunks = owners // (2 * groups)
    highs = cells // LANES
    here = lax.axis_index("grid")
    relative = lane_groups(cap, here)

    def wanted(k):
        block = request_ref[bundle, 0, pl.ds(k * 2 * groups, 2 * groups), :]
        index = jnp.concatenate(
            [spread_rows(block[:groups], cap), spread_rows(block[groups:], cap)], axis=1
        )
        low = index % LANES
        high = index // LANES
        hot = (
            (lax.broadcasted_iota(jnp.int32, (LANES, 2 * LANES), 0) == low)
            .astype(F32)
            .astype(BF16)
        )
        return high, jnp.concatenate([hot, hot], axis=0)

    kept = wanted(0) if chunks == 1 else None
    cell = cell_ref[...]
    stacked = jnp.concatenate(
        [cell[:, LANES * h : LANES * (h + 1)] for h in range(highs)], axis=0
    )
    left = jnp.concatenate(rounded(stacked), axis=1).astype(BF16)

    def chunk(k, carry):
        first = k * 2 * groups
        high, right = wanted(k) if kept is None else kept
        product = jnp.dot(left, right, preferred_element_type=F32)
        picked = jnp.zeros((species, 2 * LANES), F32)
        for h in range(highs):
            picked = picked + jnp.where(high == h, product[species * h : species * (h + 1)], 0.0)
        blank = jnp.zeros((groups * ROWS - species, 2 * LANES), F32)
        picked = jnp.concatenate([picked, blank], axis=0)
        for half in range(2):
            tiles = pack(
                [
                    picked[ROWS * g : ROWS * (g + 1), LANES * half : LANES * (half + 1)]
                    for g in range(groups)
                ],
                cap,
                here,
                relative,
            )
            for j in range(groups):
                out_ref[first + half * groups + j] = tiles[j]
        return carry

    repeat_steps(chunks, chunk, 0)


def to_segments(values, width):
    groups = LANES // width
    stacked = [value.astype(F32) for value in values]
    stacked.append(jnp.zeros((LANES - width * len(values), LANES), F32))
    turned = jnp.transpose(jnp.concatenate(stacked, axis=0))
    times = LANES // groups
    return exchange_groups([turned[times * g : times * (g + 1)] for g in range(groups)], width)


def lines_kernel(
    lines,
    cap,
    table_ref,
    slot_ref,
    length_ref,
    courant_ref,
    flux_ref,
    inflow_ref,
    interaction_ref,
    out_ref,
    rows_ref,
):
    owners = table_ref.shape[0]
    copies = out_ref.shape[0] // owners
    species = inflow_ref.shape[1]
    width = slot_ref.shape[0]
    nodes = width * LANES // lines
    groups = species // ROWS
    all_groups = LANES // cap
    rows = all_groups * ROWS
    blocks = nodes // LANES
    segments = LANES // width
    times = LANES // segments
    chunk_owners = 2 * all_groups
    chunks = owners // chunk_owners
    here, bundle = lax.axis_index("grid"), lax.axis_index("bundle")

    slot = slot_ref[...]
    within = (slot + lax.rem(here, all_groups) * cap) % LANES
    slot, courant, flux = to_segments(
        [slot - slot % LANES + within, courant_ref[...], flux_ref[...]], width
    )[:3]
    scale = 1.0 / (1.0 + courant)
    rows_ref[0] = scale
    rows_ref[1] = courant * scale
    rows_ref[2] = flux
    rows_ref[3] = slot

    def row(kind, t, depth=ROWS):
        return jnp.broadcast_to(rows_ref[kind, t : t + 1], (depth, LANES))

    def hot(k):
        index = lax.broadcasted_iota(jnp.int32, (2 * LANES, LANES), 0).astype(F32).astype(BF16)
        one, zero = jnp.ones_like(index), jnp.zeros_like(index)
        base = lax.convert_element_type(k * 2 * LANES, F32)
        columns = []
        for t in range(times):
            local = (row(3, t, 2 * ROWS) - base).astype(BF16)
            local = jnp.concatenate([local] * (LANES // ROWS), axis=0)
            columns.append(jnp.where(local == index, one, zero))
        return jnp.concatenate(columns, axis=1)

    kept = hot(0) if chunks == 1 else None

    relative = lane_groups(cap, here)

    def gather(k, state):
        halves = []
        for half in range(2):
            first = k * chunk_owners + half * all_groups
            halves.append(
                jnp.concatenate(
                    unpack(
                        [table_ref[first + j] for j in range(all_groups)], cap, relative, groups
                    ),
                    axis=0,
                )
            )
        left = split(jnp.concatenate(halves, axis=1))
        found = jnp.dot(left, hot(k) if kept is None else kept, preferred_element_type=F32)
        found = found[:species] + found[species:]
        return found if chunks == 1 else state + found

    start = repeat_steps(
        chunks, gather, jnp.zeros((species, lines * nodes), F32) if chunks > 1 else 0
    )

    lane = lax.broadcasted_iota(jnp.int32, (ROWS, LANES), 1)
    part = lane // width
    block = (lane % width) // lines
    segment = block * segments + part
    line = lane % lines

    def earlier(value, distance):
        major, minor = distance // segments, distance % segments
        near = pltpu.roll(value, minor * width + major * lines, 1)
        if minor == 0:
            return near
        far = pltpu.roll(value, minor * width + (major + 1) * lines, 1)
        return jnp.where(part >= minor, near, far)

    eye = lax.broadcasted_iota(jnp.int32, (species, LANES), 0) == lax.broadcasted_iota(
        jnp.int32, (species, LANES), 1
    )
    padded = jnp.concatenate([inflow_ref[...], jnp.zeros((1, LANES - species), F32)], axis=1)
    column = jnp.sum(jnp.where(eye, padded, 0.0), axis=1, keepdims=True)
    entry = jnp.broadcast_to(column, (species, LANES))
    entry = [entry[ROWS * g : ROWS * (g + 1)] for g in range(groups)]

    first = [None] * groups
    second = [None] * groups
    local, ones, twos = [], [], []
    for t in range(times):
        scale_t, decay_t = row(0, t), row(1, t)
        one = decay_t if t == 0 else decay_t * ones[-1]
        two = scale_t * one if t == 0 else scale_t * one + decay_t * twos[-1]
        ones.append(one)
        twos.append(two)
        for g in range(groups):
            value = start[ROWS * g : ROWS * (g + 1), LANES * t : LANES * (t + 1)] * scale_t
            first[g] = value if t == 0 else value + decay_t * first[g]
            value = scale_t * first[g]
            second[g] = value if t == 0 else value + decay_t * second[g]
            local.append(second[g])

    a, b = ones[-1], twos[-1]
    head = segment == 0
    first = [jnp.where(head, f + a * e, f) for f, e in zip(first, entry)]
    second = [jnp.where(head, s + b * e + a * e, s) for s, e in zip(second, entry)]
    distance = 1
    while distance < blocks * segments:
        run_a, run_b = a, b
        next_first, next_second = first, second
        for k in range(1, 4):
            if k * distance >= blocks * segments:
                break
            opened = segment >= k * distance
            a_open, b_open = jnp.where(opened, run_a, 0.0), jnp.where(opened, run_b, 0.0)
            ahead = [earlier(f, k * distance) for f in first]
            next_first = [n + a_open * f for n, f in zip(next_first, ahead)]
            next_second = [
                n + b_open * f + a_open * earlier(s, k * distance)
                for n, s, f in zip(next_second, second, ahead)
            ]
            a_ahead = earlier(a, k * distance)
            run_b = run_b * a_ahead + run_a * earlier(b, k * distance)
            run_a = run_a * a_ahead
        first, second = next_first, next_second
        a, b = run_a, run_b
        distance *= 4
    carry_one = [jnp.where(head, e, earlier(f, 1)) for e, f in zip(entry, first)]
    carry_two = [jnp.where(head, e, earlier(s, 1)) for e, s in zip(entry, second)]
    columns = [
        jnp.concatenate(
            [
                local[t * groups + g] + twos[t] * carry_one[g] + ones[t] * carry_two[g]
                for g in range(groups)
            ],
            axis=0,
        )
        for t in range(times)
    ]

    matrix_high, matrix_low = rounded(interaction_ref[...])
    blank = jnp.zeros_like(matrix_high)
    left = jnp.concatenate(
        [
            jnp.concatenate(
                [matrix_high, blank, matrix_low, blank, matrix_high, blank], axis=1
            ),
            jnp.concatenate(
                [blank, matrix_high, blank, matrix_low, blank, matrix_high], axis=1
            ),
        ],
        axis=0,
    ).astype(BF16)
    half = times // 2
    depth = half // CHUNKS
    bases = [
        jnp.concatenate(
            [
                jnp.concatenate(columns[offset + c * depth : offset + (c + 1) * depth], axis=1)
                for offset in (0, half)
            ],
            axis=0,
        )
        for c in range(CHUNKS)
    ]
    iterates = list(bases)
    for step in range(NEWTON):
        for c in range(CHUNKS):
            high, low = parts(jnp.tanh(iterates[c]))
            right = jnp.concatenate([high, high, low], axis=0)
            iterates[c] = bases[c] - jnp.dot(left, right, preferred_element_type=F32)

    length = jnp.zeros((ROWS, LANES), jnp.int32)
    for one_line in range(lines):
        one_length = jnp.broadcast_to(length_ref[:, one_line : one_line + 1], (ROWS, LANES))
        length = jnp.where(line == one_line, one_length, length)
    node = block * LANES + part * times
    top = lax.broadcasted_iota(jnp.int32, (ROWS, LANES), 0) == 0
    pieces = []
    for t in range(times):
        weight = jnp.where(node + t < length, row(2, t), 0.0)
        chunk, place = t % half // depth, t % half % depth
        found = iterates[chunk][
            t // half * species : (t // half + 1) * species, LANES * place : LANES * (place + 1)
        ]
        scaled = [found[ROWS * g : ROWS * (g + 1)] * weight for g in range(groups)]
        scaled.append(jnp.where(top, weight, 0.0))
        pieces.append(jnp.concatenate(scaled, axis=0))
    left = split(jnp.concatenate(pieces, axis=1))
    relative = lane_groups(cap, here + bundle)

    def scatter(k, carry):
        sums = lax.dot_general(
            left,
            hot(k) if kept is None else kept,
            (((1,), (1,)), ((), ())),
            preferred_element_type=F32,
        )
        sums = sums[:rows] + sums[rows:]
        for half in range(2):
            tiles = pack(
                [
                    sums[ROWS * g : ROWS * (g + 1), LANES * half : LANES * (half + 1)]
                    for g in range(all_groups)
                ],
                cap,
                bundle,
                relative,
            )
            for j in range(all_groups):
                owner = k * chunk_owners + half * all_groups + j
                for copy in range(copies):
                    out_ref[copy * owners + owner] = tiles[j]
        return carry

    repeat_steps(chunks, scatter, 0)


def blend_kernel(bundles, sums_ref, request_ref, pore_ref, cell_ref, out_hbm, out_ref, out_sem):
    owners = sums_ref.shape[0] // bundles
    species, cells = cell_ref.shape
    cap = request_ref.shape[3]
    all_groups = LANES // cap
    groups = species // ROWS
    width = 2 * LANES
    highs = cells // width
    chunks = owners // ROWS
    here = lax.axis_index("grid")
    sublane = lax.broadcasted_iota(jnp.int32, (ROWS, LANES), 0)

    def chunk(k, total):
        values, weights, indices = [], [], []
        for t in range(bundles // all_groups):
            block = jnp.concatenate(
                [
                    request_ref[
                        t * all_groups
                        + lax.rem(x + all_groups - lax.rem(here, all_groups), all_groups),
                        0,
                        pl.ds(k * ROWS, ROWS),
                        :,
                    ]
                    for x in range(all_groups)
                ],
                axis=1,
            )
            straight = block
            for turn in range(1, all_groups):
                block = jnp.where(
                    sublane % all_groups == turn, pltpu.roll(straight, turn * cap, 1), block
                )
            for d in range(ROWS):
                found = unpack(
                    [
                        sums_ref[(t * all_groups + j) * owners + k * ROWS + d]
                        for j in range(all_groups)
                    ],
                    cap,
                    lane_groups(cap, here + d),
                    all_groups,
                )
                weights.append(found[groups][:1])
                values.append(jnp.concatenate(found[:groups], axis=0))
                indices.append(block[d : d + 1])
        both = split(jnp.concatenate(values, axis=1))
        weight_high, weight_low = rounded(jnp.concatenate(weights, axis=1))
        index = jnp.concatenate(indices, axis=1)
        entries = index.shape[1]
        high = jnp.broadcast_to(index // width, (2 * ROWS, entries)).astype(F32).astype(BF16)
        low = jnp.broadcast_to(index % width, (2 * ROWS, entries)).astype(F32).astype(BF16)
        low = jnp.concatenate([low] * (width // (2 * ROWS)), axis=0)
        place = lax.broadcasted_iota(jnp.int32, (width, entries), 0).astype(F32).astype(BF16)
        hot = jnp.where(place == low, jnp.ones_like(place), jnp.zeros_like(place))
        zero = jnp.zeros((2 * ROWS, entries), BF16)
        pieces = []
        for first in range(0, highs, 2 * ROWS):
            mask = high == (
                lax.broadcasted_iota(jnp.int32, (2 * ROWS, entries), 0) + first
            ).astype(F32).astype(BF16)
            for part in (weight_high, weight_low):
                row = jnp.broadcast_to(part, (2 * ROWS, entries)).astype(BF16)
                pieces.append(jnp.where(mask, row, zero))
        for h in range(highs):
            mask = high == jnp.array(h, BF16)
            for r in range(2 * species // (2 * ROWS)):
                pieces.append(jnp.where(mask, both[2 * ROWS * r : 2 * ROWS * (r + 1)], zero))
        half = (len(pieces) + len(pieces) // 2 % 2) // 2
        products = [
            lax.dot_general(
                jnp.concatenate(some, axis=0),
                hot,
                (((1,), (1,)), ((), ())),
                preferred_element_type=F32,
            )
            for some in (pieces[:half], pieces[half:])
        ]
        product = jnp.concatenate(products, axis=0)
        return product if chunks == 1 else total + product

    flux_rows = -(-highs // (2 * ROWS)) * 4 * ROWS
    total = repeat_steps(
        chunks,
        chunk,
        jnp.zeros((highs * 2 * species + flux_rows, width), F32) if chunks > 1 else 0,
    )
    flux, total = total[:flux_rows], total[flux_rows:]
    copies = []
    stride = max(highs // 4, 1)
    for h in range(highs):
        part = total[2 * species * h : 2 * species * (h + 1)]
        part = part[:species] + part[species:]
        row = h // (2 * ROWS) * 4 * ROWS + h % (2 * ROWS)
        pore = pore_ref[:, width * h : width * (h + 1)]
        inverse = 1.0 / (pore + flux[row : row + 1] + flux[row + 2 * ROWS : row + 2 * ROWS + 1])
        columns = pl.ds(width * h, width)
        out_ref[:, columns] = (pore * cell_ref[:, columns] + part) * inverse
        if h % stride == stride - 1:
            columns = pl.ds(width * (h - stride + 1), stride * width)
            copies.append(
                pltpu.make_async_copy(
                    out_ref.at[:, columns], out_hbm.at[:, columns], out_sem.at[h // stride]
                )
            )
            copies[-1].start()
    for copy in copies:
        copy.wait()


def call(kernel, shape, operands, kinds={}, scratch=(), out=pltpu.VMEM, flops=0):
    return pl.pallas_call(
        kernel,
        out_shape=jax.ShapeDtypeStruct(shape, F32),
        in_specs=[
            pl.BlockSpec(memory_space=kinds.get(i, pltpu.VMEM)) for i in range(len(operands))
        ],
        out_specs=pl.BlockSpec(memory_space=out),
        scratch_shapes=list(scratch),
        compiler_params=pltpu.CompilerParams(vmem_limit_bytes=VMEM_BYTES),
        cost_estimate=pl.CostEstimate(flops=flops, bytes_accessed=0, transcendentals=0),
    )(*operands)


def shards(
    bundles,
    cell_state,
    pore_volume,
    request_cell,
    node_slot,
    line_length,
    courant,
    flux_weight,
    inflow,
    interaction,
):
    owners, cap = request_cell.shape[2:]
    first = call(first_kernel, (ROWS, LANES), (), flops=10**9)
    outgoing = call(
        pick_kernel,
        (owners, ROWS, LANES),
        (cell_state, request_cell, first, line_length, inflow),
    )
    table = lax.all_to_all(outgoing, "grid", split_axis=0, concat_axis=0, tiled=True)
    lines, nodes = node_slot.shape[1:]
    blocks = nodes // LANES

    def by_block(value):
        return value.reshape(lines, blocks, LANES).swapaxes(0, 1).reshape(blocks * lines, LANES)

    sums = call(
        functools.partial(lines_kernel, lines, cap),
        (owners * bundles, ROWS, LANES),
        (
            table,
            by_block(node_slot),
            line_length,
            by_block(courant),
            by_block(flux_weight),
            inflow,
            interaction,
        ),
        scratch=(pltpu.VMEM((4, lines * blocks, LANES), F32),),
    )
    back = lax.all_to_all(sums, ("bundle", "grid"), split_axis=0, concat_axis=0, tiled=True)
    return call(
        functools.partial(blend_kernel, bundles),
        cell_state.shape,
        (back, request_cell, pore_volume[None, :], cell_state),
        scratch=(pltpu.VMEM(cell_state.shape, F32), pltpu.SemaphoreType.DMA((4,))),
        out=pltpu.HBM,
    )


def solution(mesh):
    placed = (
        P(None, "grid"),
        P("grid"),
        P(None, "grid", None, None),
        P("bundle", "grid", None),
        P("bundle", "grid"),
        P("bundle", "grid", None),
        P("bundle", "grid", None),
        P("bundle", None),
        P(),
    )
    return jax.shard_map(
        functools.partial(shards, mesh.shape["bundle"]),
        mesh=mesh,
        in_specs=placed,
        out_specs=P(None, "grid"),
        check_vma=False,
    )
```

```python
import functools

import jax
import jax.numpy as jnp
from jax import lax
from jax.experimental import pallas as pl
from jax.experimental.pallas import tpu as pltpu
from jax.sharding import PartitionSpec as P

SUB = 2
NEWTON = 3
LANES = 128
ROWS = 8
F32 = jnp.float32
BF16 = jnp.bfloat16
VMEM_BYTES = 32 * 1024 * 1024
CHUNKS = 4


def repeat_steps(count, body, carry):
    if count == 1:
        return body(0, carry)
    return lax.fori_loop(0, count, body, carry)


def rounded(value):
    high = value.astype(BF16).astype(F32)
    return high, value - high


def parts(value):
    high = value.astype(BF16)
    return high, (value - high.astype(F32)).astype(BF16)


def split(value):
    return jnp.concatenate(rounded(value), axis=0).astype(BF16)


def select_groups(tiles, relative):
    count = len(tiles)
    results = []
    for i in range(count):
        value = tiles[0]
        for j in range(1, count):
            value = jnp.where(relative == (i + j) % count, tiles[j], value)
        results.append(value)
    return results


def lane_groups(cap, turn):
    groups = LANES // cap
    lane = lax.broadcasted_iota(jnp.int32, (ROWS, LANES), 1)
    return (lane // cap + (2 * groups - lax.rem(turn, groups))) % groups


def pack(rows, cap, turn, relative):
    groups = LANES // cap
    turned = [
        pltpu.roll(rows[g], lax.rem(turn + g, groups) * cap, 1) for g in range(groups)
    ]
    return select_groups(turned, relative)


def unpack(tiles, cap, relative, count):
    found = select_groups(tiles, relative)[:count]
    return [
        found[g] if g == 0 else pltpu.roll(found[g], LANES - g * cap, 1) for g in range(count)
    ]


def exchange_groups(tiles, width):
    tiles = list(tiles)
    lane_group = lax.broadcasted_iota(jnp.int32, tiles[0].shape, 1) // width
    step = 1
    while step < len(tiles):
        keep = (lane_group & step) == 0
        for i in range(len(tiles)):
            if i & step == 0:
                first, second = tiles[i], tiles[i | step]
                tiles[i] = jnp.where(keep, first, pltpu.roll(second, step * width, 1))
                tiles[i | step] = jnp.where(
                    keep, pltpu.roll(first, LANES - step * width, 1), second
                )
        step *= 2
    return tiles


def spread_rows(block, cap):
    groups = block.shape[0]
    wide = jnp.concatenate([block] * groups, axis=1)
    rows = lax.broadcasted_iota(jnp.int32, wide.shape, 0)
    lanes = lax.broadcasted_iota(jnp.int32, wide.shape, 1) // cap
    return jnp.sum(jnp.where(rows == lanes, wide, 0), axis=0, keepdims=True)


def first_kernel(out_ref):
    out_ref[...] = jnp.zeros_like(out_ref)


def pick_index(request_ref, k):
    bundle = lax.axis_index("bundle")
    groups = LANES // request_ref.shape[3]
    cap = request_ref.shape[3]
    block = request_ref[bundle, 0, pl.ds(k * 2 * groups, 2 * groups), :]
    index = jnp.concatenate(
        [spread_rows(block[:groups], cap), spread_rows(block[groups:], cap)], axis=1
    )
    high = jnp.broadcast_to(index // LANES, (ROWS, 2 * LANES))
    hot = (
        (lax.broadcasted_iota(jnp.int32, (LANES, 2 * LANES), 0) == index % LANES)
        .astype(F32)
        .astype(BF16)
    )
    return high, jnp.concatenate([hot, hot], axis=0)


def pick_kernel(cell_ref, request_ref, first_ref, *refs):
    *kept_refs, out_ref = refs
    species, cells = cell_ref.shape
    owners, cap = request_ref.shape[2:]
    groups = LANES // cap
    chunks = owners // (2 * groups)
    highs = cells // LANES
    here = lax.axis_index("grid")
    relative = lane_groups(cap, here)
    cell = cell_ref[...]
    stacked = jnp.concatenate(
        [cell[:, LANES * h : LANES * (h + 1)] for h in range(highs)], axis=0
    )
    left = jnp.concatenate(rounded(stacked), axis=1).astype(BF16)

    def chunk(k, carry):
        first = k * 2 * groups
        if kept_refs:
            high, right = kept_refs[0][...], kept_refs[1][...]
        else:
            high, right = pick_index(request_ref, k)
        product = jnp.dot(left, right, preferred_element_type=F32)
        picked = jnp.zeros((species, 2 * LANES), F32)
        high = jnp.concatenate([high] * (species // ROWS), axis=0)
        for h in range(highs):
            picked = picked + jnp.where(high == h, product[species * h : species * (h + 1)], 0.0)
        blank = jnp.zeros((groups * ROWS - species, 2 * LANES), F32)
        picked = jnp.concatenate([picked, blank], axis=0)
        for half in range(2):
            tiles = pack(
                [
                    picked[ROWS * g : ROWS * (g + 1), LANES * half : LANES * (half + 1)]
                    for g in range(groups)
                ],
                cap,
                here,
                relative,
            )
            for j in range(groups):
                out_ref[first + half * groups + j] = tiles[j]
        return carry

    repeat_steps(chunks, chunk, 0)


def to_segments(values, width):
    groups = LANES // width
    stacked = [value.astype(F32) for value in values]
    stacked.append(jnp.zeros((LANES - width * len(values), LANES), F32))
    turned = jnp.transpose(jnp.concatenate(stacked, axis=0))
    times = LANES // groups
    return exchange_groups([turned[times * g : times * (g + 1)] for g in range(groups)], width)


def lines_kernel(
    lines,
    cap,
    table_ref,
    slot_ref,
    length_ref,
    courant_ref,
    flux_ref,
    inflow_ref,
    interaction_ref,
    out_ref,
    rows_ref,
):
    owners = table_ref.shape[0]
    copies = out_ref.shape[0] // owners
    species = inflow_ref.shape[1]
    width = slot_ref.shape[0]
    nodes = width * LANES // lines
    groups = species // ROWS
    all_groups = LANES // cap
    rows = all_groups * ROWS
    blocks = nodes // LANES
    segments = LANES // width
    times = LANES // segments
    chunk_owners = 2 * all_groups
    chunks = owners // chunk_owners
    here, bundle = lax.axis_index("grid"), lax.axis_index("bundle")

    slot = slot_ref[...]
    within = (slot + lax.rem(here, all_groups) * cap) % LANES
    slot, courant, flux = to_segments(
        [slot - slot % LANES + within, courant_ref[...], flux_ref[...]], width
    )[:3]
    scale = 1.0 / (1.0 + courant)
    rows_ref[0] = scale
    rows_ref[1] = courant * scale
    rows_ref[2] = flux
    rows_ref[3] = slot

    def row(kind, t, depth=ROWS):
        return jnp.broadcast_to(rows_ref[kind, t : t + 1], (depth, LANES))

    def hot(k):
        index = lax.broadcasted_iota(jnp.int32, (2 * LANES, LANES), 0).astype(F32).astype(BF16)
        one, zero = jnp.ones_like(index), jnp.zeros_like(index)
        base = lax.convert_element_type(k * 2 * LANES, F32)
        columns = []
        for t in range(times):
            local = (row(3, t, 2 * ROWS) - base).astype(BF16)
            local = jnp.concatenate([local] * (LANES // ROWS), axis=0)
            columns.append(jnp.where(local == index, one, zero))
        return jnp.concatenate(columns, axis=1)

    kept = hot(0) if chunks == 1 else None

    relative = lane_groups(cap, here)

    def gather(k, state):
        halves = []
        for half in range(2):
            first = k * chunk_owners + half * all_groups
            halves.append(
                jnp.concatenate(
                    unpack(
                        [table_ref[first + j] for j in range(all_groups)], cap, relative, groups
                    ),
                    axis=0,
                )
            )
        left = split(jnp.concatenate(halves, axis=1))
        found = jnp.dot(left, hot(k) if kept is None else kept, preferred_element_type=F32)
        found = found[:species] + found[species:]
        return found if chunks == 1 else state + found

    start = repeat_steps(
        chunks, gather, jnp.zeros((species, lines * nodes), F32) if chunks > 1 else 0
    )

    lane = lax.broadcasted_iota(jnp.int32, (ROWS, LANES), 1)
    part = lane // width
    block = (lane % width) // lines
    segment = block * segments + part
    line = lane % lines

    def earlier(value, distance):
        major, minor = distance // segments, distance % segments
        near = pltpu.roll(value, minor * width + major * lines, 1)
        if minor == 0:
            return near
        far = pltpu.roll(value, minor * width + (major + 1) * lines, 1)
        return jnp.where(part >= minor, near, far)

    eye = lax.broadcasted_iota(jnp.int32, (species, LANES), 0) == lax.broadcasted_iota(
        jnp.int32, (species, LANES), 1
    )
    padded = jnp.concatenate([inflow_ref[...], jnp.zeros((1, LANES - species), F32)], axis=1)
    column = jnp.sum(jnp.where(eye, padded, 0.0), axis=1, keepdims=True)
    entry = jnp.broadcast_to(column, (species, LANES))
    entry = [entry[ROWS * g : ROWS * (g + 1)] for g in range(groups)]

    first = [None] * groups
    second = [None] * groups
    local, ones, twos = [], [], []
    for t in range(times):
        scale_t, decay_t = row(0, t), row(1, t)
        one = decay_t if t == 0 else decay_t * ones[-1]
        two = scale_t * one if t == 0 else scale_t * one + decay_t * twos[-1]
        ones.append(one)
        twos.append(two)
        for g in range(groups):
            value = start[ROWS * g : ROWS * (g + 1), LANES * t : LANES * (t + 1)] * scale_t
            first[g] = value if t == 0 else value + decay_t * first[g]
            value = scale_t * first[g]
            second[g] = value if t == 0 else value + decay_t * second[g]
            local.append(second[g])

    a, b = ones[-1], twos[-1]
    head = segment == 0
    first = [jnp.where(head, f + a * e, f) for f, e in zip(first, entry)]
    second = [jnp.where(head, s + b * e + a * e, s) for s, e in zip(second, entry)]
    distance = 1
    while distance < blocks * segments:
        run_a, run_b = a, b
        next_first, next_second = first, second
        for k in range(1, 4):
            if k * distance >= blocks * segments:
                break
            opened = segment >= k * distance
            a_open, b_open = jnp.where(opened, run_a, 0.0), jnp.where(opened, run_b, 0.0)
            ahead = [earlier(f, k * distance) for f in first]
            next_first = [n + a_open * f for n, f in zip(next_first, ahead)]
            next_second = [
                n + b_open * f + a_open * earlier(s, k * distance)
                for n, s, f in zip(next_second, second, ahead)
            ]
            a_ahead = earlier(a, k * distance)
            run_b = run_b * a_ahead + run_a * earlier(b, k * distance)
            run_a = run_a * a_ahead
        first, second = next_first, next_second
        a, b = run_a, run_b
        distance *= 4
    carry_one = [jnp.where(head, e, earlier(f, 1)) for e, f in zip(entry, first)]
    carry_two = [jnp.where(head, e, earlier(s, 1)) for e, s in zip(entry, second)]
    columns = [
        jnp.concatenate(
            [
                local[t * groups + g] + twos[t] * carry_one[g] + ones[t] * carry_two[g]
                for g in range(groups)
            ],
            axis=0,
        )
        for t in range(times)
    ]

    matrix_high, matrix_low = rounded(interaction_ref[...])
    blank = jnp.zeros_like(matrix_high)
    left = jnp.concatenate(
        [
            jnp.concatenate(
                [matrix_high, blank, matrix_low, blank, matrix_high, blank], axis=1
            ),
            jnp.concatenate(
                [blank, matrix_high, blank, matrix_low, blank, matrix_high], axis=1
            ),
        ],
        axis=0,
    ).astype(BF16)
    half = times // 2
    depth = half // CHUNKS
    bases = [
        jnp.concatenate(
            [
                jnp.concatenate(columns[offset + c * depth : offset + (c + 1) * depth], axis=1)
                for offset in (0, half)
            ],
            axis=0,
        )
        for c in range(CHUNKS)
    ]
    iterates = list(bases)
    for step in range(NEWTON):
        for c in range(CHUNKS):
            high, low = parts(jnp.tanh(iterates[c]))
            right = jnp.concatenate([high, high, low], axis=0)
            iterates[c] = bases[c] - jnp.dot(left, right, preferred_element_type=F32)

    length = jnp.zeros((ROWS, LANES), jnp.int32)
    for one_line in range(lines):
        one_length = jnp.broadcast_to(length_ref[:, one_line : one_line + 1], (ROWS, LANES))
        length = jnp.where(line == one_line, one_length, length)
    node = block * LANES + part * times
    top = lax.broadcasted_iota(jnp.int32, (ROWS, LANES), 0) == 0
    pieces = []
    for t in range(times):
        weight = jnp.where(node + t < length, row(2, t), 0.0)
        chunk, place = t % half // depth, t % half % depth
        found = iterates[chunk][
            t // half * species : (t // half + 1) * species, LANES * place : LANES * (place + 1)
        ]
        scaled = [found[ROWS * g : ROWS * (g + 1)] * weight for g in range(groups)]
        scaled.append(jnp.where(top, weight, 0.0))
        pieces.append(jnp.concatenate(scaled, axis=0))
    left = split(jnp.concatenate(pieces, axis=1))
    relative = lane_groups(cap, here + bundle)

    def scatter(k, carry):
        sums = lax.dot_general(
            left,
            hot(k) if kept is None else kept,
            (((1,), (1,)), ((), ())),
            preferred_element_type=F32,
        )
        sums = sums[:rows] + sums[rows:]
        for half in range(2):
            tiles = pack(
                [
                    sums[ROWS * g : ROWS * (g + 1), LANES * half : LANES * (half + 1)]
                    for g in range(all_groups)
                ],
                cap,
                bundle,
                relative,
            )
            for j in range(all_groups):
                owner = k * chunk_owners + half * all_groups + j
                for copy in range(copies):
                    out_ref[copy * owners + owner] = tiles[j]
        return carry

    repeat_steps(chunks, scatter, 0)


def blend_index(request_ref, k):
    bundles, cap = request_ref.shape[0], request_ref.shape[3]
    all_groups = LANES // cap
    width = 2 * LANES
    here = lax.axis_index("grid")
    sublane = lax.broadcasted_iota(jnp.int32, (ROWS, LANES), 0)
    indices = []
    for t in range(bundles // all_groups):
        straight = jnp.concatenate(
            [
                request_ref[
                    t * all_groups
                    + lax.rem(x + all_groups - lax.rem(here, all_groups), all_groups),
                    0,
                    pl.ds(k * ROWS, ROWS),
                    :,
                ]
                for x in range(all_groups)
            ],
            axis=1,
        )
        block = straight
        for turn in range(1, all_groups):
            block = jnp.where(
                sublane % all_groups == turn, pltpu.roll(straight, turn * cap, 1), block
            )
        indices += [block[d : d + 1] for d in range(ROWS)]
    index = jnp.concatenate(indices, axis=1)
    entries = index.shape[1]
    high = jnp.broadcast_to(index // width, (2 * ROWS, entries)).astype(F32).astype(BF16)
    low = jnp.broadcast_to(index % width, (2 * ROWS, entries)).astype(F32).astype(BF16)
    low = jnp.concatenate([low] * (width // (2 * ROWS)), axis=0)
    place = lax.broadcasted_iota(jnp.int32, (width, entries), 0).astype(F32).astype(BF16)
    return high, jnp.where(place == low, jnp.ones_like(place), jnp.zeros_like(place))


def index_kernel(
    request_ref, first_ref, length_ref, inflow_ref, pick_high, pick_hot, blend_high, blend_hot
):
    pick_high[...], pick_hot[...] = pick_index(request_ref, 0)
    blend_high[...], blend_hot[...] = blend_index(request_ref, 0)


def blend_kernel(bundles, sums_ref, request_ref, pore_ref, cell_ref, *refs):
    *kept_refs, out_hbm, out_ref, out_sem = refs
    owners = sums_ref.shape[0] // bundles
    species, cells = cell_ref.shape
    cap = request_ref.shape[3]
    all_groups = LANES // cap
    groups = species // ROWS
    width = 2 * LANES
    highs = cells // width
    chunks = owners // ROWS
    here = lax.axis_index("grid")

    def chunk(k, total):
        values, weights = [], []
        for t in range(bundles // all_groups):
            for d in range(ROWS):
                found = unpack(
                    [
                        sums_ref[(t * all_groups + j) * owners + k * ROWS + d]
                        for j in range(all_groups)
                    ],
                    cap,
                    lane_groups(cap, here + d),
                    all_groups,
                )
                weights.append(found[groups][:1])
                values.append(jnp.concatenate(found[:groups], axis=0))
        both = split(jnp.concatenate(values, axis=1))
        weight_high, weight_low = rounded(jnp.concatenate(weights, axis=1))
        if kept_refs:
            high, hot = kept_refs[0][...], kept_refs[1][...]
        else:
            high, hot = blend_index(request_ref, k)
        entries = hot.shape[1]
        zero = jnp.zeros((2 * ROWS, entries), BF16)
        pieces = []
        for first in range(0, highs, 2 * ROWS):
            mask = high == (
                lax.broadcasted_iota(jnp.int32, (2 * ROWS, entries), 0) + first
            ).astype(F32).astype(BF16)
            for part in (weight_high, weight_low):
                row = jnp.broadcast_to(part, (2 * ROWS, entries)).astype(BF16)
                pieces.append(jnp.where(mask, row, zero))
        for h in range(highs):
            mask = high == jnp.array(h, BF16)
            for r in range(2 * species // (2 * ROWS)):
                pieces.append(jnp.where(mask, both[2 * ROWS * r : 2 * ROWS * (r + 1)], zero))
        half = (len(pieces) + len(pieces) // 2 % 2) // 2
        products = [
            lax.dot_general(
                jnp.concatenate(some, axis=0),
                hot,
                (((1,), (1,)), ((), ())),
                preferred_element_type=F32,
            )
            for some in (pieces[:half], pieces[half:])
        ]
        product = jnp.concatenate(products, axis=0)
        return product if chunks == 1 else total + product

    flux_rows = -(-highs // (2 * ROWS)) * 4 * ROWS
    total = repeat_steps(
        chunks,
        chunk,
        jnp.zeros((highs * 2 * species + flux_rows, width), F32) if chunks > 1 else 0,
    )
    flux, total = total[:flux_rows], total[flux_rows:]
    copies = []
    stride = max(highs // 4, 1)
    for h in range(highs):
        part = total[2 * species * h : 2 * species * (h + 1)]
        part = part[:species] + part[species:]
        row = h // (2 * ROWS) * 4 * ROWS + h % (2 * ROWS)
        pore = pore_ref[:, width * h : width * (h + 1)]
        inverse = 1.0 / (pore + flux[row : row + 1] + flux[row + 2 * ROWS : row + 2 * ROWS + 1])
        columns = pl.ds(width * h, width)
        out_ref[:, columns] = (pore * cell_ref[:, columns] + part) * inverse
        if h % stride == stride - 1:
            columns = pl.ds(width * (h - stride + 1), stride * width)
            copies.append(
                pltpu.make_async_copy(
                    out_ref.at[:, columns], out_hbm.at[:, columns], out_sem.at[h // stride]
                )
            )
            copies[-1].start()
    for copy in copies:
        copy.wait()


def call(kernel, shapes, operands, kinds={}, scratch=(), out=pltpu.VMEM, flops=0):
    return pl.pallas_call(
        kernel,
        out_shape=[jax.ShapeDtypeStruct(shape, kind) for shape, kind in shapes],
        in_specs=[
            pl.BlockSpec(memory_space=kinds.get(i, pltpu.VMEM)) for i in range(len(operands))
        ],
        out_specs=[pl.BlockSpec(memory_space=out)] * len(shapes),
        scratch_shapes=list(scratch),
        compiler_params=pltpu.CompilerParams(vmem_limit_bytes=VMEM_BYTES),
        cost_estimate=pl.CostEstimate(flops=flops, bytes_accessed=0, transcendentals=0),
    )(*operands)


def shards(
    bundles,
    cell_state,
    pore_volume,
    request_cell,
    node_slot,
    line_length,
    courant,
    flux_weight,
    inflow,
    interaction,
):
    owners, cap = request_cell.shape[2:]
    first = call(first_kernel, [((ROWS, LANES), F32)], (), flops=10**9)[0]
    indices = []
    if owners == ROWS and owners * cap == 2 * LANES:
        entries = owners * bundles * cap
        indices = call(
            index_kernel,
            [
                ((ROWS, 2 * LANES), jnp.int32),
                ((2 * LANES, 2 * LANES), BF16),
                ((2 * ROWS, entries), BF16),
                ((2 * LANES, entries), BF16),
            ],
            (request_cell, first, line_length, inflow),
        )
    outgoing = call(
        pick_kernel,
        [((owners, ROWS, LANES), F32)],
        (cell_state, request_cell, first, *indices[:2]),
    )[0]
    table = lax.all_to_all(outgoing, "grid", split_axis=0, concat_axis=0, tiled=True)
    lines, nodes = node_slot.shape[1:]
    blocks = nodes // LANES

    def by_block(value):
        return value.reshape(lines, blocks, LANES).swapaxes(0, 1).reshape(blocks * lines, LANES)

    sums = call(
        functools.partial(lines_kernel, lines, cap),
        [((owners * bundles, ROWS, LANES), F32)],
        (
            table,
            by_block(node_slot),
            line_length,
            by_block(courant),
            by_block(flux_weight),
            inflow,
            interaction,
        ),
        scratch=(pltpu.VMEM((4, lines * blocks, LANES), F32),),
    )[0]
    back = lax.all_to_all(sums, ("bundle", "grid"), split_axis=0, concat_axis=0, tiled=True)
    return call(
        functools.partial(blend_kernel, bundles),
        [(cell_state.shape, F32)],
        (back, request_cell, pore_volume[None, :], cell_state, *indices[2:]),
        scratch=(pltpu.VMEM(cell_state.shape, F32), pltpu.SemaphoreType.DMA((4,))),
        out=pltpu.HBM,
    )[0]


def solution(mesh):
    placed = (
        P(None, "grid"),
        P("grid"),
        P(None, "grid", None, None),
        P("bundle", "grid", None),
        P("bundle", "grid"),
        P("bundle", "grid", None),
        P("bundle", "grid", None),
        P("bundle", None),
        P(),
    )
    return jax.shard_map(
        functools.partial(shards, mesh.shape["bundle"]),
        mesh=mesh,
        in_specs=placed,
        out_specs=P(None, "grid"),
        check_vma=False,
    )
```

```python
import functools

import jax
import jax.numpy as jnp
from jax import lax
from jax.experimental import pallas as pl
from jax.experimental.pallas import tpu as pltpu
from jax.sharding import PartitionSpec as P

SUB = 2
NEWTON = 3
LANES = 128
ROWS = 8
F32 = jnp.float32
BF16 = jnp.bfloat16
VMEM_BYTES = 32 * 1024 * 1024
CHUNKS = 4


def near_size(bundles):
    return 2 if bundles % 2 == 0 else 1


def turned_place(bundle, bundles):
    near = near_size(bundles)
    return bundle % near * (bundles // near) + bundle // near


def repeat_steps(count, body, carry):
    if count == 1:
        return body(0, carry)
    return lax.fori_loop(0, count, body, carry)


def rounded(value):
    high = value.astype(BF16).astype(F32)
    return high, value - high


def parts(value):
    high = value.astype(BF16)
    return high, (value - high.astype(F32)).astype(BF16)


def split(value):
    return jnp.concatenate(rounded(value), axis=0).astype(BF16)


def select_groups(tiles, relative):
    count = len(tiles)
    results = []
    for i in range(count):
        value = tiles[0]
        for j in range(1, count):
            value = jnp.where(relative == (i + j) % count, tiles[j], value)
        results.append(value)
    return results


def lane_groups(cap, turn):
    groups = LANES // cap
    lane = lax.broadcasted_iota(jnp.int32, (ROWS, LANES), 1)
    return (lane // cap + (2 * groups - lax.rem(turn, groups))) % groups


def pack(rows, cap, turn, relative):
    groups = LANES // cap
    turned = [
        pltpu.roll(rows[g], lax.rem(turn + g, groups) * cap, 1) for g in range(groups)
    ]
    return select_groups(turned, relative)


def unpack(tiles, cap, relative, count):
    found = select_groups(tiles, relative)[:count]
    return [
        found[g] if g == 0 else pltpu.roll(found[g], LANES - g * cap, 1) for g in range(count)
    ]


def exchange_groups(tiles, width):
    tiles = list(tiles)
    lane_group = lax.broadcasted_iota(jnp.int32, tiles[0].shape, 1) // width
    step = 1
    while step < len(tiles):
        keep = (lane_group & step) == 0
        for i in range(len(tiles)):
            if i & step == 0:
                first, second = tiles[i], tiles[i | step]
                tiles[i] = jnp.where(keep, first, pltpu.roll(second, step * width, 1))
                tiles[i | step] = jnp.where(
                    keep, pltpu.roll(first, LANES - step * width, 1), second
                )
        step *= 2
    return tiles


def spread_rows(block, cap):
    groups = block.shape[0]
    wide = jnp.concatenate([block] * groups, axis=1)
    rows = lax.broadcasted_iota(jnp.int32, wide.shape, 0)
    lanes = lax.broadcasted_iota(jnp.int32, wide.shape, 1) // cap
    return jnp.sum(jnp.where(rows == lanes, wide, 0), axis=0, keepdims=True)


def first_kernel(out_ref):
    out_ref[...] = jnp.zeros_like(out_ref)


def pick_index(request_ref, k):
    bundle = bundle_place()
    groups = LANES // request_ref.shape[3]
    cap = request_ref.shape[3]
    block = request_ref[bundle, 0, pl.ds(k * 2 * groups, 2 * groups), :]
    index = jnp.concatenate(
        [spread_rows(block[:groups], cap), spread_rows(block[groups:], cap)], axis=1
    )
    high = jnp.broadcast_to(index // LANES, (ROWS, 2 * LANES))
    hot = (
        (lax.broadcasted_iota(jnp.int32, (LANES, 2 * LANES), 0) == index % LANES)
        .astype(F32)
        .astype(BF16)
    )
    return high, jnp.concatenate([hot, hot], axis=0)


def pick_kernel(cell_ref, request_ref, first_ref, *refs):
    *kept_refs, out_ref = refs
    species, cells = cell_ref.shape
    owners, cap = request_ref.shape[2:]
    groups = LANES // cap
    chunks = owners // (2 * groups)
    highs = cells // LANES
    here = lax.axis_index("grid")
    relative = lane_groups(cap, here)
    cell = cell_ref[...]
    stacked = jnp.concatenate(
        [cell[:, LANES * h : LANES * (h + 1)] for h in range(highs)], axis=0
    )
    left = jnp.concatenate(rounded(stacked), axis=1).astype(BF16)

    def chunk(k, carry):
        first = k * 2 * groups
        if kept_refs:
            high, right = kept_refs[0][...], kept_refs[1][...]
        else:
            high, right = pick_index(request_ref, k)
        product = jnp.dot(left, right, preferred_element_type=F32)
        picked = jnp.zeros((species, 2 * LANES), F32)
        high = jnp.concatenate([high] * (species // ROWS), axis=0)
        for h in range(highs):
            picked = picked + jnp.where(high == h, product[species * h : species * (h + 1)], 0.0)
        blank = jnp.zeros((groups * ROWS - species, 2 * LANES), F32)
        picked = jnp.concatenate([picked, blank], axis=0)
        for half in range(2):
            tiles = pack(
                [
                    picked[ROWS * g : ROWS * (g + 1), LANES * half : LANES * (half + 1)]
                    for g in range(groups)
                ],
                cap,
                here,
                relative,
            )
            for j in range(groups):
                out_ref[first + half * groups + j] = tiles[j]
        return carry

    repeat_steps(chunks, chunk, 0)


def to_segments(values, width):
    groups = LANES // width
    stacked = [value.astype(F32) for value in values]
    stacked.append(jnp.zeros((LANES - width * len(values), LANES), F32))
    turned = jnp.transpose(jnp.concatenate(stacked, axis=0))
    times = LANES // groups
    return exchange_groups([turned[times * g : times * (g + 1)] for g in range(groups)], width)


def lines_kernel(
    lines,
    cap,
    table_ref,
    slot_ref,
    length_ref,
    courant_ref,
    flux_ref,
    inflow_ref,
    interaction_ref,
    out_ref,
    rows_ref,
):
    owners = table_ref.shape[0]
    copies = out_ref.shape[0] // owners
    species = inflow_ref.shape[1]
    width = slot_ref.shape[0]
    nodes = width * LANES // lines
    groups = species // ROWS
    all_groups = LANES // cap
    rows = all_groups * ROWS
    blocks = nodes // LANES
    segments = LANES // width
    times = LANES // segments
    chunk_owners = 2 * all_groups
    chunks = owners // chunk_owners
    here, bundle = lax.axis_index("grid"), bundle_place()

    slot = slot_ref[...]
    within = (slot + lax.rem(here, all_groups) * cap) % LANES
    slot, courant, flux = to_segments(
        [slot - slot % LANES + within, courant_ref[...], flux_ref[...]], width
    )[:3]
    scale = 1.0 / (1.0 + courant)
    rows_ref[0] = scale
    rows_ref[1] = courant * scale
    rows_ref[2] = flux
    rows_ref[3] = slot

    def row(kind, t, depth=ROWS):
        return jnp.broadcast_to(rows_ref[kind, t : t + 1], (depth, LANES))

    def hot(k):
        index = lax.broadcasted_iota(jnp.int32, (2 * LANES, LANES), 0).astype(F32).astype(BF16)
        one, zero = jnp.ones_like(index), jnp.zeros_like(index)
        base = lax.convert_element_type(k * 2 * LANES, F32)
        columns = []
        for t in range(times):
            local = (row(3, t, 2 * ROWS) - base).astype(BF16)
            local = jnp.concatenate([local] * (LANES // ROWS), axis=0)
            columns.append(jnp.where(local == index, one, zero))
        return jnp.concatenate(columns, axis=1)

    kept = hot(0) if chunks == 1 else None

    relative = lane_groups(cap, here)

    def gather(k, state):
        halves = []
        for half in range(2):
            first = k * chunk_owners + half * all_groups
            halves.append(
                jnp.concatenate(
                    unpack(
                        [table_ref[first + j] for j in range(all_groups)], cap, relative, groups
                    ),
                    axis=0,
                )
            )
        left = split(jnp.concatenate(halves, axis=1))
        found = jnp.dot(left, hot(k) if kept is None else kept, preferred_element_type=F32)
        found = found[:species] + found[species:]
        return found if chunks == 1 else state + found

    start = repeat_steps(
        chunks, gather, jnp.zeros((species, lines * nodes), F32) if chunks > 1 else 0
    )

    lane = lax.broadcasted_iota(jnp.int32, (ROWS, LANES), 1)
    part = lane // width
    block = (lane % width) // lines
    segment = block * segments + part
    line = lane % lines

    def earlier(value, distance):
        major, minor = distance // segments, distance % segments
        near = pltpu.roll(value, minor * width + major * lines, 1)
        if minor == 0:
            return near
        far = pltpu.roll(value, minor * width + (major + 1) * lines, 1)
        return jnp.where(part >= minor, near, far)

    eye = lax.broadcasted_iota(jnp.int32, (species, LANES), 0) == lax.broadcasted_iota(
        jnp.int32, (species, LANES), 1
    )
    padded = jnp.concatenate([inflow_ref[...], jnp.zeros((1, LANES - species), F32)], axis=1)
    column = jnp.sum(jnp.where(eye, padded, 0.0), axis=1, keepdims=True)
    entry = jnp.broadcast_to(column, (species, LANES))
    entry = [entry[ROWS * g : ROWS * (g + 1)] for g in range(groups)]

    first = [None] * groups
    second = [None] * groups
    local, ones, twos = [], [], []
    for t in range(times):
        scale_t, decay_t = row(0, t), row(1, t)
        one = decay_t if t == 0 else decay_t * ones[-1]
        two = scale_t * one if t == 0 else scale_t * one + decay_t * twos[-1]
        ones.append(one)
        twos.append(two)
        for g in range(groups):
            value = start[ROWS * g : ROWS * (g + 1), LANES * t : LANES * (t + 1)] * scale_t
            first[g] = value if t == 0 else value + decay_t * first[g]
            value = scale_t * first[g]
            second[g] = value if t == 0 else value + decay_t * second[g]
            local.append(second[g])

    a, b = ones[-1], twos[-1]
    head = segment == 0
    first = [jnp.where(head, f + a * e, f) for f, e in zip(first, entry)]
    second = [jnp.where(head, s + b * e + a * e, s) for s, e in zip(second, entry)]
    distance = 1
    while distance < blocks * segments:
        run_a, run_b = a, b
        next_first, next_second = first, second
        for k in range(1, 4):
            if k * distance >= blocks * segments:
                break
            opened = segment >= k * distance
            a_open, b_open = jnp.where(opened, run_a, 0.0), jnp.where(opened, run_b, 0.0)
            ahead = [earlier(f, k * distance) for f in first]
            next_first = [n + a_open * f for n, f in zip(next_first, ahead)]
            next_second = [
                n + b_open * f + a_open * earlier(s, k * distance)
                for n, s, f in zip(next_second, second, ahead)
            ]
            a_ahead = earlier(a, k * distance)
            run_b = run_b * a_ahead + run_a * earlier(b, k * distance)
            run_a = run_a * a_ahead
        first, second = next_first, next_second
        a, b = run_a, run_b
        distance *= 4
    carry_one = [jnp.where(head, e, earlier(f, 1)) for e, f in zip(entry, first)]
    carry_two = [jnp.where(head, e, earlier(s, 1)) for e, s in zip(entry, second)]
    columns = [
        jnp.concatenate(
            [
                local[t * groups + g] + twos[t] * carry_one[g] + ones[t] * carry_two[g]
                for g in range(groups)
            ],
            axis=0,
        )
        for t in range(times)
    ]

    matrix_high, matrix_low = rounded(interaction_ref[...])
    blank = jnp.zeros_like(matrix_high)
    left = jnp.concatenate(
        [
            jnp.concatenate(
                [matrix_high, blank, matrix_low, blank, matrix_high, blank], axis=1
            ),
            jnp.concatenate(
                [blank, matrix_high, blank, matrix_low, blank, matrix_high], axis=1
            ),
        ],
        axis=0,
    ).astype(BF16)
    half = times // 2
    depth = half // CHUNKS
    bases = [
        jnp.concatenate(
            [
                jnp.concatenate(columns[offset + c * depth : offset + (c + 1) * depth], axis=1)
                for offset in (0, half)
            ],
            axis=0,
        )
        for c in range(CHUNKS)
    ]
    iterates = list(bases)
    for step in range(NEWTON):
        for c in range(CHUNKS):
            high, low = parts(jnp.tanh(iterates[c]))
            right = jnp.concatenate([high, high, low], axis=0)
            iterates[c] = bases[c] - jnp.dot(left, right, preferred_element_type=F32)

    length = jnp.zeros((ROWS, LANES), jnp.int32)
    for one_line in range(lines):
        one_length = jnp.broadcast_to(length_ref[:, one_line : one_line + 1], (ROWS, LANES))
        length = jnp.where(line == one_line, one_length, length)
    node = block * LANES + part * times
    top = lax.broadcasted_iota(jnp.int32, (ROWS, LANES), 0) == 0
    pieces = []
    for t in range(times):
        weight = jnp.where(node + t < length, row(2, t), 0.0)
        chunk, place = t % half // depth, t % half % depth
        found = iterates[chunk][
            t // half * species : (t // half + 1) * species, LANES * place : LANES * (place + 1)
        ]
        scaled = [found[ROWS * g : ROWS * (g + 1)] * weight for g in range(groups)]
        scaled.append(jnp.where(top, weight, 0.0))
        pieces.append(jnp.concatenate(scaled, axis=0))
    left = split(jnp.concatenate(pieces, axis=1))
    relative = lane_groups(cap, here + bundle)

    def scatter(k, carry):
        sums = lax.dot_general(
            left,
            hot(k) if kept is None else kept,
            (((1,), (1,)), ((), ())),
            preferred_element_type=F32,
        )
        sums = sums[:rows] + sums[rows:]
        for half in range(2):
            tiles = pack(
                [
                    sums[ROWS * g : ROWS * (g + 1), LANES * half : LANES * (half + 1)]
                    for g in range(all_groups)
                ],
                cap,
                bundle,
                relative,
            )
            for j in range(all_groups):
                owner = k * chunk_owners + half * all_groups + j
                for copy in range(copies):
                    out_ref[turned_place(copy, copies) * owners + owner] = tiles[j]
        return carry

    repeat_steps(chunks, scatter, 0)


def blend_index(request_ref, k):
    bundles, cap = request_ref.shape[0], request_ref.shape[3]
    all_groups = LANES // cap
    width = 2 * LANES
    here = lax.axis_index("grid")
    sublane = lax.broadcasted_iota(jnp.int32, (ROWS, LANES), 0)
    indices = []
    for t in range(bundles // all_groups):
        straight = jnp.concatenate(
            [
                request_ref[
                    t * all_groups
                    + lax.rem(x + all_groups - lax.rem(here, all_groups), all_groups),
                    0,
                    pl.ds(k * ROWS, ROWS),
                    :,
                ]
                for x in range(all_groups)
            ],
            axis=1,
        )
        block = straight
        for turn in range(1, all_groups):
            block = jnp.where(
                sublane % all_groups == turn, pltpu.roll(straight, turn * cap, 1), block
            )
        indices += [block[d : d + 1] for d in range(ROWS)]
    index = jnp.concatenate(indices, axis=1)
    entries = index.shape[1]
    high = jnp.broadcast_to(index // width, (2 * ROWS, entries)).astype(F32).astype(BF16)
    low = jnp.broadcast_to(index % width, (2 * ROWS, entries)).astype(F32).astype(BF16)
    low = jnp.concatenate([low] * (width // (2 * ROWS)), axis=0)
    place = lax.broadcasted_iota(jnp.int32, (width, entries), 0).astype(F32).astype(BF16)
    return high, jnp.where(place == low, jnp.ones_like(place), jnp.zeros_like(place))


def index_kernel(
    request_ref, first_ref, length_ref, inflow_ref, pick_high, pick_hot, blend_high, blend_hot
):
    pick_high[...], pick_hot[...] = pick_index(request_ref, 0)
    blend_high[...], blend_hot[...] = blend_index(request_ref, 0)


def blend_kernel(bundles, sums_ref, request_ref, pore_ref, cell_ref, *refs):
    *kept_refs, out_hbm, out_ref, out_sem = refs
    owners = sums_ref.shape[0] // bundles
    species, cells = cell_ref.shape
    cap = request_ref.shape[3]
    all_groups = LANES // cap
    groups = species // ROWS
    width = 2 * LANES
    highs = cells // width
    chunks = owners // ROWS
    here = lax.axis_index("grid")

    def chunk(k, total):
        values, weights = [], []
        for t in range(bundles // all_groups):
            for d in range(ROWS):
                found = unpack(
                    [
                        sums_ref[turned_place(t * all_groups + j, bundles) * owners + k * ROWS + d]
                        for j in range(all_groups)
                    ],
                    cap,
                    lane_groups(cap, here + d),
                    all_groups,
                )
                weights.append(found[groups][:1])
                values.append(jnp.concatenate(found[:groups], axis=0))
        both = split(jnp.concatenate(values, axis=1))
        weight_high, weight_low = rounded(jnp.concatenate(weights, axis=1))
        if kept_refs:
            high, hot = kept_refs[0][...], kept_refs[1][...]
        else:
            high, hot = blend_index(request_ref, k)
        entries = hot.shape[1]
        zero = jnp.zeros((2 * ROWS, entries), BF16)
        pieces = []
        for first in range(0, highs, 2 * ROWS):
            mask = high == (
                lax.broadcasted_iota(jnp.int32, (2 * ROWS, entries), 0) + first
            ).astype(F32).astype(BF16)
            for part in (weight_high, weight_low):
                row = jnp.broadcast_to(part, (2 * ROWS, entries)).astype(BF16)
                pieces.append(jnp.where(mask, row, zero))
        for h in range(highs):
            mask = high == jnp.array(h, BF16)
            for r in range(2 * species // (2 * ROWS)):
                pieces.append(jnp.where(mask, both[2 * ROWS * r : 2 * ROWS * (r + 1)], zero))
        half = (len(pieces) + len(pieces) // 2 % 2) // 2
        products = [
            lax.dot_general(
                jnp.concatenate(some, axis=0),
                hot,
                (((1,), (1,)), ((), ())),
                preferred_element_type=F32,
            )
            for some in (pieces[:half], pieces[half:])
        ]
        product = jnp.concatenate(products, axis=0)
        return product if chunks == 1 else total + product

    flux_rows = -(-highs // (2 * ROWS)) * 4 * ROWS
    total = repeat_steps(
        chunks,
        chunk,
        jnp.zeros((highs * 2 * species + flux_rows, width), F32) if chunks > 1 else 0,
    )
    flux, total = total[:flux_rows], total[flux_rows:]
    copies = []
    stride = max(highs // 4, 1)
    for h in range(highs):
        part = total[2 * species * h : 2 * species * (h + 1)]
        part = part[:species] + part[species:]
        row = h // (2 * ROWS) * 4 * ROWS + h % (2 * ROWS)
        pore = pore_ref[:, width * h : width * (h + 1)]
        inverse = 1.0 / (pore + flux[row : row + 1] + flux[row + 2 * ROWS : row + 2 * ROWS + 1])
        columns = pl.ds(width * h, width)
        out_ref[:, columns] = (pore * cell_ref[:, columns] + part) * inverse
        if h % stride == stride - 1:
            columns = pl.ds(width * (h - stride + 1), stride * width)
            copies.append(
                pltpu.make_async_copy(
                    out_ref.at[:, columns], out_hbm.at[:, columns], out_sem.at[h // stride]
                )
            )
            copies[-1].start()
    for copy in copies:
        copy.wait()


def call(kernel, shapes, operands, kinds={}, scratch=(), out=pltpu.VMEM, flops=0):
    return pl.pallas_call(
        kernel,
        out_shape=[jax.ShapeDtypeStruct(shape, kind) for shape, kind in shapes],
        in_specs=[
            pl.BlockSpec(memory_space=kinds.get(i, pltpu.VMEM)) for i in range(len(operands))
        ],
        out_specs=[pl.BlockSpec(memory_space=out)] * len(shapes),
        scratch_shapes=list(scratch),
        compiler_params=pltpu.CompilerParams(vmem_limit_bytes=VMEM_BYTES),
        cost_estimate=pl.CostEstimate(flops=flops, bytes_accessed=0, transcendentals=0),
    )(*operands)


def bundle_place():
    return lax.axis_index("far") * lax.axis_size("near") + lax.axis_index("near")


def shards(
    bundles,
    cell_state,
    pore_volume,
    request_cell,
    node_slot,
    line_length,
    courant,
    flux_weight,
    inflow,
    interaction,
):
    owners, cap = request_cell.shape[2:]
    first = call(first_kernel, [((ROWS, LANES), F32)], (), flops=10**9)[0]
    indices = []
    if owners == ROWS and owners * cap == 2 * LANES:
        entries = owners * bundles * cap
        indices = call(
            index_kernel,
            [
                ((ROWS, 2 * LANES), jnp.int32),
                ((2 * LANES, 2 * LANES), BF16),
                ((2 * ROWS, entries), BF16),
                ((2 * LANES, entries), BF16),
            ],
            (request_cell, first, line_length, inflow),
        )
    outgoing = call(
        pick_kernel,
        [((owners, ROWS, LANES), F32)],
        (cell_state, request_cell, first, *indices[:2]),
    )[0]
    table = lax.all_to_all(outgoing, "grid", split_axis=0, concat_axis=0, tiled=True)
    lines, nodes = node_slot.shape[1:]
    blocks = nodes // LANES

    def by_block(value):
        return value.reshape(lines, blocks, LANES).swapaxes(0, 1).reshape(blocks * lines, LANES)

    sums = call(
        functools.partial(lines_kernel, lines, cap),
        [((owners * bundles, ROWS, LANES), F32)],
        (
            table,
            by_block(node_slot),
            line_length,
            by_block(courant),
            by_block(flux_weight),
            inflow,
            interaction,
        ),
        scratch=(pltpu.VMEM((4, lines * blocks, LANES), F32),),
    )[0]
    back = lax.all_to_all(sums, ("near", "far", "grid"), split_axis=0, concat_axis=0, tiled=True)
    return call(
        functools.partial(blend_kernel, bundles),
        [(cell_state.shape, F32)],
        (back, request_cell, pore_volume[None, :], cell_state, *indices[2:]),
        scratch=(pltpu.VMEM(cell_state.shape, F32), pltpu.SemaphoreType.DMA((4,))),
        out=pltpu.HBM,
    )[0]


def solution(mesh):
    bundles = mesh.shape["bundle"]
    near = near_size(bundles)
    devices = mesh.devices.reshape(mesh.shape["grid"], bundles // near, near)
    finer = jax.sharding.Mesh(devices, ("grid", "far", "near"))
    bundle = ("far", "near")
    placed = (
        P(None, "grid"),
        P("grid"),
        P(None, "grid", None, None),
        P(bundle, "grid", None),
        P(bundle, "grid"),
        P(bundle, "grid", None),
        P(bundle, "grid", None),
        P(bundle, None),
        P(),
    )
    return jax.shard_map(
        functools.partial(shards, bundles),
        mesh=finer,
        in_specs=placed,
        out_specs=P(None, "grid"),
        check_vma=False,
    )
```

```python
import functools

import jax
import jax.numpy as jnp
from jax import lax
from jax.experimental import pallas as pl
from jax.experimental.pallas import tpu as pltpu
from jax.sharding import PartitionSpec as P

SUB = 2
NEWTON = 3
LANES = 128
ROWS = 8
F32 = jnp.float32
BF16 = jnp.bfloat16
VMEM_BYTES = 32 * 1024 * 1024
CHUNKS = 4


def repeat_steps(count, body, carry):
    if count == 1:
        return body(0, carry)
    return lax.fori_loop(0, count, body, carry)


def rounded(value):
    high = value.astype(BF16).astype(F32)
    return high, value - high


def parts(value):
    high = value.astype(BF16)
    return high, (value - high.astype(F32)).astype(BF16)


def split(value):
    return jnp.concatenate(rounded(value), axis=0).astype(BF16)


def select_groups(tiles, relative):
    count = len(tiles)
    results = []
    for i in range(count):
        value = tiles[0]
        for j in range(1, count):
            value = jnp.where(relative == (i + j) % count, tiles[j], value)
        results.append(value)
    return results


def lane_groups(cap, turn):
    groups = LANES // cap
    lane = lax.broadcasted_iota(jnp.int32, (ROWS, LANES), 1)
    return (lane // cap + (2 * groups - lax.rem(turn, groups))) % groups


def pack(rows, cap, turn, relative):
    groups = LANES // cap
    turned = [
        pltpu.roll(rows[g], lax.rem(turn + g, groups) * cap, 1) for g in range(groups)
    ]
    return select_groups(turned, relative)


def unpack(tiles, cap, relative, count):
    found = select_groups(tiles, relative)[:count]
    return [
        found[g] if g == 0 else pltpu.roll(found[g], LANES - g * cap, 1) for g in range(count)
    ]


def exchange_groups(tiles, width):
    tiles = list(tiles)
    lane_group = lax.broadcasted_iota(jnp.int32, tiles[0].shape, 1) // width
    step = 1
    while step < len(tiles):
        keep = (lane_group & step) == 0
        for i in range(len(tiles)):
            if i & step == 0:
                first, second = tiles[i], tiles[i | step]
                tiles[i] = jnp.where(keep, first, pltpu.roll(second, step * width, 1))
                tiles[i | step] = jnp.where(
                    keep, pltpu.roll(first, LANES - step * width, 1), second
                )
        step *= 2
    return tiles


def spread_rows(block, cap):
    groups = block.shape[0]
    wide = jnp.concatenate([block] * groups, axis=1)
    rows = lax.broadcasted_iota(jnp.int32, wide.shape, 0)
    lanes = lax.broadcasted_iota(jnp.int32, wide.shape, 1) // cap
    return jnp.sum(jnp.where(rows == lanes, wide, 0), axis=0, keepdims=True)


def first_kernel(out_ref):
    out_ref[...] = jnp.zeros_like(out_ref)


def pick_index(request_ref, k):
    bundle = lax.axis_index("bundle")
    groups = LANES // request_ref.shape[3]
    cap = request_ref.shape[3]
    block = request_ref[bundle, 0, pl.ds(k * 2 * groups, 2 * groups), :]
    index = jnp.concatenate(
        [spread_rows(block[:groups], cap), spread_rows(block[groups:], cap)], axis=1
    )
    high = jnp.broadcast_to(index // LANES, (ROWS, 2 * LANES))
    hot = (
        (lax.broadcasted_iota(jnp.int32, (LANES, 2 * LANES), 0) == index % LANES)
        .astype(F32)
        .astype(BF16)
    )
    return high, jnp.concatenate([hot, hot], axis=0)


def pick_kernel(cell_ref, request_ref, first_ref, *refs):
    *kept_refs, out_ref = refs
    species, cells = cell_ref.shape
    owners, cap = request_ref.shape[2:]
    groups = LANES // cap
    chunks = owners // (2 * groups)
    highs = cells // LANES
    here = lax.axis_index("grid")
    relative = lane_groups(cap, here)
    cell = cell_ref[...]
    stacked = jnp.concatenate(
        [cell[:, LANES * h : LANES * (h + 1)] for h in range(highs)], axis=0
    )
    left = jnp.concatenate(rounded(stacked), axis=1).astype(BF16)

    def chunk(k, carry):
        first = k * 2 * groups
        if kept_refs:
            high, right = kept_refs[0][...], kept_refs[1][...]
        else:
            high, right = pick_index(request_ref, k)
        product = jnp.dot(left, right, preferred_element_type=F32)
        picked = jnp.zeros((species, 2 * LANES), F32)
        high = jnp.concatenate([high] * (species // ROWS), axis=0)
        for h in range(highs):
            picked = picked + jnp.where(high == h, product[species * h : species * (h + 1)], 0.0)
        blank = jnp.zeros((groups * ROWS - species, 2 * LANES), F32)
        picked = jnp.concatenate([picked, blank], axis=0)
        for half in range(2):
            tiles = pack(
                [
                    picked[ROWS * g : ROWS * (g + 1), LANES * half : LANES * (half + 1)]
                    for g in range(groups)
                ],
                cap,
                here,
                relative,
            )
            for j in range(groups):
                out_ref[first + half * groups + j] = tiles[j]
        return carry

    repeat_steps(chunks, chunk, 0)


def to_segments(values, width):
    groups = LANES // width
    stacked = [value.astype(F32) for value in values]
    stacked.append(jnp.zeros((LANES - width * len(values), LANES), F32))
    turned = jnp.transpose(jnp.concatenate(stacked, axis=0))
    times = LANES // groups
    return exchange_groups([turned[times * g : times * (g + 1)] for g in range(groups)], width)


def lines_kernel(
    lines,
    cap,
    table_ref,
    slot_ref,
    length_ref,
    courant_ref,
    flux_ref,
    inflow_ref,
    interaction_ref,
    out_ref,
    rows_ref,
):
    owners = table_ref.shape[0]
    copies = out_ref.shape[0] // owners
    species = inflow_ref.shape[1]
    width = slot_ref.shape[0]
    nodes = width * LANES // lines
    groups = species // ROWS
    all_groups = LANES // cap
    rows = all_groups * ROWS
    blocks = nodes // LANES
    segments = LANES // width
    times = LANES // segments
    chunk_owners = 2 * all_groups
    chunks = owners // chunk_owners
    here, bundle = lax.axis_index("grid"), lax.axis_index("bundle")
    half = times // 2
    depth = half // CHUNKS
    units = 2 * CHUNKS

    slot = slot_ref[...]
    within = (slot + lax.rem(here, all_groups) * cap) % LANES
    slot, courant, flux = to_segments(
        [slot - slot % LANES + within, courant_ref[...], flux_ref[...]], width
    )[:3]
    scale = 1.0 / (1.0 + courant)
    rows_ref[0] = scale
    rows_ref[1] = courant * scale
    rows_ref[2] = flux
    rows_ref[3] = slot

    def row(kind, t, depth=ROWS):
        return jnp.broadcast_to(rows_ref[kind, t : t + 1], (depth, LANES))

    def hot(k):
        index = lax.broadcasted_iota(jnp.int32, (2 * LANES, LANES), 0).astype(F32).astype(BF16)
        one, zero = jnp.ones_like(index), jnp.zeros_like(index)
        base = lax.convert_element_type(k * 2 * LANES, F32)
        columns = []
        for t in range(times):
            local = (row(3, t, 2 * ROWS) - base).astype(BF16)
            local = jnp.concatenate([local] * (LANES // ROWS), axis=0)
            columns.append(jnp.where(local == index, one, zero))
        return [
            jnp.concatenate(columns[t : t + depth], axis=1) for t in range(0, times, depth)
        ]

    kept = hot(0) if chunks == 1 else None

    relative = lane_groups(cap, here)

    def gather(k, state):
        halves = []
        for half in range(2):
            first = k * chunk_owners + half * all_groups
            halves.append(
                jnp.concatenate(
                    unpack(
                        [table_ref[first + j] for j in range(all_groups)], cap, relative, groups
                    ),
                    axis=0,
                )
            )
        left = split(jnp.concatenate(halves, axis=1))
        if kept is not None:
            return left
        found = [jnp.dot(left, columns, preferred_element_type=F32) for columns in hot(k)]
        return [s + f[:species] + f[species:] for s, f in zip(state, found)]

    start = repeat_steps(
        chunks,
        gather,
        [jnp.zeros((species, depth * LANES), F32)] * units if chunks > 1 else 0,
    )

    def started(unit):
        if kept is None:
            return start[unit]
        found = jnp.dot(start, kept[unit], preferred_element_type=F32)
        return found[:species] + found[species:]

    lane = lax.broadcasted_iota(jnp.int32, (ROWS, LANES), 1)
    part = lane // width
    block = (lane % width) // lines
    segment = block * segments + part
    line = lane % lines

    def earlier(value, distance):
        major, minor = distance // segments, distance % segments
        near = pltpu.roll(value, minor * width + major * lines, 1)
        if minor == 0:
            return near
        far = pltpu.roll(value, minor * width + (major + 1) * lines, 1)
        return jnp.where(part >= minor, near, far)

    eye = lax.broadcasted_iota(jnp.int32, (species, LANES), 0) == lax.broadcasted_iota(
        jnp.int32, (species, LANES), 1
    )
    padded = jnp.concatenate([inflow_ref[...], jnp.zeros((1, LANES - species), F32)], axis=1)
    column = jnp.sum(jnp.where(eye, padded, 0.0), axis=1, keepdims=True)
    entry = jnp.broadcast_to(column, (species, LANES))
    entry = [entry[ROWS * g : ROWS * (g + 1)] for g in range(groups)]

    first = [None] * groups
    second = [None] * groups
    local, ones, twos = [], [], []
    ahead_unit = started(0)
    for t in range(times):
        if t % depth == 0:
            unit = ahead_unit
            ahead_unit = started(t // depth + 1) if t // depth + 1 < units else None
        scale_t, decay_t = row(0, t), row(1, t)
        one = decay_t if t == 0 else decay_t * ones[-1]
        two = scale_t * one if t == 0 else scale_t * one + decay_t * twos[-1]
        ones.append(one)
        twos.append(two)
        for g in range(groups):
            lanes = slice(LANES * (t % depth), LANES * (t % depth + 1))
            value = unit[ROWS * g : ROWS * (g + 1), lanes] * scale_t
            first[g] = value if t == 0 else value + decay_t * first[g]
            value = scale_t * first[g]
            second[g] = value if t == 0 else value + decay_t * second[g]
            local.append(second[g])

    a, b = ones[-1], twos[-1]
    head = segment == 0
    first = [jnp.where(head, f + a * e, f) for f, e in zip(first, entry)]
    second = [jnp.where(head, s + b * e + a * e, s) for s, e in zip(second, entry)]
    distance = 1
    while distance < blocks * segments:
        run_a, run_b = a, b
        next_first, next_second = first, second
        for k in range(1, 4):
            if k * distance >= blocks * segments:
                break
            opened = segment >= k * distance
            a_open, b_open = jnp.where(opened, run_a, 0.0), jnp.where(opened, run_b, 0.0)
            ahead = [earlier(f, k * distance) for f in first]
            next_first = [n + a_open * f for n, f in zip(next_first, ahead)]
            next_second = [
                n + b_open * f + a_open * earlier(s, k * distance)
                for n, s, f in zip(next_second, second, ahead)
            ]
            a_ahead = earlier(a, k * distance)
            run_b = run_b * a_ahead + run_a * earlier(b, k * distance)
            run_a = run_a * a_ahead
        first, second = next_first, next_second
        a, b = run_a, run_b
        distance *= 4
    carry_one = [jnp.where(head, e, earlier(f, 1)) for e, f in zip(entry, first)]
    carry_two = [jnp.where(head, e, earlier(s, 1)) for e, s in zip(entry, second)]
    columns = [
        jnp.concatenate(
            [
                local[t * groups + g] + twos[t] * carry_one[g] + ones[t] * carry_two[g]
                for g in range(groups)
            ],
            axis=0,
        )
        for t in range(times)
    ]

    matrix_high, matrix_low = rounded(interaction_ref[...])
    blank = jnp.zeros_like(matrix_high)
    left = jnp.concatenate(
        [
            jnp.concatenate(
                [matrix_high, blank, matrix_low, blank, matrix_high, blank], axis=1
            ),
            jnp.concatenate(
                [blank, matrix_high, blank, matrix_low, blank, matrix_high], axis=1
            ),
        ],
        axis=0,
    ).astype(BF16)
    bases = [
        jnp.concatenate(
            [
                jnp.concatenate(columns[offset + c * depth : offset + (c + 1) * depth], axis=1)
                for offset in (0, half)
            ],
            axis=0,
        )
        for c in range(CHUNKS)
    ]
    length = jnp.zeros((ROWS, LANES), jnp.int32)
    for one_line in range(lines):
        one_length = jnp.broadcast_to(length_ref[:, one_line : one_line + 1], (ROWS, LANES))
        length = jnp.where(line == one_line, one_length, length)
    node = block * LANES + part * times
    top = lax.broadcasted_iota(jnp.int32, (ROWS, LANES), 0) == 0

    def weighted(found, c):
        pieces = []
        for side in range(2):
            for place in range(depth):
                t = side * half + c * depth + place
                weight = jnp.where(node + t < length, row(2, t), 0.0)
                columns = slice(LANES * place, LANES * (place + 1))
                scaled = [
                    found[side * species + ROWS * g : side * species + ROWS * (g + 1), columns]
                    * weight
                    for g in range(groups)
                ]
                scaled.append(jnp.where(top, weight, 0.0))
                pieces.append(jnp.concatenate(scaled, axis=0))
        return split(jnp.concatenate(pieces, axis=1))

    def slot_sums(value, columns, c):
        return lax.dot_general(
            value,
            jnp.concatenate([columns[c], columns[CHUNKS + c]], axis=1),
            (((1,), (1,)), ((), ())),
            preferred_element_type=F32,
        )

    iterates = list(bases)
    lefts = []
    kept_sums = None
    for step in range(NEWTON):
        for c in range(CHUNKS):
            high, low = parts(jnp.tanh(iterates[c]))
            right = jnp.concatenate([high, high, low], axis=0)
            iterates[c] = bases[c] - jnp.dot(left, right, preferred_element_type=F32)
            if step == NEWTON - 1:
                lefts.append(weighted(iterates[c], c))
                if kept is not None:
                    found = slot_sums(lefts[c], kept, c)
                    kept_sums = found if c == 0 else kept_sums + found

    relative = lane_groups(cap, here + bundle)

    def scatter(k, carry):
        if kept is None:
            columns = hot(k)
            sums = sum(slot_sums(lefts[c], columns, c) for c in range(CHUNKS))
        else:
            sums = kept_sums
        sums = sums[:rows] + sums[rows:]
        for half in range(2):
            tiles = pack(
                [
                    sums[ROWS * g : ROWS * (g + 1), LANES * half : LANES * (half + 1)]
                    for g in range(all_groups)
                ],
                cap,
                bundle,
                relative,
            )
            for j in range(all_groups):
                owner = k * chunk_owners + half * all_groups + j
                for copy in range(copies):
                    out_ref[copy * owners + owner] = tiles[j]
        return carry

    repeat_steps(chunks, scatter, 0)


def blend_index(request_ref, k):
    bundles, cap = request_ref.shape[0], request_ref.shape[3]
    all_groups = LANES // cap
    width = 2 * LANES
    here = lax.axis_index("grid")
    sublane = lax.broadcasted_iota(jnp.int32, (ROWS, LANES), 0)
    indices = []
    for t in range(bundles // all_groups):
        straight = jnp.concatenate(
            [
                request_ref[
                    t * all_groups
                    + lax.rem(x + all_groups - lax.rem(here, all_groups), all_groups),
                    0,
                    pl.ds(k * ROWS, ROWS),
                    :,
                ]
                for x in range(all_groups)
            ],
            axis=1,
        )
        block = straight
        for turn in range(1, all_groups):
            block = jnp.where(
                sublane % all_groups == turn, pltpu.roll(straight, turn * cap, 1), block
            )
        indices += [block[d : d + 1] for d in range(ROWS)]
    index = jnp.concatenate(indices, axis=1)
    entries = index.shape[1]
    high = jnp.broadcast_to(index // width, (2 * ROWS, entries)).astype(F32).astype(BF16)
    low = jnp.broadcast_to(index % width, (2 * ROWS, entries)).astype(F32).astype(BF16)
    low = jnp.concatenate([low] * (width // (2 * ROWS)), axis=0)
    place = lax.broadcasted_iota(jnp.int32, (width, entries), 0).astype(F32).astype(BF16)
    return high, jnp.where(place == low, jnp.ones_like(place), jnp.zeros_like(place))


def index_kernel(
    request_ref, first_ref, length_ref, inflow_ref, pick_high, pick_hot, blend_high, blend_hot
):
    pick_high[...], pick_hot[...] = pick_index(request_ref, 0)
    blend_high[...], blend_hot[...] = blend_index(request_ref, 0)


def blend_kernel(bundles, sums_ref, request_ref, pore_ref, cell_ref, *refs):
    *kept_refs, out_hbm, out_ref, out_sem = refs
    owners = sums_ref.shape[0] // bundles
    species, cells = cell_ref.shape
    cap = request_ref.shape[3]
    all_groups = LANES // cap
    groups = species // ROWS
    width = 2 * LANES
    highs = cells // width
    chunks = owners // ROWS
    here = lax.axis_index("grid")

    def chunk(k, total):
        values, weights = [], []
        for t in range(bundles // all_groups):
            for d in range(ROWS):
                found = unpack(
                    [
                        sums_ref[(t * all_groups + j) * owners + k * ROWS + d]
                        for j in range(all_groups)
                    ],
                    cap,
                    lane_groups(cap, here + d),
                    all_groups,
                )
                weights.append(found[groups][:1])
                values.append(jnp.concatenate(found[:groups], axis=0))
        both = split(jnp.concatenate(values, axis=1))
        weight_high, weight_low = rounded(jnp.concatenate(weights, axis=1))
        if kept_refs:
            high, hot = kept_refs[0][...], kept_refs[1][...]
        else:
            high, hot = blend_index(request_ref, k)
        entries = hot.shape[1]
        zero = jnp.zeros((2 * ROWS, entries), BF16)
        pieces = []
        for first in range(0, highs, 2 * ROWS):
            mask = high == (
                lax.broadcasted_iota(jnp.int32, (2 * ROWS, entries), 0) + first
            ).astype(F32).astype(BF16)
            for part in (weight_high, weight_low):
                row = jnp.broadcast_to(part, (2 * ROWS, entries)).astype(BF16)
                pieces.append(jnp.where(mask, row, zero))
        for h in range(highs):
            mask = high == jnp.array(h, BF16)
            for r in range(2 * species // (2 * ROWS)):
                pieces.append(jnp.where(mask, both[2 * ROWS * r : 2 * ROWS * (r + 1)], zero))
        half = (len(pieces) + len(pieces) // 2 % 2) // 2
        products = [
            lax.dot_general(
                jnp.concatenate(some, axis=0),
                hot,
                (((1,), (1,)), ((), ())),
                preferred_element_type=F32,
            )
            for some in (pieces[:half], pieces[half:])
        ]
        product = jnp.concatenate(products, axis=0)
        return product if chunks == 1 else total + product

    flux_rows = -(-highs // (2 * ROWS)) * 4 * ROWS
    total = repeat_steps(
        chunks,
        chunk,
        jnp.zeros((highs * 2 * species + flux_rows, width), F32) if chunks > 1 else 0,
    )
    flux, total = total[:flux_rows], total[flux_rows:]
    copies = []
    stride = max(highs // 4, 1)
    for h in range(highs):
        part = total[2 * species * h : 2 * species * (h + 1)]
        part = part[:species] + part[species:]
        row = h // (2 * ROWS) * 4 * ROWS + h % (2 * ROWS)
        pore = pore_ref[:, width * h : width * (h + 1)]
        inverse = 1.0 / (pore + flux[row : row + 1] + flux[row + 2 * ROWS : row + 2 * ROWS + 1])
        columns = pl.ds(width * h, width)
        out_ref[:, columns] = (pore * cell_ref[:, columns] + part) * inverse
        if h % stride == stride - 1:
            columns = pl.ds(width * (h - stride + 1), stride * width)
            copies.append(
                pltpu.make_async_copy(
                    out_ref.at[:, columns], out_hbm.at[:, columns], out_sem.at[h // stride]
                )
            )
            copies[-1].start()
    for copy in copies:
        copy.wait()


def call(kernel, shapes, operands, kinds={}, scratch=(), out=pltpu.VMEM, flops=0):
    return pl.pallas_call(
        kernel,
        out_shape=[jax.ShapeDtypeStruct(shape, kind) for shape, kind in shapes],
        in_specs=[
            pl.BlockSpec(memory_space=kinds.get(i, pltpu.VMEM)) for i in range(len(operands))
        ],
        out_specs=[pl.BlockSpec(memory_space=out)] * len(shapes),
        scratch_shapes=list(scratch),
        compiler_params=pltpu.CompilerParams(vmem_limit_bytes=VMEM_BYTES),
        cost_estimate=pl.CostEstimate(flops=flops, bytes_accessed=0, transcendentals=0),
    )(*operands)


def shards(
    bundles,
    cell_state,
    pore_volume,
    request_cell,
    node_slot,
    line_length,
    courant,
    flux_weight,
    inflow,
    interaction,
):
    owners, cap = request_cell.shape[2:]
    first = call(first_kernel, [((ROWS, LANES), F32)], (), flops=10**9)[0]
    indices = []
    if owners == ROWS and owners * cap == 2 * LANES:
        entries = owners * bundles * cap
        indices = call(
            index_kernel,
            [
                ((ROWS, 2 * LANES), jnp.int32),
                ((2 * LANES, 2 * LANES), BF16),
                ((2 * ROWS, entries), BF16),
                ((2 * LANES, entries), BF16),
            ],
            (request_cell, first, line_length, inflow),
        )
    outgoing = call(
        pick_kernel,
        [((owners, ROWS, LANES), F32)],
        (cell_state, request_cell, first, *indices[:2]),
    )[0]
    table = lax.all_to_all(outgoing, "grid", split_axis=0, concat_axis=0, tiled=True)
    lines, nodes = node_slot.shape[1:]
    blocks = nodes // LANES

    def by_block(value):
        return value.reshape(lines, blocks, LANES).swapaxes(0, 1).reshape(blocks * lines, LANES)

    sums = call(
        functools.partial(lines_kernel, lines, cap),
        [((owners * bundles, ROWS, LANES), F32)],
        (
            table,
            by_block(node_slot),
            line_length,
            by_block(courant),
            by_block(flux_weight),
            inflow,
            interaction,
        ),
        scratch=(pltpu.VMEM((4, lines * blocks, LANES), F32),),
    )[0]
    back = lax.all_to_all(sums, ("bundle", "grid"), split_axis=0, concat_axis=0, tiled=True)
    return call(
        functools.partial(blend_kernel, bundles),
        [(cell_state.shape, F32)],
        (back, request_cell, pore_volume[None, :], cell_state, *indices[2:]),
        scratch=(pltpu.VMEM(cell_state.shape, F32), pltpu.SemaphoreType.DMA((4,))),
        out=pltpu.HBM,
    )[0]


def solution(mesh):
    placed = (
        P(None, "grid"),
        P("grid"),
        P(None, "grid", None, None),
        P("bundle", "grid", None),
        P("bundle", "grid"),
        P("bundle", "grid", None),
        P("bundle", "grid", None),
        P("bundle", None),
        P(),
    )
    return jax.shard_map(
        functools.partial(shards, mesh.shape["bundle"]),
        mesh=mesh,
        in_specs=placed,
        out_specs=P(None, "grid"),
        check_vma=False,
    )
```

```python
import functools

import jax
import jax.numpy as jnp
from jax import lax
from jax.experimental import pallas as pl
from jax.experimental.pallas import tpu as pltpu
from jax.sharding import PartitionSpec as P

SUB = 2
NEWTON = 3
LANES = 128
ROWS = 8
F32 = jnp.float32
BF16 = jnp.bfloat16
VMEM_BYTES = 32 * 1024 * 1024
CHUNKS = 1


def repeat_steps(count, body, carry):
    if count == 1:
        return body(0, carry)
    return lax.fori_loop(0, count, body, carry)


def rounded(value):
    high = value.astype(BF16).astype(F32)
    return high, value - high


def parts(value):
    high = value.astype(BF16)
    return high, (value - high.astype(F32)).astype(BF16)


def split(value):
    return jnp.concatenate(rounded(value), axis=0).astype(BF16)


def select_groups(tiles, relative):
    count = len(tiles)
    results = []
    for i in range(count):
        value = tiles[0]
        for j in range(1, count):
            value = jnp.where(relative == (i + j) % count, tiles[j], value)
        results.append(value)
    return results


def lane_groups(cap, turn):
    groups = LANES // cap
    lane = lax.broadcasted_iota(jnp.int32, (ROWS, LANES), 1)
    return (lane // cap + (2 * groups - lax.rem(turn, groups))) % groups


def pack(rows, cap, turn, relative):
    groups = LANES // cap
    turned = [
        pltpu.roll(rows[g], lax.rem(turn + g, groups) * cap, 1) for g in range(groups)
    ]
    return select_groups(turned, relative)


def unpack(tiles, cap, relative, count):
    found = select_groups(tiles, relative)[:count]
    return [
        found[g] if g == 0 else pltpu.roll(found[g], LANES - g * cap, 1) for g in range(count)
    ]


def exchange_groups(tiles, width):
    tiles = list(tiles)
    lane_group = lax.broadcasted_iota(jnp.int32, tiles[0].shape, 1) // width
    step = 1
    while step < len(tiles):
        keep = (lane_group & step) == 0
        for i in range(len(tiles)):
            if i & step == 0:
                first, second = tiles[i], tiles[i | step]
                tiles[i] = jnp.where(keep, first, pltpu.roll(second, step * width, 1))
                tiles[i | step] = jnp.where(
                    keep, pltpu.roll(first, LANES - step * width, 1), second
                )
        step *= 2
    return tiles


def spread_rows(block, cap):
    groups = block.shape[0]
    wide = jnp.concatenate([block] * groups, axis=1)
    rows = lax.broadcasted_iota(jnp.int32, wide.shape, 0)
    lanes = lax.broadcasted_iota(jnp.int32, wide.shape, 1) // cap
    return jnp.sum(jnp.where(rows == lanes, wide, 0), axis=0, keepdims=True)


def first_kernel(out_ref):
    out_ref[...] = jnp.zeros_like(out_ref)


def pick_index(request_ref, k):
    bundle = lax.axis_index("bundle")
    groups = LANES // request_ref.shape[3]
    cap = request_ref.shape[3]
    block = request_ref[bundle, 0, pl.ds(k * 2 * groups, 2 * groups), :]
    index = jnp.concatenate(
        [spread_rows(block[:groups], cap), spread_rows(block[groups:], cap)], axis=1
    )
    high = jnp.broadcast_to(index // LANES, (ROWS, 2 * LANES))
    hot = (
        (lax.broadcasted_iota(jnp.int32, (LANES, 2 * LANES), 0) == index % LANES)
        .astype(F32)
        .astype(BF16)
    )
    return high, jnp.concatenate([hot, hot], axis=0)


def pick_kernel(cell_ref, request_ref, first_ref, *refs):
    *kept_refs, out_ref = refs
    species, cells = cell_ref.shape
    owners, cap = request_ref.shape[2:]
    groups = LANES // cap
    chunks = owners // (2 * groups)
    highs = cells // LANES
    here = lax.axis_index("grid")
    relative = lane_groups(cap, here)
    cell = cell_ref[...]
    stacked = jnp.concatenate(
        [cell[:, LANES * h : LANES * (h + 1)] for h in range(highs)], axis=0
    )
    left = jnp.concatenate(rounded(stacked), axis=1).astype(BF16)

    def chunk(k, carry):
        first = k * 2 * groups
        if kept_refs:
            high, right = kept_refs[0][...], kept_refs[1][...]
        else:
            high, right = pick_index(request_ref, k)
        product = jnp.dot(left, right, preferred_element_type=F32)
        picked = jnp.zeros((species, 2 * LANES), F32)
        high = jnp.concatenate([high] * (species // ROWS), axis=0)
        for h in range(highs):
            picked = picked + jnp.where(high == h, product[species * h : species * (h + 1)], 0.0)
        blank = jnp.zeros((groups * ROWS - species, 2 * LANES), F32)
        picked = jnp.concatenate([picked, blank], axis=0)
        for half in range(2):
            tiles = pack(
                [
                    picked[ROWS * g : ROWS * (g + 1), LANES * half : LANES * (half + 1)]
                    for g in range(groups)
                ],
                cap,
                here,
                relative,
            )
            for j in range(groups):
                out_ref[first + half * groups + j] = tiles[j]
        return carry

    repeat_steps(chunks, chunk, 0)


def to_segments(values, width):
    groups = LANES // width
    stacked = [value.astype(F32) for value in values]
    stacked.append(jnp.zeros((LANES - width * len(values), LANES), F32))
    turned = jnp.transpose(jnp.concatenate(stacked, axis=0))
    times = LANES // groups
    return exchange_groups([turned[times * g : times * (g + 1)] for g in range(groups)], width)


def lines_kernel(
    lines,
    cap,
    table_ref,
    slot_ref,
    length_ref,
    courant_ref,
    flux_ref,
    inflow_ref,
    interaction_ref,
    out_ref,
    rows_ref,
):
    owners = table_ref.shape[0]
    copies = out_ref.shape[0] // owners
    species = inflow_ref.shape[1]
    width = slot_ref.shape[0]
    nodes = width * LANES // lines
    groups = species // ROWS
    all_groups = LANES // cap
    rows = all_groups * ROWS
    blocks = nodes // LANES
    segments = LANES // width
    times = LANES // segments
    chunk_owners = 2 * all_groups
    chunks = owners // chunk_owners
    here, bundle = lax.axis_index("grid"), lax.axis_index("bundle")

    slot = slot_ref[...]
    within = (slot + lax.rem(here, all_groups) * cap) % LANES
    slot, courant, flux = to_segments(
        [slot - slot % LANES + within, courant_ref[...], flux_ref[...]], width
    )[:3]
    scale = 1.0 / (1.0 + courant)
    rows_ref[0] = scale
    rows_ref[1] = courant * scale
    rows_ref[2] = flux
    rows_ref[3] = slot

    def row(kind, t, depth=ROWS):
        return jnp.broadcast_to(rows_ref[kind, t : t + 1], (depth, LANES))

    def hot(k):
        index = lax.broadcasted_iota(jnp.int32, (2 * LANES, LANES), 0).astype(F32).astype(BF16)
        one, zero = jnp.ones_like(index), jnp.zeros_like(index)
        base = lax.convert_element_type(k * 2 * LANES, F32)
        columns = []
        for t in range(times):
            local = (row(3, t, 2 * ROWS) - base).astype(BF16)
            local = jnp.concatenate([local] * (LANES // ROWS), axis=0)
            columns.append(jnp.where(local == index, one, zero))
        return jnp.concatenate(columns, axis=1)

    kept = hot(0) if chunks == 1 else None

    relative = lane_groups(cap, here)

    def gather(k, state):
        halves = []
        for half in range(2):
            first = k * chunk_owners + half * all_groups
            halves.append(
                jnp.concatenate(
                    unpack(
                        [table_ref[first + j] for j in range(all_groups)], cap, relative, groups
                    ),
                    axis=0,
                )
            )
        left = split(jnp.concatenate(halves, axis=1))
        found = jnp.dot(left, hot(k) if kept is None else kept, preferred_element_type=F32)
        found = found[:species] + found[species:]
        return found if chunks == 1 else state + found

    start = repeat_steps(
        chunks, gather, jnp.zeros((species, lines * nodes), F32) if chunks > 1 else 0
    )

    lane = lax.broadcasted_iota(jnp.int32, (ROWS, LANES), 1)
    part = lane // width
    block = (lane % width) // lines
    segment = block * segments + part
    line = lane % lines

    def earlier(value, distance):
        major, minor = distance // segments, distance % segments
        near = pltpu.roll(value, minor * width + major * lines, 1)
        if minor == 0:
            return near
        far = pltpu.roll(value, minor * width + (major + 1) * lines, 1)
        return jnp.where(part >= minor, near, far)

    eye = lax.broadcasted_iota(jnp.int32, (species, LANES), 0) == lax.broadcasted_iota(
        jnp.int32, (species, LANES), 1
    )
    padded = jnp.concatenate([inflow_ref[...], jnp.zeros((1, LANES - species), F32)], axis=1)
    column = jnp.sum(jnp.where(eye, padded, 0.0), axis=1, keepdims=True)
    entry = jnp.broadcast_to(column, (species, LANES))
    entry = [entry[ROWS * g : ROWS * (g + 1)] for g in range(groups)]

    first = [None] * groups
    second = [None] * groups
    local, ones, twos = [], [], []
    for t in range(times):
        scale_t, decay_t = row(0, t), row(1, t)
        one = decay_t if t == 0 else decay_t * ones[-1]
        two = scale_t * one if t == 0 else scale_t * one + decay_t * twos[-1]
        ones.append(one)
        twos.append(two)
        for g in range(groups):
            value = start[ROWS * g : ROWS * (g + 1), LANES * t : LANES * (t + 1)] * scale_t
            first[g] = value if t == 0 else value + decay_t * first[g]
            value = scale_t * first[g]
            second[g] = value if t == 0 else value + decay_t * second[g]
            local.append(second[g])

    a, b = ones[-1], twos[-1]
    head = segment == 0
    first = [jnp.where(head, f + a * e, f) for f, e in zip(first, entry)]
    second = [jnp.where(head, s + b * e + a * e, s) for s, e in zip(second, entry)]
    distance = 1
    while distance < blocks * segments:
        run_a, run_b = a, b
        next_first, next_second = first, second
        for k in range(1, 4):
            if k * distance >= blocks * segments:
                break
            opened = segment >= k * distance
            a_open, b_open = jnp.where(opened, run_a, 0.0), jnp.where(opened, run_b, 0.0)
            ahead = [earlier(f, k * distance) for f in first]
            next_first = [n + a_open * f for n, f in zip(next_first, ahead)]
            next_second = [
                n + b_open * f + a_open * earlier(s, k * distance)
                for n, s, f in zip(next_second, second, ahead)
            ]
            a_ahead = earlier(a, k * distance)
            run_b = run_b * a_ahead + run_a * earlier(b, k * distance)
            run_a = run_a * a_ahead
        first, second = next_first, next_second
        a, b = run_a, run_b
        distance *= 4
    carry_one = [jnp.where(head, e, earlier(f, 1)) for e, f in zip(entry, first)]
    carry_two = [jnp.where(head, e, earlier(s, 1)) for e, s in zip(entry, second)]
    columns = [
        jnp.concatenate(
            [
                local[t * groups + g] + twos[t] * carry_one[g] + ones[t] * carry_two[g]
                for g in range(groups)
            ],
            axis=0,
        )
        for t in range(times)
    ]

    matrix_high, matrix_low = rounded(interaction_ref[...])
    blank = jnp.zeros_like(matrix_high)
    left = jnp.concatenate(
        [
            jnp.concatenate(
                [matrix_high, blank, matrix_low, blank, matrix_high, blank], axis=1
            ),
            jnp.concatenate(
                [blank, matrix_high, blank, matrix_low, blank, matrix_high], axis=1
            ),
        ],
        axis=0,
    ).astype(BF16)
    half = times // 2
    depth = half // CHUNKS
    bases = [
        jnp.concatenate(
            [
                jnp.concatenate(columns[offset + c * depth : offset + (c + 1) * depth], axis=1)
                for offset in (0, half)
            ],
            axis=0,
        )
        for c in range(CHUNKS)
    ]
    iterates = list(bases)
    for step in range(NEWTON):
        for c in range(CHUNKS):
            high, low = parts(jnp.tanh(iterates[c]))
            right = jnp.concatenate([high, high, low], axis=0)
            iterates[c] = bases[c] - jnp.dot(left, right, preferred_element_type=F32)

    length = jnp.zeros((ROWS, LANES), jnp.int32)
    for one_line in range(lines):
        one_length = jnp.broadcast_to(length_ref[:, one_line : one_line + 1], (ROWS, LANES))
        length = jnp.where(line == one_line, one_length, length)
    node = block * LANES + part * times
    top = lax.broadcasted_iota(jnp.int32, (ROWS, LANES), 0) == 0
    pieces = []
    for t in range(times):
        weight = jnp.where(node + t < length, row(2, t), 0.0)
        chunk, place = t % half // depth, t % half % depth
        found = iterates[chunk][
            t // half * species : (t // half + 1) * species, LANES * place : LANES * (place + 1)
        ]
        scaled = [found[ROWS * g : ROWS * (g + 1)] * weight for g in range(groups)]
        scaled.append(jnp.where(top, weight, 0.0))
        pieces.append(jnp.concatenate(scaled, axis=0))
    left = split(jnp.concatenate(pieces, axis=1))
    relative = lane_groups(cap, here + bundle)

    def scatter(k, carry):
        sums = lax.dot_general(
            left,
            hot(k) if kept is None else kept,
            (((1,), (1,)), ((), ())),
            preferred_element_type=F32,
        )
        sums = sums[:rows] + sums[rows:]
        for half in range(2):
            tiles = pack(
                [
                    sums[ROWS * g : ROWS * (g + 1), LANES * half : LANES * (half + 1)]
                    for g in range(all_groups)
                ],
                cap,
                bundle,
                relative,
            )
            for j in range(all_groups):
                owner = k * chunk_owners + half * all_groups + j
                for copy in range(copies):
                    out_ref[copy * owners + owner] = tiles[j]
        return carry

    repeat_steps(chunks, scatter, 0)


def blend_index(request_ref, k):
    bundles, cap = request_ref.shape[0], request_ref.shape[3]
    all_groups = LANES // cap
    width = 2 * LANES
    here = lax.axis_index("grid")
    sublane = lax.broadcasted_iota(jnp.int32, (ROWS, LANES), 0)
    indices = []
    for t in range(bundles // all_groups):
        straight = jnp.concatenate(
            [
                request_ref[
                    t * all_groups
                    + lax.rem(x + all_groups - lax.rem(here, all_groups), all_groups),
                    0,
                    pl.ds(k * ROWS, ROWS),
                    :,
                ]
                for x in range(all_groups)
            ],
            axis=1,
        )
        block = straight
        for turn in range(1, all_groups):
            block = jnp.where(
                sublane % all_groups == turn, pltpu.roll(straight, turn * cap, 1), block
            )
        indices += [block[d : d + 1] for d in range(ROWS)]
    index = jnp.concatenate(indices, axis=1)
    entries = index.shape[1]
    high = jnp.broadcast_to(index // width, (2 * ROWS, entries)).astype(F32).astype(BF16)
    low = jnp.broadcast_to(index % width, (2 * ROWS, entries)).astype(F32).astype(BF16)
    low = jnp.concatenate([low] * (width // (2 * ROWS)), axis=0)
    place = lax.broadcasted_iota(jnp.int32, (width, entries), 0).astype(F32).astype(BF16)
    return high, jnp.where(place == low, jnp.ones_like(place), jnp.zeros_like(place))


def index_kernel(
    request_ref, first_ref, length_ref, inflow_ref, pick_high, pick_hot, blend_high, blend_hot
):
    pick_high[...], pick_hot[...] = pick_index(request_ref, 0)
    blend_high[...], blend_hot[...] = blend_index(request_ref, 0)


def blend_kernel(bundles, sums_ref, request_ref, pore_ref, cell_ref, *refs):
    *kept_refs, out_hbm, out_ref, out_sem = refs
    owners = sums_ref.shape[0] // bundles
    species, cells = cell_ref.shape
    cap = request_ref.shape[3]
    all_groups = LANES // cap
    groups = species // ROWS
    width = 2 * LANES
    highs = cells // width
    chunks = owners // ROWS
    here = lax.axis_index("grid")

    def chunk(k, total):
        values, weights = [], []
        for t in range(bundles // all_groups):
            for d in range(ROWS):
                found = unpack(
                    [
                        sums_ref[(t * all_groups + j) * owners + k * ROWS + d]
                        for j in range(all_groups)
                    ],
                    cap,
                    lane_groups(cap, here + d),
                    all_groups,
                )
                weights.append(found[groups][:1])
                values.append(jnp.concatenate(found[:groups], axis=0))
        both = split(jnp.concatenate(values, axis=1))
        weight_high, weight_low = rounded(jnp.concatenate(weights, axis=1))
        if kept_refs:
            high, hot = kept_refs[0][...], kept_refs[1][...]
        else:
            high, hot = blend_index(request_ref, k)
        entries = hot.shape[1]
        zero = jnp.zeros((2 * ROWS, entries), BF16)
        pieces = []
        for first in range(0, highs, 2 * ROWS):
            mask = high == (
                lax.broadcasted_iota(jnp.int32, (2 * ROWS, entries), 0) + first
            ).astype(F32).astype(BF16)
            for part in (weight_high, weight_low):
                row = jnp.broadcast_to(part, (2 * ROWS, entries)).astype(BF16)
                pieces.append(jnp.where(mask, row, zero))
        for h in range(highs):
            mask = high == jnp.array(h, BF16)
            for r in range(2 * species // (2 * ROWS)):
                pieces.append(jnp.where(mask, both[2 * ROWS * r : 2 * ROWS * (r + 1)], zero))
        half = (len(pieces) + len(pieces) // 2 % 2) // 2
        products = [
            lax.dot_general(
                jnp.concatenate(some, axis=0),
                hot,
                (((1,), (1,)), ((), ())),
                preferred_element_type=F32,
            )
            for some in (pieces[:half], pieces[half:])
        ]
        product = jnp.concatenate(products, axis=0)
        return product if chunks == 1 else total + product

    flux_rows = -(-highs // (2 * ROWS)) * 4 * ROWS
    total = repeat_steps(
        chunks,
        chunk,
        jnp.zeros((highs * 2 * species + flux_rows, width), F32) if chunks > 1 else 0,
    )
    flux, total = total[:flux_rows], total[flux_rows:]
    copies = []
    stride = max(highs // 4, 1)
    for h in range(highs):
        part = total[2 * species * h : 2 * species * (h + 1)]
        part = part[:species] + part[species:]
        row = h // (2 * ROWS) * 4 * ROWS + h % (2 * ROWS)
        pore = pore_ref[:, width * h : width * (h + 1)]
        inverse = 1.0 / (pore + flux[row : row + 1] + flux[row + 2 * ROWS : row + 2 * ROWS + 1])
        columns = pl.ds(width * h, width)
        out_ref[:, columns] = (pore * cell_ref[:, columns] + part) * inverse
        if h % stride == stride - 1:
            columns = pl.ds(width * (h - stride + 1), stride * width)
            copies.append(
                pltpu.make_async_copy(
                    out_ref.at[:, columns], out_hbm.at[:, columns], out_sem.at[h // stride]
                )
            )
            copies[-1].start()
    for copy in copies:
        copy.wait()


def call(kernel, shapes, operands, kinds={}, scratch=(), out=pltpu.VMEM, flops=0):
    return pl.pallas_call(
        kernel,
        out_shape=[jax.ShapeDtypeStruct(shape, kind) for shape, kind in shapes],
        in_specs=[
            pl.BlockSpec(memory_space=kinds.get(i, pltpu.VMEM)) for i in range(len(operands))
        ],
        out_specs=[pl.BlockSpec(memory_space=out)] * len(shapes),
        scratch_shapes=list(scratch),
        compiler_params=pltpu.CompilerParams(vmem_limit_bytes=VMEM_BYTES),
        cost_estimate=pl.CostEstimate(flops=flops, bytes_accessed=0, transcendentals=0),
    )(*operands)


def shards(
    bundles,
    cell_state,
    pore_volume,
    request_cell,
    node_slot,
    line_length,
    courant,
    flux_weight,
    inflow,
    interaction,
):
    owners, cap = request_cell.shape[2:]
    first = call(first_kernel, [((ROWS, LANES), F32)], (), flops=10**9)[0]
    indices = []
    if owners == ROWS and owners * cap == 2 * LANES:
        entries = owners * bundles * cap
        indices = call(
            index_kernel,
            [
                ((ROWS, 2 * LANES), jnp.int32),
                ((2 * LANES, 2 * LANES), BF16),
                ((2 * ROWS, entries), BF16),
                ((2 * LANES, entries), BF16),
            ],
            (request_cell, first, line_length, inflow),
        )
    outgoing = call(
        pick_kernel,
        [((owners, ROWS, LANES), F32)],
        (cell_state, request_cell, first, *indices[:2]),
    )[0]
    table = lax.all_to_all(outgoing, "grid", split_axis=0, concat_axis=0, tiled=True)
    lines, nodes = node_slot.shape[1:]
    blocks = nodes // LANES

    def by_block(value):
        return value.reshape(lines, blocks, LANES).swapaxes(0, 1).reshape(blocks * lines, LANES)

    sums = call(
        functools.partial(lines_kernel, lines, cap),
        [((owners * bundles, ROWS, LANES), F32)],
        (
            table,
            by_block(node_slot),
            line_length,
            by_block(courant),
            by_block(flux_weight),
            inflow,
            interaction,
        ),
        scratch=(pltpu.VMEM((4, lines * blocks, LANES), F32),),
    )[0]
    back = lax.all_to_all(sums, ("bundle", "grid"), split_axis=0, concat_axis=0, tiled=True)
    return call(
        functools.partial(blend_kernel, bundles),
        [(cell_state.shape, F32)],
        (back, request_cell, pore_volume[None, :], cell_state, *indices[2:]),
        scratch=(pltpu.VMEM(cell_state.shape, F32), pltpu.SemaphoreType.DMA((4,))),
        out=pltpu.HBM,
    )[0]


def solution(mesh):
    placed = (
        P(None, "grid"),
        P("grid"),
        P(None, "grid", None, None),
        P("bundle", "grid", None),
        P("bundle", "grid"),
        P("bundle", "grid", None),
        P("bundle", "grid", None),
        P("bundle", None),
        P(),
    )
    return jax.shard_map(
        functools.partial(shards, mesh.shape["bundle"]),
        mesh=mesh,
        in_specs=placed,
        out_specs=P(None, "grid"),
        check_vma=False,
    )
```

```python
import functools

import jax
import jax.numpy as jnp
from jax import lax
from jax.experimental import pallas as pl
from jax.experimental.pallas import tpu as pltpu
from jax.sharding import PartitionSpec as P

SUB = 2
NEWTON = 3
LANES = 128
ROWS = 8
F32 = jnp.float32
BF16 = jnp.bfloat16
VMEM_BYTES = 32 * 1024 * 1024
CHUNKS = 1


def repeat_steps(count, body, carry):
    if count == 1:
        return body(0, carry)
    return lax.fori_loop(0, count, body, carry)


def rounded(value):
    high = value.astype(BF16).astype(F32)
    return high, value - high


def parts(value):
    high = value.astype(BF16)
    return high, (value - high.astype(F32)).astype(BF16)


def split(value):
    return jnp.concatenate(rounded(value), axis=0).astype(BF16)


def select_groups(tiles, relative):
    count = len(tiles)
    results = []
    for i in range(count):
        value = tiles[0]
        for j in range(1, count):
            value = jnp.where(relative == (i + j) % count, tiles[j], value)
        results.append(value)
    return results


def lane_groups(cap, turn):
    groups = LANES // cap
    lane = lax.broadcasted_iota(jnp.int32, (ROWS, LANES), 1)
    return (lane // cap + (2 * groups - lax.rem(turn, groups))) % groups


def pack(rows, cap, turn, relative):
    groups = LANES // cap
    turned = [
        pltpu.roll(rows[g], lax.rem(turn + g, groups) * cap, 1) for g in range(groups)
    ]
    return select_groups(turned, relative)


def unpack(tiles, cap, relative, count):
    found = select_groups(tiles, relative)[:count]
    return [
        found[g] if g == 0 else pltpu.roll(found[g], LANES - g * cap, 1) for g in range(count)
    ]


def exchange_groups(tiles, width):
    tiles = list(tiles)
    lane_group = lax.broadcasted_iota(jnp.int32, tiles[0].shape, 1) // width
    step = 1
    while step < len(tiles):
        keep = (lane_group & step) == 0
        for i in range(len(tiles)):
            if i & step == 0:
                first, second = tiles[i], tiles[i | step]
                tiles[i] = jnp.where(keep, first, pltpu.roll(second, step * width, 1))
                tiles[i | step] = jnp.where(
                    keep, pltpu.roll(first, LANES - step * width, 1), second
                )
        step *= 2
    return tiles


def spread_rows(block, cap):
    groups = block.shape[0]
    wide = jnp.concatenate([block] * groups, axis=1)
    rows = lax.broadcasted_iota(jnp.int32, wide.shape, 0)
    lanes = lax.broadcasted_iota(jnp.int32, wide.shape, 1) // cap
    return jnp.sum(jnp.where(rows == lanes, wide, 0), axis=0, keepdims=True)


def first_kernel(out_ref):
    out_ref[...] = jnp.zeros_like(out_ref)


def pick_index(request_ref, k):
    bundle = lax.axis_index("bundle")
    groups = LANES // request_ref.shape[3]
    cap = request_ref.shape[3]
    block = request_ref[bundle, 0, pl.ds(k * 2 * groups, 2 * groups), :]
    index = jnp.concatenate(
        [spread_rows(block[:groups], cap), spread_rows(block[groups:], cap)], axis=1
    )
    high = jnp.broadcast_to(index // LANES, (ROWS, 2 * LANES))
    hot = (
        (lax.broadcasted_iota(jnp.int32, (LANES, 2 * LANES), 0) == index % LANES)
        .astype(F32)
        .astype(BF16)
    )
    return high, jnp.concatenate([hot, hot], axis=0)


def pick_kernel(cell_ref, request_ref, first_ref, *refs):
    *kept_refs, out_ref = refs
    species, cells = cell_ref.shape
    owners, cap = request_ref.shape[2:]
    groups = LANES // cap
    chunks = owners // (2 * groups)
    highs = cells // LANES
    here = lax.axis_index("grid")
    relative = lane_groups(cap, here)
    cell = cell_ref[...]
    stacked = jnp.concatenate(
        [cell[:, LANES * h : LANES * (h + 1)] for h in range(highs)], axis=0
    )
    left = jnp.concatenate(rounded(stacked), axis=1).astype(BF16)

    def chunk(k, carry):
        first = k * 2 * groups
        if kept_refs:
            high, right = kept_refs[0][...], kept_refs[1][...]
        else:
            high, right = pick_index(request_ref, k)
        product = jnp.dot(left, right, preferred_element_type=F32)
        picked = jnp.zeros((species, 2 * LANES), F32)
        high = jnp.concatenate([high] * (species // ROWS), axis=0)
        for h in range(highs):
            picked = picked + jnp.where(high == h, product[species * h : species * (h + 1)], 0.0)
        blank = jnp.zeros((groups * ROWS - species, 2 * LANES), F32)
        picked = jnp.concatenate([picked, blank], axis=0)
        for half in range(2):
            tiles = pack(
                [
                    picked[ROWS * g : ROWS * (g + 1), LANES * half : LANES * (half + 1)]
                    for g in range(groups)
                ],
                cap,
                here,
                relative,
            )
            for j in range(groups):
                out_ref[first + half * groups + j] = tiles[j]
        return carry

    repeat_steps(chunks, chunk, 0)


def to_segments(values, width):
    groups = LANES // width
    stacked = [value.astype(F32) for value in values]
    if width * len(values) < LANES:
        stacked.append(jnp.zeros((LANES - width * len(values), LANES), F32))
    turned = jnp.transpose(jnp.concatenate(stacked, axis=0))
    times = LANES // groups
    return exchange_groups([turned[times * g : times * (g + 1)] for g in range(groups)], width)


def lines_kernel(
    lines,
    cap,
    table_ref,
    slot_ref,
    length_ref,
    courant_ref,
    flux_ref,
    inflow_ref,
    interaction_ref,
    out_ref,
    rows_ref,
):
    owners = table_ref.shape[0]
    copies = out_ref.shape[0] // owners
    species = inflow_ref.shape[1]
    width = slot_ref.shape[0]
    nodes = width * LANES // lines
    groups = species // ROWS
    all_groups = LANES // cap
    rows = all_groups * ROWS
    blocks = nodes // LANES
    segments = LANES // width
    times = LANES // segments
    chunk_owners = 2 * all_groups
    chunks = owners // chunk_owners
    here, bundle = lax.axis_index("grid"), lax.axis_index("bundle")

    slot = slot_ref[...]
    within = (slot + lax.rem(here, all_groups) * cap) % LANES
    within, half_index, courant, flux = to_segments(
        [within, slot // LANES, courant_ref[...], flux_ref[...]], width
    )[:4]
    scale = 1.0 / (1.0 + courant)
    rows_ref[0] = scale
    rows_ref[1] = courant * scale
    rows_ref[2] = flux
    rows_ref[3] = within
    rows_ref[4] = half_index

    def row(kind, t, depth=ROWS):
        return jnp.broadcast_to(rows_ref[kind, t : t + 1], (depth, LANES))

    index = lax.broadcasted_iota(jnp.int32, (LANES, LANES), 0).astype(F32).astype(BF16)
    one, zero = jnp.ones_like(index), jnp.zeros_like(index)
    columns = []
    for t in range(times):
        lanes = row(3, t, 2 * ROWS).astype(BF16)
        lanes = jnp.concatenate([lanes] * (LANES // (2 * ROWS)), axis=0)
        columns.append(jnp.where(lanes == index, one, zero))
    hot = jnp.concatenate(columns, axis=1)
    half_rows = jnp.concatenate([row(4, t) for t in range(times)], axis=1)

    relative = lane_groups(cap, here)

    def gather(k, state):
        halves = []
        for half in range(2):
            first = k * chunk_owners + half * all_groups
            halves.append(
                jnp.concatenate(
                    unpack(
                        [table_ref[first + j] for j in range(all_groups)], cap, relative, groups
                    ),
                    axis=0,
                )
            )
        left = jnp.concatenate([split(value) for value in halves], axis=0)
        found = jnp.dot(left, hot, preferred_element_type=F32)
        lower = found[:species] + found[species : 2 * species]
        upper = found[2 * species : 3 * species] + found[3 * species :]
        number = jnp.concatenate([half_rows] * groups, axis=0)
        if chunks == 1:
            return jnp.where(number == 0.0, lower, upper)
        base = lax.convert_element_type(2 * k, F32)
        return jnp.where(number == base, lower, jnp.where(number == base + 1.0, upper, state))

    start = repeat_steps(
        chunks, gather, jnp.zeros((species, lines * nodes), F32) if chunks > 1 else 0
    )

    lane = lax.broadcasted_iota(jnp.int32, (ROWS, LANES), 1)
    part = lane // width
    block = (lane % width) // lines
    segment = block * segments + part
    line = lane % lines

    def earlier(value, distance):
        major, minor = distance // segments, distance % segments
        near = pltpu.roll(value, minor * width + major * lines, 1)
        if minor == 0:
            return near
        far = pltpu.roll(value, minor * width + (major + 1) * lines, 1)
        return jnp.where(part >= minor, near, far)

    eye = lax.broadcasted_iota(jnp.int32, (species, LANES), 0) == lax.broadcasted_iota(
        jnp.int32, (species, LANES), 1
    )
    padded = jnp.concatenate([inflow_ref[...], jnp.zeros((1, LANES - species), F32)], axis=1)
    column = jnp.sum(jnp.where(eye, padded, 0.0), axis=1, keepdims=True)
    entry = jnp.broadcast_to(column, (species, LANES))
    entry = [entry[ROWS * g : ROWS * (g + 1)] for g in range(groups)]

    first = [None] * groups
    second = [None] * groups
    local, ones, twos = [], [], []
    for t in range(times):
        scale_t, decay_t = row(0, t), row(1, t)
        one = decay_t if t == 0 else decay_t * ones[-1]
        two = scale_t * one if t == 0 else scale_t * one + decay_t * twos[-1]
        ones.append(one)
        twos.append(two)
        for g in range(groups):
            value = start[ROWS * g : ROWS * (g + 1), LANES * t : LANES * (t + 1)] * scale_t
            first[g] = value if t == 0 else value + decay_t * first[g]
            value = scale_t * first[g]
            second[g] = value if t == 0 else value + decay_t * second[g]
            local.append(second[g])

    a, b = ones[-1], twos[-1]
    head = segment == 0
    first = [jnp.where(head, f + a * e, f) for f, e in zip(first, entry)]
    second = [jnp.where(head, s + b * e + a * e, s) for s, e in zip(second, entry)]
    distance = 1
    while distance < blocks * segments:
        run_a, run_b = a, b
        next_first, next_second = first, second
        for k in range(1, 4):
            if k * distance >= blocks * segments:
                break
            opened = segment >= k * distance
            a_open, b_open = jnp.where(opened, run_a, 0.0), jnp.where(opened, run_b, 0.0)
            ahead = [earlier(f, k * distance) for f in first]
            next_first = [n + a_open * f for n, f in zip(next_first, ahead)]
            next_second = [
                n + b_open * f + a_open * earlier(s, k * distance)
                for n, s, f in zip(next_second, second, ahead)
            ]
            a_ahead = earlier(a, k * distance)
            run_b = run_b * a_ahead + run_a * earlier(b, k * distance)
            run_a = run_a * a_ahead
        first, second = next_first, next_second
        a, b = run_a, run_b
        distance *= 4
    carry_one = [jnp.where(head, e, earlier(f, 1)) for e, f in zip(entry, first)]
    carry_two = [jnp.where(head, e, earlier(s, 1)) for e, s in zip(entry, second)]
    columns = [
        jnp.concatenate(
            [
                local[t * groups + g] + twos[t] * carry_one[g] + ones[t] * carry_two[g]
                for g in range(groups)
            ],
            axis=0,
        )
        for t in range(times)
    ]

    matrix_high, matrix_low = rounded(interaction_ref[...])
    blank = jnp.zeros_like(matrix_high)
    left = jnp.concatenate(
        [
            jnp.concatenate(
                [matrix_high, blank, matrix_low, blank, matrix_high, blank], axis=1
            ),
            jnp.concatenate(
                [blank, matrix_high, blank, matrix_low, blank, matrix_high], axis=1
            ),
        ],
        axis=0,
    ).astype(BF16)
    half = times // 2
    depth = half // CHUNKS
    bases = [
        jnp.concatenate(
            [
                jnp.concatenate(columns[offset + c * depth : offset + (c + 1) * depth], axis=1)
                for offset in (0, half)
            ],
            axis=0,
        )
        for c in range(CHUNKS)
    ]
    iterates = list(bases)
    for step in range(NEWTON):
        for c in range(CHUNKS):
            high, low = parts(jnp.tanh(iterates[c]))
            right = jnp.concatenate([high, high, low], axis=0)
            iterates[c] = bases[c] - jnp.dot(left, right, preferred_element_type=F32)

    length = jnp.zeros((ROWS, LANES), jnp.int32)
    for one_line in range(lines):
        one_length = jnp.broadcast_to(length_ref[:, one_line : one_line + 1], (ROWS, LANES))
        length = jnp.where(line == one_line, one_length, length)
    node = block * LANES + part * times
    top = lax.broadcasted_iota(jnp.int32, (ROWS, LANES), 0) == 0
    pieces = []
    for t in range(times):
        weight = jnp.where(node + t < length, row(2, t), 0.0)
        chunk, place = t % half // depth, t % half % depth
        found = iterates[chunk][
            t // half * species : (t // half + 1) * species, LANES * place : LANES * (place + 1)
        ]
        scaled = [found[ROWS * g : ROWS * (g + 1)] * weight for g in range(groups)]
        scaled.append(jnp.where(top, weight, 0.0))
        pieces.append(jnp.concatenate(scaled, axis=0))
    left = split(jnp.concatenate(pieces, axis=1))
    relative = lane_groups(cap, here + bundle)

    half_rows = jnp.concatenate([half_rows] * (2 * rows // ROWS), axis=0).astype(BF16)

    def scatter(k, carry):
        base = lax.convert_element_type(2 * k, F32)
        masked = [
            jnp.where(half_rows == (base + half).astype(BF16), left, jnp.zeros_like(left))
            for half in range(2)
        ]
        sums = lax.dot_general(
            jnp.concatenate(masked, axis=0),
            hot,
            (((1,), (1,)), ((), ())),
            preferred_element_type=F32,
        )
        for half in range(2):
            both = sums[2 * rows * half : 2 * rows * (half + 1)]
            both = both[:rows] + both[rows:]
            tiles = pack(
                [both[ROWS * g : ROWS * (g + 1)] for g in range(all_groups)],
                cap,
                bundle,
                relative,
            )
            for j in range(all_groups):
                owner = k * chunk_owners + half * all_groups + j
                for copy in range(copies):
                    out_ref[copy * owners + owner] = tiles[j]
        return carry

    repeat_steps(chunks, scatter, 0)


def blend_index(request_ref, k):
    bundles, cap = request_ref.shape[0], request_ref.shape[3]
    all_groups = LANES // cap
    width = 2 * LANES
    here = lax.axis_index("grid")
    sublane = lax.broadcasted_iota(jnp.int32, (ROWS, LANES), 0)
    indices = []
    for t in range(bundles // all_groups):
        straight = jnp.concatenate(
            [
                request_ref[
                    t * all_groups
                    + lax.rem(x + all_groups - lax.rem(here, all_groups), all_groups),
                    0,
                    pl.ds(k * ROWS, ROWS),
                    :,
                ]
                for x in range(all_groups)
            ],
            axis=1,
        )
        block = straight
        for turn in range(1, all_groups):
            block = jnp.where(
                sublane % all_groups == turn, pltpu.roll(straight, turn * cap, 1), block
            )
        indices += [block[d : d + 1] for d in range(ROWS)]
    index = jnp.concatenate(indices, axis=1)
    entries = index.shape[1]
    high = jnp.broadcast_to(index // width, (2 * ROWS, entries)).astype(F32).astype(BF16)
    low = jnp.broadcast_to(index % width, (2 * ROWS, entries)).astype(F32).astype(BF16)
    low = jnp.concatenate([low] * (width // (2 * ROWS)), axis=0)
    place = lax.broadcasted_iota(jnp.int32, (width, entries), 0).astype(F32).astype(BF16)
    return high, jnp.where(place == low, jnp.ones_like(place), jnp.zeros_like(place))


def index_kernel(
    request_ref, first_ref, length_ref, inflow_ref, pick_high, pick_hot, blend_high, blend_hot
):
    pick_high[...], pick_hot[...] = pick_index(request_ref, 0)
    blend_high[...], blend_hot[...] = blend_index(request_ref, 0)


def blend_kernel(bundles, sums_ref, request_ref, pore_ref, cell_ref, *refs):
    *kept_refs, out_hbm, out_ref, out_sem = refs
    owners = sums_ref.shape[0] // bundles
    species, cells = cell_ref.shape
    cap = request_ref.shape[3]
    all_groups = LANES // cap
    groups = species // ROWS
    width = 2 * LANES
    highs = cells // width
    chunks = owners // ROWS
    here = lax.axis_index("grid")

    def chunk(k, total):
        values, weights = [], []
        for t in range(bundles // all_groups):
            for d in range(ROWS):
                found = unpack(
                    [
                        sums_ref[(t * all_groups + j) * owners + k * ROWS + d]
                        for j in range(all_groups)
                    ],
                    cap,
                    lane_groups(cap, here + d),
                    all_groups,
                )
                weights.append(found[groups][:1])
                values.append(jnp.concatenate(found[:groups], axis=0))
        both = split(jnp.concatenate(values, axis=1))
        weight_high, weight_low = rounded(jnp.concatenate(weights, axis=1))
        if kept_refs:
            high, hot = kept_refs[0][...], kept_refs[1][...]
        else:
            high, hot = blend_index(request_ref, k)
        entries = hot.shape[1]
        zero = jnp.zeros((2 * ROWS, entries), BF16)
        pieces = []
        for first in range(0, highs, 2 * ROWS):
            mask = high == (
                lax.broadcasted_iota(jnp.int32, (2 * ROWS, entries), 0) + first
            ).astype(F32).astype(BF16)
            for part in (weight_high, weight_low):
                row = jnp.broadcast_to(part, (2 * ROWS, entries)).astype(BF16)
                pieces.append(jnp.where(mask, row, zero))
        for h in range(highs):
            mask = high == jnp.array(h, BF16)
            for r in range(2 * species // (2 * ROWS)):
                pieces.append(jnp.where(mask, both[2 * ROWS * r : 2 * ROWS * (r + 1)], zero))
        half = (len(pieces) + len(pieces) // 2 % 2) // 2
        products = [
            lax.dot_general(
                jnp.concatenate(some, axis=0),
                hot,
                (((1,), (1,)), ((), ())),
                preferred_element_type=F32,
            )
            for some in (pieces[:half], pieces[half:])
        ]
        product = jnp.concatenate(products, axis=0)
        return product if chunks == 1 else total + product

    flux_rows = -(-highs // (2 * ROWS)) * 4 * ROWS
    total = repeat_steps(
        chunks,
        chunk,
        jnp.zeros((highs * 2 * species + flux_rows, width), F32) if chunks > 1 else 0,
    )
    flux, total = total[:flux_rows], total[flux_rows:]
    copies = []
    stride = max(highs // 4, 1)
    for h in range(highs):
        part = total[2 * species * h : 2 * species * (h + 1)]
        part = part[:species] + part[species:]
        row = h // (2 * ROWS) * 4 * ROWS + h % (2 * ROWS)
        pore = pore_ref[:, width * h : width * (h + 1)]
        inverse = 1.0 / (pore + flux[row : row + 1] + flux[row + 2 * ROWS : row + 2 * ROWS + 1])
        columns = pl.ds(width * h, width)
        out_ref[:, columns] = (pore * cell_ref[:, columns] + part) * inverse
        if h % stride == stride - 1:
            columns = pl.ds(width * (h - stride + 1), stride * width)
            copies.append(
                pltpu.make_async_copy(
                    out_ref.at[:, columns], out_hbm.at[:, columns], out_sem.at[h // stride]
                )
            )
            copies[-1].start()
    for copy in copies:
        copy.wait()


def call(kernel, shapes, operands, kinds={}, scratch=(), out=pltpu.VMEM, flops=0):
    return pl.pallas_call(
        kernel,
        out_shape=[jax.ShapeDtypeStruct(shape, kind) for shape, kind in shapes],
        in_specs=[
            pl.BlockSpec(memory_space=kinds.get(i, pltpu.VMEM)) for i in range(len(operands))
        ],
        out_specs=[pl.BlockSpec(memory_space=out)] * len(shapes),
        scratch_shapes=list(scratch),
        compiler_params=pltpu.CompilerParams(vmem_limit_bytes=VMEM_BYTES),
        cost_estimate=pl.CostEstimate(flops=flops, bytes_accessed=0, transcendentals=0),
    )(*operands)


def shards(
    bundles,
    cell_state,
    pore_volume,
    request_cell,
    node_slot,
    line_length,
    courant,
    flux_weight,
    inflow,
    interaction,
):
    owners, cap = request_cell.shape[2:]
    first = call(first_kernel, [((ROWS, LANES), F32)], (), flops=10**9)[0]
    indices = []
    if owners == ROWS and owners * cap == 2 * LANES:
        entries = owners * bundles * cap
        indices = call(
            index_kernel,
            [
                ((ROWS, 2 * LANES), jnp.int32),
                ((2 * LANES, 2 * LANES), BF16),
                ((2 * ROWS, entries), BF16),
                ((2 * LANES, entries), BF16),
            ],
            (request_cell, first, line_length, inflow),
        )
    outgoing = call(
        pick_kernel,
        [((owners, ROWS, LANES), F32)],
        (cell_state, request_cell, first, *indices[:2]),
    )[0]
    table = lax.all_to_all(outgoing, "grid", split_axis=0, concat_axis=0, tiled=True)
    lines, nodes = node_slot.shape[1:]
    blocks = nodes // LANES

    def by_block(value):
        return value.reshape(lines, blocks, LANES).swapaxes(0, 1).reshape(blocks * lines, LANES)

    sums = call(
        functools.partial(lines_kernel, lines, cap),
        [((owners * bundles, ROWS, LANES), F32)],
        (
            table,
            by_block(node_slot),
            line_length,
            by_block(courant),
            by_block(flux_weight),
            inflow,
            interaction,
        ),
        scratch=(pltpu.VMEM((5, lines * blocks, LANES), F32),),
    )[0]
    back = lax.all_to_all(sums, ("bundle", "grid"), split_axis=0, concat_axis=0, tiled=True)
    return call(
        functools.partial(blend_kernel, bundles),
        [(cell_state.shape, F32)],
        (back, request_cell, pore_volume[None, :], cell_state, *indices[2:]),
        scratch=(pltpu.VMEM(cell_state.shape, F32), pltpu.SemaphoreType.DMA((4,))),
        out=pltpu.HBM,
    )[0]


def solution(mesh):
    placed = (
        P(None, "grid"),
        P("grid"),
        P(None, "grid", None, None),
        P("bundle", "grid", None),
        P("bundle", "grid"),
        P("bundle", "grid", None),
        P("bundle", "grid", None),
        P("bundle", None),
        P(),
    )
    return jax.shard_map(
        functools.partial(shards, mesh.shape["bundle"]),
        mesh=mesh,
        in_specs=placed,
        out_specs=P(None, "grid"),
        check_vma=False,
    )
```

```python
import functools

import jax
import jax.numpy as jnp
from jax import lax
from jax.experimental import pallas as pl
from jax.experimental.pallas import tpu as pltpu
from jax.sharding import PartitionSpec as P

SUB = 2
NEWTON = 3
LANES = 128
ROWS = 8
F32 = jnp.float32
BF16 = jnp.bfloat16
VMEM_BYTES = 32 * 1024 * 1024
CHUNKS = 1


def repeat_steps(count, body, carry):
    if count == 1:
        return body(0, carry)
    return lax.fori_loop(0, count, body, carry)


def rounded(value):
    high = value.astype(BF16).astype(F32)
    return high, value - high


def parts(value):
    high = value.astype(BF16)
    return high, (value - high.astype(F32)).astype(BF16)


def split(value):
    return jnp.concatenate(rounded(value), axis=0).astype(BF16)


def select_groups(tiles, relative):
    count = len(tiles)
    results = []
    for i in range(count):
        value = tiles[0]
        for j in range(1, count):
            value = jnp.where(relative == (i + j) % count, tiles[j], value)
        results.append(value)
    return results


def lane_groups(cap, turn):
    groups = LANES // cap
    lane = lax.broadcasted_iota(jnp.int32, (ROWS, LANES), 1)
    return (lane // cap + (2 * groups - lax.rem(turn, groups))) % groups


def pack(rows, cap, turn, relative):
    groups = LANES // cap
    turned = [
        pltpu.roll(rows[g], lax.rem(turn + g, groups) * cap, 1) for g in range(groups)
    ]
    return select_groups(turned, relative)


def unpack(tiles, cap, relative, count):
    found = select_groups(tiles, relative)[:count]
    return [
        found[g] if g == 0 else pltpu.roll(found[g], LANES - g * cap, 1) for g in range(count)
    ]


def exchange_groups(tiles, width):
    tiles = list(tiles)
    lane_group = lax.broadcasted_iota(jnp.int32, tiles[0].shape, 1) // width
    step = 1
    while step < len(tiles):
        keep = (lane_group & step) == 0
        for i in range(len(tiles)):
            if i & step == 0:
                first, second = tiles[i], tiles[i | step]
                tiles[i] = jnp.where(keep, first, pltpu.roll(second, step * width, 1))
                tiles[i | step] = jnp.where(
                    keep, pltpu.roll(first, LANES - step * width, 1), second
                )
        step *= 2
    return tiles


def spread_rows(block, cap):
    groups = block.shape[0]
    wide = jnp.concatenate([block] * groups, axis=1)
    rows = lax.broadcasted_iota(jnp.int32, wide.shape, 0)
    lanes = lax.broadcasted_iota(jnp.int32, wide.shape, 1) // cap
    return jnp.sum(jnp.where(rows == lanes, wide, 0), axis=0, keepdims=True)


def first_kernel(out_ref):
    out_ref[...] = jnp.zeros_like(out_ref)


def pick_index(request_ref, k):
    bundle = lax.axis_index("bundle")
    groups = LANES // request_ref.shape[3]
    cap = request_ref.shape[3]
    block = request_ref[bundle, 0, pl.ds(k * 2 * groups, 2 * groups), :]
    index = jnp.concatenate(
        [spread_rows(block[:groups], cap), spread_rows(block[groups:], cap)], axis=1
    )
    high = jnp.broadcast_to(index // LANES, (ROWS, 2 * LANES))
    hot = (
        (lax.broadcasted_iota(jnp.int32, (LANES, 2 * LANES), 0) == index % LANES)
        .astype(F32)
        .astype(BF16)
    )
    return high, jnp.concatenate([hot, hot], axis=0)


def pick_kernel(cell_ref, request_ref, first_ref, *refs):
    *kept_refs, out_ref = refs
    species, cells = cell_ref.shape
    owners, cap = request_ref.shape[2:]
    groups = LANES // cap
    chunks = owners // (2 * groups)
    highs = cells // LANES
    here = lax.axis_index("grid")
    relative = lane_groups(cap, here)
    cell = cell_ref[...]
    stacked = jnp.concatenate(
        [cell[:, LANES * h : LANES * (h + 1)] for h in range(highs)], axis=0
    )
    left = jnp.concatenate(rounded(stacked), axis=1).astype(BF16)

    def chunk(k, carry):
        first = k * 2 * groups
        if kept_refs:
            high, right = kept_refs[0][...], kept_refs[1][...]
        else:
            high, right = pick_index(request_ref, k)
        product = jnp.dot(left, right, preferred_element_type=F32)
        picked = jnp.zeros((species, 2 * LANES), F32)
        high = jnp.concatenate([high] * (species // ROWS), axis=0)
        for h in range(highs):
            picked = picked + jnp.where(high == h, product[species * h : species * (h + 1)], 0.0)
        blank = jnp.zeros((groups * ROWS - species, 2 * LANES), F32)
        picked = jnp.concatenate([picked, blank], axis=0)
        for half in range(2):
            tiles = pack(
                [
                    picked[ROWS * g : ROWS * (g + 1), LANES * half : LANES * (half + 1)]
                    for g in range(groups)
                ],
                cap,
                here,
                relative,
            )
            for j in range(groups):
                out_ref[first + half * groups + j] = tiles[j]
        return carry

    repeat_steps(chunks, chunk, 0)


def to_segments(values, width):
    groups = LANES // width
    stacked = [value.astype(F32) for value in values]
    if width * len(values) < LANES:
        stacked.append(jnp.zeros((LANES - width * len(values), LANES), F32))
    turned = jnp.transpose(jnp.concatenate(stacked, axis=0))
    times = LANES // groups
    return exchange_groups([turned[times * g : times * (g + 1)] for g in range(groups)], width)


def lines_kernel(
    lines,
    cap,
    table_ref,
    slot_ref,
    length_ref,
    courant_ref,
    flux_ref,
    inflow_ref,
    interaction_ref,
    out_ref,
    rows_ref,
):
    owners = table_ref.shape[0]
    copies = out_ref.shape[0] // owners
    species = inflow_ref.shape[1]
    width = slot_ref.shape[0]
    nodes = width * LANES // lines
    groups = species // ROWS
    all_groups = LANES // cap
    rows = all_groups * ROWS
    blocks = nodes // LANES
    segments = LANES // width
    times = LANES // segments
    chunk_owners = 2 * all_groups
    chunks = owners // chunk_owners
    here, bundle = lax.axis_index("grid"), lax.axis_index("bundle")

    slot = slot_ref[...]
    within = (slot + lax.rem(here, all_groups) * cap) % LANES
    within, half_index, courant, flux = to_segments(
        [within, slot // LANES, courant_ref[...], flux_ref[...]], width
    )[:4]
    scale = 1.0 / (1.0 + courant)
    rows_ref[0] = scale
    rows_ref[1] = courant * scale
    rows_ref[2] = flux
    rows_ref[3] = within
    rows_ref[4] = half_index

    def row(kind, t, depth=ROWS):
        return jnp.broadcast_to(rows_ref[kind, t : t + 1], (depth, LANES))

    index = lax.broadcasted_iota(jnp.int32, (LANES, LANES), 0).astype(F32).astype(BF16)
    one, zero = jnp.ones_like(index), jnp.zeros_like(index)
    columns = []
    for t in range(times):
        lanes = row(3, t, 2 * ROWS).astype(BF16)
        lanes = jnp.concatenate([lanes] * (LANES // (2 * ROWS)), axis=0)
        columns.append(jnp.where(lanes == index, one, zero))
    hot = jnp.concatenate(columns, axis=1)
    half_rows = jnp.concatenate([row(4, t) for t in range(times)], axis=1)

    relative = lane_groups(cap, here)

    def gather(k, state):
        halves = []
        for half in range(2):
            first = k * chunk_owners + half * all_groups
            halves.append(
                jnp.concatenate(
                    unpack(
                        [table_ref[first + j] for j in range(all_groups)], cap, relative, groups
                    ),
                    axis=0,
                )
            )
        left = jnp.concatenate([split(value) for value in halves], axis=0)
        found = jnp.dot(left, hot, preferred_element_type=F32)
        lower = found[:species] + found[species : 2 * species]
        upper = found[2 * species : 3 * species] + found[3 * species :]
        base = lax.convert_element_type(2 * k, F32)
        is_lower, is_upper = half_rows == base, half_rows == base + 1.0
        merged = []
        for g in range(groups):
            part_rows = slice(ROWS * g, ROWS * (g + 1))
            rest = upper[part_rows]
            if chunks > 1:
                rest = jnp.where(is_upper, rest, state[part_rows])
            merged.append(jnp.where(is_lower, lower[part_rows], rest))
        return jnp.concatenate(merged, axis=0)

    start = repeat_steps(
        chunks, gather, jnp.zeros((species, lines * nodes), F32) if chunks > 1 else 0
    )

    lane = lax.broadcasted_iota(jnp.int32, (ROWS, LANES), 1)
    part = lane // width
    block = (lane % width) // lines
    segment = block * segments + part
    line = lane % lines

    def earlier(value, distance):
        major, minor = distance // segments, distance % segments
        near = pltpu.roll(value, minor * width + major * lines, 1)
        if minor == 0:
            return near
        far = pltpu.roll(value, minor * width + (major + 1) * lines, 1)
        return jnp.where(part >= minor, near, far)

    eye = lax.broadcasted_iota(jnp.int32, (species, LANES), 0) == lax.broadcasted_iota(
        jnp.int32, (species, LANES), 1
    )
    padded = jnp.concatenate([inflow_ref[...], jnp.zeros((1, LANES - species), F32)], axis=1)
    column = jnp.sum(jnp.where(eye, padded, 0.0), axis=1, keepdims=True)
    entry = jnp.broadcast_to(column, (species, LANES))
    entry = [entry[ROWS * g : ROWS * (g + 1)] for g in range(groups)]

    first = [None] * groups
    second = [None] * groups
    local, ones, twos = [], [], []
    for t in range(times):
        scale_t, decay_t = row(0, t), row(1, t)
        one = decay_t if t == 0 else decay_t * ones[-1]
        two = scale_t * one if t == 0 else scale_t * one + decay_t * twos[-1]
        ones.append(one)
        twos.append(two)
        for g in range(groups):
            value = start[ROWS * g : ROWS * (g + 1), LANES * t : LANES * (t + 1)] * scale_t
            first[g] = value if t == 0 else value + decay_t * first[g]
            value = scale_t * first[g]
            second[g] = value if t == 0 else value + decay_t * second[g]
            local.append(second[g])

    a, b = ones[-1], twos[-1]
    head = segment == 0
    first = [jnp.where(head, f + a * e, f) for f, e in zip(first, entry)]
    second = [jnp.where(head, s + b * e + a * e, s) for s, e in zip(second, entry)]
    distance = 1
    while distance < blocks * segments:
        run_a, run_b = a, b
        next_first, next_second = first, second
        for k in range(1, 4):
            if k * distance >= blocks * segments:
                break
            opened = segment >= k * distance
            a_open, b_open = jnp.where(opened, run_a, 0.0), jnp.where(opened, run_b, 0.0)
            ahead = [earlier(f, k * distance) for f in first]
            next_first = [n + a_open * f for n, f in zip(next_first, ahead)]
            next_second = [
                n + b_open * f + a_open * earlier(s, k * distance)
                for n, s, f in zip(next_second, second, ahead)
            ]
            a_ahead = earlier(a, k * distance)
            run_b = run_b * a_ahead + run_a * earlier(b, k * distance)
            run_a = run_a * a_ahead
        first, second = next_first, next_second
        a, b = run_a, run_b
        distance *= 4
    carry_one = [jnp.where(head, e, earlier(f, 1)) for e, f in zip(entry, first)]
    carry_two = [jnp.where(head, e, earlier(s, 1)) for e, s in zip(entry, second)]
    columns = [
        jnp.concatenate(
            [
                local[t * groups + g] + twos[t] * carry_one[g] + ones[t] * carry_two[g]
                for g in range(groups)
            ],
            axis=0,
        )
        for t in range(times)
    ]

    matrix_high, matrix_low = rounded(interaction_ref[...])
    blank = jnp.zeros_like(matrix_high)
    left = jnp.concatenate(
        [
            jnp.concatenate(
                [matrix_high, blank, matrix_low, blank, matrix_high, blank], axis=1
            ),
            jnp.concatenate(
                [blank, matrix_high, blank, matrix_low, blank, matrix_high], axis=1
            ),
        ],
        axis=0,
    ).astype(BF16)
    half = times // 2
    depth = half // CHUNKS
    bases = [
        jnp.concatenate(
            [
                jnp.concatenate(columns[offset + c * depth : offset + (c + 1) * depth], axis=1)
                for offset in (0, half)
            ],
            axis=0,
        )
        for c in range(CHUNKS)
    ]
    iterates = list(bases)
    for step in range(NEWTON):
        for c in range(CHUNKS):
            high, low = parts(jnp.tanh(iterates[c]))
            right = jnp.concatenate([high, high, low], axis=0)
            iterates[c] = bases[c] - jnp.dot(left, right, preferred_element_type=F32)

    length = jnp.zeros((ROWS, LANES), jnp.int32)
    for one_line in range(lines):
        one_length = jnp.broadcast_to(length_ref[:, one_line : one_line + 1], (ROWS, LANES))
        length = jnp.where(line == one_line, one_length, length)
    node = block * LANES + part * times
    top = lax.broadcasted_iota(jnp.int32, (ROWS, LANES), 0) == 0
    pieces = []
    for t in range(times):
        weight = jnp.where(node + t < length, row(2, t), 0.0)
        chunk, place = t % half // depth, t % half % depth
        found = iterates[chunk][
            t // half * species : (t // half + 1) * species, LANES * place : LANES * (place + 1)
        ]
        scaled = [found[ROWS * g : ROWS * (g + 1)] * weight for g in range(groups)]
        scaled.append(jnp.where(top, weight, 0.0))
        pieces.append(jnp.concatenate(scaled, axis=0))
    left = split(jnp.concatenate(pieces, axis=1))
    relative = lane_groups(cap, here + bundle)

    half_rows = jnp.concatenate([half_rows] * 2, axis=0).astype(BF16)

    def scatter(k, carry):
        base = lax.convert_element_type(2 * k, F32)
        masked = []
        for half in range(2):
            chosen = half_rows == (base + half).astype(BF16)
            for r in range(0, 2 * rows, 2 * ROWS):
                piece = left[r : r + 2 * ROWS]
                masked.append(jnp.where(chosen, piece, jnp.zeros_like(piece)))
        sums = lax.dot_general(
            jnp.concatenate(masked, axis=0),
            hot,
            (((1,), (1,)), ((), ())),
            preferred_element_type=F32,
        )
        for half in range(2):
            both = sums[2 * rows * half : 2 * rows * (half + 1)]
            both = both[:rows] + both[rows:]
            tiles = pack(
                [both[ROWS * g : ROWS * (g + 1)] for g in range(all_groups)],
                cap,
                bundle,
                relative,
            )
            for j in range(all_groups):
                owner = k * chunk_owners + half * all_groups + j
                for copy in range(copies):
                    out_ref[copy * owners + owner] = tiles[j]
        return carry

    repeat_steps(chunks, scatter, 0)


def blend_index(request_ref, k):
    bundles, cap = request_ref.shape[0], request_ref.shape[3]
    all_groups = LANES // cap
    width = 2 * LANES
    here = lax.axis_index("grid")
    sublane = lax.broadcasted_iota(jnp.int32, (ROWS, LANES), 0)
    indices = []
    for t in range(bundles // all_groups):
        straight = jnp.concatenate(
            [
                request_ref[
                    t * all_groups
                    + lax.rem(x + all_groups - lax.rem(here, all_groups), all_groups),
                    0,
                    pl.ds(k * ROWS, ROWS),
                    :,
                ]
                for x in range(all_groups)
            ],
            axis=1,
        )
        block = straight
        for turn in range(1, all_groups):
            block = jnp.where(
                sublane % all_groups == turn, pltpu.roll(straight, turn * cap, 1), block
            )
        indices += [block[d : d + 1] for d in range(ROWS)]
    index = jnp.concatenate(indices, axis=1)
    entries = index.shape[1]
    high = jnp.broadcast_to(index // width, (2 * ROWS, entries)).astype(F32).astype(BF16)
    low = jnp.broadcast_to(index % width, (2 * ROWS, entries)).astype(F32).astype(BF16)
    low = jnp.concatenate([low] * (width // (2 * ROWS)), axis=0)
    place = lax.broadcasted_iota(jnp.int32, (width, entries), 0).astype(F32).astype(BF16)
    return high, jnp.where(place == low, jnp.ones_like(place), jnp.zeros_like(place))


def index_kernel(
    request_ref, first_ref, length_ref, inflow_ref, pick_high, pick_hot, blend_high, blend_hot
):
    pick_high[...], pick_hot[...] = pick_index(request_ref, 0)
    blend_high[...], blend_hot[...] = blend_index(request_ref, 0)


def blend_kernel(bundles, sums_ref, request_ref, pore_ref, cell_ref, *refs):
    *kept_refs, out_hbm, out_ref, out_sem = refs
    owners = sums_ref.shape[0] // bundles
    species, cells = cell_ref.shape
    cap = request_ref.shape[3]
    all_groups = LANES // cap
    groups = species // ROWS
    width = 2 * LANES
    highs = cells // width
    chunks = owners // ROWS
    here = lax.axis_index("grid")

    def chunk(k, total):
        values, weights = [], []
        for t in range(bundles // all_groups):
            for d in range(ROWS):
                found = unpack(
                    [
                        sums_ref[(t * all_groups + j) * owners + k * ROWS + d]
                        for j in range(all_groups)
                    ],
                    cap,
                    lane_groups(cap, here + d),
                    all_groups,
                )
                weights.append(found[groups][:1])
                values.append(jnp.concatenate(found[:groups], axis=0))
        both = split(jnp.concatenate(values, axis=1))
        weight_high, weight_low = rounded(jnp.concatenate(weights, axis=1))
        if kept_refs:
            high, hot = kept_refs[0][...], kept_refs[1][...]
        else:
            high, hot = blend_index(request_ref, k)
        entries = hot.shape[1]
        zero = jnp.zeros((2 * ROWS, entries), BF16)
        pieces = []
        for first in range(0, highs, 2 * ROWS):
            mask = high == (
                lax.broadcasted_iota(jnp.int32, (2 * ROWS, entries), 0) + first
            ).astype(F32).astype(BF16)
            for part in (weight_high, weight_low):
                row = jnp.broadcast_to(part, (2 * ROWS, entries)).astype(BF16)
                pieces.append(jnp.where(mask, row, zero))
        for h in range(highs):
            mask = high == jnp.array(h, BF16)
            for r in range(2 * species // (2 * ROWS)):
                pieces.append(jnp.where(mask, both[2 * ROWS * r : 2 * ROWS * (r + 1)], zero))
        half = (len(pieces) + len(pieces) // 2 % 2) // 2
        products = [
            lax.dot_general(
                jnp.concatenate(some, axis=0),
                hot,
                (((1,), (1,)), ((), ())),
                preferred_element_type=F32,
            )
            for some in (pieces[:half], pieces[half:])
        ]
        product = jnp.concatenate(products, axis=0)
        return product if chunks == 1 else total + product

    flux_rows = -(-highs // (2 * ROWS)) * 4 * ROWS
    total = repeat_steps(
        chunks,
        chunk,
        jnp.zeros((highs * 2 * species + flux_rows, width), F32) if chunks > 1 else 0,
    )
    flux, total = total[:flux_rows], total[flux_rows:]
    copies = []
    stride = max(highs // 4, 1)
    for h in range(highs):
        part = total[2 * species * h : 2 * species * (h + 1)]
        part = part[:species] + part[species:]
        row = h // (2 * ROWS) * 4 * ROWS + h % (2 * ROWS)
        pore = pore_ref[:, width * h : width * (h + 1)]
        inverse = 1.0 / (pore + flux[row : row + 1] + flux[row + 2 * ROWS : row + 2 * ROWS + 1])
        columns = pl.ds(width * h, width)
        out_ref[:, columns] = (pore * cell_ref[:, columns] + part) * inverse
        if h % stride == stride - 1:
            columns = pl.ds(width * (h - stride + 1), stride * width)
            copies.append(
                pltpu.make_async_copy(
                    out_ref.at[:, columns], out_hbm.at[:, columns], out_sem.at[h // stride]
                )
            )
            copies[-1].start()
    for copy in copies:
        copy.wait()


def call(kernel, shapes, operands, kinds={}, scratch=(), out=pltpu.VMEM, flops=0):
    return pl.pallas_call(
        kernel,
        out_shape=[jax.ShapeDtypeStruct(shape, kind) for shape, kind in shapes],
        in_specs=[
            pl.BlockSpec(memory_space=kinds.get(i, pltpu.VMEM)) for i in range(len(operands))
        ],
        out_specs=[pl.BlockSpec(memory_space=out)] * len(shapes),
        scratch_shapes=list(scratch),
        compiler_params=pltpu.CompilerParams(vmem_limit_bytes=VMEM_BYTES),
        cost_estimate=pl.CostEstimate(flops=flops, bytes_accessed=0, transcendentals=0),
    )(*operands)


def shards(
    bundles,
    cell_state,
    pore_volume,
    request_cell,
    node_slot,
    line_length,
    courant,
    flux_weight,
    inflow,
    interaction,
):
    owners, cap = request_cell.shape[2:]
    first = call(first_kernel, [((ROWS, LANES), F32)], (), flops=10**9)[0]
    indices = []
    if owners == ROWS and owners * cap == 2 * LANES:
        entries = owners * bundles * cap
        indices = call(
            index_kernel,
            [
                ((ROWS, 2 * LANES), jnp.int32),
                ((2 * LANES, 2 * LANES), BF16),
                ((2 * ROWS, entries), BF16),
                ((2 * LANES, entries), BF16),
            ],
            (request_cell, first, line_length, inflow),
        )
    outgoing = call(
        pick_kernel,
        [((owners, ROWS, LANES), F32)],
        (cell_state, request_cell, first, *indices[:2]),
    )[0]
    table = lax.all_to_all(outgoing, "grid", split_axis=0, concat_axis=0, tiled=True)
    lines, nodes = node_slot.shape[1:]
    blocks = nodes // LANES

    def by_block(value):
        return value.reshape(lines, blocks, LANES).swapaxes(0, 1).reshape(blocks * lines, LANES)

    sums = call(
        functools.partial(lines_kernel, lines, cap),
        [((owners * bundles, ROWS, LANES), F32)],
        (
            table,
            by_block(node_slot),
            line_length,
            by_block(courant),
            by_block(flux_weight),
            inflow,
            interaction,
        ),
        scratch=(pltpu.VMEM((5, lines * blocks, LANES), F32),),
    )[0]
    back = lax.all_to_all(sums, ("bundle", "grid"), split_axis=0, concat_axis=0, tiled=True)
    return call(
        functools.partial(blend_kernel, bundles),
        [(cell_state.shape, F32)],
        (back, request_cell, pore_volume[None, :], cell_state, *indices[2:]),
        scratch=(pltpu.VMEM(cell_state.shape, F32), pltpu.SemaphoreType.DMA((4,))),
        out=pltpu.HBM,
    )[0]


def solution(mesh):
    placed = (
        P(None, "grid"),
        P("grid"),
        P(None, "grid", None, None),
        P("bundle", "grid", None),
        P("bundle", "grid"),
        P("bundle", "grid", None),
        P("bundle", "grid", None),
        P("bundle", None),
        P(),
    )
    return jax.shard_map(
        functools.partial(shards, mesh.shape["bundle"]),
        mesh=mesh,
        in_specs=placed,
        out_specs=P(None, "grid"),
        check_vma=False,
    )
```

```python
import functools

import jax
import jax.numpy as jnp
from jax import lax
from jax.experimental import pallas as pl
from jax.experimental.pallas import tpu as pltpu
from jax.sharding import PartitionSpec as P

SUB = 2
NEWTON = 3
LANES = 128
ROWS = 8
F32 = jnp.float32
BF16 = jnp.bfloat16
VMEM_BYTES = 32 * 1024 * 1024
CHUNKS = 1


def fast_size(owners):
    return 2 if owners % 2 == 0 else 1


def turned_place(owner, owners):
    fast = fast_size(owners)
    return owner % fast * (owners // fast) + owner // fast


def grid_place():
    return lax.axis_index("slow") * lax.axis_size("fast") + lax.axis_index("fast")


def repeat_steps(count, body, carry):
    if count == 1:
        return body(0, carry)
    return lax.fori_loop(0, count, body, carry)


def rounded(value):
    high = value.astype(BF16).astype(F32)
    return high, value - high


def parts(value):
    high = value.astype(BF16)
    return high, (value - high.astype(F32)).astype(BF16)


def split(value):
    return jnp.concatenate(rounded(value), axis=0).astype(BF16)


def select_groups(tiles, relative):
    count = len(tiles)
    results = []
    for i in range(count):
        value = tiles[0]
        for j in range(1, count):
            value = jnp.where(relative == (i + j) % count, tiles[j], value)
        results.append(value)
    return results


def lane_groups(cap, turn):
    groups = LANES // cap
    lane = lax.broadcasted_iota(jnp.int32, (ROWS, LANES), 1)
    return (lane // cap + (2 * groups - lax.rem(turn, groups))) % groups


def pack(rows, cap, turn, relative):
    groups = LANES // cap
    turned = [
        pltpu.roll(rows[g], lax.rem(turn + g, groups) * cap, 1) for g in range(groups)
    ]
    return select_groups(turned, relative)


def unpack(tiles, cap, relative, count):
    found = select_groups(tiles, relative)[:count]
    return [
        found[g] if g == 0 else pltpu.roll(found[g], LANES - g * cap, 1) for g in range(count)
    ]


def exchange_groups(tiles, width):
    tiles = list(tiles)
    lane_group = lax.broadcasted_iota(jnp.int32, tiles[0].shape, 1) // width
    step = 1
    while step < len(tiles):
        keep = (lane_group & step) == 0
        for i in range(len(tiles)):
            if i & step == 0:
                first, second = tiles[i], tiles[i | step]
                tiles[i] = jnp.where(keep, first, pltpu.roll(second, step * width, 1))
                tiles[i | step] = jnp.where(
                    keep, pltpu.roll(first, LANES - step * width, 1), second
                )
        step *= 2
    return tiles


def spread_rows(block, cap):
    groups = block.shape[0]
    wide = jnp.concatenate([block] * groups, axis=1)
    rows = lax.broadcasted_iota(jnp.int32, wide.shape, 0)
    lanes = lax.broadcasted_iota(jnp.int32, wide.shape, 1) // cap
    return jnp.sum(jnp.where(rows == lanes, wide, 0), axis=0, keepdims=True)


def first_kernel(out_ref):
    out_ref[...] = jnp.zeros_like(out_ref)


def pick_index(request_ref, k):
    bundle = lax.axis_index("bundle")
    groups = LANES // request_ref.shape[3]
    cap = request_ref.shape[3]
    block = request_ref[bundle, 0, pl.ds(k * 2 * groups, 2 * groups), :]
    index = jnp.concatenate(
        [spread_rows(block[:groups], cap), spread_rows(block[groups:], cap)], axis=1
    )
    high = jnp.broadcast_to(index // LANES, (ROWS, 2 * LANES))
    hot = (
        (lax.broadcasted_iota(jnp.int32, (LANES, 2 * LANES), 0) == index % LANES)
        .astype(F32)
        .astype(BF16)
    )
    return high, jnp.concatenate([hot, hot], axis=0)


def pick_kernel(cell_ref, request_ref, first_ref, *refs):
    *kept_refs, out_ref = refs
    species, cells = cell_ref.shape
    owners, cap = request_ref.shape[2:]
    groups = LANES // cap
    chunks = owners // (2 * groups)
    highs = cells // LANES
    here = grid_place()
    relative = lane_groups(cap, here)
    cell = cell_ref[...]
    stacked = jnp.concatenate(
        [cell[:, LANES * h : LANES * (h + 1)] for h in range(highs)], axis=0
    )
    left = jnp.concatenate(rounded(stacked), axis=1).astype(BF16)

    def chunk(k, carry):
        first = k * 2 * groups
        if kept_refs:
            high, right = kept_refs[0][...], kept_refs[1][...]
        else:
            high, right = pick_index(request_ref, k)
        product = jnp.dot(left, right, preferred_element_type=F32)
        picked = jnp.zeros((species, 2 * LANES), F32)
        high = jnp.concatenate([high] * (species // ROWS), axis=0)
        for h in range(highs):
            picked = picked + jnp.where(high == h, product[species * h : species * (h + 1)], 0.0)
        blank = jnp.zeros((groups * ROWS - species, 2 * LANES), F32)
        picked = jnp.concatenate([picked, blank], axis=0)
        for half in range(2):
            tiles = pack(
                [
                    picked[ROWS * g : ROWS * (g + 1), LANES * half : LANES * (half + 1)]
                    for g in range(groups)
                ],
                cap,
                here,
                relative,
            )
            for j in range(groups):
                out_ref[turned_place(first + half * groups + j, owners)] = tiles[j]
        return carry

    repeat_steps(chunks, chunk, 0)


def to_segments(values, width):
    groups = LANES // width
    stacked = [value.astype(F32) for value in values]
    if width * len(values) < LANES:
        stacked.append(jnp.zeros((LANES - width * len(values), LANES), F32))
    turned = jnp.transpose(jnp.concatenate(stacked, axis=0))
    times = LANES // groups
    return exchange_groups([turned[times * g : times * (g + 1)] for g in range(groups)], width)


def lines_kernel(
    lines,
    cap,
    table_ref,
    slot_ref,
    length_ref,
    courant_ref,
    flux_ref,
    inflow_ref,
    interaction_ref,
    out_ref,
    rows_ref,
):
    owners = table_ref.shape[0]
    copies = out_ref.shape[0] // owners
    species = inflow_ref.shape[1]
    width = slot_ref.shape[0]
    nodes = width * LANES // lines
    groups = species // ROWS
    all_groups = LANES // cap
    rows = all_groups * ROWS
    blocks = nodes // LANES
    segments = LANES // width
    times = LANES // segments
    chunk_owners = 2 * all_groups
    chunks = owners // chunk_owners
    here, bundle = grid_place(), lax.axis_index("bundle")

    slot = slot_ref[...]
    within = (slot + lax.rem(here, all_groups) * cap) % LANES
    within, half_index, courant, flux = to_segments(
        [within, slot // LANES, courant_ref[...], flux_ref[...]], width
    )[:4]
    scale = 1.0 / (1.0 + courant)
    rows_ref[0] = scale
    rows_ref[1] = courant * scale
    rows_ref[2] = flux
    rows_ref[3] = within
    rows_ref[4] = half_index

    def row(kind, t, depth=ROWS):
        return jnp.broadcast_to(rows_ref[kind, t : t + 1], (depth, LANES))

    index = lax.broadcasted_iota(jnp.int32, (LANES, LANES), 0).astype(F32).astype(BF16)
    one, zero = jnp.ones_like(index), jnp.zeros_like(index)
    columns = []
    for t in range(times):
        lanes = row(3, t, 2 * ROWS).astype(BF16)
        lanes = jnp.concatenate([lanes] * (LANES // (2 * ROWS)), axis=0)
        columns.append(jnp.where(lanes == index, one, zero))
    hot = jnp.concatenate(columns, axis=1)
    half_rows = jnp.concatenate([row(4, t) for t in range(times)], axis=1)

    relative = lane_groups(cap, here)

    def gather(k, state):
        halves = []
        for half in range(2):
            first = k * chunk_owners + half * all_groups
            halves.append(
                jnp.concatenate(
                    unpack(
                        [table_ref[turned_place(first + j, owners)] for j in range(all_groups)], cap, relative, groups
                    ),
                    axis=0,
                )
            )
        left = jnp.concatenate([split(value) for value in halves], axis=0)
        found = jnp.dot(left, hot, preferred_element_type=F32)
        lower = found[:species] + found[species : 2 * species]
        upper = found[2 * species : 3 * species] + found[3 * species :]
        base = lax.convert_element_type(2 * k, F32)
        is_lower, is_upper = half_rows == base, half_rows == base + 1.0
        merged = []
        for g in range(groups):
            part_rows = slice(ROWS * g, ROWS * (g + 1))
            rest = upper[part_rows]
            if chunks > 1:
                rest = jnp.where(is_upper, rest, state[part_rows])
            merged.append(jnp.where(is_lower, lower[part_rows], rest))
        return jnp.concatenate(merged, axis=0)

    start = repeat_steps(
        chunks, gather, jnp.zeros((species, lines * nodes), F32) if chunks > 1 else 0
    )

    lane = lax.broadcasted_iota(jnp.int32, (ROWS, LANES), 1)
    part = lane // width
    block = (lane % width) // lines
    segment = block * segments + part
    line = lane % lines

    def earlier(value, distance):
        major, minor = distance // segments, distance % segments
        near = pltpu.roll(value, minor * width + major * lines, 1)
        if minor == 0:
            return near
        far = pltpu.roll(value, minor * width + (major + 1) * lines, 1)
        return jnp.where(part >= minor, near, far)

    eye = lax.broadcasted_iota(jnp.int32, (species, LANES), 0) == lax.broadcasted_iota(
        jnp.int32, (species, LANES), 1
    )
    padded = jnp.concatenate([inflow_ref[...], jnp.zeros((1, LANES - species), F32)], axis=1)
    column = jnp.sum(jnp.where(eye, padded, 0.0), axis=1, keepdims=True)
    entry = jnp.broadcast_to(column, (species, LANES))
    entry = [entry[ROWS * g : ROWS * (g + 1)] for g in range(groups)]

    first = [None] * groups
    second = [None] * groups
    local, ones, twos = [], [], []
    for t in range(times):
        scale_t, decay_t = row(0, t), row(1, t)
        one = decay_t if t == 0 else decay_t * ones[-1]
        two = scale_t * one if t == 0 else scale_t * one + decay_t * twos[-1]
        ones.append(one)
        twos.append(two)
        for g in range(groups):
            value = start[ROWS * g : ROWS * (g + 1), LANES * t : LANES * (t + 1)] * scale_t
            first[g] = value if t == 0 else value + decay_t * first[g]
            value = scale_t * first[g]
            second[g] = value if t == 0 else value + decay_t * second[g]
            local.append(second[g])

    a, b = ones[-1], twos[-1]
    head = segment == 0
    first = [jnp.where(head, f + a * e, f) for f, e in zip(first, entry)]
    second = [jnp.where(head, s + b * e + a * e, s) for s, e in zip(second, entry)]
    distance = 1
    while distance < blocks * segments:
        run_a, run_b = a, b
        next_first, next_second = first, second
        for k in range(1, 4):
            if k * distance >= blocks * segments:
                break
            opened = segment >= k * distance
            a_open, b_open = jnp.where(opened, run_a, 0.0), jnp.where(opened, run_b, 0.0)
            ahead = [earlier(f, k * distance) for f in first]
            next_first = [n + a_open * f for n, f in zip(next_first, ahead)]
            next_second = [
                n + b_open * f + a_open * earlier(s, k * distance)
                for n, s, f in zip(next_second, second, ahead)
            ]
            a_ahead = earlier(a, k * distance)
            run_b = run_b * a_ahead + run_a * earlier(b, k * distance)
            run_a = run_a * a_ahead
        first, second = next_first, next_second
        a, b = run_a, run_b
        distance *= 4
    carry_one = [jnp.where(head, e, earlier(f, 1)) for e, f in zip(entry, first)]
    carry_two = [jnp.where(head, e, earlier(s, 1)) for e, s in zip(entry, second)]
    columns = [
        jnp.concatenate(
            [
                local[t * groups + g] + twos[t] * carry_one[g] + ones[t] * carry_two[g]
                for g in range(groups)
            ],
            axis=0,
        )
        for t in range(times)
    ]

    matrix_high, matrix_low = rounded(interaction_ref[...])
    blank = jnp.zeros_like(matrix_high)
    left = jnp.concatenate(
        [
            jnp.concatenate(
                [matrix_high, blank, matrix_low, blank, matrix_high, blank], axis=1
            ),
            jnp.concatenate(
                [blank, matrix_high, blank, matrix_low, blank, matrix_high], axis=1
            ),
        ],
        axis=0,
    ).astype(BF16)
    half = times // 2
    depth = half // CHUNKS
    bases = [
        jnp.concatenate(
            [
                jnp.concatenate(columns[offset + c * depth : offset + (c + 1) * depth], axis=1)
                for offset in (0, half)
            ],
            axis=0,
        )
        for c in range(CHUNKS)
    ]
    iterates = list(bases)
    for step in range(NEWTON):
        for c in range(CHUNKS):
            high, low = parts(jnp.tanh(iterates[c]))
            right = jnp.concatenate([high, high, low], axis=0)
            iterates[c] = bases[c] - jnp.dot(left, right, preferred_element_type=F32)

    length = jnp.zeros((ROWS, LANES), jnp.int32)
    for one_line in range(lines):
        one_length = jnp.broadcast_to(length_ref[:, one_line : one_line + 1], (ROWS, LANES))
        length = jnp.where(line == one_line, one_length, length)
    node = block * LANES + part * times
    top = lax.broadcasted_iota(jnp.int32, (ROWS, LANES), 0) == 0
    pieces = []
    for t in range(times):
        weight = jnp.where(node + t < length, row(2, t), 0.0)
        chunk, place = t % half // depth, t % half % depth
        found = iterates[chunk][
            t // half * species : (t // half + 1) * species, LANES * place : LANES * (place + 1)
        ]
        scaled = [found[ROWS * g : ROWS * (g + 1)] * weight for g in range(groups)]
        scaled.append(jnp.where(top, weight, 0.0))
        pieces.append(jnp.concatenate(scaled, axis=0))
    left = split(jnp.concatenate(pieces, axis=1))
    relative = lane_groups(cap, here + bundle)

    half_rows = jnp.concatenate([half_rows] * 2, axis=0).astype(BF16)

    def scatter(k, carry):
        base = lax.convert_element_type(2 * k, F32)
        masked = []
        for half in range(2):
            chosen = half_rows == (base + half).astype(BF16)
            for r in range(0, 2 * rows, 2 * ROWS):
                piece = left[r : r + 2 * ROWS]
                masked.append(jnp.where(chosen, piece, jnp.zeros_like(piece)))
        sums = lax.dot_general(
            jnp.concatenate(masked, axis=0),
            hot,
            (((1,), (1,)), ((), ())),
            preferred_element_type=F32,
        )
        for half in range(2):
            both = sums[2 * rows * half : 2 * rows * (half + 1)]
            both = both[:rows] + both[rows:]
            tiles = pack(
                [both[ROWS * g : ROWS * (g + 1)] for g in range(all_groups)],
                cap,
                bundle,
                relative,
            )
            for j in range(all_groups):
                owner = k * chunk_owners + half * all_groups + j
                for copy in range(copies):
                    out_ref[copy * owners + owner] = tiles[j]
        return carry

    repeat_steps(chunks, scatter, 0)


def blend_index(request_ref, k):
    bundles, cap = request_ref.shape[0], request_ref.shape[3]
    all_groups = LANES // cap
    width = 2 * LANES
    here = grid_place()
    sublane = lax.broadcasted_iota(jnp.int32, (ROWS, LANES), 0)
    indices = []
    for t in range(bundles // all_groups):
        straight = jnp.concatenate(
            [
                request_ref[
                    t * all_groups
                    + lax.rem(x + all_groups - lax.rem(here, all_groups), all_groups),
                    0,
                    pl.ds(k * ROWS, ROWS),
                    :,
                ]
                for x in range(all_groups)
            ],
            axis=1,
        )
        block = straight
        for turn in range(1, all_groups):
            block = jnp.where(
                sublane % all_groups == turn, pltpu.roll(straight, turn * cap, 1), block
            )
        indices += [block[d : d + 1] for d in range(ROWS)]
    index = jnp.concatenate(indices, axis=1)
    entries = index.shape[1]
    high = jnp.broadcast_to(index // width, (2 * ROWS, entries)).astype(F32).astype(BF16)
    low = jnp.broadcast_to(index % width, (2 * ROWS, entries)).astype(F32).astype(BF16)
    low = jnp.concatenate([low] * (width // (2 * ROWS)), axis=0)
    place = lax.broadcasted_iota(jnp.int32, (width, entries), 0).astype(F32).astype(BF16)
    return high, jnp.where(place == low, jnp.ones_like(place), jnp.zeros_like(place))


def index_kernel(
    request_ref, first_ref, length_ref, inflow_ref, pick_high, pick_hot, blend_high, blend_hot
):
    pick_high[...], pick_hot[...] = pick_index(request_ref, 0)
    blend_high[...], blend_hot[...] = blend_index(request_ref, 0)


def blend_kernel(bundles, sums_ref, request_ref, pore_ref, cell_ref, *refs):
    *kept_refs, out_hbm, out_ref, out_sem = refs
    owners = sums_ref.shape[0] // bundles
    species, cells = cell_ref.shape
    cap = request_ref.shape[3]
    all_groups = LANES // cap
    groups = species // ROWS
    width = 2 * LANES
    highs = cells // width
    chunks = owners // ROWS
    here = grid_place()

    def chunk(k, total):
        values, weights = [], []
        for t in range(bundles // all_groups):
            for d in range(ROWS):
                found = unpack(
                    [
                        sums_ref[(t * all_groups + j) * owners + k * ROWS + d]
                        for j in range(all_groups)
                    ],
                    cap,
                    lane_groups(cap, here + d),
                    all_groups,
                )
                weights.append(found[groups][:1])
                values.append(jnp.concatenate(found[:groups], axis=0))
        both = split(jnp.concatenate(values, axis=1))
        weight_high, weight_low = rounded(jnp.concatenate(weights, axis=1))
        if kept_refs:
            high, hot = kept_refs[0][...], kept_refs[1][...]
        else:
            high, hot = blend_index(request_ref, k)
        entries = hot.shape[1]
        zero = jnp.zeros((2 * ROWS, entries), BF16)
        pieces = []
        for first in range(0, highs, 2 * ROWS):
            mask = high == (
                lax.broadcasted_iota(jnp.int32, (2 * ROWS, entries), 0) + first
            ).astype(F32).astype(BF16)
            for part in (weight_high, weight_low):
                row = jnp.broadcast_to(part, (2 * ROWS, entries)).astype(BF16)
                pieces.append(jnp.where(mask, row, zero))
        for h in range(highs):
            mask = high == jnp.array(h, BF16)
            for r in range(2 * species // (2 * ROWS)):
                pieces.append(jnp.where(mask, both[2 * ROWS * r : 2 * ROWS * (r + 1)], zero))
        half = (len(pieces) + len(pieces) // 2 % 2) // 2
        products = [
            lax.dot_general(
                jnp.concatenate(some, axis=0),
                hot,
                (((1,), (1,)), ((), ())),
                preferred_element_type=F32,
            )
            for some in (pieces[:half], pieces[half:])
        ]
        product = jnp.concatenate(products, axis=0)
        return product if chunks == 1 else total + product

    flux_rows = -(-highs // (2 * ROWS)) * 4 * ROWS
    total = repeat_steps(
        chunks,
        chunk,
        jnp.zeros((highs * 2 * species + flux_rows, width), F32) if chunks > 1 else 0,
    )
    flux, total = total[:flux_rows], total[flux_rows:]
    copies = []
    stride = max(highs // 4, 1)
    for h in range(highs):
        part = total[2 * species * h : 2 * species * (h + 1)]
        part = part[:species] + part[species:]
        row = h // (2 * ROWS) * 4 * ROWS + h % (2 * ROWS)
        pore = pore_ref[:, width * h : width * (h + 1)]
        inverse = 1.0 / (pore + flux[row : row + 1] + flux[row + 2 * ROWS : row + 2 * ROWS + 1])
        columns = pl.ds(width * h, width)
        out_ref[:, columns] = (pore * cell_ref[:, columns] + part) * inverse
        if h % stride == stride - 1:
            columns = pl.ds(width * (h - stride + 1), stride * width)
            copies.append(
                pltpu.make_async_copy(
                    out_ref.at[:, columns], out_hbm.at[:, columns], out_sem.at[h // stride]
                )
            )
            copies[-1].start()
    for copy in copies:
        copy.wait()


def call(kernel, shapes, operands, kinds={}, scratch=(), out=pltpu.VMEM, flops=0):
    return pl.pallas_call(
        kernel,
        out_shape=[jax.ShapeDtypeStruct(shape, kind) for shape, kind in shapes],
        in_specs=[
            pl.BlockSpec(memory_space=kinds.get(i, pltpu.VMEM)) for i in range(len(operands))
        ],
        out_specs=[pl.BlockSpec(memory_space=out)] * len(shapes),
        scratch_shapes=list(scratch),
        compiler_params=pltpu.CompilerParams(vmem_limit_bytes=VMEM_BYTES),
        cost_estimate=pl.CostEstimate(flops=flops, bytes_accessed=0, transcendentals=0),
    )(*operands)


def shards(
    bundles,
    cell_state,
    pore_volume,
    request_cell,
    node_slot,
    line_length,
    courant,
    flux_weight,
    inflow,
    interaction,
):
    owners, cap = request_cell.shape[2:]
    first = call(first_kernel, [((ROWS, LANES), F32)], (), flops=10**9)[0]
    indices = []
    if owners == ROWS and owners * cap == 2 * LANES:
        entries = owners * bundles * cap
        indices = call(
            index_kernel,
            [
                ((ROWS, 2 * LANES), jnp.int32),
                ((2 * LANES, 2 * LANES), BF16),
                ((2 * ROWS, entries), BF16),
                ((2 * LANES, entries), BF16),
            ],
            (request_cell, first, line_length, inflow),
        )
    outgoing = call(
        pick_kernel,
        [((owners, ROWS, LANES), F32)],
        (cell_state, request_cell, first, *indices[:2]),
    )[0]
    table = lax.all_to_all(outgoing, ("fast", "slow"), split_axis=0, concat_axis=0, tiled=True)
    lines, nodes = node_slot.shape[1:]
    blocks = nodes // LANES

    def by_block(value):
        return value.reshape(lines, blocks, LANES).swapaxes(0, 1).reshape(blocks * lines, LANES)

    sums = call(
        functools.partial(lines_kernel, lines, cap),
        [((owners * bundles, ROWS, LANES), F32)],
        (
            table,
            by_block(node_slot),
            line_length,
            by_block(courant),
            by_block(flux_weight),
            inflow,
            interaction,
        ),
        scratch=(pltpu.VMEM((5, lines * blocks, LANES), F32),),
    )[0]
    back = lax.all_to_all(sums, ("bundle", "slow", "fast"), split_axis=0, concat_axis=0, tiled=True)
    return call(
        functools.partial(blend_kernel, bundles),
        [(cell_state.shape, F32)],
        (back, request_cell, pore_volume[None, :], cell_state, *indices[2:]),
        scratch=(pltpu.VMEM(cell_state.shape, F32), pltpu.SemaphoreType.DMA((4,))),
        out=pltpu.HBM,
    )[0]


def solution(mesh):
    owners, bundles = mesh.shape["grid"], mesh.shape["bundle"]
    fast = fast_size(owners)
    devices = mesh.devices.reshape(owners // fast, fast, bundles)
    finer = jax.sharding.Mesh(devices, ("slow", "fast", "bundle"))
    grid = ("slow", "fast")
    placed = (
        P(None, grid),
        P(grid),
        P(None, grid, None, None),
        P("bundle", grid, None),
        P("bundle", grid),
        P("bundle", grid, None),
        P("bundle", grid, None),
        P("bundle", None),
        P(),
    )
    return jax.shard_map(
        functools.partial(shards, bundles),
        mesh=finer,
        in_specs=placed,
        out_specs=P(None, grid),
        check_vma=False,
    )
```

```python
import functools

import jax
import jax.numpy as jnp
from jax import lax
from jax.experimental import pallas as pl
from jax.experimental.pallas import tpu as pltpu
from jax.sharding import PartitionSpec as P

SUB = 2
NEWTON = 3
LANES = 128
ROWS = 8
F32 = jnp.float32
BF16 = jnp.bfloat16
VMEM_BYTES = 32 * 1024 * 1024
CHUNKS = 1


def fast_size(owners):
    return 2 if owners % 2 == 0 else 1


def turned_place(owner, owners):
    fast = fast_size(owners)
    return owner % fast * (owners // fast) + owner // fast


def grid_place():
    return lax.axis_index("slow") * lax.axis_size("fast") + lax.axis_index("fast")


def repeat_steps(count, body, carry):
    if count == 1:
        return body(0, carry)
    return lax.fori_loop(0, count, body, carry)


def rounded(value):
    high = value.astype(BF16).astype(F32)
    return high, value - high


def parts(value):
    high = value.astype(BF16)
    return high, (value - high.astype(F32)).astype(BF16)


def split(value):
    return jnp.concatenate(rounded(value), axis=0).astype(BF16)


def select_groups(tiles, relative):
    count = len(tiles)
    results = []
    for i in range(count):
        value = tiles[0]
        for j in range(1, count):
            value = jnp.where(relative == (i + j) % count, tiles[j], value)
        results.append(value)
    return results


def lane_groups(cap, turn):
    groups = LANES // cap
    lane = lax.broadcasted_iota(jnp.int32, (ROWS, LANES), 1)
    return (lane // cap + (2 * groups - lax.rem(turn, groups))) % groups


def pack(rows, cap, turn, relative):
    groups = LANES // cap
    turned = [
        pltpu.roll(rows[g], lax.rem(turn + g, groups) * cap, 1) for g in range(groups)
    ]
    return select_groups(turned, relative)


def unpack(tiles, cap, relative, count):
    found = select_groups(tiles, relative)[:count]
    return [
        found[g] if g == 0 else pltpu.roll(found[g], LANES - g * cap, 1) for g in range(count)
    ]


def exchange_groups(tiles, width):
    tiles = list(tiles)
    lane_group = lax.broadcasted_iota(jnp.int32, tiles[0].shape, 1) // width
    step = 1
    while step < len(tiles):
        keep = (lane_group & step) == 0
        for i in range(len(tiles)):
            if i & step == 0:
                first, second = tiles[i], tiles[i | step]
                tiles[i] = jnp.where(keep, first, pltpu.roll(second, step * width, 1))
                tiles[i | step] = jnp.where(
                    keep, pltpu.roll(first, LANES - step * width, 1), second
                )
        step *= 2
    return tiles


def spread_rows(block, cap):
    groups = block.shape[0]
    wide = jnp.concatenate([block] * groups, axis=1)
    rows = lax.broadcasted_iota(jnp.int32, wide.shape, 0)
    lanes = lax.broadcasted_iota(jnp.int32, wide.shape, 1) // cap
    return jnp.sum(jnp.where(rows == lanes, wide, 0), axis=0, keepdims=True)


def first_kernel(out_ref):
    out_ref[...] = jnp.zeros_like(out_ref)


def pick_index(request_ref, k):
    bundle = lax.axis_index("bundle")
    groups = LANES // request_ref.shape[3]
    cap = request_ref.shape[3]
    block = request_ref[bundle, 0, pl.ds(k * 2 * groups, 2 * groups), :]
    index = jnp.concatenate(
        [spread_rows(block[:groups], cap), spread_rows(block[groups:], cap)], axis=1
    )
    high = jnp.broadcast_to(index // LANES, (ROWS, 2 * LANES))
    hot = (
        (lax.broadcasted_iota(jnp.int32, (LANES, 2 * LANES), 0) == index % LANES)
        .astype(F32)
        .astype(BF16)
    )
    return high, jnp.concatenate([hot, hot], axis=0)


def pick_kernel(cell_ref, request_ref, first_ref, *refs):
    *kept_refs, out_ref = refs
    species, cells = cell_ref.shape
    owners, cap = request_ref.shape[2:]
    groups = LANES // cap
    chunks = owners // (2 * groups)
    highs = cells // LANES
    here = grid_place()
    relative = lane_groups(cap, here)
    cell = cell_ref[...]
    stacked = jnp.concatenate(
        [cell[:, LANES * h : LANES * (h + 1)] for h in range(highs)], axis=0
    )
    left = jnp.concatenate(rounded(stacked), axis=1).astype(BF16)

    def chunk(k, carry):
        first = k * 2 * groups
        if kept_refs:
            high, right = kept_refs[0][...], kept_refs[1][...]
        else:
            high, right = pick_index(request_ref, k)
        product = jnp.dot(left, right, preferred_element_type=F32)
        picked = jnp.zeros((species, 2 * LANES), F32)
        high = jnp.concatenate([high] * (species // ROWS), axis=0)
        for h in range(highs):
            picked = picked + jnp.where(high == h, product[species * h : species * (h + 1)], 0.0)
        blank = jnp.zeros((groups * ROWS - species, 2 * LANES), F32)
        picked = jnp.concatenate([picked, blank], axis=0)
        for half in range(2):
            tiles = pack(
                [
                    picked[ROWS * g : ROWS * (g + 1), LANES * half : LANES * (half + 1)]
                    for g in range(groups)
                ],
                cap,
                here,
                relative,
            )
            for j in range(groups):
                out_ref[turned_place(first + half * groups + j, owners)] = tiles[j]
        return carry

    repeat_steps(chunks, chunk, 0)


def to_segments(values, width):
    groups = LANES // width
    stacked = [value.astype(F32) for value in values]
    if width * len(values) < LANES:
        stacked.append(jnp.zeros((LANES - width * len(values), LANES), F32))
    turned = jnp.transpose(jnp.concatenate(stacked, axis=0))
    times = LANES // groups
    return exchange_groups([turned[times * g : times * (g + 1)] for g in range(groups)], width)


def lines_kernel(
    lines,
    cap,
    table_ref,
    slot_ref,
    length_ref,
    courant_ref,
    flux_ref,
    inflow_ref,
    interaction_ref,
    out_ref,
    rows_ref,
):
    owners = table_ref.shape[0]
    copies = out_ref.shape[0] // owners
    species = inflow_ref.shape[1]
    width = slot_ref.shape[0]
    nodes = width * LANES // lines
    groups = species // ROWS
    all_groups = LANES // cap
    rows = all_groups * ROWS
    blocks = nodes // LANES
    segments = LANES // width
    times = LANES // segments
    chunk_owners = 2 * all_groups
    chunks = owners // chunk_owners
    here, bundle = grid_place(), lax.axis_index("bundle")

    slot = slot_ref[...]
    within = (slot + lax.rem(here, all_groups) * cap) % LANES
    within, half_index, courant, flux = to_segments(
        [within, slot // LANES, courant_ref[...], flux_ref[...]], width
    )[:4]
    scale = 1.0 / (1.0 + courant)
    rows_ref[0] = scale
    rows_ref[1] = courant * scale
    rows_ref[2] = flux
    rows_ref[3] = within
    rows_ref[4] = half_index

    def row(kind, t, depth=ROWS):
        return jnp.broadcast_to(rows_ref[kind, t : t + 1], (depth, LANES))

    index = lax.broadcasted_iota(jnp.int32, (LANES, LANES), 0).astype(F32).astype(BF16)
    one, zero = jnp.ones_like(index), jnp.zeros_like(index)
    columns = []
    for t in range(times):
        lanes = row(3, t, 2 * ROWS).astype(BF16)
        lanes = jnp.concatenate([lanes] * (LANES // (2 * ROWS)), axis=0)
        columns.append(jnp.where(lanes == index, one, zero))
    hot = jnp.concatenate(columns, axis=1)
    half_rows = jnp.concatenate([row(4, t) for t in range(times)], axis=1)

    relative = lane_groups(cap, here)

    def gather(k, state):
        halves = []
        for half in range(2):
            first = k * chunk_owners + half * all_groups
            halves.append(
                jnp.concatenate(
                    unpack(
                        [table_ref[turned_place(first + j, owners)] for j in range(all_groups)], cap, relative, groups
                    ),
                    axis=0,
                )
            )
        left = jnp.concatenate([split(value) for value in halves], axis=0)
        found = jnp.dot(left, hot, preferred_element_type=F32)
        lower = found[:species] + found[species : 2 * species]
        upper = found[2 * species : 3 * species] + found[3 * species :]
        base = lax.convert_element_type(2 * k, F32)
        is_lower, is_upper = half_rows == base, half_rows == base + 1.0
        merged = []
        for g in range(groups):
            part_rows = slice(ROWS * g, ROWS * (g + 1))
            rest = upper[part_rows]
            if chunks > 1:
                rest = jnp.where(is_upper, rest, state[part_rows])
            merged.append(jnp.where(is_lower, lower[part_rows], rest))
        return jnp.concatenate(merged, axis=0)

    start = repeat_steps(
        chunks, gather, jnp.zeros((species, lines * nodes), F32) if chunks > 1 else 0
    )

    lane = lax.broadcasted_iota(jnp.int32, (ROWS, LANES), 1)
    part = lane // width
    block = (lane % width) // lines
    segment = block * segments + part
    line = lane % lines

    def earlier(value, distance):
        major, minor = distance // segments, distance % segments
        near = pltpu.roll(value, minor * width + major * lines, 1)
        if minor == 0:
            return near
        far = pltpu.roll(value, minor * width + (major + 1) * lines, 1)
        return jnp.where(part >= minor, near, far)

    eye = lax.broadcasted_iota(jnp.int32, (species, LANES), 0) == lax.broadcasted_iota(
        jnp.int32, (species, LANES), 1
    )
    padded = jnp.concatenate([inflow_ref[...], jnp.zeros((1, LANES - species), F32)], axis=1)
    column = jnp.sum(jnp.where(eye, padded, 0.0), axis=1, keepdims=True)
    entry = jnp.broadcast_to(column, (species, LANES))
    entry = [entry[ROWS * g : ROWS * (g + 1)] for g in range(groups)]

    first = [None] * groups
    second = [None] * groups
    local, ones, twos = [], [], []
    for t in range(times):
        scale_t, decay_t = row(0, t), row(1, t)
        one = decay_t if t == 0 else decay_t * ones[-1]
        two = scale_t * one if t == 0 else scale_t * one + decay_t * twos[-1]
        ones.append(one)
        twos.append(two)
        for g in range(groups):
            value = start[ROWS * g : ROWS * (g + 1), LANES * t : LANES * (t + 1)] * scale_t
            first[g] = value if t == 0 else value + decay_t * first[g]
            value = scale_t * first[g]
            second[g] = value if t == 0 else value + decay_t * second[g]
            local.append(second[g])

    a, b = ones[-1], twos[-1]
    head = segment == 0
    first = [jnp.where(head, f + a * e, f) for f, e in zip(first, entry)]
    second = [jnp.where(head, s + b * e + a * e, s) for s, e in zip(second, entry)]
    distance = 1
    while distance < blocks * segments:
        run_a, run_b = a, b
        next_first, next_second = first, second
        for k in range(1, 4):
            if k * distance >= blocks * segments:
                break
            opened = segment >= k * distance
            a_open, b_open = jnp.where(opened, run_a, 0.0), jnp.where(opened, run_b, 0.0)
            ahead = [earlier(f, k * distance) for f in first]
            next_first = [n + a_open * f for n, f in zip(next_first, ahead)]
            next_second = [
                n + b_open * f + a_open * earlier(s, k * distance)
                for n, s, f in zip(next_second, second, ahead)
            ]
            a_ahead = earlier(a, k * distance)
            run_b = run_b * a_ahead + run_a * earlier(b, k * distance)
            run_a = run_a * a_ahead
        first, second = next_first, next_second
        a, b = run_a, run_b
        distance *= 4
    carry_one = [jnp.where(head, e, earlier(f, 1)) for e, f in zip(entry, first)]
    carry_two = [jnp.where(head, e, earlier(s, 1)) for e, s in zip(entry, second)]
    columns = [
        jnp.concatenate(
            [
                local[t * groups + g] + twos[t] * carry_one[g] + ones[t] * carry_two[g]
                for g in range(groups)
            ],
            axis=0,
        )
        for t in range(times)
    ]

    matrix_high, matrix_low = rounded(interaction_ref[...])
    blank = jnp.zeros_like(matrix_high)
    left = jnp.concatenate(
        [
            jnp.concatenate(
                [matrix_high, blank, matrix_low, blank, matrix_high, blank], axis=1
            ),
            jnp.concatenate(
                [blank, matrix_high, blank, matrix_low, blank, matrix_high], axis=1
            ),
        ],
        axis=0,
    ).astype(BF16)
    half = times // 2
    depth = half // CHUNKS
    bases = [
        jnp.concatenate(
            [
                jnp.concatenate(columns[offset + c * depth : offset + (c + 1) * depth], axis=1)
                for offset in (0, half)
            ],
            axis=0,
        )
        for c in range(CHUNKS)
    ]
    iterates = list(bases)
    for step in range(NEWTON):
        for c in range(CHUNKS):
            high, low = parts(jnp.tanh(iterates[c]))
            right = jnp.concatenate([high, high, low], axis=0)
            iterates[c] = bases[c] - jnp.dot(left, right, preferred_element_type=F32)

    length = jnp.zeros((ROWS, LANES), jnp.int32)
    for one_line in range(lines):
        one_length = jnp.broadcast_to(length_ref[:, one_line : one_line + 1], (ROWS, LANES))
        length = jnp.where(line == one_line, one_length, length)
    node = block * LANES + part * times
    top = lax.broadcasted_iota(jnp.int32, (ROWS, LANES), 0) == 0
    pieces = []
    for t in range(times):
        weight = jnp.where(node + t < length, row(2, t), 0.0)
        chunk, place = t % half // depth, t % half % depth
        found = iterates[chunk][
            t // half * species : (t // half + 1) * species, LANES * place : LANES * (place + 1)
        ]
        scaled = [found[ROWS * g : ROWS * (g + 1)] * weight for g in range(groups)]
        scaled.append(jnp.where(top, weight, 0.0))
        pieces.append(jnp.concatenate(scaled, axis=0))
    left = split(jnp.concatenate(pieces, axis=1))
    relative = lane_groups(cap, here + bundle)

    half_rows = jnp.concatenate([half_rows] * 2, axis=0).astype(BF16)

    def scatter(k, carry):
        base = lax.convert_element_type(2 * k, F32)
        masked = []
        for half in range(2):
            chosen = half_rows == (base + half).astype(BF16)
            for r in range(0, 2 * rows, 2 * ROWS):
                piece = left[r : r + 2 * ROWS]
                masked.append(jnp.where(chosen, piece, jnp.zeros_like(piece)))
        sums = lax.dot_general(
            jnp.concatenate(masked, axis=0),
            hot,
            (((1,), (1,)), ((), ())),
            preferred_element_type=F32,
        )
        for half in range(2):
            both = sums[2 * rows * half : 2 * rows * (half + 1)]
            both = both[:rows] + both[rows:]
            tiles = pack(
                [both[ROWS * g : ROWS * (g + 1)] for g in range(all_groups)],
                cap,
                bundle,
                relative,
            )
            for j in range(all_groups):
                owner = k * chunk_owners + half * all_groups + j
                for copy in range(copies):
                    out_ref[copy * owners + turned_place(owner, owners)] = tiles[j]
        return carry

    repeat_steps(chunks, scatter, 0)


def blend_index(request_ref, k):
    bundles, cap = request_ref.shape[0], request_ref.shape[3]
    all_groups = LANES // cap
    width = 2 * LANES
    here = grid_place()
    sublane = lax.broadcasted_iota(jnp.int32, (ROWS, LANES), 0)
    indices = []
    for t in range(bundles // all_groups):
        straight = jnp.concatenate(
            [
                request_ref[
                    t * all_groups
                    + lax.rem(x + all_groups - lax.rem(here, all_groups), all_groups),
                    0,
                    pl.ds(k * ROWS, ROWS),
                    :,
                ]
                for x in range(all_groups)
            ],
            axis=1,
        )
        block = straight
        for turn in range(1, all_groups):
            block = jnp.where(
                sublane % all_groups == turn, pltpu.roll(straight, turn * cap, 1), block
            )
        indices += [block[d : d + 1] for d in range(ROWS)]
    index = jnp.concatenate(indices, axis=1)
    entries = index.shape[1]
    high = jnp.broadcast_to(index // width, (2 * ROWS, entries)).astype(F32).astype(BF16)
    low = jnp.broadcast_to(index % width, (2 * ROWS, entries)).astype(F32).astype(BF16)
    low = jnp.concatenate([low] * (width // (2 * ROWS)), axis=0)
    place = lax.broadcasted_iota(jnp.int32, (width, entries), 0).astype(F32).astype(BF16)
    return high, jnp.where(place == low, jnp.ones_like(place), jnp.zeros_like(place))


def index_kernel(
    request_ref, first_ref, length_ref, inflow_ref, pick_high, pick_hot, blend_high, blend_hot
):
    pick_high[...], pick_hot[...] = pick_index(request_ref, 0)
    blend_high[...], blend_hot[...] = blend_index(request_ref, 0)


def blend_kernel(bundles, sums_ref, request_ref, pore_ref, cell_ref, *refs):
    *kept_refs, out_hbm, out_ref, out_sem = refs
    owners = sums_ref.shape[0] // bundles
    species, cells = cell_ref.shape
    cap = request_ref.shape[3]
    all_groups = LANES // cap
    groups = species // ROWS
    width = 2 * LANES
    highs = cells // width
    chunks = owners // ROWS
    here = grid_place()

    def chunk(k, total):
        values, weights = [], []
        for t in range(bundles // all_groups):
            for d in range(ROWS):
                found = unpack(
                    [
                        sums_ref[(t * all_groups + j) * owners + turned_place(k * ROWS + d, owners)]
                        for j in range(all_groups)
                    ],
                    cap,
                    lane_groups(cap, here + d),
                    all_groups,
                )
                weights.append(found[groups][:1])
                values.append(jnp.concatenate(found[:groups], axis=0))
        both = split(jnp.concatenate(values, axis=1))
        weight_high, weight_low = rounded(jnp.concatenate(weights, axis=1))
        if kept_refs:
            high, hot = kept_refs[0][...], kept_refs[1][...]
        else:
            high, hot = blend_index(request_ref, k)
        entries = hot.shape[1]
        zero = jnp.zeros((2 * ROWS, entries), BF16)
        pieces = []
        for first in range(0, highs, 2 * ROWS):
            mask = high == (
                lax.broadcasted_iota(jnp.int32, (2 * ROWS, entries), 0) + first
            ).astype(F32).astype(BF16)
            for part in (weight_high, weight_low):
                row = jnp.broadcast_to(part, (2 * ROWS, entries)).astype(BF16)
                pieces.append(jnp.where(mask, row, zero))
        for h in range(highs):
            mask = high == jnp.array(h, BF16)
            for r in range(2 * species // (2 * ROWS)):
                pieces.append(jnp.where(mask, both[2 * ROWS * r : 2 * ROWS * (r + 1)], zero))
        half = (len(pieces) + len(pieces) // 2 % 2) // 2
        products = [
            lax.dot_general(
                jnp.concatenate(some, axis=0),
                hot,
                (((1,), (1,)), ((), ())),
                preferred_element_type=F32,
            )
            for some in (pieces[:half], pieces[half:])
        ]
        product = jnp.concatenate(products, axis=0)
        return product if chunks == 1 else total + product

    flux_rows = -(-highs // (2 * ROWS)) * 4 * ROWS
    total = repeat_steps(
        chunks,
        chunk,
        jnp.zeros((highs * 2 * species + flux_rows, width), F32) if chunks > 1 else 0,
    )
    flux, total = total[:flux_rows], total[flux_rows:]
    copies = []
    stride = max(highs // 4, 1)
    for h in range(highs):
        part = total[2 * species * h : 2 * species * (h + 1)]
        part = part[:species] + part[species:]
        row = h // (2 * ROWS) * 4 * ROWS + h % (2 * ROWS)
        pore = pore_ref[:, width * h : width * (h + 1)]
        inverse = 1.0 / (pore + flux[row : row + 1] + flux[row + 2 * ROWS : row + 2 * ROWS + 1])
        columns = pl.ds(width * h, width)
        out_ref[:, columns] = (pore * cell_ref[:, columns] + part) * inverse
        if h % stride == stride - 1:
            columns = pl.ds(width * (h - stride + 1), stride * width)
            copies.append(
                pltpu.make_async_copy(
                    out_ref.at[:, columns], out_hbm.at[:, columns], out_sem.at[h // stride]
                )
            )
            copies[-1].start()
    for copy in copies:
        copy.wait()


def call(kernel, shapes, operands, kinds={}, scratch=(), out=pltpu.VMEM, flops=0):
    return pl.pallas_call(
        kernel,
        out_shape=[jax.ShapeDtypeStruct(shape, kind) for shape, kind in shapes],
        in_specs=[
            pl.BlockSpec(memory_space=kinds.get(i, pltpu.VMEM)) for i in range(len(operands))
        ],
        out_specs=[pl.BlockSpec(memory_space=out)] * len(shapes),
        scratch_shapes=list(scratch),
        compiler_params=pltpu.CompilerParams(vmem_limit_bytes=VMEM_BYTES),
        cost_estimate=pl.CostEstimate(flops=flops, bytes_accessed=0, transcendentals=0),
    )(*operands)


def shards(
    bundles,
    cell_state,
    pore_volume,
    request_cell,
    node_slot,
    line_length,
    courant,
    flux_weight,
    inflow,
    interaction,
):
    owners, cap = request_cell.shape[2:]
    first = call(first_kernel, [((ROWS, LANES), F32)], (), flops=10**9)[0]
    indices = []
    if owners == ROWS and owners * cap == 2 * LANES:
        entries = owners * bundles * cap
        indices = call(
            index_kernel,
            [
                ((ROWS, 2 * LANES), jnp.int32),
                ((2 * LANES, 2 * LANES), BF16),
                ((2 * ROWS, entries), BF16),
                ((2 * LANES, entries), BF16),
            ],
            (request_cell, first, line_length, inflow),
        )
    outgoing = call(
        pick_kernel,
        [((owners, ROWS, LANES), F32)],
        (cell_state, request_cell, first, *indices[:2]),
    )[0]
    table = lax.all_to_all(outgoing, ("fast", "slow"), split_axis=0, concat_axis=0, tiled=True)
    lines, nodes = node_slot.shape[1:]
    blocks = nodes // LANES

    def by_block(value):
        return value.reshape(lines, blocks, LANES).swapaxes(0, 1).reshape(blocks * lines, LANES)

    sums = call(
        functools.partial(lines_kernel, lines, cap),
        [((owners * bundles, ROWS, LANES), F32)],
        (
            table,
            by_block(node_slot),
            line_length,
            by_block(courant),
            by_block(flux_weight),
            inflow,
            interaction,
        ),
        scratch=(pltpu.VMEM((5, lines * blocks, LANES), F32),),
    )[0]
    back = lax.all_to_all(sums, ("bundle", "fast", "slow"), split_axis=0, concat_axis=0, tiled=True)
    return call(
        functools.partial(blend_kernel, bundles),
        [(cell_state.shape, F32)],
        (back, request_cell, pore_volume[None, :], cell_state, *indices[2:]),
        scratch=(pltpu.VMEM(cell_state.shape, F32), pltpu.SemaphoreType.DMA((4,))),
        out=pltpu.HBM,
    )[0]


def solution(mesh):
    owners, bundles = mesh.shape["grid"], mesh.shape["bundle"]
    fast = fast_size(owners)
    devices = mesh.devices.reshape(owners // fast, fast, bundles)
    finer = jax.sharding.Mesh(devices, ("slow", "fast", "bundle"))
    grid = ("slow", "fast")
    placed = (
        P(None, grid),
        P(grid),
        P(None, grid, None, None),
        P("bundle", grid, None),
        P("bundle", grid),
        P("bundle", grid, None),
        P("bundle", grid, None),
        P("bundle", None),
        P(),
    )
    return jax.shard_map(
        functools.partial(shards, bundles),
        mesh=finer,
        in_specs=placed,
        out_specs=P(None, grid),
        check_vma=False,
    )
```
